256 devices in a mesh: band: 64 (over z, y, core), pw: 4 (over x).
Axes of the slice: x: 4, y: 4, z: 8, core: 2. Of those that a mesh axis runs over, the one named last changes fastest.
Arguments:
- densities: float32 [2, 1024, 10240], P(None, 'band', 'pw'), may hold values from -6 to 6
- screened: float32 [2, 4, 2560, 10240], P(None, None, 'band', 'pw'), may hold values from -0.0625 to 0.0625
- pairs: int32 [256, 2], replicated, may hold values from 0 to 63, as said below
- owners: int32 [256], replicated, may hold values from 0 to 63, as said below
Outputs:
- kernel_panel: float32 [64, 12, 2, 16, 16], P('band', None, None, 'pw')
The draws below stay inside these ranges and needn't reach their ends.
Inputs may be any that keep to these rules, and one draw needn't show every extreme that they name: `pairs`: every block number is some slot's left block; the right blocks take exactly 32 distinct values. `owners`: at most 12 slots share an owner and some owner has exactly 12; every block number owns some slot.
All inputs are finite; a program needn't handle non-finite values.
Results may differ from the reference program's by a relative error of at most 0.000096.
Values sent between devices are 32-bit elements; how exact they have to be, the bound alone decides.
No kernel may reach another device: no remote copies, remote signals or barrier semaphores. Data moves between devices by JAX's collectives and lax.ppermute only.
A program may use at most 128 MiB of HBM per device.

```python
import jax
import jax.numpy as jnp
from jax import lax

NG = 10240
PAIR_BLK = 16
BLOCKS = 64
ROWS = 1024
NGP = 2560
SLOTS = 256
CAP = 12
JUSED = 32
N_PW = 4


def draw_pairs(key, part):
    key = jax.random.fold_in(key, 11)
    keys = jax.random.split(key, 5)
    used = jax.random.permutation(keys[0], BLOCKS)[:JUSED]
    spread = jax.random.permutation(keys[1], BLOCKS)
    position = jnp.arange(SLOTS)
    valence = jnp.where(position < BLOCKS, spread[position % BLOCKS], jax.random.randint(keys[2], (SLOTS,), 0, BLOCKS))
    conduction = jnp.where(position < JUSED, used[position % JUSED], used[jax.random.randint(keys[3], (SLOTS,), 0, JUSED)])
    order = jax.random.permutation(keys[4], SLOTS)
    return jnp.stack([valence, conduction], axis=1)[order].astype(jnp.int32)


def draw_owners(key, part):
    key = jax.random.fold_in(key, 23)
    keys = jax.random.split(key, 2)
    spread = jax.random.permutation(keys[0], BLOCKS)
    position = jnp.arange(SLOTS)
    rank_group = jnp.where(position < CAP, 0, 1 + (position - CAP) * (BLOCKS - 1) // (SLOTS - CAP))
    order = jax.random.permutation(keys[1], SLOTS)
    return spread[rank_group][order].astype(jnp.int32)


def block_scale(key, shape, pieces, least, top_value):
    loudness, own = 1.0, jax.random.fold_in(key, 6)
    for dim, blocks in pieces:
        draws = jnp.exp(jax.random.uniform(jax.random.fold_in(own, dim), (blocks,), jnp.float32, least / len(pieces), top_value / len(pieces)))
        loudness = loudness * jnp.repeat(draws, shape[dim] // blocks).reshape([-1 if axis == dim else 1 for axis in range(len(shape))])
    return loudness


def scatter_about(key, dims, width, reach, cuts=(), kind=jnp.bfloat16):
    level = block_scale(key, dims, cuts, -0.22, 0.18) if cuts else 1.0
    result = jax.random.normal(key, dims, jnp.float32) * width * level
    return jnp.minimum(jnp.maximum(result, -reach), reach).astype(kind)


def setup_inputs(seed: int = 0) -> dict:
    seeds = jax.random.split(jax.random.key(seed), 5)
    densities = scatter_about(seeds[0], (2, ROWS, NG), 1.0, 6.0, ((1, 64), (2, 4)), jnp.float32)
    screened = scatter_about(seeds[1], (2, N_PW, NGP, NG), NG ** -0.5, 0.0625, ((2, 64), (3, 4)), jnp.float32)
    pairs = draw_pairs(jax.random.fold_in(seeds[4], 71), 0)
    owners = draw_owners(jax.random.fold_in(seeds[4], 71), 0)
    return dict(densities=densities, screened=screened, pairs=pairs, owners=owners)


PRECISE = lax.Precision.HIGHEST


def contract_last(former, latter):
    return lax.dot_general(former, latter, (((1,), (1,)), ((), ())), precision=PRECISE, preferred_element_type=jnp.float32)


def slot_ranks(owners):
    member = (owners[:, None] == jnp.arange(BLOCKS, dtype=jnp.int32)[None, :]).astype(jnp.int32)
    before = jnp.cumsum(member, axis=0) - member
    return jnp.sum(before * member, axis=1).astype(jnp.int32)


def reference(densities, screened, pairs, owners):
    interaction = screened.reshape(2, NG, NG)
    applied_real = contract_last(densities[0], interaction[0]) - contract_last(densities[1], interaction[1])
    applied_imag = contract_last(densities[0], interaction[1]) + contract_last(densities[1], interaction[0])
    norm_scale = NG ** -0.5

    def one_slot(slot_pair):
        left_rows = lax.dynamic_slice_in_dim(densities, slot_pair[0] * PAIR_BLK, PAIR_BLK, 1)
        right_real = lax.dynamic_slice_in_dim(applied_real, slot_pair[1] * PAIR_BLK, PAIR_BLK, 0)
        right_imag = lax.dynamic_slice_in_dim(applied_imag, slot_pair[1] * PAIR_BLK, PAIR_BLK, 0)
        kernel_real = contract_last(left_rows[0], right_real) + contract_last(left_rows[1], right_imag)
        kernel_imag = contract_last(left_rows[0], right_imag) - contract_last(left_rows[1], right_real)
        return jnp.stack([kernel_real, kernel_imag]) * norm_scale

    kernels = lax.map(one_slot, pairs)
    slot_rank = slot_ranks(owners)
    kernel_panel = jnp.zeros((BLOCKS, CAP, 2, PAIR_BLK, PAIR_BLK), jnp.float32)
    return kernel_panel.at[owners, slot_rank].set(kernels)
```

```python
import functools

import jax
import jax.numpy as jnp
from jax import lax
from jax.experimental import pallas as pl
from jax.experimental.pallas import tpu as pltpu
from jax.sharding import Mesh
from jax.sharding import PartitionSpec as P

NG = 10240
CAP = 12
BLK = 16
USED = 32
HALF = USED // 2 * BLK
BAND = ("z", "y", "core")
SWAP = ((0, 1), (1, 0))
VMEM_LIMIT = 56 * 1024 * 1024


def ring(n, shift):
    return [(i, (i + shift) % n) for i in range(n)]


def split(x):
    high = lax.reduce_precision(x, 8, 7)
    return high.astype(jnp.bfloat16), (x - high).astype(jnp.bfloat16)


def dot(former, latter):
    return jnp.dot(former, latter, preferred_element_type=jnp.float32)


def plan(pairs, owners):
    blocks = 64
    ids = jnp.arange(blocks, dtype=jnp.int32)
    left, right = pairs[:, 0], pairs[:, 1]
    used = jnp.any(right[:, None] == ids[None, :], axis=0).astype(jnp.int32)
    rank = jnp.sum(used[None, :] * (ids[None, :] < ids[:, None]), axis=1)
    slots = jnp.arange(USED, dtype=jnp.int32)
    used_list = jnp.sum(
        jnp.where((rank[None, :] == slots[:, None]) & (used[None, :] > 0), ids[None, :], 0), axis=1
    )
    right_rank = jnp.sum(used[None, :] * (ids[None, :] < right[:, None]), axis=1)
    count = jnp.sum((owners[:, None] == ids[None, :]).astype(jnp.int32), axis=0)
    offset = jnp.sum(count[None, :] * (ids[None, :] < ids[:, None]), axis=1)
    order = jnp.arange(owners.shape[0], dtype=jnp.int32)
    ahead = (owners[None, :] < owners[:, None]) | (
        (owners[None, :] == owners[:, None]) & (order[None, :] < order[:, None])
    )
    place = jnp.sum(ahead.astype(jnp.int32), axis=1)
    hit = place[None, :] == order[:, None]
    left_at = jnp.sum(jnp.where(hit, left[None, :], 0), axis=1)
    right_at = jnp.sum(jnp.where(hit, right_rank[None, :], 0), axis=1)
    return used_list, left_at, right_at, offset, count


def main_kernel(table, right_ref, high_ref, low_ref, left_high, left_low, out_ref, rh, rl, kern):
    chips, span = right_ref.shape[0], right_ref.shape[1] // 2
    for chip in range(chips):
        for part in range(2):
            block = right_ref[chip, part * span : (part + 1) * span, :]
            top = block.astype(jnp.bfloat16)
            rest = (block - top.astype(jnp.float32)).astype(jnp.bfloat16)
            rows, cols = pl.ds(chip * span, span), pl.ds(part * HALF, HALF)
            rh[rows, cols] = top
            rl[rows, cols] = rest
    right_high, right_low = rh[...], rl[...]
    product = (
        dot(high_ref[...], right_high) + dot(high_ref[...], right_low) + dot(low_ref[...], right_high)
    )
    mid = product.shape[0] // 2
    real = product[:mid, :HALF] - product[mid:, HALF:]
    imag = product[mid:, :HALF] + product[:mid, HALF:]
    scale = NG ** (-0.5)
    applied = scale * jnp.concatenate(
        [jnp.concatenate([real, imag], axis=0), jnp.concatenate([imag, -real], axis=0)], axis=1
    )
    top = applied.astype(jnp.bfloat16)
    rest = (applied - top.astype(jnp.float32)).astype(jnp.bfloat16)
    kern[...] = dot(left_high[...], top) + dot(left_high[...], rest) + dot(left_low[...], top)

    lane = lax.broadcasted_iota(jnp.int32, (8, 128), 1) // BLK

    def group(g, carry):
        tiles = [[jnp.zeros((8, 128), jnp.float32) for _ in range(2)] for _ in range(2)]
        for u in range(8):
            row = pl.multiple_of(table[0, g * 8 + u] * BLK, BLK)
            column = pl.multiple_of(table[1, g * 8 + u] * 128, 128)
            shift = table[2, g * 8 + u]
            target = table[3, g * 8 + u]
            for part in range(2):
                for half in range(2):
                    tile = kern[pl.ds(row + half * 8, 8), pl.ds(column + part * HALF, 128)]
                    tile = pltpu.roll(tile, shift, 1)
                    tiles[part][half] = jnp.where(lane == target, tile, tiles[part][half])
        for part in range(2):
            for half in range(2):
                out_ref[part, half, :, pl.ds(pl.multiple_of(g * 128, 128), 128)] = tiles[part][half]
        return carry

    lax.fori_loop(0, table.shape[1] // 8, group, 0)


def main_call(table, right_all, screen_high, screen_low, left_high, left_low):
    slots = table.shape[1]
    depth = right_all.shape[0] * right_all.shape[1] // 2
    return pl.pallas_call(
        main_kernel,
        out_shape=jax.ShapeDtypeStruct((2, 2, 8, slots * BLK), jnp.float32),
        in_specs=[pl.BlockSpec(memory_space=pltpu.SMEM)] + [pl.BlockSpec(memory_space=pltpu.VMEM)] * 5,
        out_specs=pl.BlockSpec(memory_space=pltpu.VMEM),
        scratch_shapes=[
            pltpu.VMEM((depth, 2 * HALF), jnp.bfloat16),
            pltpu.VMEM((depth, 2 * HALF), jnp.bfloat16),
            pltpu.VMEM((left_high.shape[0], 2 * HALF), jnp.float32),
        ],
        compiler_params=pltpu.CompilerParams(vmem_limit_bytes=VMEM_LIMIT),
    )(table, right_all, screen_high, screen_low, left_high, left_low)


def shards(densities, screened, pairs, owners):
    core, x = lax.axis_index("core"), lax.axis_index("x")
    chip = lax.axis_index("z") * lax.axis_size("y") + lax.axis_index("y")
    span = screened.shape[2]
    used_list, left_at, right_at, offset, count = plan(pairs, owners)

    other = lax.ppermute(screened, "core", SWAP)
    screen = jnp.stack([screened, other], axis=1).reshape(2 * 2 * 4 * span, -1)
    screen_high, screen_low = split(screen)

    pieces = densities.reshape(2, BLK, 64, span).transpose(2, 3, 0, 1).reshape(64, 1, -1)
    mine = lax.all_to_all(pieces, BAND, 0, 0, tiled=True)
    mine = mine.reshape(64, span, 2, BLK)

    def rows_of(which):
        chosen = jnp.take(mine, lax.dynamic_slice_in_dim(used_list, which * (USED // 2), USED // 2), axis=0)
        return chosen.transpose(2, 1, 0, 3).reshape(2, span, HALF)

    keep, give = rows_of(core), rows_of(1 - core)
    take = lax.ppermute(give, "core", SWAP)
    first = jnp.where(core == 0, keep, take)
    second = jnp.where(core == 0, take, keep)
    shard = jnp.concatenate([first, second], axis=1).reshape(2 * 2 * span, HALF)
    right_all = lax.all_gather(shard, ("z", "y"), axis=0, tiled=False)

    flat = mine.reshape(64 * span * 2 * BLK // 128, 128)
    around = jnp.stack([flat] + [lax.ppermute(flat, "x", ring(4, s)) for s in (1, 2, 3)])
    at = (x - jnp.arange(4)) % 4
    around = jnp.take(around, at, axis=0)
    both = jnp.stack([around, lax.ppermute(around, "core", SWAP)])
    left = both.reshape(8, 64, span, 2, BLK).transpose(1, 4, 3, 0, 2).reshape(64 * BLK, -1)
    left_high, left_low = split(left)

    local = right_at - core * (USED // 2)
    valid = (local >= 0) & (local < USED // 2)
    local = jnp.where(valid, local, 0)
    lane = jnp.arange(local.shape[0], dtype=jnp.int32) % 8
    table = jnp.stack(
        [left_at, local // 8, (lane - local % 8) % 8 * BLK, jnp.where(valid, lane, -1)]
    ).astype(jnp.int32)
    kern = main_call(table, right_all, screen_high, screen_low, left_high, left_low)

    own = lax.dynamic_index_in_dim(kern, core, 0, keepdims=False)
    sent = lax.dynamic_index_in_dim(kern, 1 - core, 0, keepdims=False)
    own = own + lax.ppermute(sent, "core", SWAP)
    own = own.reshape(4, 4, -1)
    own = jnp.sum(lax.all_to_all(own, "x", 0, 0, tiled=True).reshape(4, 4, -1), axis=0)
    own = own.reshape(4, -1, BLK)
    at = (offset[:, None] + jnp.arange(CAP)[None, :]).reshape(-1)
    spread = jnp.take(own, jnp.minimum(at, own.shape[1] - 1), axis=1)
    spread = spread.reshape(4, 32, 2, CAP, BLK).transpose(1, 2, 3, 0, 4).reshape(32, 1, -1)
    gathered = lax.all_to_all(spread, ("z", "y"), 0, 0, tiled=True)
    total = jnp.sum(gathered.reshape(32, 2, CAP, 4, BLK), axis=0)
    own = lax.dynamic_index_in_dim(total, core, 0, keepdims=False)
    sent = lax.dynamic_index_in_dim(total, 1 - core, 0, keepdims=False)
    come = lax.ppermute(sent, "core", SWAP)
    real = jnp.where(core == 0, own, come)
    imag = jnp.where(core == 0, come, own)
    result = jnp.stack([real, imag], axis=1)
    held = lax.dynamic_index_in_dim(count, chip * 2 + core, 0, keepdims=False)
    result = jnp.where(jnp.arange(CAP)[:, None, None, None] < held, result, 0.0)
    return result[None]


def solution(mesh):
    fine = Mesh(mesh.devices.reshape(8, 4, 2, 4), ("z", "y", "core", "x"))
    in_specs = (P(None, BAND, "x"), P(None, None, BAND, "x"), P(), P())
    out_specs = P(BAND, None, None, "x", None)
    return jax.shard_map(shards, mesh=fine, in_specs=in_specs, out_specs=out_specs, check_vma=False)
```

```python
import functools

import jax
import jax.numpy as jnp
from jax import lax
from jax.experimental import pallas as pl
from jax.experimental.pallas import tpu as pltpu
from jax.sharding import Mesh
from jax.sharding import PartitionSpec as P

NG = 10240
CAP = 12
BLK = 16
USED = 32
HALF = USED // 2 * BLK
BAND = ("z", "y", "core")
SWAP = ((0, 1), (1, 0))
SMEM = pl.BlockSpec(memory_space=pltpu.SMEM)
VMEM = pl.BlockSpec(memory_space=pltpu.VMEM)
PLANE = 320
PAIR = 2 * PLANE


def ring(n, shift):
    return [(i, (i + shift) % n) for i in range(n)]


def params(mib):
    return pltpu.CompilerParams(vmem_limit_bytes=mib * 1024 * 1024)


def split(x):
    high = x.astype(jnp.bfloat16)
    return high, (x - high.astype(jnp.float32)).astype(jnp.bfloat16)


def dot(former, latter):
    return jnp.dot(former, latter, preferred_element_type=jnp.float32)


def dot3(high, low, former, latter):
    return dot(high, former) + dot(high, latter) + dot(low, former)


def plan(pairs, owners):
    blocks = 64
    ids = jnp.arange(blocks, dtype=jnp.int32)
    left, right = pairs[:, 0], pairs[:, 1]
    used = jnp.any(right[:, None] == ids[None, :], axis=0).astype(jnp.int32)
    rank = jnp.sum(used[None, :] * (ids[None, :] < ids[:, None]), axis=1)
    slots = jnp.arange(USED, dtype=jnp.int32)
    used_list = jnp.sum(
        jnp.where((rank[None, :] == slots[:, None]) & (used[None, :] > 0), ids[None, :], 0), axis=1
    )
    right_rank = jnp.sum(used[None, :] * (ids[None, :] < right[:, None]), axis=1)
    count = jnp.sum((owners[:, None] == ids[None, :]).astype(jnp.int32), axis=0)
    offset = jnp.sum(count[None, :] * (ids[None, :] < ids[:, None]), axis=1)
    order = jnp.arange(owners.shape[0], dtype=jnp.int32)
    ahead = (owners[None, :] < owners[:, None]) | (
        (owners[None, :] == owners[:, None]) & (order[None, :] < order[:, None])
    )
    place = jnp.sum(ahead.astype(jnp.int32), axis=1)
    hit = place[None, :] == order[:, None]
    left_at = jnp.sum(jnp.where(hit, left[None, :], 0), axis=1)
    right_at = jnp.sum(jnp.where(hit, right_rank[None, :], 0), axis=1)
    return used_list, left_at, right_at, offset, count


def screen_kernel(place, own_ref, other_ref, high_ref, low_ref):
    z = place[0]
    rows = 16
    lane = lax.broadcasted_iota(jnp.int32, (rows, 128), 1)
    for source, ref in enumerate((own_ref, other_ref)):

        def body(step, carry):
            part = step // 10
            start = pl.multiple_of(step * rows, rows)
            target = pl.multiple_of(part * PLANE + source * (PLANE // 2) + (step - part * 10) * rows, rows)
            for pair, (one, two) in enumerate(((7, 1), (6, 2), (5, 3), (0, 4))):
                parts = []
                for place_in, delta in ((0, one), (64, two)):
                    plane = lax.rem(z + delta, 8)
                    odd = lax.rem(plane, 2)
                    column = pl.multiple_of(plane * PLANE - odd * 64, 128)
                    window = ref[pl.ds(start, rows), pl.ds(column, 384)]
                    turned = pltpu.roll(window, 320 if place_in == 0 else 64, 1)
                    plain = (odd == 0) if place_in == 0 else (odd == 1)
                    parts.append(jnp.where(plain, window, turned))
                a, b = parts
                middle = jnp.where(lane < 64, a[:, 256:], b[:, :128])
                whole = jnp.concatenate([a[:, :256], middle, b[:, 128:]], axis=1)
                top, rest = split(whole)
                high_ref[pl.ds(target, rows), pair * PAIR : (pair + 1) * PAIR] = top
                low_ref[pl.ds(target, rows), pair * PAIR : (pair + 1) * PAIR] = rest
            return carry

        lax.fori_loop(0, 20, body, 0)


def screen_call(place, own, other):
    shape = jax.ShapeDtypeStruct((2 * own.shape[0], own.shape[1]), jnp.bfloat16)
    return pl.pallas_call(
        screen_kernel,
        out_shape=(shape, shape),
        in_specs=[SMEM, VMEM, VMEM],
        out_specs=(VMEM, VMEM),
        compiler_params=params(20),
        name="screen",
    )(place, own, other)


def left_kernel(place, *refs):
    pieces, (high_ref, low_ref, work) = refs[:8], refs[8:]
    x = place[1]
    span = pieces[0].shape[0] // 2
    for core in range(2):
        for shift in range(4):
            shard = lax.rem(x - shift + 4, 4)
            for part in range(2):
                row = pl.multiple_of(part * 8 * span + core * 4 * span + shard * span, 8)
                work[pl.ds(row, span), :] = pieces[core * 4 + shift][part * span : (part + 1) * span, :]
    for block in range(work.shape[1] // 128):
        turned = work[:, block * 128 : (block + 1) * 128].T
        top, rest = split(turned)
        high_ref[block * 128 : (block + 1) * 128, :] = top
        low_ref[block * 128 : (block + 1) * 128, :] = rest


def left_call(place, pieces):
    depth, width = pieces[0].shape
    shape = jax.ShapeDtypeStruct((width, 8 * depth), jnp.bfloat16)
    return pl.pallas_call(
        left_kernel,
        out_shape=(shape, shape),
        in_specs=[SMEM] + [VMEM] * 8,
        out_specs=(VMEM, VMEM),
        scratch_shapes=[pltpu.VMEM((8 * depth, width), jnp.float32)],
        compiler_params=params(20),
        name="left",
    )(place, *pieces)


def load_right(place, refs, high, low):
    y = place[2]
    span = refs[0].shape[0] // 8
    for plane, ref in enumerate(refs):
        for at, delta in enumerate((0, 3, 1, 2)):
            row = pl.multiple_of(plane * PLANE + lax.rem(y + delta, 4) * span, 16)
            for part in range(2):
                start = (at * 2 + part) * span
                top, rest = split(ref[start : start + span, :])
                high[pl.ds(row, span), part * HALF : (part + 1) * HALF] = top
                low[pl.ds(row, span), part * HALF : (part + 1) * HALF] = rest


def group_kernel(first, place, one_ref, two_ref, high_ref, low_ref, *refs):
    sum_ref, (out_ref, rh, rl) = (None if first else refs[0]), refs[-3:]
    load_right(place, (one_ref, two_ref), rh, rl)
    value = dot3(high_ref[...], low_ref[...], rh[...], rl[...])
    out_ref[...] = value if first else value + sum_ref[...]


def screen_spec(index):
    return pl.BlockSpec((PAIR, PAIR), lambda i: (0, index))


def group_call(index, place, one, two, screen_high, screen_low, total):
    whole = lambda shape: pl.BlockSpec(shape, lambda i: (0, 0))
    first = total is None
    return pl.pallas_call(
        functools.partial(group_kernel, first),
        grid=(1,),
        out_shape=jax.ShapeDtypeStruct((PAIR, 2 * HALF), jnp.float32),
        in_specs=[SMEM, whole(one.shape), whole(two.shape), screen_spec(index), screen_spec(index)]
        + ([] if first else [whole((PAIR, 2 * HALF))]),
        out_specs=whole((PAIR, 2 * HALF)),
        scratch_shapes=[pltpu.VMEM((PAIR, 2 * HALF), jnp.bfloat16)] * 2,
        compiler_params=params(24),
        name="group",
    )(place, one, two, screen_high, screen_low, *([] if first else [total]))


def pair_kernel(place, table, one_ref, two_ref, high_ref, low_ref, sum_ref, left_high, left_low, keep_ref, give_ref, rh, rl, kern):
    load_right(place, (one_ref, two_ref), rh, rl)
    product = sum_ref[...] + dot3(high_ref[...], low_ref[...], rh[...], rl[...])
    mid = product.shape[0] // 2
    real = product[:mid, :HALF] - product[mid:, HALF:]
    imag = product[mid:, :HALF] + product[:mid, HALF:]
    applied = NG ** (-0.5) * jnp.concatenate(
        [jnp.concatenate([real, imag], axis=0), jnp.concatenate([imag, -real], axis=0)], axis=1
    )
    kern[...] = dot3(left_high[...], left_low[...], *split(applied))

    lane = lax.broadcasted_iota(jnp.int32, (8, 128), 1) // BLK
    core = place[3]

    def group(g, carry):
        tiles = [[jnp.zeros((8, 128), jnp.float32) for _ in range(2)] for _ in range(2)]
        for u in range(8):
            row = pl.multiple_of(table[0, g * 8 + u] * BLK, BLK)
            column = pl.multiple_of(table[1, g * 8 + u] * 128, 128)
            shift = table[2, g * 8 + u]
            target = table[3, g * 8 + u]
            for part in range(2):
                for half in range(2):
                    tile = kern[pl.ds(row + half * 8, 8), pl.ds(column + part * HALF, 128)]
                    tile = pltpu.roll(tile, shift, 1)
                    tiles[part][half] = jnp.where(lane == target, tile, tiles[part][half])
        lanes = pl.ds(pl.multiple_of(g * 128, 128), 128)
        for half in range(2):
            keep_ref[half, :, lanes] = jnp.where(core == 0, tiles[0][half], tiles[1][half])
            give_ref[half, :, lanes] = jnp.where(core == 0, tiles[1][half], tiles[0][half])
        return carry

    lax.fori_loop(0, table.shape[1] // 8, group, 0)


def pair_call(place, table, one, two, screen_high, screen_low, total, left_high, left_low):
    whole = lambda array: pl.BlockSpec(array.shape, lambda i: (0, 0))
    shape = jax.ShapeDtypeStruct((2, 8, table.shape[1] * BLK), jnp.float32)
    out = pl.BlockSpec(shape.shape, lambda i: (0, 0, 0))
    return pl.pallas_call(
        pair_kernel,
        grid=(1,),
        out_shape=(shape, shape),
        in_specs=[SMEM, SMEM, whole(one), whole(two), screen_spec(3), screen_spec(3)]
        + [whole(total), whole(left_high), whole(left_low)],
        out_specs=(out, out),
        scratch_shapes=[pltpu.VMEM((PAIR, 2 * HALF), jnp.bfloat16)] * 2
        + [pltpu.VMEM((left_high.shape[0], 2 * HALF), jnp.float32)],
        compiler_params=params(36),
        name="pair",
    )(place, table, one, two, screen_high, screen_low, total, left_high, left_low)


def rows_kernel(keep_ref, come_ref, out_ref):
    upper = lax.broadcasted_iota(jnp.int32, out_ref.shape[1:], 0) < 4
    width = out_ref.shape[2]
    for half in range(2):
        total = keep_ref[half] + come_ref[half]
        top, bottom = total[:, :width], total[:, width:]
        out_ref[2 * half] = jnp.where(upper, top, pltpu.roll(bottom, 4, 0))
        out_ref[2 * half + 1] = jnp.where(upper, pltpu.roll(top, 4, 0), bottom)


def rows_call(keep, come):
    return pl.pallas_call(
        rows_kernel,
        out_shape=jax.ShapeDtypeStruct((4, 8, keep.shape[2] // 2), jnp.float32),
        in_specs=[VMEM, VMEM],
        out_specs=VMEM,
        name="rows",
    )(keep, come)


def owner_kernel(offset, parts_ref, out_ref, work):
    total = parts_ref[0] + parts_ref[1] + parts_ref[2] + parts_ref[3]
    width = total.shape[1]
    upper = lax.broadcasted_iota(jnp.int32, total.shape, 0) < 4
    turned = pltpu.roll(total, 4, 0)
    work[:, :width] = jnp.where(upper, total, turned)
    work[:, width : 2 * width] = jnp.where(upper, turned, total)
    work[:, 2 * width :] = jnp.zeros((8, work.shape[1] - 2 * width), jnp.float32)
    first = lax.broadcasted_iota(jnp.int32, (8, 384), 0) < 4

    def body(chip, carry):
        windows = []
        for core in range(2):
            start = offset[chip * 2 + core]
            column = pl.multiple_of(start // 8 * 128, 128)
            shift = lax.rem(384 - lax.rem(start, 8) * BLK, 384)
            windows.append(pltpu.roll(work[:, pl.ds(column, 384)], shift, 1))
        out_ref[chip] = jnp.where(first, *windows)[:, :256]
        return carry

    lax.fori_loop(0, out_ref.shape[0], body, 0)


def owner_call(offset, parts):
    return pl.pallas_call(
        owner_kernel,
        out_shape=jax.ShapeDtypeStruct((32, 8, 256), jnp.float32),
        in_specs=[SMEM, VMEM],
        out_specs=VMEM,
        scratch_shapes=[pltpu.VMEM((8, 2 * parts.shape[2] + 384), jnp.float32)],
        name="owner",
    )(offset, parts)


def sum_kernel(in_ref, out_ref):
    total = in_ref[0]
    for chip in range(1, in_ref.shape[0]):
        total = total + in_ref[chip]
    out_ref[...] = total


def sum_call(parts):
    return pl.pallas_call(
        sum_kernel,
        out_shape=jax.ShapeDtypeStruct(parts.shape[1:], jnp.float32),
        in_specs=[VMEM],
        out_specs=VMEM,
        name="total",
    )(parts)


def last_kernel(place, own_ref, come_ref, out_ref):
    core, held = place[3], place[4]
    own, come = own_ref[...], come_ref[...]
    real = jnp.where(core == 0, own, come)
    imag = jnp.where(core == 0, come, own)
    upper = lax.broadcasted_iota(jnp.int32, own.shape, 0) < 4
    mine = jnp.where(
        core == 0,
        jnp.where(upper, real, pltpu.roll(imag, 4, 0)),
        jnp.where(upper, pltpu.roll(real, 4, 0), imag),
    )
    for slot in range(CAP):
        tile = mine[:, slot // 8 * 128 : slot // 8 * 128 + 128]
        tile = pltpu.roll(tile, (128 - slot % 8 * BLK) % 128, 1)
        out_ref[slot] = jnp.where(slot < held, tile[:, :BLK], 0.0)


def last_call(place, own, come):
    return pl.pallas_call(
        last_kernel,
        out_shape=jax.ShapeDtypeStruct((CAP, 8, BLK), jnp.float32),
        in_specs=[SMEM, VMEM, VMEM],
        out_specs=VMEM,
        name="last",
    )(place, own, come)


def shards(densities, screened, pairs, owners):
    core, x = lax.axis_index("core"), lax.axis_index("x")
    z, y = lax.axis_index("z"), lax.axis_index("y")
    chip = z * lax.axis_size("y") + y
    span = screened.shape[2]
    used_list, left_at, right_at, offset, count = plan(pairs, owners)
    held = lax.dynamic_index_in_dim(count, chip * 2 + core, 0, keepdims=False)
    place = jnp.stack([z, x, y, core, held]).astype(jnp.int32)

    screen = screened.reshape(2 * 4 * span, -1)
    other = lax.ppermute(screen, "core", SWAP)
    screen_high, screen_low = screen_call(place, screen, other)

    pieces = densities.reshape(2, BLK, 64, span).transpose(2, 3, 0, 1).reshape(64, 1, -1)
    mine = lax.all_to_all(pieces, BAND, 0, 0, tiled=True)
    mine = mine.reshape(64, span, 2, BLK)

    def rows_of(which):
        chosen = jnp.take(
            mine, lax.dynamic_slice_in_dim(used_list, which * (USED // 2), USED // 2), axis=0, mode="clip"
        )
        return chosen.transpose(2, 1, 0, 3).reshape(2, span, HALF)

    keep, give = rows_of(core), rows_of(1 - core)
    take = lax.ppermute(give, "core", SWAP)
    first = jnp.where(core == 0, keep, take)
    second = jnp.where(core == 0, take, keep)
    shard = jnp.concatenate([first, second], axis=1).reshape(2 * 2 * span, HALF)

    shift = lambda array, axis, by: lax.ppermute(array, axis, ring(lax.axis_size(axis), by))
    from_below, from_above = shift(shard, "y", 1), shift(shard, "y", -1)
    across = shift(from_below, "y", 1)
    plane = jnp.concatenate([shard, from_below, from_above, across], axis=0)
    below = [plane]
    above = [plane]
    for step in range(3):
        below.append(shift(below[-1], "z", 1))
        above.append(shift(above[-1], "z", -1))
    far = shift(below[-1], "z", 1)

    columns = mine.transpose(2, 1, 0, 3).reshape(2 * span, -1)
    around = [columns] + [shift(columns, "x", by) for by in (1, 2, 3)]
    swapped = lax.ppermute(jnp.concatenate(around, axis=0), "core", SWAP)
    swapped = [swapped[at * 2 * span : (at + 1) * 2 * span] for at in range(4)]
    left_high, left_low = left_call(place, around + swapped)

    local = right_at - core * (USED // 2)
    valid = (local >= 0) & (local < USED // 2)
    local = jnp.where(valid, local, 0)
    lane = jnp.arange(local.shape[0], dtype=jnp.int32) % 8
    table = jnp.stack(
        [left_at, local // 8, (lane - local % 8) % 8 * BLK, jnp.where(valid, lane, -1)]
    ).astype(jnp.int32)

    total = None
    for index in range(3):
        total = group_call(index, place, below[index + 1], above[index + 1], screen_high, screen_low, total)
    keep, give = pair_call(place, table, plane, far, screen_high, screen_low, total, left_high, left_low)

    parts = rows_call(keep, lax.ppermute(give, "core", SWAP))
    parts = lax.all_to_all(parts, "x", 0, 0, tiled=True)
    parts = owner_call(offset, parts)
    parts = lax.all_to_all(parts, ("z", "y"), 0, 0, tiled=True)
    own = sum_call(parts)
    result = last_call(place, own, lax.ppermute(own, "core", SWAP))
    return result.reshape(1, CAP, 2, 4, BLK)


def solution(mesh):
    fine = Mesh(mesh.devices.reshape(8, 4, 2, 4), ("z", "y", "core", "x"))
    in_specs = (P(None, BAND, "x"), P(None, None, BAND, "x"), P(), P())
    out_specs = P(BAND, None, None, "x", None)
    return jax.shard_map(shards, mesh=fine, in_specs=in_specs, out_specs=out_specs, check_vma=False)
```

```python
import functools

import jax
import jax.numpy as jnp
from jax import lax
from jax.experimental import pallas as pl
from jax.experimental.pallas import tpu as pltpu
from jax.sharding import Mesh
from jax.sharding import PartitionSpec as P

NG = 10240
CAP = 12
BLK = 16
USED = 32
HALF = USED // 2 * BLK
BAND = ("z", "y", "core")
SWAP = ((0, 1), (1, 0))
SMEM = pl.BlockSpec(memory_space=pltpu.SMEM)
VMEM = pl.BlockSpec(memory_space=pltpu.VMEM)
PLANE = 320
PAIR = 2 * PLANE


def ring(n, shift):
    return [(i, (i + shift) % n) for i in range(n)]


def params(mib):
    return pltpu.CompilerParams(vmem_limit_bytes=mib * 1024 * 1024)


def split(x):
    high = x.astype(jnp.bfloat16)
    return high, (x - high.astype(jnp.float32)).astype(jnp.bfloat16)


def dot(former, latter):
    return jnp.dot(former, latter, preferred_element_type=jnp.float32)


def dot3(high, low, former, latter):
    return dot(high, former) + dot(high, latter) + dot(low, former)


def plan(pairs, owners):
    blocks = 64
    ids = jnp.arange(blocks, dtype=jnp.int32)
    left, right = pairs[:, 0], pairs[:, 1]
    used = jnp.any(right[:, None] == ids[None, :], axis=0).astype(jnp.int32)
    rank = jnp.sum(used[None, :] * (ids[None, :] < ids[:, None]), axis=1)
    slots = jnp.arange(USED, dtype=jnp.int32)
    used_list = jnp.sum(
        jnp.where((rank[None, :] == slots[:, None]) & (used[None, :] > 0), ids[None, :], 0), axis=1
    )
    right_rank = jnp.sum(used[None, :] * (ids[None, :] < right[:, None]), axis=1)
    count = jnp.sum((owners[:, None] == ids[None, :]).astype(jnp.int32), axis=0)
    offset = jnp.sum(count[None, :] * (ids[None, :] < ids[:, None]), axis=1)
    order = jnp.arange(owners.shape[0], dtype=jnp.int32)
    ahead = (owners[None, :] < owners[:, None]) | (
        (owners[None, :] == owners[:, None]) & (order[None, :] < order[:, None])
    )
    place = jnp.sum(ahead.astype(jnp.int32), axis=1)
    hit = place[None, :] == order[:, None]
    left_at = jnp.sum(jnp.where(hit, left[None, :], 0), axis=1)
    right_at = jnp.sum(jnp.where(hit, right_rank[None, :], 0), axis=1)
    return used_list, left_at, right_at, offset, count


def screen_kernel(place, own_ref, other_ref, high_ref, low_ref):
    z = place[0]
    rows = 16
    lane = lax.broadcasted_iota(jnp.int32, (rows, 128), 1)
    for source, ref in enumerate((own_ref, other_ref)):

        def body(step, carry):
            part = step // 10
            start = pl.multiple_of(step * rows, rows)
            target = pl.multiple_of(part * PLANE + source * (PLANE // 2) + (step - part * 10) * rows, rows)
            for pair, (one, two) in enumerate(((7, 1), (6, 2), (5, 3), (0, 4))):
                parts = []
                for place_in, delta in ((0, one), (64, two)):
                    plane = lax.rem(z + delta, 8)
                    odd = lax.rem(plane, 2)
                    column = pl.multiple_of(plane * PLANE - odd * 64, 128)
                    window = ref[pl.ds(start, rows), pl.ds(column, 384)]
                    turned = pltpu.roll(window, 320 if place_in == 0 else 64, 1)
                    plain = (odd == 0) if place_in == 0 else (odd == 1)
                    parts.append(jnp.where(plain, window, turned))
                a, b = parts
                middle = jnp.where(lane < 64, a[:, 256:], b[:, :128])
                whole = jnp.concatenate([a[:, :256], middle, b[:, 128:]], axis=1)
                top, rest = split(whole)
                high_ref[pl.ds(target, rows), pair * PAIR : (pair + 1) * PAIR] = top
                low_ref[pl.ds(target, rows), pair * PAIR : (pair + 1) * PAIR] = rest
            return carry

        lax.fori_loop(0, 20, body, 0)


def screen_call(place, own, other):
    shape = jax.ShapeDtypeStruct((2 * own.shape[0], own.shape[1]), jnp.bfloat16)
    return pl.pallas_call(
        screen_kernel,
        out_shape=(shape, shape),
        in_specs=[SMEM, VMEM, VMEM],
        out_specs=(VMEM, VMEM),
        compiler_params=params(20),
        name="screen",
    )(place, own, other)


def left_kernel(place, *refs):
    pieces, (high_ref, low_ref, work) = refs[:8], refs[8:]
    x = place[1]
    span = pieces[0].shape[0] // 2
    for core in range(2):
        for shift in range(4):
            shard = lax.rem(x - shift + 4, 4)
            for part in range(2):
                row = pl.multiple_of(part * 8 * span + core * 4 * span + shard * span, 8)
                work[pl.ds(row, span), :] = pieces[core * 4 + shift][part * span : (part + 1) * span, :]
    for block in range(work.shape[1] // 128):
        turned = work[:, block * 128 : (block + 1) * 128].T
        top, rest = split(turned)
        high_ref[block * 128 : (block + 1) * 128, :] = top
        low_ref[block * 128 : (block + 1) * 128, :] = rest


def left_call(place, pieces):
    depth, width = pieces[0].shape
    shape = jax.ShapeDtypeStruct((width, 8 * depth), jnp.bfloat16)
    return pl.pallas_call(
        left_kernel,
        out_shape=(shape, shape),
        in_specs=[SMEM] + [VMEM] * 8,
        out_specs=(VMEM, VMEM),
        scratch_shapes=[pltpu.VMEM((8 * depth, width), jnp.float32)],
        compiler_params=params(20),
        name="left",
    )(place, *pieces)


def load_right(place, refs, high, low):
    y = place[2]
    span = refs[0].shape[0] // 8
    for plane, ref in enumerate(refs):
        for at, delta in enumerate((0, 3, 1, 2)):
            row = pl.multiple_of(plane * PLANE + lax.rem(y + delta, 4) * span, 16)
            for part in range(2):
                start = (at * 2 + part) * span
                top, rest = split(ref[start : start + span, :])
                high[pl.ds(row, span), part * HALF : (part + 1) * HALF] = top
                low[pl.ds(row, span), part * HALF : (part + 1) * HALF] = rest


def group_kernel(first, place, one_ref, two_ref, high_ref, low_ref, *refs):
    sum_ref, (out_ref, rh, rl) = (None if first else refs[0]), refs[-3:]
    load_right(place, (one_ref, two_ref), rh, rl)
    value = dot3(high_ref[...], low_ref[...], rh[...], rl[...])
    out_ref[...] = value if first else value + sum_ref[...]


def screen_spec(index):
    return pl.BlockSpec((PAIR, PAIR), lambda i: (0, index))


def group_call(index, place, one, two, screen_high, screen_low, total):
    whole = lambda shape: pl.BlockSpec(shape, lambda i: (0, 0))
    first = total is None
    return pl.pallas_call(
        functools.partial(group_kernel, first),
        grid=(1,),
        out_shape=jax.ShapeDtypeStruct((PAIR, 2 * HALF), jnp.float32),
        in_specs=[SMEM, whole(one.shape), whole(two.shape), screen_spec(index), screen_spec(index)]
        + ([] if first else [whole((PAIR, 2 * HALF))]),
        out_specs=whole((PAIR, 2 * HALF)),
        scratch_shapes=[pltpu.VMEM((PAIR, 2 * HALF), jnp.bfloat16)] * 2,
        compiler_params=params(24),
        name="group",
    )(place, one, two, screen_high, screen_low, *([] if first else [total]))


def pair_kernel(place, table, one_ref, two_ref, high_ref, low_ref, sum_ref, left_high, left_low, keep_ref, give_ref, rh, rl, kern):
    load_right(place, (one_ref, two_ref), rh, rl)
    product = sum_ref[...] + dot3(high_ref[...], low_ref[...], rh[...], rl[...])
    mid = product.shape[0] // 2
    real = product[:mid, :HALF] - product[mid:, HALF:]
    imag = product[mid:, :HALF] + product[:mid, HALF:]
    applied = NG ** (-0.5) * jnp.concatenate(
        [jnp.concatenate([real, imag], axis=0), jnp.concatenate([imag, -real], axis=0)], axis=1
    )
    kern[...] = dot3(left_high[...], left_low[...], *split(applied))

    lane = lax.broadcasted_iota(jnp.int32, (8, 128), 1) // BLK
    core = place[3]

    def group(g, carry):
        tiles = [[jnp.zeros((8, 128), jnp.float32) for _ in range(2)] for _ in range(2)]
        for u in range(8):
            row = pl.multiple_of(table[0, g * 8 + u] * BLK, BLK)
            column = pl.multiple_of(table[1, g * 8 + u] * 128, 128)
            shift = table[2, g * 8 + u]
            target = table[3, g * 8 + u]
            for part in range(2):
                for half in range(2):
                    tile = kern[pl.ds(row + half * 8, 8), pl.ds(column + part * HALF, 128)]
                    tile = pltpu.roll(tile, shift, 1)
                    tiles[part][half] = jnp.where(lane == target, tile, tiles[part][half])
        lanes = pl.ds(pl.multiple_of(g * 128, 128), 128)
        for half in range(2):
            keep_ref[half, :, lanes] = jnp.where(core == 0, tiles[0][half], tiles[1][half])
            give_ref[half, :, lanes] = jnp.where(core == 0, tiles[1][half], tiles[0][half])
        return carry

    lax.fori_loop(0, table.shape[1] // 8, group, 0)


def pair_call(place, table, one, two, screen_high, screen_low, total, left_high, left_low):
    whole = lambda array: pl.BlockSpec(array.shape, lambda i: (0, 0))
    shape = jax.ShapeDtypeStruct((2, 8, table.shape[1] * BLK), jnp.float32)
    out = pl.BlockSpec(shape.shape, lambda i: (0, 0, 0))
    return pl.pallas_call(
        pair_kernel,
        grid=(1,),
        out_shape=(shape, shape),
        in_specs=[SMEM, SMEM, whole(one), whole(two), screen_spec(3), screen_spec(3)]
        + [whole(total), whole(left_high), whole(left_low)],
        out_specs=(out, out),
        scratch_shapes=[pltpu.VMEM((PAIR, 2 * HALF), jnp.bfloat16)] * 2
        + [pltpu.VMEM((left_high.shape[0], 2 * HALF), jnp.float32)],
        compiler_params=params(36),
        name="pair",
    )(place, table, one, two, screen_high, screen_low, total, left_high, left_low)


def rows_kernel(keep_ref, come_ref, out_ref):
    upper = lax.broadcasted_iota(jnp.int32, out_ref.shape[1:], 0) < 4
    width = out_ref.shape[2]
    for half in range(2):
        total = keep_ref[half] + come_ref[half]
        top, bottom = total[:, :width], total[:, width:]
        out_ref[2 * half] = jnp.where(upper, top, pltpu.roll(bottom, 4, 0))
        out_ref[2 * half + 1] = jnp.where(upper, pltpu.roll(top, 4, 0), bottom)


def rows_call(keep, come):
    return pl.pallas_call(
        rows_kernel,
        out_shape=jax.ShapeDtypeStruct((4, 8, keep.shape[2] // 2), jnp.float32),
        in_specs=[VMEM, VMEM],
        out_specs=VMEM,
        name="rows",
    )(keep, come)


def owner_kernel(offset, parts_ref, out_ref, work):
    total = parts_ref[0] + parts_ref[1] + parts_ref[2] + parts_ref[3]
    width = total.shape[1]
    upper = lax.broadcasted_iota(jnp.int32, total.shape, 0) < 4
    turned = pltpu.roll(total, 4, 0)
    work[:, :width] = jnp.where(upper, total, turned)
    work[:, width : 2 * width] = jnp.where(upper, turned, total)
    work[:, 2 * width :] = jnp.zeros((8, work.shape[1] - 2 * width), jnp.float32)
    first = lax.broadcasted_iota(jnp.int32, (8, 384), 0) < 4

    for chip in range(out_ref.shape[0]):
        windows = []
        for core in range(2):
            start = offset[chip * 2 + core]
            column = pl.multiple_of(start // 8 * 128, 128)
            shift = lax.rem(384 - lax.rem(start, 8) * BLK, 384)
            windows.append(pltpu.roll(work[:, pl.ds(column, 384)], shift, 1))
        out_ref[chip] = jnp.where(first, *windows)[:, :256]


def owner_call(offset, parts):
    return pl.pallas_call(
        owner_kernel,
        out_shape=jax.ShapeDtypeStruct((32, 8, 256), jnp.float32),
        in_specs=[SMEM, VMEM],
        out_specs=VMEM,
        scratch_shapes=[pltpu.VMEM((8, 2 * parts.shape[2] + 384), jnp.float32)],
        name="owner",
    )(offset, parts)


def sum_kernel(in_ref, out_ref):
    total = in_ref[0]
    for chip in range(1, in_ref.shape[0]):
        total = total + in_ref[chip]
    out_ref[...] = total


def sum_call(parts):
    return pl.pallas_call(
        sum_kernel,
        out_shape=jax.ShapeDtypeStruct(parts.shape[1:], jnp.float32),
        in_specs=[VMEM],
        out_specs=VMEM,
        name="total",
    )(parts)


def last_kernel(place, own_ref, come_ref, out_ref):
    core, held = place[3], place[4]
    own, come = own_ref[...], come_ref[...]
    real = jnp.where(core == 0, own, come)
    imag = jnp.where(core == 0, come, own)
    upper = lax.broadcasted_iota(jnp.int32, own.shape, 0) < 4
    mine = jnp.where(
        core == 0,
        jnp.where(upper, real, pltpu.roll(imag, 4, 0)),
        jnp.where(upper, pltpu.roll(real, 4, 0), imag),
    )
    for slot in range(CAP):
        tile = mine[:, slot // 8 * 128 : slot // 8 * 128 + 128]
        tile = pltpu.roll(tile, (128 - slot % 8 * BLK) % 128, 1)
        out_ref[slot] = jnp.where(slot < held, tile[:, :BLK], 0.0)


def last_call(place, own, come):
    return pl.pallas_call(
        last_kernel,
        out_shape=jax.ShapeDtypeStruct((CAP, 8, BLK), jnp.float32),
        in_specs=[SMEM, VMEM, VMEM],
        out_specs=VMEM,
        name="last",
    )(place, own, come)


def pack_kernel(place, own_ref, other_ref, out_ref, work):
    core = place[3]
    width = own_ref.shape[2]
    for block in range(width // 128):
        lanes = pl.ds(block * 128, 128)
        rows = []
        for part in range(2):
            own, other = own_ref[part, :, lanes], other_ref[part, :, lanes]
            rows += [jnp.where(core == 0, own, other), jnp.where(core == 0, other, own)]
        rows = jnp.concatenate(rows + rows, axis=0)
        work[block * 128 : (block + 1) * 128, :] = rows.T
    half = lax.broadcasted_iota(jnp.int32, (8, 128), 1) < 64
    for chip in range(32):
        at = pl.multiple_of(chip * 80 + core * 40, 8)
        tiles = [work[pl.ds(at + 8 * t, 8), :] for t in range(5)]
        out_ref[chip * 20 : chip * 20 + 8, :] = jnp.where(half, tiles[0], tiles[1])
        out_ref[chip * 20 + 8 : chip * 20 + 16, :] = jnp.where(half, tiles[2], tiles[3])
        last = jnp.where(half, tiles[4], pltpu.roll(tiles[4], 4, 0))
        out_ref[chip * 20 + 16 : chip * 20 + 20, :] = last[:4]


def pack_call(place, own, other):
    width = own.shape[2]
    return pl.pallas_call(
        pack_kernel,
        out_shape=jax.ShapeDtypeStruct((32 * 20, 128), jnp.float32),
        in_specs=[SMEM, VMEM, VMEM],
        out_specs=VMEM,
        scratch_shapes=[pltpu.VMEM((width, 128), jnp.float32)],
        name="pack",
    )(place, own, other)


def unpack_kernel(place, used, in_ref, columns_ref, keep_ref, give_ref):
    core = place[3]
    quarter = lax.broadcasted_iota(jnp.int32, (8, 128), 1) // 32
    upper = lax.broadcasted_iota(jnp.int32, (8, 128), 0) < 4
    for group in range(8):
        tiles = [[None] * 5 for _ in range(2)]
        for u in range(4):
            at = (group * 4 + u) * 20
            one, two = in_ref[at : at + 8, :], in_ref[at + 8 : at + 16, :]
            end = in_ref[at + 12 : at + 20, :]
            end = jnp.where(upper, pltpu.roll(end, 4, 0), pltpu.roll(end, 64, 1))
            for t, (source, first) in enumerate(((one, 0), (one, 64), (two, 0), (two, 64), (end, 0))):
                for part in range(2):
                    by = (u * 32 - first - part * 32) % 128
                    turned = pltpu.roll(source, by, 1) if by else source
                    old = tiles[part][t]
                    tiles[part][t] = turned if old is None else jnp.where(quarter == u, turned, old)
        for part in range(2):
            for t in range(5):
                row = part * 40 + t * 8
                columns_ref[row : row + 8, group * 128 : (group + 1) * 128] = tiles[part][t]
    eighth = lax.broadcasted_iota(jnp.int32, (80, 128), 1) // BLK
    for ref, which in ((give_ref, 1 - core), (keep_ref, core)):
        for group in range(2):
            slab = None
            for u in range(8):
                block = used[which * (USED // 2) + group * 8 + u]
                column = pl.multiple_of(block // 8 * 128, 128)
                by = lax.rem(u * BLK + 128 - lax.rem(block, 8) * BLK, 128)
                turned = pltpu.roll(columns_ref[:, pl.ds(column, 128)], by, 1)
                slab = turned if slab is None else jnp.where(eighth == u, turned, slab)
            ref[:, group * 128 : (group + 1) * 128] = slab


def unpack_call(place, used, pieces):
    return pl.pallas_call(
        unpack_kernel,
        out_shape=(
            jax.ShapeDtypeStruct((80, 1024), jnp.float32),
            jax.ShapeDtypeStruct((80, HALF), jnp.float32),
            jax.ShapeDtypeStruct((80, HALF), jnp.float32),
        ),
        in_specs=[SMEM, SMEM, VMEM],
        out_specs=(VMEM, VMEM, VMEM),
        name="unpack",
    )(place, used, pieces)


def shard_kernel(place, keep_ref, take_ref, out_ref):
    core = place[3]
    for part in range(2):
        out_ref[pl.ds(pl.multiple_of(part * 80 + core * 40, 8), 40), :] = keep_ref[part * 40 : part * 40 + 40, :]
        out_ref[pl.ds(pl.multiple_of(part * 80 + 40 - core * 40, 8), 40), :] = take_ref[part * 40 : part * 40 + 40, :]


def shard_call(place, keep, take):
    return pl.pallas_call(
        shard_kernel,
        out_shape=jax.ShapeDtypeStruct((160, HALF), jnp.float32),
        in_specs=[SMEM, VMEM, VMEM],
        out_specs=VMEM,
        name="shard",
    )(place, keep, take)


def after(array, *others):
    return lax.optimization_barrier((array, *others))[0]


def shards(densities, screened, pairs, owners):
    core, x = lax.axis_index("core"), lax.axis_index("x")
    z, y = lax.axis_index("z"), lax.axis_index("y")
    chip = z * lax.axis_size("y") + y
    span = screened.shape[2]
    used_list, left_at, right_at, offset, count = plan(pairs, owners)
    held = lax.dynamic_index_in_dim(count, chip * 2 + core, 0, keepdims=False)
    place = jnp.stack([z, x, y, core, held]).astype(jnp.int32)

    local = right_at - core * (USED // 2)
    valid = (local >= 0) & (local < USED // 2)
    local = jnp.where(valid, local, 0)
    lane = jnp.arange(local.shape[0], dtype=jnp.int32) % 8
    table = jnp.stack(
        [left_at, local // 8, (lane - local % 8) % 8 * BLK, jnp.where(valid, lane, -1)]
    ).astype(jnp.int32)

    pieces = pack_call(place, densities, lax.ppermute(densities, "core", SWAP))
    mine = lax.all_to_all(pieces.reshape(32, 1, -1), ("z", "y"), 0, 0, tiled=True).reshape(pieces.shape)
    mine, table, offset = lax.optimization_barrier((mine, table, offset))

    screen = screened.reshape(2 * 4 * span, -1)
    other = lax.ppermute(after(screen, pieces), "core", SWAP)
    screen_high, screen_low = screen_call(place, screen, other)

    columns, keep, give = unpack_call(place, used_list, mine)
    shard = shard_call(place, keep, lax.ppermute(give, "core", SWAP))

    shift = lambda array, axis, by: lax.ppermute(array, axis, ring(lax.axis_size(axis), by))
    from_below, from_above = shift(shard, "y", 1), shift(shard, "y", -1)
    across = shift(from_below, "y", 1)
    plane = jnp.concatenate([shard, from_below, from_above, across], axis=0)
    below, above = shift(plane, "z", 1), shift(plane, "z", -1)

    columns = after(columns, plane)
    around = [columns] + [shift(columns, "x", by) for by in (1, 2, 3)]
    swapped = lax.ppermute(jnp.concatenate(around, axis=0), "core", SWAP)
    swapped = [swapped[at * 2 * span : (at + 1) * 2 * span] for at in range(4)]

    below, above, screen_high, screen_low = lax.optimization_barrier((below, above, screen_high, screen_low))
    below2, above2 = shift(below, "z", 1), shift(above, "z", -1)
    left_high, left_low = left_call(place, around + swapped)
    total = group_call(0, place, below, above, screen_high, screen_low, None)
    below2, above2, total, left_high, left_low = lax.optimization_barrier(
        (below2, above2, total, left_high, left_low)
    )
    below3, above3 = shift(below2, "z", 1), shift(above2, "z", -1)
    total = group_call(1, place, below2, above2, screen_high, screen_low, total)
    below3, above3, total = lax.optimization_barrier((below3, above3, total))
    far = shift(below3, "z", 1)
    total = group_call(2, place, below3, above3, screen_high, screen_low, total)
    far, total = lax.optimization_barrier((far, total))
    keep, give = pair_call(place, table, plane, far, screen_high, screen_low, total, left_high, left_low)

    parts = rows_call(keep, lax.ppermute(give, "core", SWAP))
    parts = lax.all_to_all(parts, "x", 0, 0, tiled=True)
    parts = owner_call(offset, parts)
    parts = lax.all_to_all(parts, ("z", "y"), 0, 0, tiled=True)
    own = sum_call(parts)
    result = last_call(place, own, lax.ppermute(own, "core", SWAP))
    return result.reshape(1, CAP, 2, 4, BLK)


def solution(mesh):
    fine = Mesh(mesh.devices.reshape(8, 4, 2, 4), ("z", "y", "core", "x"))
    in_specs = (P(None, BAND, "x"), P(None, None, BAND, "x"), P(), P())
    out_specs = P(BAND, None, None, "x", None)
    return jax.shard_map(shards, mesh=fine, in_specs=in_specs, out_specs=out_specs, check_vma=False)
```

```python
import functools

import jax
import jax.numpy as jnp
from jax import lax
from jax.experimental import pallas as pl
from jax.experimental.pallas import tpu as pltpu
from jax.sharding import Mesh
from jax.sharding import PartitionSpec as P

NG = 10240
CAP = 12
BLK = 16
USED = 32
HALF = USED // 2 * BLK
BAND = ("z", "y", "core")
SWAP = ((0, 1), (1, 0))
SMEM = pl.BlockSpec(memory_space=pltpu.SMEM)
VMEM = pl.BlockSpec(memory_space=pltpu.VMEM)
PLANE = 320
PAIR = 2 * PLANE


def ring(n, shift):
    return [(i, (i + shift) % n) for i in range(n)]


def params(mib):
    return pltpu.CompilerParams(vmem_limit_bytes=mib * 1024 * 1024)


def split(x):
    high = x.astype(jnp.bfloat16)
    return high, (x - high.astype(jnp.float32)).astype(jnp.bfloat16)


def dot(former, latter):
    return jnp.dot(former, latter, preferred_element_type=jnp.float32)


def dot3(high, low, former, latter):
    return dot(high, former) + dot(high, latter) + dot(low, former)


def plan(pairs, owners):
    blocks = 64
    ids = jnp.arange(blocks, dtype=jnp.int32)
    left, right = pairs[:, 0], pairs[:, 1]
    used = jnp.any(right[:, None] == ids[None, :], axis=0).astype(jnp.int32)
    rank = jnp.sum(used[None, :] * (ids[None, :] < ids[:, None]), axis=1)
    slots = jnp.arange(USED, dtype=jnp.int32)
    used_list = jnp.sum(
        jnp.where((rank[None, :] == slots[:, None]) & (used[None, :] > 0), ids[None, :], 0), axis=1
    )
    right_rank = jnp.sum(used[None, :] * (ids[None, :] < right[:, None]), axis=1)
    count = jnp.sum((owners[:, None] == ids[None, :]).astype(jnp.int32), axis=0)
    offset = jnp.sum(count[None, :] * (ids[None, :] < ids[:, None]), axis=1)
    order = jnp.arange(owners.shape[0], dtype=jnp.int32)
    ahead = (owners[None, :] < owners[:, None]) | (
        (owners[None, :] == owners[:, None]) & (order[None, :] < order[:, None])
    )
    place = jnp.sum(ahead.astype(jnp.int32), axis=1)
    hit = place[None, :] == order[:, None]
    left_at = jnp.sum(jnp.where(hit, left[None, :], 0), axis=1)
    right_at = jnp.sum(jnp.where(hit, right_rank[None, :], 0), axis=1)
    return used_list, left_at, right_at, offset, count


def screen_kernel(place, own_ref, other_ref, high_ref, low_ref):
    z = place[0]
    rows = 16
    lane = lax.broadcasted_iota(jnp.int32, (rows, 128), 1)
    for source, ref in enumerate((own_ref, other_ref)):

        def body(step, carry):
            part = step // 10
            start = pl.multiple_of(step * rows, rows)
            target = pl.multiple_of(part * PLANE + source * (PLANE // 2) + (step - part * 10) * rows, rows)
            for pair, (one, two) in enumerate(((7, 1), (6, 2), (5, 3), (0, 4))):
                parts = []
                for place_in, delta in ((0, one), (64, two)):
                    plane = lax.rem(z + delta, 8)
                    odd = lax.rem(plane, 2)
                    column = pl.multiple_of(plane * PLANE - odd * 64, 128)
                    window = ref[pl.ds(start, rows), pl.ds(column, 384)]
                    turned = pltpu.roll(window, 320 if place_in == 0 else 64, 1)
                    plain = (odd == 0) if place_in == 0 else (odd == 1)
                    parts.append(jnp.where(plain, window, turned))
                a, b = parts
                middle = jnp.where(lane < 64, a[:, 256:], b[:, :128])
                whole = jnp.concatenate([a[:, :256], middle, b[:, 128:]], axis=1)
                top, rest = split(whole)
                high_ref[pl.ds(target, rows), pair * PAIR : (pair + 1) * PAIR] = top
                low_ref[pl.ds(target, rows), pair * PAIR : (pair + 1) * PAIR] = rest
            return carry

        lax.fori_loop(0, 20, body, 0)


def screen_call(place, own, other):
    shape = jax.ShapeDtypeStruct((2 * own.shape[0], own.shape[1]), jnp.bfloat16)
    return pl.pallas_call(
        screen_kernel,
        out_shape=(shape, shape),
        in_specs=[SMEM, VMEM, VMEM],
        out_specs=(VMEM, VMEM),
        compiler_params=params(20),
        name="screen",
    )(place, own, other)


def left_kernel(place, *refs):
    pieces, (high_ref, low_ref, work) = refs[:8], refs[8:]
    x = place[1]
    span = pieces[0].shape[0] // 2
    for core in range(2):
        for shift in range(4):
            shard = lax.rem(x - shift + 4, 4)
            for part in range(2):
                row = pl.multiple_of(part * 8 * span + core * 4 * span + shard * span, 8)
                work[pl.ds(row, span), :] = pieces[core * 4 + shift][part * span : (part + 1) * span, :]
    for block in range(work.shape[1] // 128):
        turned = work[:, block * 128 : (block + 1) * 128].T
        top, rest = split(turned)
        high_ref[block * 128 : (block + 1) * 128, :] = top
        low_ref[block * 128 : (block + 1) * 128, :] = rest


def left_call(place, pieces):
    depth, width = pieces[0].shape
    shape = jax.ShapeDtypeStruct((width, 8 * depth), jnp.bfloat16)
    return pl.pallas_call(
        left_kernel,
        out_shape=(shape, shape),
        in_specs=[SMEM] + [VMEM] * 8,
        out_specs=(VMEM, VMEM),
        scratch_shapes=[pltpu.VMEM((8 * depth, width), jnp.float32)],
        compiler_params=params(20),
        name="left",
    )(place, *pieces)


def load_right(place, planes, high, low):
    y = place[2]
    span = PLANE // 4
    for plane, refs in enumerate(planes):
        each = 4 // len(refs)
        for at, delta in enumerate((0, 3, 1, 2)):
            row = pl.multiple_of(plane * PLANE + lax.rem(y + delta, 4) * span, 16)
            for part in range(2):
                start = (at % each * 2 + part) * span
                top, rest = split(refs[at // each][start : start + span, :])
                high[pl.ds(row, span), part * HALF : (part + 1) * HALF] = top
                low[pl.ds(row, span), part * HALF : (part + 1) * HALF] = rest


def group_kernel(first, place, one_ref, two_ref, high_ref, low_ref, *refs):
    sum_ref, (out_ref, rh, rl) = (None if first else refs[0]), refs[-3:]
    load_right(place, ((one_ref,), (two_ref,)), rh, rl)
    value = dot3(high_ref[...], low_ref[...], rh[...], rl[...])
    out_ref[...] = value if first else value + sum_ref[...]


def screen_spec(index):
    return pl.BlockSpec((PAIR, PAIR), lambda i: (0, index))


def group_call(index, place, one, two, screen_high, screen_low, total):
    whole = lambda shape: pl.BlockSpec(shape, lambda i: (0, 0))
    first = total is None
    return pl.pallas_call(
        functools.partial(group_kernel, first),
        grid=(1,),
        out_shape=jax.ShapeDtypeStruct((PAIR, 2 * HALF), jnp.float32),
        in_specs=[SMEM, whole(one.shape), whole(two.shape), screen_spec(index), screen_spec(index)]
        + ([] if first else [whole((PAIR, 2 * HALF))]),
        out_specs=whole((PAIR, 2 * HALF)),
        scratch_shapes=[pltpu.VMEM((PAIR, 2 * HALF), jnp.bfloat16)] * 2,
        compiler_params=params(24),
        name="group",
    )(place, one, two, screen_high, screen_low, *([] if first else [total]))


def pair_kernel(place, table, one_ref, two_ref, three_ref, high_ref, low_ref, sum_ref, left_high, left_low, keep_ref, give_ref, rh, rl, kern):
    load_right(place, ((one_ref,), (two_ref, three_ref)), rh, rl)
    product = sum_ref[...] + dot3(high_ref[...], low_ref[...], rh[...], rl[...])
    mid = product.shape[0] // 2
    real = product[:mid, :HALF] - product[mid:, HALF:]
    imag = product[mid:, :HALF] + product[:mid, HALF:]
    applied = NG ** (-0.5) * jnp.concatenate(
        [jnp.concatenate([real, imag], axis=0), jnp.concatenate([imag, -real], axis=0)], axis=1
    )
    kern[...] = dot3(left_high[...], left_low[...], *split(applied))

    lane = lax.broadcasted_iota(jnp.int32, (8, 128), 1) // BLK
    core = place[3]

    def group(g, carry):
        tiles = [[jnp.zeros((8, 128), jnp.float32) for _ in range(2)] for _ in range(2)]
        for u in range(8):
            row = pl.multiple_of(table[0, g * 8 + u] * BLK, BLK)
            column = pl.multiple_of(table[1, g * 8 + u] * 128, 128)
            shift = table[2, g * 8 + u]
            target = table[3, g * 8 + u]
            for part in range(2):
                for half in range(2):
                    tile = kern[pl.ds(row + half * 8, 8), pl.ds(column + part * HALF, 128)]
                    tile = pltpu.roll(tile, shift, 1)
                    tiles[part][half] = jnp.where(lane == target, tile, tiles[part][half])
        lanes = pl.ds(pl.multiple_of(g * 128, 128), 128)
        for half in range(2):
            keep_ref[half, :, lanes] = jnp.where(core == 0, tiles[0][half], tiles[1][half])
            give_ref[half, :, lanes] = jnp.where(core == 0, tiles[1][half], tiles[0][half])
        return carry

    lax.fori_loop(0, table.shape[1] // 8, group, 0)


def pair_call(place, table, one, two, three, screen_high, screen_low, total, left_high, left_low):
    whole = lambda array: pl.BlockSpec(array.shape, lambda i: (0, 0))
    shape = jax.ShapeDtypeStruct((2, 8, table.shape[1] * BLK), jnp.float32)
    out = pl.BlockSpec(shape.shape, lambda i: (0, 0, 0))
    return pl.pallas_call(
        pair_kernel,
        grid=(1,),
        out_shape=(shape, shape),
        in_specs=[SMEM, SMEM, whole(one), whole(two), whole(three), screen_spec(3), screen_spec(3)]
        + [whole(total), whole(left_high), whole(left_low)],
        out_specs=(out, out),
        scratch_shapes=[pltpu.VMEM((PAIR, 2 * HALF), jnp.bfloat16)] * 2
        + [pltpu.VMEM((left_high.shape[0], 2 * HALF), jnp.float32)],
        compiler_params=params(36),
        name="pair",
    )(place, table, one, two, three, screen_high, screen_low, total, left_high, left_low)


def rows_kernel(keep_ref, come_ref, out_ref):
    upper = lax.broadcasted_iota(jnp.int32, out_ref.shape[1:], 0) < 4
    width = out_ref.shape[2]
    for half in range(2):
        total = keep_ref[half] + come_ref[half]
        top, bottom = total[:, :width], total[:, width:]
        out_ref[2 * half] = jnp.where(upper, top, pltpu.roll(bottom, 4, 0))
        out_ref[2 * half + 1] = jnp.where(upper, pltpu.roll(top, 4, 0), bottom)


def rows_call(keep, come):
    return pl.pallas_call(
        rows_kernel,
        out_shape=jax.ShapeDtypeStruct((4, 8, keep.shape[2] // 2), jnp.float32),
        in_specs=[VMEM, VMEM],
        out_specs=VMEM,
        name="rows",
    )(keep, come)


def owner_kernel(offset, parts_ref, out_ref, work):
    total = parts_ref[0] + parts_ref[1] + parts_ref[2] + parts_ref[3]
    width = total.shape[1]
    upper = lax.broadcasted_iota(jnp.int32, total.shape, 0) < 4
    turned = pltpu.roll(total, 4, 0)
    work[:, :width] = jnp.where(upper, total, turned)
    work[:, width : 2 * width] = jnp.where(upper, turned, total)
    work[:, 2 * width :] = jnp.zeros((8, work.shape[1] - 2 * width), jnp.float32)
    first = lax.broadcasted_iota(jnp.int32, (8, 384), 0) < 4

    for chip in range(out_ref.shape[0]):
        windows = []
        for core in range(2):
            start = offset[chip * 2 + core]
            column = pl.multiple_of(start // 8 * 128, 128)
            shift = lax.rem(384 - lax.rem(start, 8) * BLK, 384)
            windows.append(pltpu.roll(work[:, pl.ds(column, 384)], shift, 1))
        out_ref[chip] = jnp.where(first, *windows)[:, :256]


def owner_call(offset, parts):
    return pl.pallas_call(
        owner_kernel,
        out_shape=jax.ShapeDtypeStruct((32, 8, 256), jnp.float32),
        in_specs=[SMEM, VMEM],
        out_specs=VMEM,
        scratch_shapes=[pltpu.VMEM((8, 2 * parts.shape[2] + 384), jnp.float32)],
        name="owner",
    )(offset, parts)


def sum_kernel(in_ref, out_ref):
    total = in_ref[0]
    for chip in range(1, in_ref.shape[0]):
        total = total + in_ref[chip]
    out_ref[...] = total


def sum_call(parts):
    return pl.pallas_call(
        sum_kernel,
        out_shape=jax.ShapeDtypeStruct(parts.shape[1:], jnp.float32),
        in_specs=[VMEM],
        out_specs=VMEM,
        name="total",
    )(parts)


def last_kernel(place, held_ref, own_ref, come_ref, out_ref):
    core, held = place[3], held_ref[0]
    own, come = own_ref[...], come_ref[...]
    real = jnp.where(core == 0, own, come)
    imag = jnp.where(core == 0, come, own)
    upper = lax.broadcasted_iota(jnp.int32, own.shape, 0) < 4
    mine = jnp.where(
        core == 0,
        jnp.where(upper, real, pltpu.roll(imag, 4, 0)),
        jnp.where(upper, pltpu.roll(real, 4, 0), imag),
    )
    for slot in range(CAP):
        tile = mine[:, slot // 8 * 128 : slot // 8 * 128 + 128]
        tile = pltpu.roll(tile, (128 - slot % 8 * BLK) % 128, 1)
        out_ref[slot] = jnp.where(slot < held, tile[:, :BLK], 0.0)


def last_call(place, held, own, come):
    return pl.pallas_call(
        last_kernel,
        out_shape=jax.ShapeDtypeStruct((CAP, 8, BLK), jnp.float32),
        in_specs=[SMEM, SMEM, VMEM, VMEM],
        out_specs=VMEM,
        name="last",
    )(place, held, own, come)


def pack_kernel(place, own_ref, other_ref, out_ref, work):
    core = place[3]
    width = own_ref.shape[2]
    for block in range(width // 128):
        lanes = pl.ds(block * 128, 128)
        rows = []
        for part in range(2):
            own, other = own_ref[part, :, lanes], other_ref[part, :, lanes]
            rows += [jnp.where(core == 0, own, other), jnp.where(core == 0, other, own)]
        rows = jnp.concatenate(rows + rows, axis=0)
        work[block * 128 : (block + 1) * 128, :] = rows.T
    half = lax.broadcasted_iota(jnp.int32, (8, 128), 1) < 64
    for chip in range(32):
        at = pl.multiple_of(chip * 80 + core * 40, 8)
        tiles = [work[pl.ds(at + 8 * t, 8), :] for t in range(5)]
        out_ref[chip * 20 : chip * 20 + 8, :] = jnp.where(half, tiles[0], tiles[1])
        out_ref[chip * 20 + 8 : chip * 20 + 16, :] = jnp.where(half, tiles[2], tiles[3])
        last = jnp.where(half, tiles[4], pltpu.roll(tiles[4], 4, 0))
        out_ref[chip * 20 + 16 : chip * 20 + 20, :] = last[:4]


def pack_call(place, own, other):
    width = own.shape[2]
    return pl.pallas_call(
        pack_kernel,
        out_shape=jax.ShapeDtypeStruct((32 * 20, 128), jnp.float32),
        in_specs=[SMEM, VMEM, VMEM],
        out_specs=VMEM,
        scratch_shapes=[pltpu.VMEM((width, 128), jnp.float32)],
        name="pack",
    )(place, own, other)


def unpack_kernel(place, used, in_ref, columns_ref, keep_ref, give_ref):
    core = place[3]
    quarter = lax.broadcasted_iota(jnp.int32, (8, 128), 1) // 32
    upper = lax.broadcasted_iota(jnp.int32, (8, 128), 0) < 4
    for group in range(8):
        tiles = [[None] * 5 for _ in range(2)]
        for u in range(4):
            at = (group * 4 + u) * 20
            one, two = in_ref[at : at + 8, :], in_ref[at + 8 : at + 16, :]
            end = in_ref[at + 12 : at + 20, :]
            end = jnp.where(upper, pltpu.roll(end, 4, 0), pltpu.roll(end, 64, 1))
            for t, (source, first) in enumerate(((one, 0), (one, 64), (two, 0), (two, 64), (end, 0))):
                for part in range(2):
                    by = (u * 32 - first - part * 32) % 128
                    turned = pltpu.roll(source, by, 1) if by else source
                    old = tiles[part][t]
                    tiles[part][t] = turned if old is None else jnp.where(quarter == u, turned, old)
        for part in range(2):
            for t in range(5):
                row = part * 40 + t * 8
                columns_ref[row : row + 8, group * 128 : (group + 1) * 128] = tiles[part][t]
    eighth = lax.broadcasted_iota(jnp.int32, (80, 128), 1) // BLK
    for ref, which in ((give_ref, 1 - core), (keep_ref, core)):
        for group in range(2):
            slab = None
            for u in range(8):
                block = used[which * (USED // 2) + group * 8 + u]
                column = pl.multiple_of(block // 8 * 128, 128)
                by = lax.rem(u * BLK + 128 - lax.rem(block, 8) * BLK, 128)
                turned = pltpu.roll(columns_ref[:, pl.ds(column, 128)], by, 1)
                slab = turned if slab is None else jnp.where(eighth == u, turned, slab)
            ref[:, group * 128 : (group + 1) * 128] = slab


def unpack_call(place, used, pieces):
    return pl.pallas_call(
        unpack_kernel,
        out_shape=(
            jax.ShapeDtypeStruct((80, 1024), jnp.float32),
            jax.ShapeDtypeStruct((80, HALF), jnp.float32),
            jax.ShapeDtypeStruct((80, HALF), jnp.float32),
        ),
        in_specs=[SMEM, SMEM, VMEM],
        out_specs=(VMEM, VMEM, VMEM),
        name="unpack",
    )(place, used, pieces)


def shard_kernel(place, keep_ref, take_ref, out_ref):
    core = place[3]
    for part in range(2):
        out_ref[pl.ds(pl.multiple_of(part * 80 + core * 40, 8), 40), :] = keep_ref[part * 40 : part * 40 + 40, :]
        out_ref[pl.ds(pl.multiple_of(part * 80 + 40 - core * 40, 8), 40), :] = take_ref[part * 40 : part * 40 + 40, :]


def shard_call(place, keep, take):
    return pl.pallas_call(
        shard_kernel,
        out_shape=jax.ShapeDtypeStruct((160, HALF), jnp.float32),
        in_specs=[SMEM, VMEM, VMEM],
        out_specs=VMEM,
        name="shard",
    )(place, keep, take)


def after(array, *others):
    return lax.optimization_barrier((array, *others))[0]


def shards(densities, screened, pairs, owners):
    core, x = lax.axis_index("core"), lax.axis_index("x")
    z, y = lax.axis_index("z"), lax.axis_index("y")
    chip = z * lax.axis_size("y") + y
    span = screened.shape[2]
    used_list, left_at, right_at, offset, count = plan(pairs, owners)
    held = lax.dynamic_slice_in_dim(count, chip * 2 + core, 1)
    place = jnp.stack([z, x, y, core]).astype(jnp.int32)

    local = right_at - core * (USED // 2)
    valid = (local >= 0) & (local < USED // 2)
    local = jnp.where(valid, local, 0)
    lane = jnp.arange(local.shape[0], dtype=jnp.int32) % 8
    table = jnp.stack(
        [left_at, local // 8, (lane - local % 8) % 8 * BLK, jnp.where(valid, lane, -1)]
    ).astype(jnp.int32)

    pieces = pack_call(place, densities, lax.ppermute(densities, "core", SWAP))
    mine = lax.all_to_all(pieces.reshape(32, 1, -1), ("z", "y"), 0, 0, tiled=True).reshape(pieces.shape)
    mine, table, offset, held = lax.optimization_barrier((mine, table, offset, held))

    screen = screened.reshape(2 * 4 * span, -1)
    other = lax.ppermute(after(screen, pieces), "core", SWAP)
    screen_high, screen_low = screen_call(place, screen, other)

    columns, keep, give = unpack_call(place, used_list, mine)
    shard = shard_call(place, keep, lax.ppermute(give, "core", SWAP))

    shift = lambda array, axis, by: lax.ppermute(array, axis, ring(lax.axis_size(axis), by))
    from_below, from_above = shift(shard, "y", 1), shift(shard, "y", -1)
    across = shift(from_below, "y", 1)
    plane = jnp.concatenate([shard, from_below, from_above, across], axis=0)
    below, above = shift(plane, "z", 1), shift(plane, "z", -1)

    below, above, screen_high, screen_low = lax.optimization_barrier((below, above, screen_high, screen_low))
    below2, above2 = shift(below, "z", 1), shift(above, "z", -1)
    columns = after(columns, screen_high)
    around = [columns] + [shift(columns, "x", by) for by in (1, 2, 3)]
    total = group_call(0, place, below, above, screen_high, screen_low, None)
    below2, above2, total = lax.optimization_barrier((below2, above2, total))
    below3, above3 = shift(below2, "z", 1), shift(above2, "z", -1)
    total = group_call(1, place, below2, above2, screen_high, screen_low, total)
    below3, above3, total = lax.optimization_barrier((below3, above3, total))
    around = lax.optimization_barrier((*around, total))[:4]
    swapped = lax.ppermute(jnp.concatenate(around, axis=0), "core", SWAP)
    swapped = [swapped[at * 2 * span : (at + 1) * 2 * span] for at in range(4)]
    left_high, left_low = left_call(place, list(around) + swapped)
    middle = below3.shape[0] // 2
    far, near = shift(below3[:middle], "z", 1), shift(above3[middle:], "z", -1)
    total = group_call(2, place, below3, above3, screen_high, screen_low, total)
    far, near, total, left_high, left_low = lax.optimization_barrier((far, near, total, left_high, left_low))
    keep, give = pair_call(place, table, plane, far, near, screen_high, screen_low, total, left_high, left_low)

    parts = rows_call(keep, lax.ppermute(give, "core", SWAP))
    parts = lax.all_to_all(parts, "x", 0, 0, tiled=True)
    parts = owner_call(offset, parts)
    parts = lax.all_to_all(parts, ("z", "y"), 0, 0, tiled=True)
    own = sum_call(parts)
    result = last_call(place, held, own, lax.ppermute(own, "core", SWAP))
    return result.reshape(1, CAP, 2, 4, BLK)


def solution(mesh):
    fine = Mesh(mesh.devices.reshape(8, 4, 2, 4), ("z", "y", "core", "x"))
    in_specs = (P(None, BAND, "x"), P(None, None, BAND, "x"), P(), P())
    out_specs = P(BAND, None, None, "x", None)
    return jax.shard_map(shards, mesh=fine, in_specs=in_specs, out_specs=out_specs, check_vma=False)
```

```python
import functools

import jax
import jax.numpy as jnp
from jax import lax
from jax.experimental import pallas as pl
from jax.experimental.pallas import tpu as pltpu
from jax.sharding import Mesh
from jax.sharding import PartitionSpec as P

NG = 10240
CAP = 12
BLK = 16
USED = 32
HALF = USED // 2 * BLK
BAND = ("z", "y", "core")
SWAP = ((0, 1), (1, 0))
SMEM = pl.BlockSpec(memory_space=pltpu.SMEM)
VMEM = pl.BlockSpec(memory_space=pltpu.VMEM)
SPAN = 80
PLANE = 2 * SPAN
ORDER = (0, 7, 1, 6, 2, 5, 3, 4)
GROUPS = ((0, 5, 896), (5, 7, 384), (7, 8, 256))
TURN = 2560 - 256


def ring(n, shift):
    return [(i, (i + shift) % n) for i in range(n)]


def params(mib):
    return pltpu.CompilerParams(vmem_limit_bytes=mib * 1024 * 1024)


def split(x):
    high = x.astype(jnp.bfloat16)
    return high, (x - high.astype(jnp.float32)).astype(jnp.bfloat16)


def dot(former, latter):
    return jnp.dot(former, latter, preferred_element_type=jnp.float32)


def dot3(high, low, former, latter):
    return dot(high, former) + dot(high, latter) + dot(low, former)


def plan(pairs, owners):
    blocks = 64
    ids = jnp.arange(blocks, dtype=jnp.int32)
    left, right = pairs[:, 0], pairs[:, 1]
    used = jnp.any(right[:, None] == ids[None, :], axis=0).astype(jnp.int32)
    rank = jnp.sum(used[None, :] * (ids[None, :] < ids[:, None]), axis=1)
    slots = jnp.arange(USED, dtype=jnp.int32)
    used_list = jnp.sum(
        jnp.where((rank[None, :] == slots[:, None]) & (used[None, :] > 0), ids[None, :], 0), axis=1
    )
    right_rank = jnp.sum(used[None, :] * (ids[None, :] < right[:, None]), axis=1)
    count = jnp.sum((owners[:, None] == ids[None, :]).astype(jnp.int32), axis=0)
    offset = jnp.sum(count[None, :] * (ids[None, :] < ids[:, None]), axis=1)
    order = jnp.arange(owners.shape[0], dtype=jnp.int32)
    ahead = (owners[None, :] < owners[:, None]) | (
        (owners[None, :] == owners[:, None]) & (order[None, :] < order[:, None])
    )
    place = jnp.sum(ahead.astype(jnp.int32), axis=1)
    hit = place[None, :] == order[:, None]
    left_at = jnp.sum(jnp.where(hit, left[None, :], 0), axis=1)
    right_at = jnp.sum(jnp.where(hit, right_rank[None, :], 0), axis=1)
    return used_list, left_at, right_at, offset, count


def stripes(ref, row, first, z, slots, count):
    tiles = [None] * count
    for delta, base in slots:
        for upper in range(2):
            source = lax.rem(z + delta, 8) * (4 * SPAN) + (first + 2 * upper) * SPAN
            column = pl.multiple_of(jnp.minimum(source // 128 * 128, TURN), 128)
            target = base + upper * SPAN
            inner, at = target % 128, target // 128
            by = lax.rem(inner + 256 - (source - column), 256)
            window = pltpu.roll(ref[row, pl.ds(column, 256)], by, 1)
            end = inner + SPAN
            lane = lax.broadcasted_iota(jnp.int32, (window.shape[0], 128), 1)
            old = jnp.zeros((window.shape[0], 128), jnp.float32) if tiles[at] is None else tiles[at]
            tiles[at] = jnp.where((lane >= inner) & (lane < end), window[:, :128], old)
            if end > 128:
                tiles[at + 1] = jnp.where(lane < end - 128, window[:, 128:], 0.0)
    return [jnp.zeros((16, 128), jnp.float32) if tile is None else tile for tile in tiles]


def give_kernel(place, in_ref, *outs):
    z, y = place[0], place[2]
    first = lax.rem(y + 1, 2)
    slots = [(delta, slot * PLANE) for slot, delta in enumerate(ORDER)]
    start = 0
    for out_ref in outs:

        def body(step, carry, start=start, out_ref=out_ref):
            row = pl.ds(pl.multiple_of(start + step * 16, 16), 16)
            tiles = stripes(in_ref, row, first, z, slots, 10)
            for at, tile in enumerate(tiles):
                out_ref[pl.ds(pl.multiple_of(step * 16, 16), 16), at * 128 : (at + 1) * 128] = tile
            return carry

        lax.fori_loop(0, out_ref.shape[0] // 16, body, 0)
        start += out_ref.shape[0]


def give_call(place, screen, chunks):
    width = screen.shape[1] // 2
    return pl.pallas_call(
        give_kernel,
        out_shape=[jax.ShapeDtypeStruct((rows, width), jnp.float32) for rows in chunks],
        in_specs=[SMEM, VMEM],
        out_specs=[VMEM] * len(chunks),
        compiler_params=params(12),
        name="give",
    )(place, screen)


def store_groups(outs, row, tiles):
    column = 0
    for group, (_, _, width) in enumerate(GROUPS):
        block = jnp.concatenate(tiles[column // 128 : (column + width) // 128], axis=1)
        top, rest = split(block)
        outs[2 * group][row, :] = top
        outs[2 * group + 1][row, :] = rest
        column += width


def own_kernel(place, *refs):
    sources, outs = refs[:2], refs[2:]
    z, y = place[0], place[2]
    first = lax.rem(y, 2)
    slots, base = [], 0
    for one, two, width in GROUPS:
        slots += [(ORDER[slot], base + (slot - one) * PLANE) for slot in range(one, two)]
        base += width
    for index, ref in enumerate(sources):
        count = ref.shape[0]

        def body(step, carry, index=index, ref=ref, count=count):
            tiles = stripes(ref, pl.ds(pl.multiple_of(step * 16, 16), 16), first, z, slots, base // 128)
            store_groups(outs, pl.ds(pl.multiple_of(index * count + step * 16, 16), 16), tiles)
            return carry

        lax.fori_loop(0, count // 16, body, 0)


def come_kernel(*refs):
    sources, outs = refs[:-6], refs[-6:]
    start = 0
    for ref in sources:

        def body(step, carry, start=start, ref=ref):
            row = pl.ds(pl.multiple_of(step * 16, 16), 16)
            tiles = []
            for one, two, width in GROUPS:
                low, high = one * PLANE, two * PLANE
                aligned = low // 128 * 128
                block = ref[row, aligned : (high + 127) // 128 * 128]
                if low > aligned:
                    block = pltpu.roll(block, block.shape[1] - (low - aligned), 1)
                if block.shape[1] < width:
                    pad = jnp.zeros((16, width - block.shape[1]), jnp.float32)
                    block = jnp.concatenate([block, pad], axis=1)
                lane = lax.broadcasted_iota(jnp.int32, (16, width), 1)
                block = jnp.where(lane < high - low, block[:, :width], 0.0)
                tiles += [block[:, at : at + 128] for at in range(0, width, 128)]
            store_groups(outs, pl.ds(pl.multiple_of(start + step * 16, 16), 16), tiles)
            return carry

        lax.fori_loop(0, ref.shape[0] // 16, body, 0)
        start += ref.shape[0]


def screen_call(place, sources):
    kernel, first = (come_kernel, []) if place is None else (own_kernel, [place])
    rows = sum(source.shape[0] for source in sources)
    return pl.pallas_call(
        kernel,
        out_shape=[jax.ShapeDtypeStruct((rows, width), jnp.bfloat16) for _, _, width in GROUPS for _ in range(2)],
        in_specs=[SMEM] * len(first) + [VMEM] * len(sources),
        out_specs=[VMEM] * 6,
        compiler_params=params(24),
        name="come" if place is None else "own",
    )(*first, *sources)


def left_kernel(place, *refs):
    pieces, (high_ref, low_ref, work) = refs[:8], refs[8:]
    x = place[1]
    span = pieces[0].shape[0] // 4
    for core in range(2):
        for shift in range(4):
            shard = lax.rem(x - shift + 4, 4)
            for chip in range(2):
                for part in range(2):
                    row = ((chip * 2 + core) * 2 + part) * 4 * span + shard * span
                    start = (chip * 2 + part) * span
                    work[pl.ds(pl.multiple_of(row, 8), span), :] = pieces[core * 4 + shift][start : start + span, :]
    for block in range(work.shape[1] // 128):
        turned = work[:, block * 128 : (block + 1) * 128].T
        top, rest = split(turned)
        high_ref[block * 128 : (block + 1) * 128, :] = top
        low_ref[block * 128 : (block + 1) * 128, :] = rest


def left_call(place, pieces):
    depth, width = pieces[0].shape
    shape = jax.ShapeDtypeStruct((width, 8 * depth), jnp.bfloat16)
    return pl.pallas_call(
        left_kernel,
        out_shape=(shape, shape),
        in_specs=[SMEM] + [VMEM] * 8,
        out_specs=(VMEM, VMEM),
        scratch_shapes=[pltpu.VMEM((8 * depth, width), jnp.float32)],
        compiler_params=params(30),
        name="left",
    )(place, *pieces)


def load_right(place, planes, high, low):
    second = place[2] // 2
    for plane, refs in enumerate(planes):
        for at in range(2):
            place_in = second if at == 0 else 1 - second
            row = pl.multiple_of(plane * PLANE + place_in * SPAN, 16)
            ref, base = (refs[0], at * 2 * SPAN) if len(refs) == 1 else (refs[at], 0)
            for part in range(2):
                start = base + part * SPAN
                top, rest = split(ref[start : start + SPAN, :])
                high[pl.ds(row, SPAN), part * HALF : (part + 1) * HALF] = top
                low[pl.ds(row, SPAN), part * HALF : (part + 1) * HALF] = rest
    used = len(planes) * PLANE
    for ref in (high, low):
        ref[used:, :] = jnp.zeros((ref.shape[0] - used, ref.shape[1]), ref.dtype)


def group_kernel(planes, place, *refs):
    rights, screens, rest = refs[:planes], refs[planes : planes + 4], refs[planes + 4 :]
    out_ref, rh, rl = rest[-3:]
    load_right(place, [(ref,) for ref in rights], rh, rl)
    half = out_ref.shape[0] // 2
    for at in range(2):
        rows = slice(at * half, (at + 1) * half)
        value = dot3(screens[2 * at][...], screens[2 * at + 1][...], rh[...], rl[...])
        out_ref[rows, :] = value if len(rest) == 3 else value + rest[0][rows, :]


def group_call(place, rights, screens, total):
    rows, width = screens[0].shape
    return pl.pallas_call(
        functools.partial(group_kernel, len(rights)),
        out_shape=jax.ShapeDtypeStruct((2 * rows, 2 * HALF), jnp.float32),
        in_specs=[SMEM] + [VMEM] * (len(rights) + 4 + len(total)),
        out_specs=VMEM,
        scratch_shapes=[pltpu.VMEM((width, 2 * HALF), jnp.bfloat16)] * 2,
        compiler_params=params(32),
        name="group",
    )(place, *rights, *screens, *total)


def pair_kernel(place, table, one_ref, two_ref, *refs):
    screens, (sum_ref, left_high, left_low, keep_ref, give_ref, rh, rl, kern) = refs[:4], refs[4:]
    load_right(place, ((one_ref, two_ref),), rh, rl)
    half = sum_ref.shape[0] // 2
    mid = half // 4
    applied = []
    for at in range(2):
        product = dot3(screens[2 * at][...], screens[2 * at + 1][...], rh[...], rl[...])
        product = product + sum_ref[at * half : (at + 1) * half, :]
        for source in range(2):
            top = product[2 * source * mid : (2 * source + 1) * mid]
            low = product[(2 * source + 1) * mid : (2 * source + 2) * mid]
            real = top[:, :HALF] - low[:, HALF:]
            imag = low[:, :HALF] + top[:, HALF:]
            applied += [jnp.concatenate([real, imag], axis=1), jnp.concatenate([imag, -real], axis=1)]
    applied = NG ** (-0.5) * jnp.concatenate(applied, axis=0)
    kern[...] = dot3(left_high[...], left_low[...], *split(applied))

    lane = lax.broadcasted_iota(jnp.int32, (8, 128), 1) // BLK
    core = place[3]

    def group(g, carry):
        tiles = [[jnp.zeros((8, 128), jnp.float32) for _ in range(2)] for _ in range(2)]
        for u in range(8):
            row = pl.multiple_of(table[0, g * 8 + u] * BLK, BLK)
            column = pl.multiple_of(table[1, g * 8 + u] * 128, 128)
            shift = table[2, g * 8 + u]
            target = table[3, g * 8 + u]
            for part in range(2):
                for half in range(2):
                    tile = kern[pl.ds(row + half * 8, 8), pl.ds(column + part * HALF, 128)]
                    tile = pltpu.roll(tile, shift, 1)
                    tiles[part][half] = jnp.where(lane == target, tile, tiles[part][half])
        lanes = pl.ds(pl.multiple_of(g * 128, 128), 128)
        for half in range(2):
            keep_ref[half, :, lanes] = jnp.where(core == 0, tiles[0][half], tiles[1][half])
            give_ref[half, :, lanes] = jnp.where(core == 0, tiles[1][half], tiles[0][half])
        return carry

    lax.fori_loop(0, table.shape[1] // 8, group, 0)


def pair_call(place, table, one, two, screens, total, left_high, left_low):
    shape = jax.ShapeDtypeStruct((2, 8, table.shape[1] * BLK), jnp.float32)
    return pl.pallas_call(
        pair_kernel,
        out_shape=(shape, shape),
        in_specs=[SMEM, SMEM] + [VMEM] * 9,
        out_specs=(VMEM, VMEM),
        scratch_shapes=[pltpu.VMEM((screens[0].shape[1], 2 * HALF), jnp.bfloat16)] * 2
        + [pltpu.VMEM((left_high.shape[0], 2 * HALF), jnp.float32)],
        compiler_params=params(44),
        name="pair",
    )(place, table, one, two, *screens, total, left_high, left_low)


def rows_kernel(keep_ref, come_ref, out_ref):
    upper = lax.broadcasted_iota(jnp.int32, out_ref.shape[1:], 0) < 4
    width = out_ref.shape[2]
    for half in range(2):
        total = keep_ref[half] + come_ref[half]
        top, bottom = total[:, :width], total[:, width:]
        out_ref[2 * half] = jnp.where(upper, top, pltpu.roll(bottom, 4, 0))
        out_ref[2 * half + 1] = jnp.where(upper, pltpu.roll(top, 4, 0), bottom)


def rows_call(keep, come):
    return pl.pallas_call(
        rows_kernel,
        out_shape=jax.ShapeDtypeStruct((4, 8, keep.shape[2] // 2), jnp.float32),
        in_specs=[VMEM, VMEM],
        out_specs=VMEM,
        name="rows",
    )(keep, come)


def owner_kernel(offset, parts_ref, out_ref, work):
    total = parts_ref[0] + parts_ref[1] + parts_ref[2] + parts_ref[3]
    width = total.shape[1]
    upper = lax.broadcasted_iota(jnp.int32, total.shape, 0) < 4
    turned = pltpu.roll(total, 4, 0)
    work[:, :width] = jnp.where(upper, total, turned)
    work[:, width : 2 * width] = jnp.where(upper, turned, total)
    work[:, 2 * width :] = jnp.zeros((8, work.shape[1] - 2 * width), jnp.float32)
    first = lax.broadcasted_iota(jnp.int32, (8, 384), 0) < 4

    for chip in range(out_ref.shape[0]):
        windows = []
        for core in range(2):
            start = offset[chip * 2 + core]
            column = pl.multiple_of(start // 8 * 128, 128)
            shift = lax.rem(384 - lax.rem(start, 8) * BLK, 384)
            windows.append(pltpu.roll(work[:, pl.ds(column, 384)], shift, 1))
        out_ref[chip] = jnp.where(first, *windows)[:, :256]


def owner_call(offset, parts):
    return pl.pallas_call(
        owner_kernel,
        out_shape=jax.ShapeDtypeStruct((32, 8, 256), jnp.float32),
        in_specs=[SMEM, VMEM],
        out_specs=VMEM,
        scratch_shapes=[pltpu.VMEM((8, 2 * parts.shape[2] + 384), jnp.float32)],
        name="owner",
    )(offset, parts)


def sum_kernel(in_ref, out_ref):
    total = in_ref[0]
    for chip in range(1, in_ref.shape[0]):
        total = total + in_ref[chip]
    out_ref[...] = total


def sum_call(parts):
    return pl.pallas_call(
        sum_kernel,
        out_shape=jax.ShapeDtypeStruct(parts.shape[1:], jnp.float32),
        in_specs=[VMEM],
        out_specs=VMEM,
        name="total",
    )(parts)


def last_kernel(place, held_ref, own_ref, come_ref, out_ref):
    core, held = place[3], held_ref[0]
    own, come = own_ref[...], come_ref[...]
    real = jnp.where(core == 0, own, come)
    imag = jnp.where(core == 0, come, own)
    upper = lax.broadcasted_iota(jnp.int32, own.shape, 0) < 4
    mine = jnp.where(
        core == 0,
        jnp.where(upper, real, pltpu.roll(imag, 4, 0)),
        jnp.where(upper, pltpu.roll(real, 4, 0), imag),
    )
    for slot in range(CAP):
        tile = mine[:, slot // 8 * 128 : slot // 8 * 128 + 128]
        tile = pltpu.roll(tile, (128 - slot % 8 * BLK) % 128, 1)
        out_ref[slot] = jnp.where(slot < held, tile[:, :BLK], 0.0)


def last_call(place, held, own, come):
    return pl.pallas_call(
        last_kernel,
        out_shape=jax.ShapeDtypeStruct((CAP, 8, BLK), jnp.float32),
        in_specs=[SMEM, SMEM, VMEM, VMEM],
        out_specs=VMEM,
        name="last",
    )(place, held, own, come)


def pack_kernel(place, own_ref, other_ref, out_ref, work):
    core = place[3]
    width = own_ref.shape[2]
    for block in range(width // 128):
        lanes = pl.ds(block * 128, 128)
        rows = []
        for part in range(2):
            own, other = own_ref[part, :, lanes], other_ref[part, :, lanes]
            rows += [jnp.where(core == 0, own, other), jnp.where(core == 0, other, own)]
        rows = jnp.concatenate(rows + rows, axis=0)
        work[block * 128 : (block + 1) * 128, :] = rows.T
    half = lax.broadcasted_iota(jnp.int32, (8, 128), 1) < 64
    for chip in range(32):
        at = pl.multiple_of(chip * 80 + core * 40, 8)
        tiles = [work[pl.ds(at + 8 * t, 8), :] for t in range(5)]
        out_ref[chip * 20 : chip * 20 + 8, :] = jnp.where(half, tiles[0], tiles[1])
        out_ref[chip * 20 + 8 : chip * 20 + 16, :] = jnp.where(half, tiles[2], tiles[3])
        last = jnp.where(half, tiles[4], pltpu.roll(tiles[4], 4, 0))
        out_ref[chip * 20 + 16 : chip * 20 + 20, :] = last[:4]


def pack_call(place, own, other):
    width = own.shape[2]
    return pl.pallas_call(
        pack_kernel,
        out_shape=jax.ShapeDtypeStruct((32 * 20, 128), jnp.float32),
        in_specs=[SMEM, VMEM, VMEM],
        out_specs=VMEM,
        scratch_shapes=[pltpu.VMEM((width, 128), jnp.float32)],
        name="pack",
    )(place, own, other)


def unpack_kernel(place, used, in_ref, columns_ref, keep_ref, give_ref):
    core = place[3]
    quarter = lax.broadcasted_iota(jnp.int32, (8, 128), 1) // 32
    upper = lax.broadcasted_iota(jnp.int32, (8, 128), 0) < 4
    for group in range(8):
        tiles = [[None] * 5 for _ in range(2)]
        for u in range(4):
            at = (group * 4 + u) * 20
            one, two = in_ref[at : at + 8, :], in_ref[at + 8 : at + 16, :]
            end = in_ref[at + 12 : at + 20, :]
            end = jnp.where(upper, pltpu.roll(end, 4, 0), pltpu.roll(end, 64, 1))
            for t, (source, first) in enumerate(((one, 0), (one, 64), (two, 0), (two, 64), (end, 0))):
                for part in range(2):
                    by = (u * 32 - first - part * 32) % 128
                    turned = pltpu.roll(source, by, 1) if by else source
                    old = tiles[part][t]
                    tiles[part][t] = turned if old is None else jnp.where(quarter == u, turned, old)
        for part in range(2):
            for t in range(5):
                row = part * 40 + t * 8
                columns_ref[row : row + 8, group * 128 : (group + 1) * 128] = tiles[part][t]
    eighth = lax.broadcasted_iota(jnp.int32, (80, 128), 1) // BLK
    for ref, which in ((give_ref, 1 - core), (keep_ref, core)):
        for group in range(2):
            slab = None
            for u in range(8):
                block = used[which * (USED // 2) + group * 8 + u]
                column = pl.multiple_of(block // 8 * 128, 128)
                by = lax.rem(u * BLK + 128 - lax.rem(block, 8) * BLK, 128)
                turned = pltpu.roll(columns_ref[:, pl.ds(column, 128)], by, 1)
                slab = turned if slab is None else jnp.where(eighth == u, turned, slab)
            ref[:, group * 128 : (group + 1) * 128] = slab


def unpack_call(place, used, pieces):
    return pl.pallas_call(
        unpack_kernel,
        out_shape=(
            jax.ShapeDtypeStruct((80, 1024), jnp.float32),
            jax.ShapeDtypeStruct((80, HALF), jnp.float32),
            jax.ShapeDtypeStruct((80, HALF), jnp.float32),
        ),
        in_specs=[SMEM, SMEM, VMEM],
        out_specs=(VMEM, VMEM, VMEM),
        name="unpack",
    )(place, used, pieces)


def shard_kernel(place, keep_ref, take_ref, out_ref):
    core = place[3]
    for part in range(2):
        out_ref[pl.ds(pl.multiple_of(part * 80 + core * 40, 8), 40), :] = keep_ref[part * 40 : part * 40 + 40, :]
        out_ref[pl.ds(pl.multiple_of(part * 80 + 40 - core * 40, 8), 40), :] = take_ref[part * 40 : part * 40 + 40, :]


def shard_call(place, keep, take):
    return pl.pallas_call(
        shard_kernel,
        out_shape=jax.ShapeDtypeStruct((160, HALF), jnp.float32),
        in_specs=[SMEM, VMEM, VMEM],
        out_specs=VMEM,
        name="shard",
    )(place, keep, take)


def after(array, *others):
    return lax.optimization_barrier((array, *others))[0]


def shards(densities, screened, pairs, owners):
    core, x = lax.axis_index("core"), lax.axis_index("x")
    z, y = lax.axis_index("z"), lax.axis_index("y")
    chip = z * lax.axis_size("y") + y
    span = screened.shape[2]
    used_list, left_at, right_at, offset, count = plan(pairs, owners)
    held = lax.dynamic_slice_in_dim(count, chip * 2 + core, 1)
    place = jnp.stack([z, x, y, core]).astype(jnp.int32)

    local = right_at - core * (USED // 2)
    valid = (local >= 0) & (local < USED // 2)
    local = jnp.where(valid, local, 0)
    lane = jnp.arange(local.shape[0], dtype=jnp.int32) % 8
    table = jnp.stack(
        [left_at, local // 8, (lane - local % 8) % 8 * BLK, jnp.where(valid, lane, -1)]
    ).astype(jnp.int32)

    shift = lambda array, axis, by: lax.ppermute(array, axis, ring(lax.axis_size(axis), by))
    partner = lambda array: lax.ppermute(array, "y", ((0, 1), (1, 0), (2, 3), (3, 2)))
    swap = lambda array: lax.ppermute(array, "core", SWAP)
    hold = lax.optimization_barrier

    screen = screened.reshape(2 * 4 * span, -1)
    others = swap(densities)
    chunks = give_call(place, screen, (192, 64, 64))
    come = [partner(chunks[0])]

    pieces = pack_call(place, densities, after(others, chunks[0]))
    mine = lax.all_to_all(pieces.reshape(32, 1, -1), ("z", "y"), 0, 0, tiled=True).reshape(pieces.shape)
    other = swap(after(screen, pieces))
    mine, table, offset, held, come[0], other = hold((mine, table, offset, held, come[0], other))

    come.append(partner(after(chunks[1], mine)))
    columns, keep, give = unpack_call(place, used_list, mine)
    give = swap(give)
    turned = [swap(come[0])]
    give, come[1], turned[0] = hold((give, come[1], turned[0]))
    shard = shard_call(place, keep, give)

    come.append(partner(after(chunks[2], give)))
    turned.append(swap(come[1]))
    columns = after(columns, give)
    columns = jnp.concatenate([columns, partner(columns)], axis=0)
    plane = jnp.concatenate([shard, shift(shard, "y", 2)], axis=0)
    plane, columns, come[2], turned[1] = hold((plane, columns, come[2], turned[1]))

    below, above = shift(plane, "z", 1), shift(plane, "z", -1)
    turned.append(swap(come[2]))
    own = screen_call(place, (screen, other))
    around = [columns] + [shift(columns, "x", by) for by in (1, 2, 3)]
    below, above, turned[2], *own = hold((below, above, turned[2], *own))

    below2, above2 = shift(below, "z", 1), shift(above, "z", -1)
    paired = screen_call(None, (*come, *turned))
    below2, above2, around[1], around[3], *paired = hold((below2, above2, around[1], around[3], *paired))

    below3, above3 = shift(below2, "z", 1), shift(above2, "z", -1)
    screens = [own[2 * at : 2 * at + 2] + paired[2 * at : 2 * at + 2] for at in range(3)]
    total = group_call(place, (plane, below, above, below2, above2), screens[0], ())
    swapped = swap(around[0])
    below3, above3, total, around[2], swapped = hold((below3, above3, total, around[2], swapped))

    middle = below3.shape[0] // 2
    far, near = shift(below3[:middle], "z", 1), shift(above3[middle:], "z", -1)
    total = group_call(place, (below3, above3), screens[1], (total,))
    left_high, left_low = left_call(place, around + [swapped] + [swap(array) for array in around[1:]])
    far, near, total, left_high, left_low = hold((far, near, total, left_high, left_low))
    keep, give = pair_call(place, table, far, near, screens[2], total, left_high, left_low)

    parts = rows_call(keep, lax.ppermute(give, "core", SWAP))
    parts = lax.all_to_all(parts, "x", 0, 0, tiled=True)
    parts = owner_call(offset, parts)
    parts = lax.all_to_all(parts, ("z", "y"), 0, 0, tiled=True)
    own = sum_call(parts)
    result = last_call(place, held, own, lax.ppermute(own, "core", SWAP))
    return result.reshape(1, CAP, 2, 4, BLK)


def solution(mesh):
    fine = Mesh(mesh.devices.reshape(8, 4, 2, 4), ("z", "y", "core", "x"))
    in_specs = (P(None, BAND, "x"), P(None, None, BAND, "x"), P(), P())
    out_specs = P(BAND, None, None, "x", None)
    return jax.shard_map(shards, mesh=fine, in_specs=in_specs, out_specs=out_specs, check_vma=False)
```

```python
import functools

import jax
import jax.numpy as jnp
from jax import lax
from jax.experimental import pallas as pl
from jax.experimental.pallas import tpu as pltpu
from jax.sharding import Mesh
from jax.sharding import PartitionSpec as P

NG = 10240
CAP = 12
BLK = 16
USED = 32
HALF = USED // 2 * BLK
BAND = ("z", "y", "core")
SWAP = ((0, 1), (1, 0))
SMEM = pl.BlockSpec(memory_space=pltpu.SMEM)
VMEM = pl.BlockSpec(memory_space=pltpu.VMEM)
SPAN = 80
PLANE = 320
NEAR = (0, 7, 1, 6, 2)
FAR = (5, 3, 4)


def ring(n, shift):
    return [(i, (i + shift) % n) for i in range(n)]


def params(mib):
    return pltpu.CompilerParams(vmem_limit_bytes=mib * 1024 * 1024)


def split(x):
    high = x.astype(jnp.bfloat16)
    return high, (x - high.astype(jnp.float32)).astype(jnp.bfloat16)


def dot(former, latter):
    return jnp.dot(former, latter, preferred_element_type=jnp.float32)


def dot3(high, low, former, latter):
    return dot(high, former) + dot(high, latter) + dot(low, former)


def plan(pairs, owners):
    blocks = 64
    ids = jnp.arange(blocks, dtype=jnp.int32)
    left, right = pairs[:, 0], pairs[:, 1]
    used = jnp.any(right[:, None] == ids[None, :], axis=0).astype(jnp.int32)
    rank = jnp.sum(used[None, :] * (ids[None, :] < ids[:, None]), axis=1)
    slots = jnp.arange(USED, dtype=jnp.int32)
    used_list = jnp.sum(
        jnp.where((rank[None, :] == slots[:, None]) & (used[None, :] > 0), ids[None, :], 0), axis=1
    )
    right_rank = jnp.sum(used[None, :] * (ids[None, :] < right[:, None]), axis=1)
    count = jnp.sum((owners[:, None] == ids[None, :]).astype(jnp.int32), axis=0)
    offset = jnp.sum(count[None, :] * (ids[None, :] < ids[:, None]), axis=1)
    order = jnp.arange(owners.shape[0], dtype=jnp.int32)
    ahead = (owners[None, :] < owners[:, None]) | (
        (owners[None, :] == owners[:, None]) & (order[None, :] < order[:, None])
    )
    place = jnp.sum(ahead.astype(jnp.int32), axis=1)
    hit = place[None, :] == order[:, None]
    left_at = jnp.sum(jnp.where(hit, left[None, :], 0), axis=1)
    right_at = jnp.sum(jnp.where(hit, right_rank[None, :], 0), axis=1)
    return used_list, left_at, right_at, offset, count


def padded(planes):
    return (len(planes) * PLANE + 127) // 128 * 128


def screen_kernel(place, own_ref, other_ref, *outs):
    z = place[0]
    rows = 16
    lane = lax.broadcasted_iota(jnp.int32, (rows, 128), 1)

    def plane_of(ref, row, delta, offset):
        plane = lax.rem(z + delta, 8)
        odd = lax.rem(plane, 2)
        column = pl.multiple_of(plane * PLANE - odd * 64, 128)
        window = ref[row, pl.ds(column, 384)]
        turned = pltpu.roll(window, 64 if offset else 320, 1)
        return jnp.where((odd == 1) if offset else (odd == 0), window, turned)

    for source, ref in enumerate((own_ref, other_ref)):

        def body(step, carry, source=source, ref=ref):
            part = step // 10
            row = pl.ds(pl.multiple_of(step * rows, rows), rows)
            target = pl.multiple_of(part * PLANE + source * (PLANE // 2) + (step - part * 10) * rows, rows)
            for group, planes in enumerate((NEAR, FAR)):
                for at in range(0, len(planes), 2):
                    a = plane_of(ref, row, planes[at], False)
                    if at + 1 < len(planes):
                        b = plane_of(ref, row, planes[at + 1], True)
                        middle = jnp.where(lane < 64, a[:, 256:], b[:, :128])
                        whole = jnp.concatenate([a[:, :256], middle, b[:, 128:]], axis=1)
                    else:
                        whole = jnp.concatenate([a[:, :256], jnp.where(lane < 64, a[:, 256:], 0.0)], axis=1)
                    top, rest = split(whole)
                    columns = slice(at * PLANE, at * PLANE + whole.shape[1])
                    outs[2 * group][pl.ds(target, rows), columns] = top
                    outs[2 * group + 1][pl.ds(target, rows), columns] = rest
            return carry

        lax.fori_loop(0, 20, body, 0)


def screen_call(place, own, other):
    shapes = [
        jax.ShapeDtypeStruct((2 * own.shape[0], padded(planes)), jnp.bfloat16)
        for planes in (NEAR, FAR)
        for _ in range(2)
    ]
    return pl.pallas_call(
        screen_kernel,
        out_shape=shapes,
        in_specs=[SMEM, VMEM, VMEM],
        out_specs=[VMEM] * 4,
        compiler_params=params(20),
        name="screen",
    )(place, own, other)


def left_kernel(place, *refs):
    pieces, (high_ref, low_ref, work) = refs[:8], refs[8:]
    x = place[1]
    span = pieces[0].shape[0] // 2
    for core in range(2):
        for shift in range(4):
            shard = lax.rem(x - shift + 4, 4)
            for part in range(2):
                row = pl.multiple_of(part * 8 * span + core * 4 * span + shard * span, 8)
                work[pl.ds(row, span), :] = pieces[core * 4 + shift][part * span : (part + 1) * span, :]
    for block in range(work.shape[1] // 128):
        turned = work[:, block * 128 : (block + 1) * 128].T
        top, rest = split(turned)
        high_ref[block * 128 : (block + 1) * 128, :] = top
        low_ref[block * 128 : (block + 1) * 128, :] = rest


def left_call(place, pieces):
    depth, width = pieces[0].shape
    shape = jax.ShapeDtypeStruct((width, 8 * depth), jnp.bfloat16)
    return pl.pallas_call(
        left_kernel,
        out_shape=(shape, shape),
        in_specs=[SMEM] + [VMEM] * 8,
        out_specs=(VMEM, VMEM),
        scratch_shapes=[pltpu.VMEM((8 * depth, width), jnp.float32)],
        compiler_params=params(20),
        name="left",
    )(place, *pieces)


def load_right(place, units, planes, high, low):
    y = place[2]
    for delta, plane, part, ref, start in units:
        row = pl.multiple_of(plane * PLANE + lax.rem(y + delta, 4) * SPAN, 16)
        top, rest = split(ref[start : start + SPAN, :])
        high[pl.ds(row, SPAN), part * HALF : (part + 1) * HALF] = top
        low[pl.ds(row, SPAN), part * HALF : (part + 1) * HALF] = rest
    used = planes * PLANE
    for ref in (high, low):
        ref[used:, :] = jnp.zeros((ref.shape[0] - used, ref.shape[1]), ref.dtype)


def units_of(planes, own, below, above, two_below, two_above):
    units = []
    for unit in range(2 * planes):
        half, at = (two_below, unit) if unit < planes else (two_above, unit - planes)
        for delta, (ref, start), index in ((0, own, unit), (3, below, unit), (1, above, unit), (2, half, at)):
            units.append((delta, unit // 2, unit % 2, ref, start + index * SPAN))
    return units


def group_kernel(place, own, below, above, two_below, two_above, high_ref, low_ref, out_ref, rh, rl):
    sources = [(ref, 0) for ref in (own, below, above, two_below, two_above)]
    load_right(place, units_of(len(NEAR), *sources), len(NEAR), rh, rl)
    out_ref[...] = dot3(high_ref[...], low_ref[...], rh[...], rl[...])


def group_call(place, rights, high, low):
    rows, width = high.shape
    return pl.pallas_call(
        group_kernel,
        out_shape=jax.ShapeDtypeStruct((rows, 2 * HALF), jnp.float32),
        in_specs=[SMEM] + [VMEM] * 7,
        out_specs=VMEM,
        scratch_shapes=[pltpu.VMEM((width, 2 * HALF), jnp.bfloat16)] * 2,
        compiler_params=params(32),
        name="group",
    )(place, *rights, high, low)


def pair_kernel(place, table, own, below, above, two_below, two_above, high_ref, low_ref, sum_ref, left_high, left_low, keep_ref, give_ref, rh, rl, kern):
    skip = len(NEAR) * SPAN
    sources = [(own, 0), (below, skip), (above, skip), (two_below, 0), (two_above, 0)]
    load_right(place, units_of(len(FAR), *sources), len(FAR), rh, rl)
    product = sum_ref[...] + dot3(high_ref[...], low_ref[...], rh[...], rl[...])
    mid = product.shape[0] // 2
    real = product[:mid, :HALF] - product[mid:, HALF:]
    imag = product[mid:, :HALF] + product[:mid, HALF:]
    applied = NG ** (-0.5) * jnp.concatenate(
        [jnp.concatenate([real, imag], axis=0), jnp.concatenate([imag, -real], axis=0)], axis=1
    )
    kern[...] = dot3(left_high[...], left_low[...], *split(applied))

    lane = lax.broadcasted_iota(jnp.int32, (8, 128), 1) // BLK
    core = place[3]

    def group(g, carry):
        tiles = [[jnp.zeros((8, 128), jnp.float32) for _ in range(2)] for _ in range(2)]
        for u in range(8):
            row = pl.multiple_of(table[0, g * 8 + u] * BLK, BLK)
            column = pl.multiple_of(table[1, g * 8 + u] * 128, 128)
            shift = table[2, g * 8 + u]
            target = table[3, g * 8 + u]
            for part in range(2):
                for half in range(2):
                    tile = kern[pl.ds(row + half * 8, 8), pl.ds(column + part * HALF, 128)]
                    tile = pltpu.roll(tile, shift, 1)
                    tiles[part][half] = jnp.where(lane == target, tile, tiles[part][half])
        lanes = pl.ds(pl.multiple_of(g * 128, 128), 128)
        for half in range(2):
            keep_ref[half, :, lanes] = jnp.where(core == 0, tiles[0][half], tiles[1][half])
            give_ref[half, :, lanes] = jnp.where(core == 0, tiles[1][half], tiles[0][half])
        return carry

    lax.fori_loop(0, table.shape[1] // 8, group, 0)


def pair_call(place, table, rights, high, low, total, left_high, left_low):
    shape = jax.ShapeDtypeStruct((2, 8, table.shape[1] * BLK), jnp.float32)
    return pl.pallas_call(
        pair_kernel,
        out_shape=(shape, shape),
        in_specs=[SMEM, SMEM] + [VMEM] * 10,
        out_specs=(VMEM, VMEM),
        scratch_shapes=[pltpu.VMEM((high.shape[1], 2 * HALF), jnp.bfloat16)] * 2
        + [pltpu.VMEM((left_high.shape[0], 2 * HALF), jnp.float32)],
        compiler_params=params(40),
        name="pair",
    )(place, table, *rights, high, low, total, left_high, left_low)


def rows_kernel(keep_ref, come_ref, out_ref):
    upper = lax.broadcasted_iota(jnp.int32, out_ref.shape[1:], 0) < 4
    width = out_ref.shape[2]
    for half in range(2):
        total = keep_ref[half] + come_ref[half]
        top, bottom = total[:, :width], total[:, width:]
        out_ref[2 * half] = jnp.where(upper, top, pltpu.roll(bottom, 4, 0))
        out_ref[2 * half + 1] = jnp.where(upper, pltpu.roll(top, 4, 0), bottom)


def rows_call(keep, come):
    return pl.pallas_call(
        rows_kernel,
        out_shape=jax.ShapeDtypeStruct((4, 8, keep.shape[2] // 2), jnp.float32),
        in_specs=[VMEM, VMEM],
        out_specs=VMEM,
        name="rows",
    )(keep, come)


def owner_kernel(offset, parts_ref, out_ref, work):
    total = parts_ref[0] + parts_ref[1] + parts_ref[2] + parts_ref[3]
    width = total.shape[1]
    upper = lax.broadcasted_iota(jnp.int32, total.shape, 0) < 4
    turned = pltpu.roll(total, 4, 0)
    work[:, :width] = jnp.where(upper, total, turned)
    work[:, width : 2 * width] = jnp.where(upper, turned, total)
    work[:, 2 * width :] = jnp.zeros((8, work.shape[1] - 2 * width), jnp.float32)
    first = lax.broadcasted_iota(jnp.int32, (8, 384), 0) < 4

    for chip in range(out_ref.shape[0]):
        windows = []
        for core in range(2):
            start = offset[chip * 2 + core]
            column = pl.multiple_of(start // 8 * 128, 128)
            shift = lax.rem(384 - lax.rem(start, 8) * BLK, 384)
            windows.append(pltpu.roll(work[:, pl.ds(column, 384)], shift, 1))
        out_ref[chip] = jnp.where(first, *windows)[:, :256]


def owner_call(offset, parts):
    return pl.pallas_call(
        owner_kernel,
        out_shape=jax.ShapeDtypeStruct((32, 8, 256), jnp.float32),
        in_specs=[SMEM, VMEM],
        out_specs=VMEM,
        scratch_shapes=[pltpu.VMEM((8, 2 * parts.shape[2] + 384), jnp.float32)],
        name="owner",
    )(offset, parts)


def sum_kernel(in_ref, out_ref):
    total = in_ref[0]
    for chip in range(1, in_ref.shape[0]):
        total = total + in_ref[chip]
    out_ref[...] = total


def sum_call(parts):
    return pl.pallas_call(
        sum_kernel,
        out_shape=jax.ShapeDtypeStruct(parts.shape[1:], jnp.float32),
        in_specs=[VMEM],
        out_specs=VMEM,
        name="total",
    )(parts)


def last_kernel(place, held_ref, own_ref, come_ref, out_ref):
    core, held = place[3], held_ref[0]
    own, come = own_ref[...], come_ref[...]
    real = jnp.where(core == 0, own, come)
    imag = jnp.where(core == 0, come, own)
    upper = lax.broadcasted_iota(jnp.int32, own.shape, 0) < 4
    mine = jnp.where(
        core == 0,
        jnp.where(upper, real, pltpu.roll(imag, 4, 0)),
        jnp.where(upper, pltpu.roll(real, 4, 0), imag),
    )
    for slot in range(CAP):
        tile = mine[:, slot // 8 * 128 : slot // 8 * 128 + 128]
        tile = pltpu.roll(tile, (128 - slot % 8 * BLK) % 128, 1)
        out_ref[slot] = jnp.where(slot < held, tile[:, :BLK], 0.0)


def last_call(place, held, own, come):
    return pl.pallas_call(
        last_kernel,
        out_shape=jax.ShapeDtypeStruct((CAP, 8, BLK), jnp.float32),
        in_specs=[SMEM, SMEM, VMEM, VMEM],
        out_specs=VMEM,
        name="last",
    )(place, held, own, come)


def pack_kernel(place, own_ref, other_ref, out_ref, work):
    core = place[3]
    width = own_ref.shape[2]
    for block in range(width // 128):
        lanes = pl.ds(block * 128, 128)
        rows = []
        for part in range(2):
            own, other = own_ref[part, :, lanes], other_ref[part, :, lanes]
            rows += [jnp.where(core == 0, own, other), jnp.where(core == 0, other, own)]
        rows = jnp.concatenate(rows + rows, axis=0)
        work[block * 128 : (block + 1) * 128, :] = rows.T
    half = lax.broadcasted_iota(jnp.int32, (8, 128), 1) < 64
    for chip in range(32):
        at = pl.multiple_of(chip * 80 + core * 40, 8)
        tiles = [work[pl.ds(at + 8 * t, 8), :] for t in range(5)]
        out_ref[chip * 20 : chip * 20 + 8, :] = jnp.where(half, tiles[0], tiles[1])
        out_ref[chip * 20 + 8 : chip * 20 + 16, :] = jnp.where(half, tiles[2], tiles[3])
        last = jnp.where(half, tiles[4], pltpu.roll(tiles[4], 4, 0))
        out_ref[chip * 20 + 16 : chip * 20 + 20, :] = last[:4]


def pack_call(place, own, other):
    width = own.shape[2]
    return pl.pallas_call(
        pack_kernel,
        out_shape=jax.ShapeDtypeStruct((32 * 20, 128), jnp.float32),
        in_specs=[SMEM, VMEM, VMEM],
        out_specs=VMEM,
        scratch_shapes=[pltpu.VMEM((width, 128), jnp.float32)],
        name="pack",
    )(place, own, other)


def unpack_kernel(place, used, in_ref, columns_ref, keep_ref, give_ref):
    core = place[3]
    quarter = lax.broadcasted_iota(jnp.int32, (8, 128), 1) // 32
    upper = lax.broadcasted_iota(jnp.int32, (8, 128), 0) < 4
    for group in range(8):
        tiles = [[None] * 5 for _ in range(2)]
        for u in range(4):
            at = (group * 4 + u) * 20
            one, two = in_ref[at : at + 8, :], in_ref[at + 8 : at + 16, :]
            end = in_ref[at + 12 : at + 20, :]
            end = jnp.where(upper, pltpu.roll(end, 4, 0), pltpu.roll(end, 64, 1))
            for t, (source, first) in enumerate(((one, 0), (one, 64), (two, 0), (two, 64), (end, 0))):
                for part in range(2):
                    by = (u * 32 - first - part * 32) % 128
                    turned = pltpu.roll(source, by, 1) if by else source
                    old = tiles[part][t]
                    tiles[part][t] = turned if old is None else jnp.where(quarter == u, turned, old)
        for part in range(2):
            for t in range(5):
                row = part * 40 + t * 8
                columns_ref[row : row + 8, group * 128 : (group + 1) * 128] = tiles[part][t]
    eighth = lax.broadcasted_iota(jnp.int32, (80, 128), 1) // BLK
    for ref, which in ((give_ref, 1 - core), (keep_ref, core)):
        for group in range(2):
            slab = None
            for u in range(8):
                block = used[which * (USED // 2) + group * 8 + u]
                column = pl.multiple_of(block // 8 * 128, 128)
                by = lax.rem(u * BLK + 128 - lax.rem(block, 8) * BLK, 128)
                turned = pltpu.roll(columns_ref[:, pl.ds(column, 128)], by, 1)
                slab = turned if slab is None else jnp.where(eighth == u, turned, slab)
            ref[:, group * 128 : (group + 1) * 128] = slab


def unpack_call(place, used, pieces):
    return pl.pallas_call(
        unpack_kernel,
        out_shape=(
            jax.ShapeDtypeStruct((80, 1024), jnp.float32),
            jax.ShapeDtypeStruct((80, HALF), jnp.float32),
            jax.ShapeDtypeStruct((80, HALF), jnp.float32),
        ),
        in_specs=[SMEM, SMEM, VMEM],
        out_specs=(VMEM, VMEM, VMEM),
        name="unpack",
    )(place, used, pieces)


def shard_kernel(place, keep_ref, take_ref, out_ref):
    core = place[3]
    for part in range(2):
        out_ref[pl.ds(pl.multiple_of(part * 80 + core * 40, 8), 40), :] = keep_ref[part * 40 : part * 40 + 40, :]
        out_ref[pl.ds(pl.multiple_of(part * 80 + 40 - core * 40, 8), 40), :] = take_ref[part * 40 : part * 40 + 40, :]


def shard_call(place, keep, take):
    return pl.pallas_call(
        shard_kernel,
        out_shape=jax.ShapeDtypeStruct((160, HALF), jnp.float32),
        in_specs=[SMEM, VMEM, VMEM],
        out_specs=VMEM,
        name="shard",
    )(place, keep, take)


def after(array, *others):
    return lax.optimization_barrier((array, *others))[0]


def shards(densities, screened, pairs, owners):
    core, x = lax.axis_index("core"), lax.axis_index("x")
    z, y = lax.axis_index("z"), lax.axis_index("y")
    chip = z * lax.axis_size("y") + y
    span = screened.shape[2]
    used_list, left_at, right_at, offset, count = plan(pairs, owners)
    held = lax.dynamic_slice_in_dim(count, chip * 2 + core, 1)
    place = jnp.stack([z, x, y, core]).astype(jnp.int32)

    local = right_at - core * (USED // 2)
    valid = (local >= 0) & (local < USED // 2)
    local = jnp.where(valid, local, 0)
    lane = jnp.arange(local.shape[0], dtype=jnp.int32) % 8
    table = jnp.stack(
        [left_at, local // 8, (lane - local % 8) % 8 * BLK, jnp.where(valid, lane, -1)]
    ).astype(jnp.int32)

    pieces = pack_call(place, densities, lax.ppermute(densities, "core", SWAP))
    mine = lax.all_to_all(pieces.reshape(32, 1, -1), ("z", "y"), 0, 0, tiled=True).reshape(pieces.shape)
    mine, table, offset, held = lax.optimization_barrier((mine, table, offset, held))

    screen = screened.reshape(2 * 4 * span, -1)
    other = lax.ppermute(after(screen, pieces), "core", SWAP)

    columns, keep, give = unpack_call(place, used_list, mine)
    shard = shard_call(place, keep, lax.ppermute(give, "core", SWAP))

    shift = lambda array, axis, by: lax.ppermute(array, axis, ring(lax.axis_size(axis), by))
    join = lambda *arrays: jnp.concatenate(arrays, axis=0)
    hold = lax.optimization_barrier
    below, above = shift(shard, "z", 1), shift(shard, "z", -1)
    around = [columns] + [shift(after(columns, shard), "x", by) for by in (1, 2, 3)]
    below, above = hold((below, above))
    below2, above2 = shift(below, "z", 1), shift(above, "z", -1)
    below2, above2, around[1], around[3] = hold((below2, above2, around[1], around[3]))
    near = join(shard, below, above, below2, above2)
    near_down, near_up = shift(near, "y", 1), shift(near, "y", -1)
    below3, above3 = shift(below2, "z", 1), shift(above2, "z", -1)
    below3, above3 = hold((below3, above3))
    far_low, far_high = shift(below3[:SPAN], "z", 1), shift(above3[SPAN:], "z", -1)
    far = join(below3, above3, far_low, far_high)
    near_high, near_low, far_top, far_rest = screen_call(place, screen, other)
    near_down, near_up, far, around[2], near_high, near_low, far_top, far_rest = hold(
        (near_down, near_up, far, around[2], near_high, near_low, far_top, far_rest)
    )

    half = len(NEAR) * SPAN
    down, up = shift(join(near_down[:half], far), "y", 1), shift(join(near_up[half:], far), "y", -1)
    swapped = lax.ppermute(join(*around), "core", SWAP)
    swapped = [swapped[at * 2 * span : (at + 1) * 2 * span] for at in range(4)]
    left_high, left_low = left_call(place, list(around) + swapped)
    down, up, left_high, left_low = hold((down, up, left_high, left_low))

    cut = half + len(FAR) * SPAN
    last_down, last_up = shift(down[half:cut], "y", 1), shift(up[cut:], "y", -1)
    total = group_call(place, (near, near_down, near_up, down, up), near_high, near_low)
    last_down, last_up, total = hold((last_down, last_up, total))
    rights = (far, down, up, last_down, last_up)
    keep, give = pair_call(place, table, rights, far_top, far_rest, total, left_high, left_low)

    parts = rows_call(keep, lax.ppermute(give, "core", SWAP))
    parts = lax.all_to_all(parts, "x", 0, 0, tiled=True)
    parts = owner_call(offset, parts)
    parts = lax.all_to_all(parts, ("z", "y"), 0, 0, tiled=True)
    own = sum_call(parts)
    result = last_call(place, held, own, lax.ppermute(own, "core", SWAP))
    return result.reshape(1, CAP, 2, 4, BLK)


def solution(mesh):
    fine = Mesh(mesh.devices.reshape(8, 4, 2, 4), ("z", "y", "core", "x"))
    in_specs = (P(None, BAND, "x"), P(None, None, BAND, "x"), P(), P())
    out_specs = P(BAND, None, None, "x", None)
    return jax.shard_map(shards, mesh=fine, in_specs=in_specs, out_specs=out_specs, check_vma=False)
```

```python
import functools

import jax
import jax.numpy as jnp
from jax import lax
from jax.experimental import pallas as pl
from jax.experimental.pallas import tpu as pltpu
from jax.sharding import Mesh
from jax.sharding import PartitionSpec as P

NG = 10240
CAP = 12
BLK = 16
USED = 32
HALF = USED // 2 * BLK
BAND = ("z", "y", "core")
SWAP = ((0, 1), (1, 0))
SMEM = pl.BlockSpec(memory_space=pltpu.SMEM)
VMEM = pl.BlockSpec(memory_space=pltpu.VMEM)
SPAN = 80
PLANE = 320
NEAR = (0, 7, 1, 6, 2)
MIDDLE = (5, 3)
FAR = (4,)
ROOM = 224


def ring(n, shift):
    return [(i, (i + shift) % n) for i in range(n)]


def params(mib):
    return pltpu.CompilerParams(vmem_limit_bytes=mib * 1024 * 1024)


def split(x):
    high = x.astype(jnp.bfloat16)
    return high, (x - high.astype(jnp.float32)).astype(jnp.bfloat16)


def dot(former, latter):
    return jnp.dot(former, latter, preferred_element_type=jnp.float32)


def dot3(high, low, former, latter):
    return dot(high, former) + dot(high, latter) + dot(low, former)


def plan_kernel(place, pairs_ref, owners_ref, out_ref):
    size = 256
    down = lax.broadcasted_iota(jnp.int32, (size, size), 0)
    across = lax.broadcasted_iota(jnp.int32, (size, size), 1)
    one = lambda condition: jnp.where(condition, 1.0, 0.0)
    to_row = lambda column: jnp.sum(jnp.where(down == across, column, 0.0), axis=0, keepdims=True)
    to_column = lambda row: jnp.sum(jnp.where(down == across, row, 0.0), axis=1, keepdims=True)
    rows, columns = down.astype(jnp.float32), across.astype(jnp.float32)
    left, right = pairs_ref[:, 0:1].astype(jnp.float32), pairs_ref[:, 1:2].astype(jnp.float32)
    owner_row = owners_ref[...].astype(jnp.float32)
    owner = to_column(owner_row)

    used = jnp.max(one(right == columns), axis=0, keepdims=True)
    used_column = to_column(used)
    rank = jnp.sum(jnp.where(columns < rows, used, 0.0), axis=1, keepdims=True)
    used_list = jnp.sum(jnp.where((rank == columns) & (used_column > 0), rows, 0.0), axis=0, keepdims=True)
    right_rank = jnp.sum(jnp.where(columns < right, used, 0.0), axis=1, keepdims=True)

    parity = lambda value: value - 2.0 * jnp.floor(value * 0.5)
    count = jnp.sum(one(owner == columns), axis=0, keepdims=True)
    same = parity(rows) == parity(columns)
    offset = jnp.sum(jnp.where((rows < columns) & same, to_column(count), 0.0), axis=0, keepdims=True)
    ahead = (owner_row < owner) | ((owner_row == owner) & (across < down))
    ahead = ahead & (parity(owner_row) == parity(owner))
    position = jnp.sum(one(ahead), axis=1, keepdims=True)

    core = place[3].astype(jnp.float32)
    local = right_rank - core * (USED // 2)
    here = (local >= 0) & (local < USED // 2)
    local = jnp.where(here, local, 0.0)
    lane = lax.broadcasted_iota(jnp.int32, (1, size), 1)
    groups = jnp.zeros((1, size), jnp.float32)
    for half in range(2):
        hit = (position == columns) & (parity(owner) == half)
        pick = lambda column: jnp.sum(jnp.where(hit, column, 0.0), axis=0, keepdims=True).astype(jnp.int32)
        at = pick(local)
        out_ref[4 * half : 4 * half + 1, :] = pick(left) * BLK
        out_ref[4 * half + 1 : 4 * half + 2, :] = at // 8 * 128
        out_ref[4 * half + 2 : 4 * half + 3, :] = (lane + 8 - at % 8) % 8 * BLK
        out_ref[4 * half + 3 : 4 * half + 4, :] = jnp.where(pick(one(here)) > 0, lane % 8, -1)
        total = jnp.sum(one(parity(owner_row) == half))
        groups = jnp.where(lane == half, jnp.floor((total + 7.0) / 8.0), groups)
    for at, row in enumerate((offset, count, used_list, groups)):
        out_ref[8 + at : 9 + at, :] = row.astype(jnp.int32)


def plan_call(place, pairs, owners):
    return pl.pallas_call(
        plan_kernel,
        out_shape=jax.ShapeDtypeStruct((16, pairs.shape[0]), jnp.int32),
        in_specs=[SMEM, VMEM, VMEM],
        out_specs=VMEM,
        name="plan",
    )(place, pairs, owners)


def padded(planes):
    return (len(planes) * PLANE + 127) // 128 * 128


def screen_kernel(place, own_ref, other_ref, *outs):
    z = place[0]
    rows = 16
    lane = lax.broadcasted_iota(jnp.int32, (rows, 128), 1)

    def plane_of(ref, row, delta, offset):
        plane = lax.rem(z + delta, 8)
        odd = lax.rem(plane, 2)
        column = pl.multiple_of(plane * PLANE - odd * 64, 128)
        window = ref[row, pl.ds(column, 384)]
        turned = pltpu.roll(window, 64 if offset else 320, 1)
        return jnp.where((odd == 1) if offset else (odd == 0), window, turned)

    for source, ref in enumerate((own_ref, other_ref)):

        def body(step, carry, source=source, ref=ref):
            part = step // 10
            row = pl.ds(pl.multiple_of(step * rows, rows), rows)
            target = pl.multiple_of(part * PLANE + source * (PLANE // 2) + (step - part * 10) * rows, rows)
            for group, planes in enumerate((NEAR, MIDDLE, FAR)):
                for at in range(0, len(planes), 2):
                    a = plane_of(ref, row, planes[at], False)
                    if at + 1 < len(planes):
                        b = plane_of(ref, row, planes[at + 1], True)
                        middle = jnp.where(lane < 64, a[:, 256:], b[:, :128])
                        whole = jnp.concatenate([a[:, :256], middle, b[:, 128:]], axis=1)
                    else:
                        whole = jnp.concatenate([a[:, :256], jnp.where(lane < 64, a[:, 256:], 0.0)], axis=1)
                    top, rest = split(whole)
                    columns = slice(at * PLANE, at * PLANE + whole.shape[1])
                    outs[2 * group][pl.ds(target, rows), columns] = top
                    outs[2 * group + 1][pl.ds(target, rows), columns] = rest
            return carry

        lax.fori_loop(0, 20, body, 0)


def screen_call(place, own, other):
    shapes = [
        jax.ShapeDtypeStruct((2 * own.shape[0], padded(planes)), jnp.bfloat16)
        for planes in (NEAR, MIDDLE, FAR)
        for _ in range(2)
    ]
    return pl.pallas_call(
        screen_kernel,
        out_shape=shapes,
        in_specs=[SMEM, VMEM, VMEM],
        out_specs=[VMEM] * 6,
        compiler_params=params(20),
        name="screen",
    )(place, own, other)


def left_kernel(place, *refs):
    pieces, (high_ref, low_ref, work) = refs[:8], refs[8:]
    x = place[1]
    span = pieces[0].shape[0] // 2
    for core in range(2):
        for shift in range(4):
            shard = lax.rem(x - shift + 4, 4)
            for part in range(2):
                row = pl.multiple_of(part * 8 * span + core * 4 * span + shard * span, 8)
                work[pl.ds(row, span), :] = pieces[core * 4 + shift][part * span : (part + 1) * span, :]
    for block in range(work.shape[1] // 128):
        turned = work[:, block * 128 : (block + 1) * 128].T
        top, rest = split(turned)
        high_ref[block * 128 : (block + 1) * 128, :] = top
        low_ref[block * 128 : (block + 1) * 128, :] = rest


def left_call(place, pieces):
    depth, width = pieces[0].shape
    shape = jax.ShapeDtypeStruct((width, 8 * depth), jnp.bfloat16)
    return pl.pallas_call(
        left_kernel,
        out_shape=(shape, shape),
        in_specs=[SMEM] + [VMEM] * 8,
        out_specs=(VMEM, VMEM),
        scratch_shapes=[pltpu.VMEM((8 * depth, width), jnp.float32)],
        compiler_params=params(20),
        name="left",
    )(place, *pieces)


def load_right(place, units, planes, high, low):
    y = place[2]
    for delta, plane, part, ref, start in units:
        row = pl.multiple_of(plane * PLANE + lax.rem(y + delta, 4) * SPAN, 16)
        top, rest = split(ref[start : start + SPAN, :])
        high[pl.ds(row, SPAN), part * HALF : (part + 1) * HALF] = top
        low[pl.ds(row, SPAN), part * HALF : (part + 1) * HALF] = rest
    used = planes * PLANE
    if used < high.shape[0]:
        for ref in (high, low):
            ref[used:, :] = jnp.zeros((ref.shape[0] - used, ref.shape[1]), ref.dtype)


def near_units(first, first_down, first_up, second, second_down, second_up, two_down, two_up):
    units = []
    for base, planes, skip, own, below, above in (
        (0, 3, 0, first, first_down, first_up),
        (3, 2, 3, second, second_down, second_up),
    ):
        for unit in range(2 * planes):
            half, at = (two_down, unit + skip) if unit < planes else (two_up, unit - planes + skip)
            for delta, ref, index in ((0, own, unit), (3, below, unit), (1, above, unit), (2, half, at)):
                units.append((delta, base + unit // 2, unit % 2, ref, index * SPAN))
    return units


def middle_units(below, above, z_below, z_above, y_below, y_above):
    units = []
    for part in range(2):
        for plane, own, sides, across in ((0, below, z_below, y_below), (1, above, z_above, y_above)):
            for delta, ref, block in ((0, own, 0), (3, sides, 0), (1, sides, 1), (2, across, 0)):
                units.append((delta, plane, part, ref, (2 * block + part) * SPAN))
    return units


def far_units(z_below, z_above, below, above, across_low, across_high):
    units = []
    for part, own, across in ((0, z_below, across_low), (1, z_above, across_high)):
        for delta, ref, start in ((0, own, 4), (3, below, part), (1, above, part), (2, across, 0)):
            units.append((delta, 0, part, ref, start * SPAN))
    return units


def group_kernel(units, planes, place, *refs):
    count = len(refs) - 5 - (units is middle_units)
    rights, (high_ref, low_ref), rest = refs[:count], refs[count : count + 2], refs[count + 2 :]
    out_ref, rh, rl = rest[-3:]
    load_right(place, units(*rights), planes, rh, rl)
    value = dot3(high_ref[...], low_ref[...], rh[...], rl[...])
    out_ref[...] = value if len(rest) == 3 else value + rest[0][...]


def group_call(units, planes, place, rights, screens, total):
    rows, width = screens[0].shape
    return pl.pallas_call(
        functools.partial(group_kernel, units, planes),
        out_shape=jax.ShapeDtypeStruct((rows, 2 * HALF), jnp.float32),
        in_specs=[SMEM] + [VMEM] * (len(rights) + 2 + len(total)),
        out_specs=VMEM,
        scratch_shapes=[pltpu.VMEM((width, 2 * HALF), jnp.bfloat16)] * 2,
        compiler_params=params(32),
        name="group",
    )(place, *rights, *screens, *total)


def pair_kernel(place, table, *refs):
    rights, (high_ref, low_ref, sum_ref, left_high, left_low, out_ref, rh, rl, kern) = refs[:6], refs[6:]
    load_right(place, far_units(*rights), len(FAR), rh, rl)
    product = sum_ref[...] + dot3(high_ref[...], low_ref[...], rh[...], rl[...])
    mid = product.shape[0] // 2
    real = product[:mid, :HALF] - product[mid:, HALF:]
    imag = product[mid:, :HALF] + product[:mid, HALF:]
    applied = NG ** (-0.5) * jnp.concatenate(
        [jnp.concatenate([real, imag], axis=0), jnp.concatenate([imag, -real], axis=0)], axis=1
    )
    kern[...] = dot3(left_high[...], left_low[...], *split(applied))

    lane = lax.broadcasted_iota(jnp.int32, (8, 128), 1) // BLK
    upper = lax.broadcasted_iota(jnp.int32, (8, 128), 0) < 4
    out_ref[...] = jnp.zeros_like(out_ref)
    for half in range(2):

        def group(g, carry, half=half):
            tiles = [[jnp.zeros((8, 128), jnp.float32) for _ in range(2)] for _ in range(2)]
            for u in range(8):
                slot = g * 8 + u
                row = pl.multiple_of(table[4 * half, slot], BLK)
                column = pl.multiple_of(table[4 * half + 1, slot], 128)
                shift = table[4 * half + 2, slot]
                target = table[4 * half + 3, slot]
                for part in range(2):
                    for side in range(2):
                        tile = kern[pl.ds(row + side * 8, 8), pl.ds(column + part * HALF, 128)]
                        tile = pltpu.roll(tile, shift, 1)
                        tiles[part][side] = jnp.where(lane == target, tile, tiles[part][side])
            lanes = pl.ds(pl.multiple_of(g * 128, 128), 128)
            for side in range(2):
                real, imag = tiles[0][side], tiles[1][side]
                out_ref[4 * half + 2 * side, :, lanes] = jnp.where(upper, real, pltpu.roll(imag, 4, 0))
                out_ref[4 * half + 2 * side + 1, :, lanes] = jnp.where(upper, pltpu.roll(real, 4, 0), imag)
            return carry

        lax.fori_loop(0, table[11, half], group, 0)


def pair_call(place, table, rights, screens, total, left_high, left_low):
    return pl.pallas_call(
        pair_kernel,
        out_shape=jax.ShapeDtypeStruct((8, 8, ROOM * BLK), jnp.float32),
        in_specs=[SMEM, SMEM] + [VMEM] * (len(rights) + 5),
        out_specs=VMEM,
        scratch_shapes=[pltpu.VMEM((screens[0].shape[1], 2 * HALF), jnp.bfloat16)] * 2
        + [pltpu.VMEM((left_high.shape[0], 2 * HALF), jnp.float32)],
        compiler_params=params(40),
        name="pair",
    )(place, table, *rights, *screens, total, left_high, left_low)


def owner_kernel(place, table, parts_ref, out_ref, work):
    total = parts_ref[0]
    for at in range(1, parts_ref.shape[0]):
        total = total + parts_ref[at]
    width = total.shape[1]
    work[:, :width] = total
    work[:, width:] = jnp.zeros((8, work.shape[1] - width), jnp.float32)
    for chip in range(out_ref.shape[0]):
        start = table[8, chip * 2 + place[3]]
        column = pl.multiple_of(start // 8 * 128, 128)
        shift = lax.rem(384 - lax.rem(start, 8) * BLK, 384)
        out_ref[chip] = pltpu.roll(work[:, pl.ds(column, 384)], shift, 1)[:, :256]


def owner_call(place, table, parts):
    return pl.pallas_call(
        owner_kernel,
        out_shape=jax.ShapeDtypeStruct((32, 8, 256), jnp.float32),
        in_specs=[SMEM, SMEM, VMEM],
        out_specs=VMEM,
        scratch_shapes=[pltpu.VMEM((8, parts.shape[2] + 384), jnp.float32)],
        name="owner",
    )(place, table, parts)


def last_kernel(place, table, parts_ref, out_ref):
    total = parts_ref[0]
    for chip in range(1, parts_ref.shape[0]):
        total = total + parts_ref[chip]
    held = table[9, (place[0] * 4 + place[2]) * 2 + place[3]]
    for slot in range(CAP):
        tile = total[:, slot // 8 * 128 : slot // 8 * 128 + 128]
        tile = pltpu.roll(tile, (128 - slot % 8 * BLK) % 128, 1)
        out_ref[slot] = jnp.where(slot < held, tile[:, :BLK], 0.0)


def last_call(place, table, parts):
    return pl.pallas_call(
        last_kernel,
        out_shape=jax.ShapeDtypeStruct((CAP, 8, BLK), jnp.float32),
        in_specs=[SMEM, SMEM, VMEM],
        out_specs=VMEM,
        name="last",
    )(place, table, parts)


def pack_kernel(place, own_ref, other_ref, out_ref, work):
    core = place[3]
    width = own_ref.shape[2]
    for block in range(width // 128):
        lanes = pl.ds(block * 128, 128)
        rows = []
        for part in range(2):
            own, other = own_ref[part, :, lanes], other_ref[part, :, lanes]
            rows += [jnp.where(core == 0, own, other), jnp.where(core == 0, other, own)]
        rows = jnp.concatenate(rows + rows, axis=0)
        work[block * 128 : (block + 1) * 128, :] = rows.T
    half = lax.broadcasted_iota(jnp.int32, (8, 128), 1) < 64
    for chip in range(32):
        at = pl.multiple_of(chip * 80 + core * 40, 8)
        tiles = [work[pl.ds(at + 8 * t, 8), :] for t in range(5)]
        out_ref[chip * 20 : chip * 20 + 8, :] = jnp.where(half, tiles[0], tiles[1])
        out_ref[chip * 20 + 8 : chip * 20 + 16, :] = jnp.where(half, tiles[2], tiles[3])
        last = jnp.where(half, tiles[4], pltpu.roll(tiles[4], 4, 0))
        out_ref[chip * 20 + 16 : chip * 20 + 20, :] = last[:4]


def pack_call(place, own, other):
    width = own.shape[2]
    return pl.pallas_call(
        pack_kernel,
        out_shape=jax.ShapeDtypeStruct((32 * 20, 128), jnp.float32),
        in_specs=[SMEM, VMEM, VMEM],
        out_specs=VMEM,
        scratch_shapes=[pltpu.VMEM((width, 128), jnp.float32)],
        name="pack",
    )(place, own, other)


def unpack_kernel(place, table, in_ref, columns_ref, keep_ref, give_ref):
    core = place[3]
    quarter = lax.broadcasted_iota(jnp.int32, (8, 128), 1) // 32
    upper = lax.broadcasted_iota(jnp.int32, (8, 128), 0) < 4
    for group in range(8):
        tiles = [[None] * 5 for _ in range(2)]
        for u in range(4):
            at = (group * 4 + u) * 20
            one, two = in_ref[at : at + 8, :], in_ref[at + 8 : at + 16, :]
            end = in_ref[at + 12 : at + 20, :]
            end = jnp.where(upper, pltpu.roll(end, 4, 0), pltpu.roll(end, 64, 1))
            for t, (source, first) in enumerate(((one, 0), (one, 64), (two, 0), (two, 64), (end, 0))):
                for part in range(2):
                    by = (u * 32 - first - part * 32) % 128
                    turned = pltpu.roll(source, by, 1) if by else source
                    old = tiles[part][t]
                    tiles[part][t] = turned if old is None else jnp.where(quarter == u, turned, old)
        for part in range(2):
            for t in range(5):
                row = part * 40 + t * 8
                columns_ref[row : row + 8, group * 128 : (group + 1) * 128] = tiles[part][t]
    eighth = lax.broadcasted_iota(jnp.int32, (80, 128), 1) // BLK
    for ref, which in ((give_ref, 1 - core), (keep_ref, core)):
        for group in range(2):
            slab = None
            for u in range(8):
                block = table[10, which * (USED // 2) + group * 8 + u]
                column = pl.multiple_of(block // 8 * 128, 128)
                by = lax.rem(u * BLK + 128 - lax.rem(block, 8) * BLK, 128)
                turned = pltpu.roll(columns_ref[:, pl.ds(column, 128)], by, 1)
                slab = turned if slab is None else jnp.where(eighth == u, turned, slab)
            ref[:, group * 128 : (group + 1) * 128] = slab


def unpack_call(place, table, pieces):
    return pl.pallas_call(
        unpack_kernel,
        out_shape=(
            jax.ShapeDtypeStruct((80, 1024), jnp.float32),
            jax.ShapeDtypeStruct((80, HALF), jnp.float32),
            jax.ShapeDtypeStruct((80, HALF), jnp.float32),
        ),
        in_specs=[SMEM, SMEM, VMEM],
        out_specs=(VMEM, VMEM, VMEM),
        name="unpack",
    )(place, table, pieces)


def shard_kernel(place, keep_ref, take_ref, out_ref):
    core = place[3]
    for part in range(2):
        out_ref[pl.ds(pl.multiple_of(part * 80 + core * 40, 8), 40), :] = keep_ref[part * 40 : part * 40 + 40, :]
        out_ref[pl.ds(pl.multiple_of(part * 80 + 40 - core * 40, 8), 40), :] = take_ref[part * 40 : part * 40 + 40, :]


def shard_call(place, keep, take):
    return pl.pallas_call(
        shard_kernel,
        out_shape=jax.ShapeDtypeStruct((160, HALF), jnp.float32),
        in_specs=[SMEM, VMEM, VMEM],
        out_specs=VMEM,
        name="shard",
    )(place, keep, take)


def after(array, *others):
    return lax.optimization_barrier((array, *others))[0]


def shards(densities, screened, pairs, owners):
    span = screened.shape[2]
    place = jnp.stack([lax.axis_index(axis) for axis in ("z", "x", "y", "core")]).astype(jnp.int32)
    shift = lambda array, axis, by: lax.ppermute(array, axis, ring(lax.axis_size(axis), by))
    swap = lambda array: lax.ppermute(array, "core", SWAP)
    join = lambda *arrays: jnp.concatenate(arrays, axis=0)
    hold = lax.optimization_barrier

    pieces = pack_call(place, densities, swap(densities))
    table = plan_call(place, after(pairs, pieces), owners.reshape(1, -1))
    mine = lax.all_to_all(pieces.reshape(32, 1, -1), ("z", "y"), 0, 0, tiled=True).reshape(pieces.shape)

    screen = screened.reshape(2 * 4 * span, -1)
    mine, other = hold((mine, swap(after(screen, pieces))))

    columns, keep, give = unpack_call(place, table, mine)
    shard = shard_call(place, keep, swap(give))

    block = 2 * SPAN
    below, above = shift(shard, "z", 1), shift(shard, "z", -1)
    around = [columns] + [shift(columns, "x", by) for by in (1, 2, 3)]
    swapped = [swap(columns)]
    below, above, around[1], swapped[0] = hold((below, above, around[1], swapped[0]))

    first = join(shard, below, above)
    below2, above2 = shift(below, "z", 1), shift(above, "z", -1)
    first_down, first_up = shift(first, "y", 1), shift(first, "y", -1)
    screens = screen_call(place, after(screen, first), other)
    below2, above2, first_down, first_up, around[3], *screens = hold(
        (below2, above2, first_down, first_up, around[3], *screens)
    )

    second = join(below2, above2)
    below3, above3 = shift(below2, "z", 1), shift(above2, "z", -1)
    second_down, second_up = shift(second, "y", 1), shift(second, "y", -1)
    below3, above3, second_down, second_up, *around = hold((below3, above3, second_down, second_up, *around))

    two_down = shift(join(first_down[: 3 * SPAN], second_down[:block]), "y", 1)
    two_up = shift(join(first_up[3 * SPAN :], second_up[block:]), "y", -1)
    z_below = shift(join(second_down[:block], second_up[:block], below3[:SPAN]), "z", 1)
    z_above = shift(join(second_down[block:], second_up[block:], above3[SPAN:]), "z", -1)
    swapped.append(swap(around[1]))
    two_down, two_up, z_below, z_above, swapped[1] = hold((two_down, two_up, z_below, z_above, swapped[1]))

    y_below, y_above = shift(z_below[:block], "y", 1), shift(z_above[block : 2 * block], "y", -1)
    far_below, far_above = shift(z_below[:block], "z", 1), shift(z_above[block : 2 * block], "z", -1)
    rights = (first, first_down, first_up, second, second_down, second_up, two_down, two_up)
    total = group_call(near_units, len(NEAR), place, rights, screens[:2], ())
    third = swap(after(around[3], two_down))
    y_below, y_above, far_below, far_above, total, third = hold((y_below, y_above, far_below, far_above, total, third))

    across_low, across_high = shift(far_below[:SPAN], "y", 1), shift(far_above[SPAN:], "y", -1)
    rights = (below3, above3, z_below, z_above, y_below, y_above)
    total = group_call(middle_units, len(MIDDLE), place, rights, screens[2:4], (total,))
    swapped += [swap(after(around[2], third)), third]
    left_high, left_low = left_call(place, list(around) + swapped)
    across_low, across_high, total, left_high, left_low = hold((across_low, across_high, total, left_high, left_low))
    rights = (z_below, z_above, far_below, far_above, across_low, across_high)
    parts = pair_call(place, table, rights, screens[4:], total, left_high, left_low)

    parts = lax.all_to_all(parts, ("core", "x"), 0, 0, tiled=True)
    parts = owner_call(place, table, parts)
    parts = lax.all_to_all(parts, ("z", "y"), 0, 0, tiled=True)
    return last_call(place, table, parts).reshape(1, CAP, 2, 4, BLK)


def solution(mesh):
    fine = Mesh(mesh.devices.reshape(8, 4, 2, 4), ("z", "y", "core", "x"))
    in_specs = (P(None, BAND, "x"), P(None, None, BAND, "x"), P(), P())
    out_specs = P(BAND, None, None, "x", None)
    return jax.shard_map(shards, mesh=fine, in_specs=in_specs, out_specs=out_specs, check_vma=False)
```

```python
import functools

import jax
import jax.numpy as jnp
from jax import lax
from jax.experimental import pallas as pl
from jax.experimental.pallas import tpu as pltpu
from jax.sharding import Mesh
from jax.sharding import PartitionSpec as P

NG = 10240
CAP = 12
BLK = 16
USED = 32
HALF = USED // 2 * BLK
BAND = ("z", "y", "core")
SWAP = ((0, 1), (1, 0))
SMEM = pl.BlockSpec(memory_space=pltpu.SMEM)
VMEM = pl.BlockSpec(memory_space=pltpu.VMEM)
SPAN = 80
PLANE = 320
NEAR = (0, 7, 1, 6, 2)
MIDDLE = (5, 3)
FAR = (4,)
ROOM = 224


def ring(n, shift):
    return [(i, (i + shift) % n) for i in range(n)]


def params(mib):
    return pltpu.CompilerParams(vmem_limit_bytes=mib * 1024 * 1024)


def split(x):
    high = x.astype(jnp.bfloat16)
    return high, (x - high.astype(jnp.float32)).astype(jnp.bfloat16)


def dot(former, latter):
    return jnp.dot(former, latter, preferred_element_type=jnp.float32)


def dot3(high, low, former, latter):
    return dot(high, former) + dot(high, latter) + dot(low, former)


def plan_kernel(place, pairs_ref, owners_ref, out_ref):
    size = 256
    down = lax.broadcasted_iota(jnp.int32, (size, size), 0)
    across = lax.broadcasted_iota(jnp.int32, (size, size), 1)
    one = lambda condition: jnp.where(condition, 1.0, 0.0)
    to_row = lambda column: jnp.sum(jnp.where(down == across, column, 0.0), axis=0, keepdims=True)
    to_column = lambda row: jnp.sum(jnp.where(down == across, row, 0.0), axis=1, keepdims=True)
    rows, columns = down.astype(jnp.float32), across.astype(jnp.float32)
    left, right = pairs_ref[:, 0:1].astype(jnp.float32), pairs_ref[:, 1:2].astype(jnp.float32)
    owner_row = owners_ref[...].astype(jnp.float32)
    owner = to_column(owner_row)

    used = jnp.max(one(right == columns), axis=0, keepdims=True)
    used_column = to_column(used)
    rank = jnp.sum(jnp.where(columns < rows, used, 0.0), axis=1, keepdims=True)
    used_list = jnp.sum(jnp.where((rank == columns) & (used_column > 0), rows, 0.0), axis=0, keepdims=True)
    right_rank = jnp.sum(jnp.where(columns < right, used, 0.0), axis=1, keepdims=True)

    parity = lambda value: value - 2.0 * jnp.floor(value * 0.5)
    count = jnp.sum(one(owner == columns), axis=0, keepdims=True)
    same = parity(rows) == parity(columns)
    offset = jnp.sum(jnp.where((rows < columns) & same, to_column(count), 0.0), axis=0, keepdims=True)
    ahead = (owner_row < owner) | ((owner_row == owner) & (across < down))
    ahead = ahead & (parity(owner_row) == parity(owner))
    position = jnp.sum(one(ahead), axis=1, keepdims=True)

    core = place[3].astype(jnp.float32)
    local = right_rank - core * (USED // 2)
    here = (local >= 0) & (local < USED // 2)
    local = jnp.where(here, local, 0.0)
    lane = lax.broadcasted_iota(jnp.int32, (1, size), 1)
    groups = jnp.zeros((1, size), jnp.float32)
    for half in range(2):
        hit = (position == columns) & (parity(owner) == half)
        pick = lambda column: jnp.sum(jnp.where(hit, column, 0.0), axis=0, keepdims=True).astype(jnp.int32)
        at = pick(local)
        out_ref[4 * half : 4 * half + 1, :] = pick(left) * BLK
        out_ref[4 * half + 1 : 4 * half + 2, :] = at // 8 * 128
        out_ref[4 * half + 2 : 4 * half + 3, :] = (lane + 8 - at % 8) % 8 * BLK
        out_ref[4 * half + 3 : 4 * half + 4, :] = jnp.where(pick(one(here)) > 0, lane % 8, -1)
        total = jnp.sum(one(parity(owner_row) == half))
        groups = jnp.where(lane == half, jnp.floor((total + 7.0) / 8.0), groups)
    for at, row in enumerate((offset, count, used_list, groups)):
        out_ref[8 + at : 9 + at, :] = row.astype(jnp.int32)


def plan_call(place, pairs, owners):
    return pl.pallas_call(
        plan_kernel,
        out_shape=jax.ShapeDtypeStruct((16, pairs.shape[0]), jnp.int32),
        in_specs=[SMEM, VMEM, VMEM],
        out_specs=VMEM,
        compiler_params=params(8),
        name="plan",
    )(place, pairs, owners)


def padded(planes):
    return (len(planes) * PLANE + 127) // 128 * 128


def screen_kernel(place, own_ref, other_ref, *outs):
    z = place[0]
    rows = 16
    lane = lax.broadcasted_iota(jnp.int32, (rows, 128), 1)

    def plane_of(ref, row, delta, offset):
        plane = lax.rem(z + delta, 8)
        odd = lax.rem(plane, 2)
        column = pl.multiple_of(plane * PLANE - odd * 64, 128)
        window = ref[row, pl.ds(column, 384)]
        turned = pltpu.roll(window, 64 if offset else 320, 1)
        return jnp.where((odd == 1) if offset else (odd == 0), window, turned)

    for source, ref in enumerate((own_ref, other_ref)):

        def body(step, carry, source=source, ref=ref):
            part = step // 10
            row = pl.ds(pl.multiple_of(step * rows, rows), rows)
            target = pl.multiple_of(part * PLANE + source * (PLANE // 2) + (step - part * 10) * rows, rows)
            for group, planes in enumerate((NEAR, MIDDLE, FAR)):
                for at in range(0, len(planes), 2):
                    a = plane_of(ref, row, planes[at], False)
                    if at + 1 < len(planes):
                        b = plane_of(ref, row, planes[at + 1], True)
                        middle = jnp.where(lane < 64, a[:, 256:], b[:, :128])
                        whole = jnp.concatenate([a[:, :256], middle, b[:, 128:]], axis=1)
                    else:
                        whole = jnp.concatenate([a[:, :256], jnp.where(lane < 64, a[:, 256:], 0.0)], axis=1)
                    top, rest = split(whole)
                    columns = slice(at * PLANE, at * PLANE + whole.shape[1])
                    outs[2 * group][pl.ds(target, rows), columns] = top
                    outs[2 * group + 1][pl.ds(target, rows), columns] = rest
            return carry

        lax.fori_loop(0, 20, body, 0)


def screen_call(place, own, other):
    shapes = [
        jax.ShapeDtypeStruct((2 * own.shape[0], padded(planes)), jnp.bfloat16)
        for planes in (NEAR, MIDDLE, FAR)
        for _ in range(2)
    ]
    return pl.pallas_call(
        screen_kernel,
        out_shape=shapes,
        in_specs=[SMEM, VMEM, VMEM],
        out_specs=[VMEM] * 6,
        compiler_params=params(20),
        name="screen",
    )(place, own, other)


def left_kernel(place, *refs):
    pieces, (high_ref, low_ref, work) = refs[:8], refs[8:]
    x = place[1]
    span = pieces[0].shape[0] // 2
    for core in range(2):
        for shift in range(4):
            shard = lax.rem(x - shift + 4, 4)
            for part in range(2):
                row = pl.multiple_of(part * 8 * span + core * 4 * span + shard * span, 8)
                work[pl.ds(row, span), :] = pieces[core * 4 + shift][part * span : (part + 1) * span, :]
    for block in range(work.shape[1] // 128):
        turned = work[:, block * 128 : (block + 1) * 128].T
        top, rest = split(turned)
        high_ref[block * 128 : (block + 1) * 128, :] = top
        low_ref[block * 128 : (block + 1) * 128, :] = rest


def left_call(place, pieces):
    depth, width = pieces[0].shape
    shape = jax.ShapeDtypeStruct((width, 8 * depth), jnp.bfloat16)
    return pl.pallas_call(
        left_kernel,
        out_shape=(shape, shape),
        in_specs=[SMEM] + [VMEM] * 8,
        out_specs=(VMEM, VMEM),
        scratch_shapes=[pltpu.VMEM((8 * depth, width), jnp.float32)],
        compiler_params=params(20),
        name="left",
    )(place, *pieces)


def load_right(place, units, planes, high, low):
    y = place[2]
    for delta, plane, part, ref, start in units:
        row = pl.multiple_of(plane * PLANE + lax.rem(y + delta, 4) * SPAN, 16)
        top, rest = split(ref[start : start + SPAN, :])
        high[pl.ds(row, SPAN), part * HALF : (part + 1) * HALF] = top
        low[pl.ds(row, SPAN), part * HALF : (part + 1) * HALF] = rest
    used = planes * PLANE
    if used < high.shape[0]:
        for ref in (high, low):
            ref[used:, :] = jnp.zeros((ref.shape[0] - used, ref.shape[1]), ref.dtype)


def near_units(first, first_down, first_up, second, second_down, second_up, two_down, two_up):
    units = []
    for base, planes, skip, own, below, above in (
        (0, 3, 0, first, first_down, first_up),
        (3, 2, 3, second, second_down, second_up),
    ):
        for unit in range(2 * planes):
            half, at = (two_down, unit + skip) if unit < planes else (two_up, unit - planes + skip)
            for delta, ref, index in ((0, own, unit), (3, below, unit), (1, above, unit), (2, half, at)):
                units.append((delta, base + unit // 2, unit % 2, ref, index * SPAN))
    return units


def middle_units(below, above, z_below, z_above, y_below, y_above):
    units = []
    for part in range(2):
        for plane, own, sides, across in ((0, below, z_below, y_below), (1, above, z_above, y_above)):
            for delta, ref, block in ((0, own, 0), (3, sides, 0), (1, sides, 1), (2, across, 0)):
                units.append((delta, plane, part, ref, (2 * block + part) * SPAN))
    return units


def far_units(z_below, z_above, below, above, across_low, across_high):
    units = []
    for part, own, across in ((0, z_below, across_low), (1, z_above, across_high)):
        for delta, ref, start in ((0, own, 4), (3, below, part), (1, above, part), (2, across, 0)):
            units.append((delta, 0, part, ref, start * SPAN))
    return units


def group_kernel(units, planes, place, *refs):
    count = len(refs) - 5 - (units is middle_units)
    rights, (high_ref, low_ref), rest = refs[:count], refs[count : count + 2], refs[count + 2 :]
    out_ref, rh, rl = rest[-3:]
    load_right(place, units(*rights), planes, rh, rl)
    value = dot3(high_ref[...], low_ref[...], rh[...], rl[...])
    out_ref[...] = value if len(rest) == 3 else value + rest[0][...]


def group_call(units, planes, place, rights, screens, total):
    rows, width = screens[0].shape
    return pl.pallas_call(
        functools.partial(group_kernel, units, planes),
        out_shape=jax.ShapeDtypeStruct((rows, 2 * HALF), jnp.float32),
        in_specs=[SMEM] + [VMEM] * (len(rights) + 2 + len(total)),
        out_specs=VMEM,
        scratch_shapes=[pltpu.VMEM((width, 2 * HALF), jnp.bfloat16)] * 2,
        compiler_params=params(32),
        name="group",
    )(place, *rights, *screens, *total)


def pair_kernel(place, table, *refs):
    rights, (high_ref, low_ref, sum_ref, left_high, left_low, give_ref, kern, rh, rl) = refs[:6], refs[6:]
    load_right(place, far_units(*rights), len(FAR), rh, rl)
    product = sum_ref[...] + dot3(high_ref[...], low_ref[...], rh[...], rl[...])
    mid = product.shape[0] // 2
    real = product[:mid, :HALF] - product[mid:, HALF:]
    imag = product[mid:, :HALF] + product[:mid, HALF:]
    applied = NG ** (-0.5) * jnp.concatenate(
        [jnp.concatenate([real, imag], axis=0), jnp.concatenate([imag, -real], axis=0)], axis=1
    )
    kern[...] = dot3(left_high[...], left_low[...], *split(applied))

    extract(table, 1 - place[3], kern, give_ref)


def extract(table, half, kern, out_ref):
    lane = lax.broadcasted_iota(jnp.int32, (8, 128), 1) // BLK
    upper = lax.broadcasted_iota(jnp.int32, (8, 128), 0) < 4

    def groups(pair, carry):
        for g in (pair * 2, pair * 2 + 1):
            tiles = [[jnp.zeros((8, 128), jnp.float32) for _ in range(2)] for _ in range(2)]
            for u in range(8):
                slot = g * 8 + u
                row = pl.multiple_of(table[4 * half, slot], BLK)
                column = pl.multiple_of(table[4 * half + 1, slot], 128)
                shift = table[4 * half + 2, slot]
                target = table[4 * half + 3, slot]
                for part in range(2):
                    for side in range(2):
                        tile = kern[pl.ds(row + side * 8, 8), pl.ds(column + part * HALF, 128)]
                        tile = pltpu.roll(tile, shift, 1)
                        tiles[part][side] = jnp.where(lane == target, tile, tiles[part][side])
            lanes = pl.ds(pl.multiple_of(g * 128, 128), 128)
            for side in range(2):
                real, imag = tiles[0][side], tiles[1][side]
                out_ref[2 * side, :, lanes] = jnp.where(upper, real, pltpu.roll(imag, 4, 0))
                out_ref[2 * side + 1, :, lanes] = jnp.where(upper, pltpu.roll(real, 4, 0), imag)
        return carry

    out_ref[...] = jnp.zeros_like(out_ref)
    lax.fori_loop(0, (table[11, half] + 1) // 2, groups, 0)


def pair_call(place, table, rights, screens, total, left_high, left_low):
    rows = left_high.shape[0]
    return pl.pallas_call(
        pair_kernel,
        out_shape=(
            jax.ShapeDtypeStruct((4, 8, ROOM * BLK), jnp.float32),
            jax.ShapeDtypeStruct((rows, 2 * HALF), jnp.float32),
        ),
        in_specs=[SMEM, SMEM] + [VMEM] * (len(rights) + 5),
        out_specs=(VMEM, VMEM),
        scratch_shapes=[pltpu.VMEM((screens[0].shape[1], 2 * HALF), jnp.bfloat16)] * 2,
        compiler_params=params(24),
        name="pair",
    )(place, table, *rights, *screens, total, left_high, left_low)


def extract_kernel(place, table, kern, out_ref):
    extract(table, place[3], kern, out_ref)


def extract_call(place, table, kern):
    return pl.pallas_call(
        extract_kernel,
        out_shape=jax.ShapeDtypeStruct((4, 8, ROOM * BLK), jnp.float32),
        in_specs=[SMEM, SMEM, VMEM],
        out_specs=VMEM,
        compiler_params=params(8),
        name="extract",
    )(place, table, kern)


def add_kernel(one_ref, two_ref, out_ref):
    out_ref[...] = one_ref[...] + two_ref[...]


def add_call(one, two):
    return pl.pallas_call(
        add_kernel,
        out_shape=jax.ShapeDtypeStruct(one.shape, one.dtype),
        in_specs=[VMEM, VMEM],
        out_specs=VMEM,
        compiler_params=params(8),
        name="add",
    )(one, two)


def owner_kernel(place, table, parts_ref, out_ref, work):
    total = parts_ref[0]
    for at in range(1, parts_ref.shape[0]):
        total = total + parts_ref[at]
    width = total.shape[1]
    work[:, :width] = total
    work[:, width:] = jnp.zeros((8, work.shape[1] - width), jnp.float32)
    for chip in range(out_ref.shape[0]):
        start = table[8, chip * 2 + place[3]]
        column = pl.multiple_of(start // 8 * 128, 128)
        shift = lax.rem(384 - lax.rem(start, 8) * BLK, 384)
        out_ref[chip] = pltpu.roll(work[:, pl.ds(column, 384)], shift, 1)[:, :256]


def owner_call(place, table, parts):
    return pl.pallas_call(
        owner_kernel,
        out_shape=jax.ShapeDtypeStruct((32, 8, 256), jnp.float32),
        in_specs=[SMEM, SMEM, VMEM],
        out_specs=VMEM,
        scratch_shapes=[pltpu.VMEM((8, parts.shape[2] + 384), jnp.float32)],
        compiler_params=params(8),
        name="owner",
    )(place, table, parts)


def last_kernel(place, table, parts_ref, out_ref):
    total = parts_ref[0]
    for chip in range(1, parts_ref.shape[0]):
        total = total + parts_ref[chip]
    held = table[9, (place[0] * 4 + place[2]) * 2 + place[3]]
    for slot in range(CAP):
        tile = total[:, slot // 8 * 128 : slot // 8 * 128 + 128]
        tile = pltpu.roll(tile, (128 - slot % 8 * BLK) % 128, 1)
        out_ref[slot] = jnp.where(slot < held, tile[:, :BLK], 0.0)


def last_call(place, table, parts):
    return pl.pallas_call(
        last_kernel,
        out_shape=jax.ShapeDtypeStruct((CAP, 8, BLK), jnp.float32),
        in_specs=[SMEM, SMEM, VMEM],
        out_specs=VMEM,
        compiler_params=params(8),
        name="last",
    )(place, table, parts)


def pack_kernel(place, own_ref, other_ref, out_ref, work):
    core = place[3]
    width = own_ref.shape[2]
    for block in range(width // 128):
        lanes = pl.ds(block * 128, 128)
        rows = []
        for part in range(2):
            own, other = own_ref[part, :, lanes], other_ref[part, :, lanes]
            rows += [jnp.where(core == 0, own, other), jnp.where(core == 0, other, own)]
        rows = jnp.concatenate(rows + rows, axis=0)
        work[block * 128 : (block + 1) * 128, :] = rows.T
    half = lax.broadcasted_iota(jnp.int32, (8, 128), 1) < 64
    for chip in range(32):
        at = pl.multiple_of(chip * 80 + core * 40, 8)
        tiles = [work[pl.ds(at + 8 * t, 8), :] for t in range(5)]
        out_ref[chip * 20 : chip * 20 + 8, :] = jnp.where(half, tiles[0], tiles[1])
        out_ref[chip * 20 + 8 : chip * 20 + 16, :] = jnp.where(half, tiles[2], tiles[3])
        last = jnp.where(half, tiles[4], pltpu.roll(tiles[4], 4, 0))
        out_ref[chip * 20 + 16 : chip * 20 + 20, :] = last[:4]


def pack_call(place, own, other):
    width = own.shape[2]
    return pl.pallas_call(
        pack_kernel,
        out_shape=jax.ShapeDtypeStruct((32 * 20, 128), jnp.float32),
        in_specs=[SMEM, VMEM, VMEM],
        out_specs=VMEM,
        scratch_shapes=[pltpu.VMEM((width, 128), jnp.float32)],
        name="pack",
    )(place, own, other)


def unpack_kernel(place, table, in_ref, columns_ref, keep_ref, give_ref):
    core = place[3]
    quarter = lax.broadcasted_iota(jnp.int32, (8, 128), 1) // 32
    upper = lax.broadcasted_iota(jnp.int32, (8, 128), 0) < 4
    for group in range(8):
        tiles = [[None] * 5 for _ in range(2)]
        for u in range(4):
            at = (group * 4 + u) * 20
            one, two = in_ref[at : at + 8, :], in_ref[at + 8 : at + 16, :]
            end = in_ref[at + 12 : at + 20, :]
            end = jnp.where(upper, pltpu.roll(end, 4, 0), pltpu.roll(end, 64, 1))
            for t, (source, first) in enumerate(((one, 0), (one, 64), (two, 0), (two, 64), (end, 0))):
                for part in range(2):
                    by = (u * 32 - first - part * 32) % 128
                    turned = pltpu.roll(source, by, 1) if by else source
                    old = tiles[part][t]
                    tiles[part][t] = turned if old is None else jnp.where(quarter == u, turned, old)
        for part in range(2):
            for t in range(5):
                row = part * 40 + t * 8
                columns_ref[row : row + 8, group * 128 : (group + 1) * 128] = tiles[part][t]
    select(table, 1 - core, columns_ref, give_ref)
    select(table, core, columns_ref, keep_ref)


def select(table, which, columns_ref, out_ref):
    eighth = lax.broadcasted_iota(jnp.int32, (80, 128), 1) // BLK
    for group in range(2):
        slab = None
        for u in range(8):
            block = table[10, which * (USED // 2) + group * 8 + u]
            column = pl.multiple_of(block // 8 * 128, 128)
            by = lax.rem(u * BLK + 128 - lax.rem(block, 8) * BLK, 128)
            turned = pltpu.roll(columns_ref[:, pl.ds(column, 128)], by, 1)
            slab = turned if slab is None else jnp.where(eighth == u, turned, slab)
        out_ref[:, group * 128 : (group + 1) * 128] = slab


def unpack_call(place, table, pieces):
    return pl.pallas_call(
        unpack_kernel,
        out_shape=(
            jax.ShapeDtypeStruct((80, 1024), jnp.float32),
            jax.ShapeDtypeStruct((80, HALF), jnp.float32),
            jax.ShapeDtypeStruct((80, HALF), jnp.float32),
        ),
        in_specs=[SMEM, SMEM, VMEM],
        out_specs=(VMEM, VMEM, VMEM),
        compiler_params=params(8),
        name="unpack",
    )(place, table, pieces)


def shard_kernel(place, keep_ref, take_ref, out_ref):
    core = place[3]
    for part in range(2):
        out_ref[pl.ds(pl.multiple_of(part * 80 + core * 40, 8), 40), :] = keep_ref[part * 40 : part * 40 + 40, :]
        out_ref[pl.ds(pl.multiple_of(part * 80 + 40 - core * 40, 8), 40), :] = take_ref[part * 40 : part * 40 + 40, :]


def shard_call(place, keep, take):
    return pl.pallas_call(
        shard_kernel,
        out_shape=jax.ShapeDtypeStruct((160, HALF), jnp.float32),
        in_specs=[SMEM, VMEM, VMEM],
        out_specs=VMEM,
        compiler_params=params(8),
        name="shard",
    )(place, keep, take)


def after(array, *others):
    return lax.optimization_barrier((array, *others))[0]


def shards(densities, screened, pairs, owners):
    span = screened.shape[2]
    place = jnp.stack([lax.axis_index(axis) for axis in ("z", "x", "y", "core")]).astype(jnp.int32)
    shift = lambda array, axis, by: lax.ppermute(array, axis, ring(lax.axis_size(axis), by))
    swap = lambda array: lax.ppermute(array, "core", SWAP)
    join = lambda *arrays: jnp.concatenate(arrays, axis=0)
    hold = lax.optimization_barrier

    pieces = pack_call(place, densities, swap(densities))
    table = plan_call(place, after(pairs, pieces), owners.reshape(1, -1))
    mine = lax.all_to_all(pieces.reshape(32, 1, -1), ("z", "y"), 0, 0, tiled=True).reshape(pieces.shape)

    screen = screened.reshape(2 * 4 * span, -1)
    mine, other = hold((mine, swap(after(screen, pieces))))

    columns, keep, give = unpack_call(place, table, mine)
    take, columns = hold((swap(give), columns))
    shard = shard_call(place, keep, take)

    block = 2 * SPAN
    below, above = shift(shard, "z", 1), shift(shard, "z", -1)
    around = [columns] + [shift(columns, "x", by) for by in (1, 2, 3)]
    swapped = [swap(columns)]
    below, above, around[1], around[3], swapped[0] = hold((below, above, around[1], around[3], swapped[0]))

    first = join(shard, below, above)
    below2, above2 = shift(below, "z", 1), shift(above, "z", -1)
    first_down, first_up = shift(first, "y", 1), shift(first, "y", -1)
    screens = screen_call(place, after(screen, first), other)
    below2, above2, first_down, first_up, around[2], *screens = hold(
        (below2, above2, first_down, first_up, around[2], *screens)
    )

    second = join(below2, above2)
    below3, above3 = shift(below2, "z", 1), shift(above2, "z", -1)
    second_down, second_up = shift(second, "y", 1), shift(second, "y", -1)
    swapped += [swap(around[1]), swap(around[3])]
    below3, above3, second_down, second_up, swapped[1], swapped[2] = hold(
        (below3, above3, second_down, second_up, swapped[1], swapped[2])
    )

    two_down = shift(join(first_down[: 3 * SPAN], second_down[:block]), "y", 1)
    two_up = shift(join(first_up[3 * SPAN :], second_up[block:]), "y", -1)
    z_below = shift(join(second_down[:block], second_up[:block], below3[:SPAN]), "z", 1)
    z_above = shift(join(second_down[block:], second_up[block:], above3[SPAN:]), "z", -1)
    swapped = [swapped[0], swapped[1], swap(around[2]), swapped[2]]
    left_high, left_low = left_call(place, list(around) + swapped)
    two_down, two_up, z_below, z_above, left_high, left_low = hold(
        (two_down, two_up, z_below, z_above, left_high, left_low)
    )

    y_below, y_above = shift(z_below[:block], "y", 1), shift(z_above[block : 2 * block], "y", -1)
    far_below, far_above = shift(z_below[:block], "z", 1), shift(z_above[block : 2 * block], "z", -1)
    rights = (first, first_down, first_up, second, second_down, second_up, two_down, two_up)
    total = group_call(near_units, len(NEAR), place, rights, screens[:2], ())
    y_below, y_above, far_below, far_above, total = hold((y_below, y_above, far_below, far_above, total))

    across_low, across_high = shift(far_below[:SPAN], "y", 1), shift(far_above[SPAN:], "y", -1)
    rights = (below3, above3, z_below, z_above, y_below, y_above)
    total = group_call(middle_units, len(MIDDLE), place, rights, screens[2:4], (total,))
    across_low, across_high, total = hold((across_low, across_high, total))
    rights = (z_below, z_above, far_below, far_above, across_low, across_high)
    give, kern = pair_call(place, table, rights, screens[4:], total, left_high, left_low)

    parts = add_call(extract_call(place, table, kern), swap(give))
    parts = lax.all_to_all(parts, "x", 0, 0, tiled=True)
    parts = owner_call(place, table, parts)
    parts = lax.all_to_all(parts, ("z", "y"), 0, 0, tiled=True)
    return last_call(place, table, parts).reshape(1, CAP, 2, 4, BLK)


def solution(mesh):
    fine = Mesh(mesh.devices.reshape(8, 4, 2, 4), ("z", "y", "core", "x"))
    in_specs = (P(None, BAND, "x"), P(None, None, BAND, "x"), P(), P())
    out_specs = P(BAND, None, None, "x", None)
    return jax.shard_map(shards, mesh=fine, in_specs=in_specs, out_specs=out_specs, check_vma=False)
```

```python
import functools

import jax
import jax.numpy as jnp
from jax import lax
from jax.experimental import pallas as pl
from jax.experimental.pallas import tpu as pltpu
from jax.sharding import Mesh
from jax.sharding import PartitionSpec as P

NG = 10240
CAP = 12
BLK = 16
USED = 32
HALF = USED // 2 * BLK
BAND = ("z", "y", "core")
SWAP = ((0, 1), (1, 0))
SMEM = pl.BlockSpec(memory_space=pltpu.SMEM)
VMEM = pl.BlockSpec(memory_space=pltpu.VMEM)
SPAN = 80
PLANE = 320
NEAR = (0, 7, 1, 6, 2)
MIDDLE = (5, 3)
FAR = (4,)
ROOM = 224


def ring(n, shift):
    return [(i, (i + shift) % n) for i in range(n)]


def params(mib):
    return pltpu.CompilerParams(vmem_limit_bytes=mib * 1024 * 1024)


def split(x):
    high = x.astype(jnp.bfloat16)
    return high, (x - high.astype(jnp.float32)).astype(jnp.bfloat16)


def dot(former, latter):
    return jnp.dot(former, latter, preferred_element_type=jnp.float32)


def dot3(high, low, former, latter):
    return dot(high, former) + dot(high, latter) + dot(low, former)


def plan_kernel(place, pairs_ref, owners_ref, out_ref):
    size = 256
    down = lax.broadcasted_iota(jnp.int32, (size, size), 0)
    across = lax.broadcasted_iota(jnp.int32, (size, size), 1)
    one = lambda condition: jnp.where(condition, 1.0, 0.0)
    to_row = lambda column: jnp.sum(jnp.where(down == across, column, 0.0), axis=0, keepdims=True)
    to_column = lambda row: jnp.sum(jnp.where(down == across, row, 0.0), axis=1, keepdims=True)
    rows, columns = down.astype(jnp.float32), across.astype(jnp.float32)
    left, right = pairs_ref[:, 0:1].astype(jnp.float32), pairs_ref[:, 1:2].astype(jnp.float32)
    owner_row = owners_ref[...].astype(jnp.float32)
    owner = to_column(owner_row)

    used = jnp.max(one(right == columns), axis=0, keepdims=True)
    used_column = to_column(used)
    rank = jnp.sum(jnp.where(columns < rows, used, 0.0), axis=1, keepdims=True)
    used_list = jnp.sum(jnp.where((rank == columns) & (used_column > 0), rows, 0.0), axis=0, keepdims=True)
    right_rank = jnp.sum(jnp.where(columns < right, used, 0.0), axis=1, keepdims=True)

    parity = lambda value: value - 2.0 * jnp.floor(value * 0.5)
    count = jnp.sum(one(owner == columns), axis=0, keepdims=True)
    same = parity(rows) == parity(columns)
    offset = jnp.sum(jnp.where((rows < columns) & same, to_column(count), 0.0), axis=0, keepdims=True)
    ahead = (owner_row < owner) | ((owner_row == owner) & (across < down))
    ahead = ahead & (parity(owner_row) == parity(owner))
    position = jnp.sum(one(ahead), axis=1, keepdims=True)

    core = place[3].astype(jnp.float32)
    local = right_rank - core * (USED // 2)
    here = (local >= 0) & (local < USED // 2)
    local = jnp.where(here, local, 0.0)
    lane = lax.broadcasted_iota(jnp.int32, (1, size), 1)
    groups = jnp.zeros((1, size), jnp.float32)
    for half in range(2):
        hit = (position == columns) & (parity(owner) == half)
        pick = lambda column: jnp.sum(jnp.where(hit, column, 0.0), axis=0, keepdims=True).astype(jnp.int32)
        at = pick(local)
        out_ref[4 * half : 4 * half + 1, :] = pick(left) * BLK
        out_ref[4 * half + 1 : 4 * half + 2, :] = at // 8 * 128
        out_ref[4 * half + 2 : 4 * half + 3, :] = (lane + 8 - at % 8) % 8 * BLK
        out_ref[4 * half + 3 : 4 * half + 4, :] = jnp.where(pick(one(here)) > 0, lane % 8, -1)
        total = jnp.sum(one(parity(owner_row) == half))
        groups = jnp.where(lane == half, jnp.floor((total + 7.0) / 8.0), groups)
    for at, row in enumerate((offset, count, used_list, groups)):
        out_ref[8 + at : 9 + at, :] = row.astype(jnp.int32)


def plan_call(place, pairs, owners):
    return pl.pallas_call(
        plan_kernel,
        out_shape=jax.ShapeDtypeStruct((16, pairs.shape[0]), jnp.int32),
        in_specs=[SMEM, VMEM, VMEM],
        out_specs=VMEM,
        compiler_params=params(8),
        name="plan",
    )(place, pairs, owners)


def padded(planes):
    return (len(planes) * PLANE + 127) // 128 * 128


def screen_kernel(place, own_ref, other_ref, *outs):
    z = place[0]
    rows = 16
    lane = lax.broadcasted_iota(jnp.int32, (rows, 128), 1)

    def plane_of(ref, row, delta, offset):
        plane = lax.rem(z + delta, 8)
        odd = lax.rem(plane, 2)
        column = pl.multiple_of(plane * PLANE - odd * 64, 128)
        window = ref[row, pl.ds(column, 384)]
        turned = pltpu.roll(window, 64 if offset else 320, 1)
        return jnp.where((odd == 1) if offset else (odd == 0), window, turned)

    for source, ref in enumerate((own_ref, other_ref)):

        def body(step, carry, source=source, ref=ref):
            part = step // 10
            row = pl.ds(pl.multiple_of(step * rows, rows), rows)
            target = pl.multiple_of(part * PLANE + source * (PLANE // 2) + (step - part * 10) * rows, rows)
            for group, planes in enumerate((NEAR, MIDDLE, FAR)):
                for at in range(0, len(planes), 2):
                    a = plane_of(ref, row, planes[at], False)
                    if at + 1 < len(planes):
                        b = plane_of(ref, row, planes[at + 1], True)
                        middle = jnp.where(lane < 64, a[:, 256:], b[:, :128])
                        whole = jnp.concatenate([a[:, :256], middle, b[:, 128:]], axis=1)
                    else:
                        whole = jnp.concatenate([a[:, :256], jnp.where(lane < 64, a[:, 256:], 0.0)], axis=1)
                    top, rest = split(whole)
                    columns = slice(at * PLANE, at * PLANE + whole.shape[1])
                    outs[2 * group][pl.ds(target, rows), columns] = top
                    outs[2 * group + 1][pl.ds(target, rows), columns] = rest
            return carry

        lax.fori_loop(0, 20, body, 0)


def screen_call(place, own, other):
    shapes = [
        jax.ShapeDtypeStruct((2 * own.shape[0], padded(planes)), jnp.bfloat16)
        for planes in (NEAR, MIDDLE, FAR)
        for _ in range(2)
    ]
    return pl.pallas_call(
        screen_kernel,
        out_shape=shapes,
        in_specs=[SMEM, VMEM, VMEM],
        out_specs=[VMEM] * 6,
        compiler_params=params(20),
        name="screen",
    )(place, own, other)


def left_kernel(place, *refs):
    pieces, (high_ref, low_ref, work) = refs[:8], refs[8:]
    x = place[1]
    span = pieces[0].shape[0] // 2
    for core in range(2):
        for shift in range(4):
            shard = lax.rem(x - shift + 4, 4)
            for part in range(2):
                row = pl.multiple_of(part * 8 * span + core * 4 * span + shard * span, 8)
                work[pl.ds(row, span), :] = pieces[core * 4 + shift][part * span : (part + 1) * span, :]
    for block in range(work.shape[1] // 128):
        turned = work[:, block * 128 : (block + 1) * 128].T
        top, rest = split(turned)
        high_ref[block * 128 : (block + 1) * 128, :] = top
        low_ref[block * 128 : (block + 1) * 128, :] = rest


def left_call(place, pieces):
    depth, width = pieces[0].shape
    shape = jax.ShapeDtypeStruct((width, 8 * depth), jnp.bfloat16)
    return pl.pallas_call(
        left_kernel,
        out_shape=(shape, shape),
        in_specs=[SMEM] + [VMEM] * 8,
        out_specs=(VMEM, VMEM),
        scratch_shapes=[pltpu.VMEM((8 * depth, width), jnp.float32)],
        compiler_params=params(20),
        name="left",
    )(place, *pieces)


def load_right(place, units, planes, high, low):
    y = place[2]
    for delta, plane, part, ref, start in units:
        row = pl.multiple_of(plane * PLANE + lax.rem(y + delta, 4) * SPAN, 16)
        top, rest = split(ref[start : start + SPAN, :])
        high[pl.ds(row, SPAN), part * HALF : (part + 1) * HALF] = top
        low[pl.ds(row, SPAN), part * HALF : (part + 1) * HALF] = rest
    used = planes * PLANE
    if used < high.shape[0]:
        for ref in (high, low):
            ref[used:, :] = jnp.zeros((ref.shape[0] - used, ref.shape[1]), ref.dtype)


def near_units(own, below, above, two_below, two_above):
    units, planes = [], len(NEAR)
    for unit in range(2 * planes):
        half, at = (two_below, unit) if unit < planes else (two_above, unit - planes)
        for delta, ref, index in ((0, own, unit), (3, below, unit), (1, above, unit), (2, half, at)):
            units.append((delta, unit // 2, unit % 2, ref, index * SPAN))
    return units


def middle_units(below, above, z_below, z_above, y_below, y_above):
    units = []
    for part in range(2):
        for plane, own, sides, across in ((0, below, z_below, y_below), (1, above, z_above, y_above)):
            for delta, ref, block in ((0, own, 0), (3, sides, 0), (1, sides, 1), (2, across, 0)):
                units.append((delta, plane, part, ref, (2 * block + part) * SPAN))
    return units


def far_units(z_below, z_above, below, above, across_low, across_high):
    units = []
    for part, own, across in ((0, z_below, across_low), (1, z_above, across_high)):
        for delta, ref, start in ((0, own, 4), (3, below, part), (1, above, part), (2, across, 0)):
            units.append((delta, 0, part, ref, start * SPAN))
    return units


def group_kernel(units, planes, place, *refs):
    count = len(refs) - 5 - (units is middle_units)
    rights, (high_ref, low_ref), rest = refs[:count], refs[count : count + 2], refs[count + 2 :]
    out_ref, rh, rl = rest[-3:]
    load_right(place, units(*rights), planes, rh, rl)
    value = dot3(high_ref[...], low_ref[...], rh[...], rl[...])
    out_ref[...] = value if len(rest) == 3 else value + rest[0][...]


def group_call(units, planes, place, rights, screens, total):
    rows, width = screens[0].shape
    return pl.pallas_call(
        functools.partial(group_kernel, units, planes),
        out_shape=jax.ShapeDtypeStruct((rows, 2 * HALF), jnp.float32),
        in_specs=[SMEM] + [VMEM] * (len(rights) + 2 + len(total)),
        out_specs=VMEM,
        scratch_shapes=[pltpu.VMEM((width, 2 * HALF), jnp.bfloat16)] * 2,
        compiler_params=params(32),
        name="group",
    )(place, *rights, *screens, *total)


def pair_kernel(place, table, *refs):
    rights, (high_ref, low_ref, sum_ref, left_high, left_low, give_ref, kern, rh, rl) = refs[:6], refs[6:]
    load_right(place, far_units(*rights), len(FAR), rh, rl)
    product = sum_ref[...] + dot3(high_ref[...], low_ref[...], rh[...], rl[...])
    mid = product.shape[0] // 2
    real = product[:mid, :HALF] - product[mid:, HALF:]
    imag = product[mid:, :HALF] + product[:mid, HALF:]
    applied = NG ** (-0.5) * jnp.concatenate(
        [jnp.concatenate([real, imag], axis=0), jnp.concatenate([imag, -real], axis=0)], axis=1
    )
    kern[...] = dot3(left_high[...], left_low[...], *split(applied))

    extract(table, 1 - place[3], kern, give_ref)


def extract(table, half, kern, out_ref):
    lane = lax.broadcasted_iota(jnp.int32, (8, 128), 1) // BLK
    upper = lax.broadcasted_iota(jnp.int32, (8, 128), 0) < 4

    def groups(pair, carry):
        for g in (pair * 2, pair * 2 + 1):
            tiles = [[jnp.zeros((8, 128), jnp.float32) for _ in range(2)] for _ in range(2)]
            for u in range(8):
                slot = g * 8 + u
                row = pl.multiple_of(table[4 * half, slot], BLK)
                column = pl.multiple_of(table[4 * half + 1, slot], 128)
                shift = table[4 * half + 2, slot]
                target = table[4 * half + 3, slot]
                for part in range(2):
                    for side in range(2):
                        tile = kern[pl.ds(row + side * 8, 8), pl.ds(column + part * HALF, 128)]
                        tile = pltpu.roll(tile, shift, 1)
                        tiles[part][side] = jnp.where(lane == target, tile, tiles[part][side])
            lanes = pl.ds(pl.multiple_of(g * 128, 128), 128)
            for side in range(2):
                real, imag = tiles[0][side], tiles[1][side]
                out_ref[2 * side, :, lanes] = jnp.where(upper, real, pltpu.roll(imag, 4, 0))
                out_ref[2 * side + 1, :, lanes] = jnp.where(upper, pltpu.roll(real, 4, 0), imag)
        return carry

    out_ref[...] = jnp.zeros_like(out_ref)
    lax.fori_loop(0, (table[11, half] + 1) // 2, groups, 0)


def pair_call(place, table, rights, screens, total, left_high, left_low):
    rows = left_high.shape[0]
    return pl.pallas_call(
        pair_kernel,
        out_shape=(
            jax.ShapeDtypeStruct((4, 8, ROOM * BLK), jnp.float32),
            jax.ShapeDtypeStruct((rows, 2 * HALF), jnp.float32),
        ),
        in_specs=[SMEM, SMEM] + [VMEM] * (len(rights) + 5),
        out_specs=(VMEM, VMEM),
        scratch_shapes=[pltpu.VMEM((screens[0].shape[1], 2 * HALF), jnp.bfloat16)] * 2,
        compiler_params=params(24),
        name="pair",
    )(place, table, *rights, *screens, total, left_high, left_low)


def extract_kernel(place, table, kern, out_ref):
    extract(table, place[3], kern, out_ref)


def extract_call(place, table, kern):
    return pl.pallas_call(
        extract_kernel,
        out_shape=jax.ShapeDtypeStruct((4, 8, ROOM * BLK), jnp.float32),
        in_specs=[SMEM, SMEM, VMEM],
        out_specs=VMEM,
        compiler_params=params(8),
        name="extract",
    )(place, table, kern)


def add_kernel(one_ref, two_ref, out_ref):
    out_ref[...] = one_ref[...] + two_ref[...]


def add_call(one, two):
    return pl.pallas_call(
        add_kernel,
        out_shape=jax.ShapeDtypeStruct(one.shape, one.dtype),
        in_specs=[VMEM, VMEM],
        out_specs=VMEM,
        compiler_params=params(8),
        name="add",
    )(one, two)


def owner_kernel(place, table, parts_ref, out_ref, work):
    total = parts_ref[0]
    for at in range(1, parts_ref.shape[0]):
        total = total + parts_ref[at]
    width = total.shape[1]
    work[:, :width] = total
    work[:, width:] = jnp.zeros((8, work.shape[1] - width), jnp.float32)
    for chip in range(out_ref.shape[0]):
        start = table[8, chip * 2 + place[3]]
        column = pl.multiple_of(start // 8 * 128, 128)
        shift = lax.rem(384 - lax.rem(start, 8) * BLK, 384)
        out_ref[chip] = pltpu.roll(work[:, pl.ds(column, 384)], shift, 1)[:, :256]


def owner_call(place, table, parts):
    return pl.pallas_call(
        owner_kernel,
        out_shape=jax.ShapeDtypeStruct((32, 8, 256), jnp.float32),
        in_specs=[SMEM, SMEM, VMEM],
        out_specs=VMEM,
        scratch_shapes=[pltpu.VMEM((8, parts.shape[2] + 384), jnp.float32)],
        compiler_params=params(8),
        name="owner",
    )(place, table, parts)


def last_kernel(place, table, parts_ref, out_ref):
    total = parts_ref[0]
    for chip in range(1, parts_ref.shape[0]):
        total = total + parts_ref[chip]
    held = table[9, (place[0] * 4 + place[2]) * 2 + place[3]]
    for slot in range(CAP):
        tile = total[:, slot // 8 * 128 : slot // 8 * 128 + 128]
        tile = pltpu.roll(tile, (128 - slot % 8 * BLK) % 128, 1)
        out_ref[slot] = jnp.where(slot < held, tile[:, :BLK], 0.0)


def last_call(place, table, parts):
    return pl.pallas_call(
        last_kernel,
        out_shape=jax.ShapeDtypeStruct((CAP, 8, BLK), jnp.float32),
        in_specs=[SMEM, SMEM, VMEM],
        out_specs=VMEM,
        compiler_params=params(8),
        name="last",
    )(place, table, parts)


def pack_kernel(place, own_ref, other_ref, out_ref, work):
    core = place[3]
    width = own_ref.shape[2]
    for block in range(width // 128):
        lanes = pl.ds(block * 128, 128)
        rows = []
        for part in range(2):
            own, other = own_ref[part, :, lanes], other_ref[part, :, lanes]
            rows += [jnp.where(core == 0, own, other), jnp.where(core == 0, other, own)]
        rows = jnp.concatenate(rows + rows, axis=0)
        work[block * 128 : (block + 1) * 128, :] = rows.T
    half = lax.broadcasted_iota(jnp.int32, (8, 128), 1) < 64
    for chip in range(32):
        at = pl.multiple_of(chip * 80 + core * 40, 8)
        tiles = [work[pl.ds(at + 8 * t, 8), :] for t in range(5)]
        out_ref[chip * 20 : chip * 20 + 8, :] = jnp.where(half, tiles[0], tiles[1])
        out_ref[chip * 20 + 8 : chip * 20 + 16, :] = jnp.where(half, tiles[2], tiles[3])
        last = jnp.where(half, tiles[4], pltpu.roll(tiles[4], 4, 0))
        out_ref[chip * 20 + 16 : chip * 20 + 20, :] = last[:4]


def pack_call(place, own, other):
    width = own.shape[2]
    return pl.pallas_call(
        pack_kernel,
        out_shape=jax.ShapeDtypeStruct((32 * 20, 128), jnp.float32),
        in_specs=[SMEM, VMEM, VMEM],
        out_specs=VMEM,
        scratch_shapes=[pltpu.VMEM((width, 128), jnp.float32)],
        name="pack",
    )(place, own, other)


def unpack_kernel(place, table, in_ref, columns_ref, keep_ref, give_ref):
    core = place[3]
    quarter = lax.broadcasted_iota(jnp.int32, (8, 128), 1) // 32
    upper = lax.broadcasted_iota(jnp.int32, (8, 128), 0) < 4
    for group in range(8):
        tiles = [[None] * 5 for _ in range(2)]
        for u in range(4):
            at = (group * 4 + u) * 20
            one, two = in_ref[at : at + 8, :], in_ref[at + 8 : at + 16, :]
            end = in_ref[at + 12 : at + 20, :]
            end = jnp.where(upper, pltpu.roll(end, 4, 0), pltpu.roll(end, 64, 1))
            for t, (source, first) in enumerate(((one, 0), (one, 64), (two, 0), (two, 64), (end, 0))):
                for part in range(2):
                    by = (u * 32 - first - part * 32) % 128
                    turned = pltpu.roll(source, by, 1) if by else source
                    old = tiles[part][t]
                    tiles[part][t] = turned if old is None else jnp.where(quarter == u, turned, old)
        for part in range(2):
            for t in range(5):
                row = part * 40 + t * 8
                columns_ref[row : row + 8, group * 128 : (group + 1) * 128] = tiles[part][t]
    select(table, 1 - core, columns_ref, give_ref)
    select(table, core, columns_ref, keep_ref)


def select(table, which, columns_ref, out_ref):
    eighth = lax.broadcasted_iota(jnp.int32, (80, 128), 1) // BLK
    for group in range(2):
        slab = None
        for u in range(8):
            block = table[10, which * (USED // 2) + group * 8 + u]
            column = pl.multiple_of(block // 8 * 128, 128)
            by = lax.rem(u * BLK + 128 - lax.rem(block, 8) * BLK, 128)
            turned = pltpu.roll(columns_ref[:, pl.ds(column, 128)], by, 1)
            slab = turned if slab is None else jnp.where(eighth == u, turned, slab)
        out_ref[:, group * 128 : (group + 1) * 128] = slab


def unpack_call(place, table, pieces):
    return pl.pallas_call(
        unpack_kernel,
        out_shape=(
            jax.ShapeDtypeStruct((80, 1024), jnp.float32),
            jax.ShapeDtypeStruct((80, HALF), jnp.float32),
            jax.ShapeDtypeStruct((80, HALF), jnp.float32),
        ),
        in_specs=[SMEM, SMEM, VMEM],
        out_specs=(VMEM, VMEM, VMEM),
        compiler_params=params(8),
        name="unpack",
    )(place, table, pieces)


def shard_kernel(place, keep_ref, take_ref, out_ref):
    core = place[3]
    for part in range(2):
        out_ref[pl.ds(pl.multiple_of(part * 80 + core * 40, 8), 40), :] = keep_ref[part * 40 : part * 40 + 40, :]
        out_ref[pl.ds(pl.multiple_of(part * 80 + 40 - core * 40, 8), 40), :] = take_ref[part * 40 : part * 40 + 40, :]


def shard_call(place, keep, take):
    return pl.pallas_call(
        shard_kernel,
        out_shape=jax.ShapeDtypeStruct((160, HALF), jnp.float32),
        in_specs=[SMEM, VMEM, VMEM],
        out_specs=VMEM,
        compiler_params=params(8),
        name="shard",
    )(place, keep, take)


def after(array, *others):
    return lax.optimization_barrier((array, *others))[0]


def shards(densities, screened, pairs, owners):
    span = screened.shape[2]
    place = jnp.stack([lax.axis_index(axis) for axis in ("z", "x", "y", "core")]).astype(jnp.int32)
    shift = lambda array, axis, by: lax.ppermute(array, axis, ring(lax.axis_size(axis), by))
    swap = lambda array: lax.ppermute(array, "core", SWAP)
    join = lambda *arrays: jnp.concatenate(arrays, axis=0)
    hold = lax.optimization_barrier

    pieces = pack_call(place, densities, swap(densities))
    table = plan_call(place, after(pairs, pieces), owners.reshape(1, -1))
    mine = lax.all_to_all(pieces.reshape(32, 1, -1), ("z", "y"), 0, 0, tiled=True).reshape(pieces.shape)

    screen = screened.reshape(2 * 4 * span, -1)
    mine, other = hold((mine, swap(after(screen, pieces))))

    columns, keep, give = unpack_call(place, table, mine)
    shard = shard_call(place, keep, swap(give))

    block, half = 2 * SPAN, len(NEAR) * SPAN
    steps = hold((columns, *(shift(shard, "z", by) for by in (1, -1, 2, -2))))
    columns, nearest = steps[0], steps[1:]
    near = join(shard, *nearest)
    near_down, near_up = shift(near, "y", 1), shift(near, "y", -1)
    below3, above3 = shift(nearest[2], "z", 1), shift(nearest[3], "z", -1)
    screens = screen_call(place, after(screen, near), other)
    around = [columns] + [shift(columns, "x", by) for by in (1, 2, 3)]
    swapped = [swap(columns), swap(around[1]), None, swap(around[3])]
    near_down, near_up, below3, above3, swapped[0], swapped[1], swapped[3], *screens = hold(
        (near_down, near_up, below3, above3, swapped[0], swapped[1], swapped[3], *screens)
    )

    two_down, two_up = shift(near_down[:half], "y", 1), shift(near_up[half:], "y", -1)
    third, fourth = slice(3 * block, 4 * block), slice(4 * block, 5 * block)
    z_below = shift(join(near_down[third], near_up[third], below3[:SPAN]), "z", 1)
    z_above = shift(join(near_down[fourth], near_up[fourth], above3[SPAN:]), "z", -1)
    swapped[2] = swap(around[2])
    left_high, left_low = left_call(place, around + swapped)
    two_down, two_up, z_below, z_above, left_high, left_low = hold(
        (two_down, two_up, z_below, z_above, left_high, left_low)
    )

    y_below, y_above = shift(z_below[:block], "y", 1), shift(z_above[block : 2 * block], "y", -1)
    far_below, far_above = shift(z_below[:block], "z", 1), shift(z_above[block : 2 * block], "z", -1)
    rights = (near, near_down, near_up, two_down, two_up)
    total = group_call(near_units, len(NEAR), place, rights, screens[:2], ())
    y_below, y_above, far_below, far_above, total = hold((y_below, y_above, far_below, far_above, total))

    across_low, across_high = shift(far_below[:SPAN], "y", 1), shift(far_above[SPAN:], "y", -1)
    rights = (below3, above3, z_below, z_above, y_below, y_above)
    total = group_call(middle_units, len(MIDDLE), place, rights, screens[2:4], (total,))
    across_low, across_high, total = hold((across_low, across_high, total))
    rights = (z_below, z_above, far_below, far_above, across_low, across_high)
    give, kern = pair_call(place, table, rights, screens[4:], total, left_high, left_low)

    parts = add_call(extract_call(place, table, kern), swap(give))
    parts = lax.all_to_all(parts, "x", 0, 0, tiled=True)
    parts = owner_call(place, table, parts)
    parts = lax.all_to_all(parts, ("z", "y"), 0, 0, tiled=True)
    return last_call(place, table, parts).reshape(1, CAP, 2, 4, BLK)


def solution(mesh):
    fine = Mesh(mesh.devices.reshape(8, 4, 2, 4), ("z", "y", "core", "x"))
    in_specs = (P(None, BAND, "x"), P(None, None, BAND, "x"), P(), P())
    out_specs = P(BAND, None, None, "x", None)
    return jax.shard_map(shards, mesh=fine, in_specs=in_specs, out_specs=out_specs, check_vma=False)
```

```python
import functools

import jax
import jax.numpy as jnp
from jax import lax
from jax.experimental import pallas as pl
from jax.experimental.pallas import tpu as pltpu
from jax.sharding import Mesh
from jax.sharding import PartitionSpec as P

NG = 10240
CAP = 12
BLK = 16
USED = 32
HALF = USED // 2 * BLK
BAND = ("z", "y", "core")
SWAP = ((0, 1), (1, 0))
SMEM = pl.BlockSpec(memory_space=pltpu.SMEM)
VMEM = pl.BlockSpec(memory_space=pltpu.VMEM)
SPAN = 80
PLANE = 320
NEAR = (0, 7, 1, 6, 2)
FAR = (5, 3, 4)
ROOM = 224


def ring(n, shift):
    return [(i, (i + shift) % n) for i in range(n)]


def params(mib):
    return pltpu.CompilerParams(vmem_limit_bytes=mib * 1024 * 1024)


def split(x):
    high = x.astype(jnp.bfloat16)
    return high, (x - high.astype(jnp.float32)).astype(jnp.bfloat16)


def dot(former, latter):
    return jnp.dot(former, latter, preferred_element_type=jnp.float32)


def dot3(high, low, former, latter):
    return dot(high, former) + dot(high, latter) + dot(low, former)


def plan_kernel(place, pairs_ref, owners_ref, out_ref):
    size = 256
    down = lax.broadcasted_iota(jnp.int32, (size, size), 0)
    across = lax.broadcasted_iota(jnp.int32, (size, size), 1)
    one = lambda condition: jnp.where(condition, 1.0, 0.0)
    to_row = lambda column: jnp.sum(jnp.where(down == across, column, 0.0), axis=0, keepdims=True)
    to_column = lambda row: jnp.sum(jnp.where(down == across, row, 0.0), axis=1, keepdims=True)
    rows, columns = down.astype(jnp.float32), across.astype(jnp.float32)
    left, right = pairs_ref[:, 0:1].astype(jnp.float32), pairs_ref[:, 1:2].astype(jnp.float32)
    owner_row = owners_ref[...].astype(jnp.float32)
    owner = to_column(owner_row)

    used = jnp.max(one(right == columns), axis=0, keepdims=True)
    used_column = to_column(used)
    rank = jnp.sum(jnp.where(columns < rows, used, 0.0), axis=1, keepdims=True)
    used_list = jnp.sum(jnp.where((rank == columns) & (used_column > 0), rows, 0.0), axis=0, keepdims=True)
    right_rank = jnp.sum(jnp.where(columns < right, used, 0.0), axis=1, keepdims=True)

    parity = lambda value: value - 2.0 * jnp.floor(value * 0.5)
    count = jnp.sum(one(owner == columns), axis=0, keepdims=True)
    same = parity(rows) == parity(columns)
    offset = jnp.sum(jnp.where((rows < columns) & same, to_column(count), 0.0), axis=0, keepdims=True)
    ahead = (owner_row < owner) | ((owner_row == owner) & (across < down))
    ahead = ahead & (parity(owner_row) == parity(owner))
    position = jnp.sum(one(ahead), axis=1, keepdims=True)

    core = place[3].astype(jnp.float32)
    local = right_rank - core * (USED // 2)
    here = (local >= 0) & (local < USED // 2)
    local = jnp.where(here, local, 0.0)
    lane = lax.broadcasted_iota(jnp.int32, (1, size), 1)
    groups = jnp.zeros((1, size), jnp.float32)
    for half in range(2):
        hit = (position == columns) & (parity(owner) == half)
        pick = lambda column: jnp.sum(jnp.where(hit, column, 0.0), axis=0, keepdims=True).astype(jnp.int32)
        at = pick(local)
        out_ref[4 * half : 4 * half + 1, :] = pick(left) * BLK
        out_ref[4 * half + 1 : 4 * half + 2, :] = at // 8 * 128
        out_ref[4 * half + 2 : 4 * half + 3, :] = (lane + 8 - at % 8) % 8 * BLK
        out_ref[4 * half + 3 : 4 * half + 4, :] = jnp.where(pick(one(here)) > 0, lane % 8, -1)
        total = jnp.sum(one(parity(owner_row) == half))
        groups = jnp.where(lane == half, jnp.floor((total + 7.0) / 8.0), groups)
    for at, row in enumerate((offset, count, used_list, groups)):
        out_ref[8 + at : 9 + at, :] = row.astype(jnp.int32)


def plan_call(place, pairs, owners):
    return pl.pallas_call(
        plan_kernel,
        out_shape=jax.ShapeDtypeStruct((16, pairs.shape[0]), jnp.int32),
        in_specs=[SMEM, VMEM, VMEM],
        out_specs=VMEM,
        compiler_params=params(8),
        name="plan",
    )(place, pairs, owners)


def padded(planes):
    return (len(planes) * PLANE + 127) // 128 * 128


def screen_kernel(place, own_ref, other_ref, *outs):
    z = place[0]
    rows = 16
    lane = lax.broadcasted_iota(jnp.int32, (rows, 128), 1)

    def plane_of(ref, row, delta, offset):
        plane = lax.rem(z + delta, 8)
        odd = lax.rem(plane, 2)
        column = pl.multiple_of(plane * PLANE - odd * 64, 128)
        window = ref[row, pl.ds(column, 384)]
        turned = pltpu.roll(window, 64 if offset else 320, 1)
        return jnp.where((odd == 1) if offset else (odd == 0), window, turned)

    for source, ref in enumerate((own_ref, other_ref)):

        def body(step, carry, source=source, ref=ref):
            part = step // 10
            row = pl.ds(pl.multiple_of(step * rows, rows), rows)
            target = pl.multiple_of(part * PLANE + source * (PLANE // 2) + (step - part * 10) * rows, rows)
            for group, planes in enumerate((NEAR, FAR)):
                for at in range(0, len(planes), 2):
                    a = plane_of(ref, row, planes[at], False)
                    if at + 1 < len(planes):
                        b = plane_of(ref, row, planes[at + 1], True)
                        middle = jnp.where(lane < 64, a[:, 256:], b[:, :128])
                        whole = jnp.concatenate([a[:, :256], middle, b[:, 128:]], axis=1)
                    else:
                        whole = jnp.concatenate([a[:, :256], jnp.where(lane < 64, a[:, 256:], 0.0)], axis=1)
                    top, rest = split(whole)
                    columns = slice(at * PLANE, at * PLANE + whole.shape[1])
                    outs[2 * group][pl.ds(target, rows), columns] = top
                    outs[2 * group + 1][pl.ds(target, rows), columns] = rest
            return carry

        lax.fori_loop(0, 20, body, 0)


def screen_call(place, own, other):
    shapes = [
        jax.ShapeDtypeStruct((2 * own.shape[0], padded(planes)), jnp.bfloat16)
        for planes in (NEAR, FAR)
        for _ in range(2)
    ]
    return pl.pallas_call(
        screen_kernel,
        out_shape=shapes,
        in_specs=[SMEM, VMEM, VMEM],
        out_specs=[VMEM] * 4,
        compiler_params=params(20),
        name="screen",
    )(place, own, other)


def left_kernel(place, *refs):
    pieces, (high_ref, low_ref, work) = refs[:8], refs[8:]
    x = place[1]
    span = pieces[0].shape[0] // 2
    for core in range(2):
        for shift in range(4):
            shard = lax.rem(x - shift + 4, 4)
            for part in range(2):
                row = pl.multiple_of(part * 8 * span + core * 4 * span + shard * span, 8)
                work[pl.ds(row, span), :] = pieces[core * 4 + shift][part * span : (part + 1) * span, :]
    for block in range(work.shape[1] // 128):
        turned = work[:, block * 128 : (block + 1) * 128].T
        top, rest = split(turned)
        high_ref[block * 128 : (block + 1) * 128, :] = top
        low_ref[block * 128 : (block + 1) * 128, :] = rest


def left_call(place, pieces):
    depth, width = pieces[0].shape
    shape = jax.ShapeDtypeStruct((width, 8 * depth), jnp.bfloat16)
    return pl.pallas_call(
        left_kernel,
        out_shape=(shape, shape),
        in_specs=[SMEM] + [VMEM] * 8,
        out_specs=(VMEM, VMEM),
        scratch_shapes=[pltpu.VMEM((8 * depth, width), jnp.float32)],
        compiler_params=params(20),
        name="left",
    )(place, *pieces)


def load_right(place, units, planes, high, low):
    y = place[2]
    for delta, plane, part, ref, start in units:
        row = pl.multiple_of(plane * PLANE + lax.rem(y + delta, 4) * SPAN, 16)
        top, rest = split(ref[start : start + SPAN, :])
        high[pl.ds(row, SPAN), part * HALF : (part + 1) * HALF] = top
        low[pl.ds(row, SPAN), part * HALF : (part + 1) * HALF] = rest
    used = planes * PLANE
    if used < high.shape[0]:
        for ref in (high, low):
            ref[used:, :] = jnp.zeros((ref.shape[0] - used, ref.shape[1]), ref.dtype)


def near_units(own, below, above, two_below, two_above):
    units, planes = [], len(NEAR)
    for unit in range(2 * planes):
        half, at = (two_below, unit) if unit < planes else (two_above, unit - planes)
        for delta, ref, index in ((0, own, unit), (3, below, unit), (1, above, unit), (2, half, at)):
            units.append((delta, unit // 2, unit % 2, ref, index * SPAN))
    return units


def far_units(below, above, z_below, z_above, y_below, y_above, far_below, far_above, across_low, across_high):
    units = []
    for part, own, across in ((0, z_below, across_low), (1, z_above, across_high)):
        for plane, at, sides, over in ((0, below, z_below, y_below), (1, above, z_above, y_above)):
            for delta, ref, block in ((0, at, 0), (3, sides, 0), (1, sides, 1), (2, over, 0)):
                units.append((delta, plane, part, ref, (2 * block + part) * SPAN))
        for delta, ref, start in ((0, own, 4), (3, far_below, part), (1, far_above, part), (2, across, 0)):
            units.append((delta, 2, part, ref, start * SPAN))
    return units


def group_kernel(place, own, below, above, two_below, two_above, high_ref, low_ref, out_ref, rh, rl):
    load_right(place, near_units(own, below, above, two_below, two_above), len(NEAR), rh, rl)
    out_ref[...] = dot3(high_ref[...], low_ref[...], rh[...], rl[...])


def group_call(place, rights, screens):
    rows, width = screens[0].shape
    return pl.pallas_call(
        group_kernel,
        out_shape=jax.ShapeDtypeStruct((rows, 2 * HALF), jnp.float32),
        in_specs=[SMEM] + [VMEM] * 7,
        out_specs=VMEM,
        scratch_shapes=[pltpu.VMEM((width, 2 * HALF), jnp.bfloat16)] * 2,
        compiler_params=params(24),
        name="group",
    )(place, *rights, *screens)


def pair_kernel(place, table, *refs):
    rights, (high_ref, low_ref, sum_ref, left_high, left_low, give_ref, kern, rh, rl) = refs[:10], refs[10:]
    load_right(place, far_units(*rights), len(FAR), rh, rl)
    product = sum_ref[...] + dot3(high_ref[...], low_ref[...], rh[...], rl[...])
    mid = product.shape[0] // 2
    real = product[:mid, :HALF] - product[mid:, HALF:]
    imag = product[mid:, :HALF] + product[:mid, HALF:]
    applied = NG ** (-0.5) * jnp.concatenate(
        [jnp.concatenate([real, imag], axis=0), jnp.concatenate([imag, -real], axis=0)], axis=1
    )
    kern[...] = dot3(left_high[...], left_low[...], *split(applied))

    extract(place, table, 1 - place[3], kern, give_ref)


def extract(place, table, half, kern, out_ref):
    at = lambda x: lax.rem(x + 4 - place[1], 4)
    lane = lax.broadcasted_iota(jnp.int32, (8, 128), 1) // BLK
    upper = lax.broadcasted_iota(jnp.int32, (8, 128), 0) < 4

    def groups(pair, carry):
        for g in (pair * 2, pair * 2 + 1):
            tiles = [[jnp.zeros((8, 128), jnp.float32) for _ in range(2)] for _ in range(2)]
            for u in range(8):
                slot = g * 8 + u
                row = pl.multiple_of(table[4 * half, slot], BLK)
                column = pl.multiple_of(table[4 * half + 1, slot], 128)
                shift = table[4 * half + 2, slot]
                target = table[4 * half + 3, slot]
                for part in range(2):
                    for side in range(2):
                        tile = kern[pl.ds(row + side * 8, 8), pl.ds(column + part * HALF, 128)]
                        tile = pltpu.roll(tile, shift, 1)
                        tiles[part][side] = jnp.where(lane == target, tile, tiles[part][side])
            lanes = pl.ds(pl.multiple_of(g * 128, 128), 128)
            for side in range(2):
                real, imag = tiles[0][side], tiles[1][side]
                out_ref[at(2 * side), :, lanes] = jnp.where(upper, real, pltpu.roll(imag, 4, 0))
                out_ref[at(2 * side + 1), :, lanes] = jnp.where(upper, pltpu.roll(real, 4, 0), imag)
        return carry

    out_ref[...] = jnp.zeros_like(out_ref)
    lax.fori_loop(0, (table[11, half] + 1) // 2, groups, 0)


def pair_call(place, table, rights, screens, total, left_high, left_low):
    rows = left_high.shape[0]
    return pl.pallas_call(
        pair_kernel,
        out_shape=(
            jax.ShapeDtypeStruct((4, 8, ROOM * BLK), jnp.float32),
            jax.ShapeDtypeStruct((rows, 2 * HALF), jnp.float32),
        ),
        in_specs=[SMEM, SMEM] + [VMEM] * (len(rights) + 5),
        out_specs=(VMEM, VMEM),
        scratch_shapes=[pltpu.VMEM((screens[0].shape[1], 2 * HALF), jnp.bfloat16)] * 2,
        compiler_params=params(24),
        name="pair",
    )(place, table, *rights, *screens, total, left_high, left_low)


def extract_kernel(place, table, kern, out_ref):
    extract(place, table, place[3], kern, out_ref)


def extract_call(place, table, kern):
    return pl.pallas_call(
        extract_kernel,
        out_shape=jax.ShapeDtypeStruct((4, 8, ROOM * BLK), jnp.float32),
        in_specs=[SMEM, SMEM, VMEM],
        out_specs=VMEM,
        compiler_params=params(8),
        name="extract",
    )(place, table, kern)


def add_kernel(one_ref, two_ref, *outs):
    for at, out_ref in enumerate(outs):
        out_ref[...] = one_ref[at] + two_ref[at]


def add_call(one, two):
    return pl.pallas_call(
        add_kernel,
        out_shape=[jax.ShapeDtypeStruct(one.shape[1:], one.dtype)] * one.shape[0],
        in_specs=[VMEM, VMEM],
        out_specs=[VMEM] * one.shape[0],
        compiler_params=params(8),
        name="add",
    )(one, two)


def owner_kernel(place, table, one_ref, two_ref, three_ref, four_ref, out_ref, work):
    total = (one_ref[...] + two_ref[...]) + (three_ref[...] + four_ref[...])
    width = total.shape[1]
    work[:, :width] = total
    work[:, width:] = jnp.zeros((8, work.shape[1] - width), jnp.float32)
    for chip in range(out_ref.shape[0]):
        start = table[8, chip * 2 + place[3]]
        column = pl.multiple_of(start // 8 * 128, 128)
        shift = lax.rem(384 - lax.rem(start, 8) * BLK, 384)
        out_ref[chip] = pltpu.roll(work[:, pl.ds(column, 384)], shift, 1)[:, :256]


def owner_call(place, table, parts):
    return pl.pallas_call(
        owner_kernel,
        out_shape=jax.ShapeDtypeStruct((32, 8, 256), jnp.float32),
        in_specs=[SMEM, SMEM] + [VMEM] * 4,
        out_specs=VMEM,
        scratch_shapes=[pltpu.VMEM((8, parts[0].shape[1] + 384), jnp.float32)],
        compiler_params=params(8),
        name="owner",
    )(place, table, *parts)


def last_kernel(place, table, parts_ref, out_ref):
    total = parts_ref[0]
    for chip in range(1, parts_ref.shape[0]):
        total = total + parts_ref[chip]
    held = table[9, (place[0] * 4 + place[2]) * 2 + place[3]]
    for slot in range(CAP):
        tile = total[:, slot // 8 * 128 : slot // 8 * 128 + 128]
        tile = pltpu.roll(tile, (128 - slot % 8 * BLK) % 128, 1)
        out_ref[slot] = jnp.where(slot < held, tile[:, :BLK], 0.0)


def last_call(place, table, parts):
    return pl.pallas_call(
        last_kernel,
        out_shape=jax.ShapeDtypeStruct((CAP, 8, BLK), jnp.float32),
        in_specs=[SMEM, SMEM, VMEM],
        out_specs=VMEM,
        compiler_params=params(8),
        name="last",
    )(place, table, parts)


def pack_kernel(place, own_ref, other_ref, out_ref, work):
    core = place[3]
    width = own_ref.shape[2]
    for block in range(width // 128):
        lanes = pl.ds(block * 128, 128)
        rows = []
        for part in range(2):
            own, other = own_ref[part, :, lanes], other_ref[part, :, lanes]
            rows += [jnp.where(core == 0, own, other), jnp.where(core == 0, other, own)]
        rows = jnp.concatenate(rows + rows, axis=0)
        work[block * 128 : (block + 1) * 128, :] = rows.T
    half = lax.broadcasted_iota(jnp.int32, (8, 128), 1) < 64
    for chip in range(32):
        at = pl.multiple_of(chip * 80 + core * 40, 8)
        tiles = [work[pl.ds(at + 8 * t, 8), :] for t in range(5)]
        out_ref[chip * 20 : chip * 20 + 8, :] = jnp.where(half, tiles[0], tiles[1])
        out_ref[chip * 20 + 8 : chip * 20 + 16, :] = jnp.where(half, tiles[2], tiles[3])
        last = jnp.where(half, tiles[4], pltpu.roll(tiles[4], 4, 0))
        out_ref[chip * 20 + 16 : chip * 20 + 20, :] = last[:4]


def pack_call(place, own, other):
    width = own.shape[2]
    return pl.pallas_call(
        pack_kernel,
        out_shape=jax.ShapeDtypeStruct((32 * 20, 128), jnp.float32),
        in_specs=[SMEM, VMEM, VMEM],
        out_specs=VMEM,
        scratch_shapes=[pltpu.VMEM((width, 128), jnp.float32)],
        name="pack",
    )(place, own, other)


def unpack_kernel(place, table, in_ref, columns_ref, keep_ref, give_ref):
    core = place[3]
    quarter = lax.broadcasted_iota(jnp.int32, (8, 128), 1) // 32
    upper = lax.broadcasted_iota(jnp.int32, (8, 128), 0) < 4
    for group in range(8):
        tiles = [[None] * 5 for _ in range(2)]
        for u in range(4):
            at = (group * 4 + u) * 20
            one, two = in_ref[at : at + 8, :], in_ref[at + 8 : at + 16, :]
            end = in_ref[at + 12 : at + 20, :]
            end = jnp.where(upper, pltpu.roll(end, 4, 0), pltpu.roll(end, 64, 1))
            for t, (source, first) in enumerate(((one, 0), (one, 64), (two, 0), (two, 64), (end, 0))):
                for part in range(2):
                    by = (u * 32 - first - part * 32) % 128
                    turned = pltpu.roll(source, by, 1) if by else source
                    old = tiles[part][t]
                    tiles[part][t] = turned if old is None else jnp.where(quarter == u, turned, old)
        for part in range(2):
            for t in range(5):
                row = part * 40 + t * 8
                columns_ref[row : row + 8, group * 128 : (group + 1) * 128] = tiles[part][t]
    select(table, 1 - core, columns_ref, give_ref)
    select(table, core, columns_ref, keep_ref)


def select(table, which, columns_ref, out_ref):
    eighth = lax.broadcasted_iota(jnp.int32, (80, 128), 1) // BLK
    for group in range(2):
        slab = None
        for u in range(8):
            block = table[10, which * (USED // 2) + group * 8 + u]
            column = pl.multiple_of(block // 8 * 128, 128)
            by = lax.rem(u * BLK + 128 - lax.rem(block, 8) * BLK, 128)
            turned = pltpu.roll(columns_ref[:, pl.ds(column, 128)], by, 1)
            slab = turned if slab is None else jnp.where(eighth == u, turned, slab)
        out_ref[:, group * 128 : (group + 1) * 128] = slab


def unpack_call(place, table, pieces):
    return pl.pallas_call(
        unpack_kernel,
        out_shape=(
            jax.ShapeDtypeStruct((80, 1024), jnp.float32),
            jax.ShapeDtypeStruct((80, HALF), jnp.float32),
            jax.ShapeDtypeStruct((80, HALF), jnp.float32),
        ),
        in_specs=[SMEM, SMEM, VMEM],
        out_specs=(VMEM, VMEM, VMEM),
        compiler_params=params(8),
        name="unpack",
    )(place, table, pieces)


def shard_kernel(place, keep_ref, take_ref, out_ref):
    core = place[3]
    for part in range(2):
        out_ref[pl.ds(pl.multiple_of(part * 80 + core * 40, 8), 40), :] = keep_ref[part * 40 : part * 40 + 40, :]
        out_ref[pl.ds(pl.multiple_of(part * 80 + 40 - core * 40, 8), 40), :] = take_ref[part * 40 : part * 40 + 40, :]


def shard_call(place, keep, take):
    return pl.pallas_call(
        shard_kernel,
        out_shape=jax.ShapeDtypeStruct((160, HALF), jnp.float32),
        in_specs=[SMEM, VMEM, VMEM],
        out_specs=VMEM,
        compiler_params=params(8),
        name="shard",
    )(place, keep, take)


def after(array, *others):
    return lax.optimization_barrier((array, *others))[0]


def shards(densities, screened, pairs, owners):
    span = screened.shape[2]
    place = jnp.stack([lax.axis_index(axis) for axis in ("z", "x", "y", "core")]).astype(jnp.int32)
    shift = lambda array, axis, by: lax.ppermute(array, axis, ring(lax.axis_size(axis), by))
    swap = lambda array: lax.ppermute(array, "core", SWAP)
    join = lambda *arrays: jnp.concatenate(arrays, axis=0)
    hold = lax.optimization_barrier

    pieces = pack_call(place, densities, swap(densities))
    table = plan_call(place, after(pairs, pieces), owners.reshape(1, -1))
    mine = lax.all_to_all(pieces.reshape(32, 1, -1), ("z", "y"), 0, 0, tiled=True).reshape(pieces.shape)

    screen = screened.reshape(2 * 4 * span, -1)
    mine, other = hold((mine, swap(after(screen, pieces))))

    columns, keep, give = unpack_call(place, table, mine)
    shard = shard_call(place, keep, swap(give))

    block, half = 2 * SPAN, len(NEAR) * SPAN
    steps = hold((columns, *(shift(shard, "z", by) for by in (1, -1, 2, -2))))
    columns, nearest = steps[0], steps[1:]
    near = join(shard, *nearest)
    near_down, near_up = shift(near, "y", 1), shift(near, "y", -1)
    below3, above3 = shift(nearest[2], "z", 1), shift(nearest[3], "z", -1)
    screens = screen_call(place, after(screen, near), other)
    around = [columns, shift(columns, "x", 1)]
    columns = after(columns, screens[0])
    around += [shift(columns, "x", 2), shift(columns, "x", 3)]
    near_down, near_up, below3, above3, around[1], *screens = hold(
        (near_down, near_up, below3, above3, around[1], *screens)
    )

    two_down, two_up = shift(near_down[:half], "y", 1), shift(near_up[half:], "y", -1)
    third, fourth = slice(3 * block, 4 * block), slice(4 * block, 5 * block)
    z_below = shift(join(near_down[third], near_up[third], below3[:SPAN]), "z", 1)
    z_above = shift(join(near_down[fourth], near_up[fourth], above3[SPAN:]), "z", -1)
    swapped = [swap(array) for array in around]
    left_high, left_low = left_call(place, around + swapped)
    two_down, two_up, z_below, z_above, left_high, left_low = hold(
        (two_down, two_up, z_below, z_above, left_high, left_low)
    )

    y_below, y_above = shift(z_below[:block], "y", 1), shift(z_above[block : 2 * block], "y", -1)
    far_below, far_above = shift(z_below[:block], "z", 1), shift(z_above[block : 2 * block], "z", -1)
    across_low, across_high = shift(z_below[2 * block :], "y", 2), shift(z_above[2 * block :], "y", -2)
    total = group_call(place, (near, near_down, near_up, two_down, two_up), screens[:2])
    *rights, total = hold((y_below, y_above, far_below, far_above, across_low, across_high, total))
    rights = (below3, above3, z_below, z_above, *rights)
    give, kern = pair_call(place, table, rights, screens[2:], total, left_high, left_low)

    parts = add_call(extract_call(place, table, kern), swap(give))
    parts = [parts[0]] + [shift(parts[by], "x", by) for by in (1, 2, 3)]
    parts = owner_call(place, table, parts)
    parts = lax.all_to_all(parts, ("z", "y"), 0, 0, tiled=True)
    return last_call(place, table, parts).reshape(1, CAP, 2, 4, BLK)


def solution(mesh):
    fine = Mesh(mesh.devices.reshape(8, 4, 2, 4), ("z", "y", "core", "x"))
    in_specs = (P(None, BAND, "x"), P(None, None, BAND, "x"), P(), P())
    out_specs = P(BAND, None, None, "x", None)
    return jax.shard_map(shards, mesh=fine, in_specs=in_specs, out_specs=out_specs, check_vma=False)
```

```python
import functools

import jax
import jax.numpy as jnp
from jax import lax
from jax.experimental import pallas as pl
from jax.experimental.pallas import tpu as pltpu
from jax.sharding import Mesh
from jax.sharding import PartitionSpec as P

NG = 10240
CAP = 12
BLK = 16
USED = 32
HALF = USED // 2 * BLK
BAND = ("z", "y", "core")
SWAP = ((0, 1), (1, 0))
SMEM = pl.BlockSpec(memory_space=pltpu.SMEM)
VMEM = pl.BlockSpec(memory_space=pltpu.VMEM)
SPAN = 80
PLANE = 320
NEAR = (0, 7, 1, 6, 2)
MIDDLE = (5, 3)
FAR = (4,)
ROOM = 224


def ring(n, shift):
    return [(i, (i + shift) % n) for i in range(n)]


def params(mib):
    return pltpu.CompilerParams(vmem_limit_bytes=mib * 1024 * 1024)


def split(x):
    high = x.astype(jnp.bfloat16)
    return high, (x - high.astype(jnp.float32)).astype(jnp.bfloat16)


def dot(former, latter):
    return jnp.dot(former, latter, preferred_element_type=jnp.float32)


def dot3(high, low, former, latter):
    return dot(high, former) + dot(high, latter) + dot(low, former)


def plan_kernel(place, pairs_ref, owners_ref, out_ref):
    size = 256
    down = lax.broadcasted_iota(jnp.int32, (size, size), 0)
    across = lax.broadcasted_iota(jnp.int32, (size, size), 1)
    one = lambda condition: jnp.where(condition, 1.0, 0.0)
    to_row = lambda column: jnp.sum(jnp.where(down == across, column, 0.0), axis=0, keepdims=True)
    to_column = lambda row: jnp.sum(jnp.where(down == across, row, 0.0), axis=1, keepdims=True)
    rows, columns = down.astype(jnp.float32), across.astype(jnp.float32)
    left, right = pairs_ref[:, 0:1].astype(jnp.float32), pairs_ref[:, 1:2].astype(jnp.float32)
    owner_row = owners_ref[...].astype(jnp.float32)
    owner = to_column(owner_row)

    used = jnp.max(one(right == columns), axis=0, keepdims=True)
    used_column = to_column(used)
    rank = jnp.sum(jnp.where(columns < rows, used, 0.0), axis=1, keepdims=True)
    used_list = jnp.sum(jnp.where((rank == columns) & (used_column > 0), rows, 0.0), axis=0, keepdims=True)
    right_rank = jnp.sum(jnp.where(columns < right, used, 0.0), axis=1, keepdims=True)

    parity = lambda value: value - 2.0 * jnp.floor(value * 0.5)
    count = jnp.sum(one(owner == columns), axis=0, keepdims=True)
    same = parity(rows) == parity(columns)
    offset = jnp.sum(jnp.where((rows < columns) & same, to_column(count), 0.0), axis=0, keepdims=True)
    ahead = (owner_row < owner) | ((owner_row == owner) & (across < down))
    ahead = ahead & (parity(owner_row) == parity(owner))
    position = jnp.sum(one(ahead), axis=1, keepdims=True)

    core = place[3].astype(jnp.float32)
    local = right_rank - core * (USED // 2)
    here = (local >= 0) & (local < USED // 2)
    local = jnp.where(here, local, 0.0)
    lane = lax.broadcasted_iota(jnp.int32, (1, size), 1)
    groups = jnp.zeros((1, size), jnp.float32)
    for half in range(2):
        hit = (position == columns) & (parity(owner) == half)
        pick = lambda column: jnp.sum(jnp.where(hit, column, 0.0), axis=0, keepdims=True).astype(jnp.int32)
        at = pick(local)
        out_ref[4 * half : 4 * half + 1, :] = pick(left) * BLK
        out_ref[4 * half + 1 : 4 * half + 2, :] = at // 8 * 128
        out_ref[4 * half + 2 : 4 * half + 3, :] = (lane + 8 - at % 8) % 8 * BLK
        out_ref[4 * half + 3 : 4 * half + 4, :] = jnp.where(pick(one(here)) > 0, lane % 8, -1)
        total = jnp.sum(one(parity(owner_row) == half))
        groups = jnp.where(lane == half, jnp.floor((total + 7.0) / 8.0), groups)
    for at, row in enumerate((offset, count, used_list, groups)):
        out_ref[8 + at : 9 + at, :] = row.astype(jnp.int32)


def plan_call(place, pairs, owners):
    return pl.pallas_call(
        plan_kernel,
        out_shape=jax.ShapeDtypeStruct((16, pairs.shape[0]), jnp.int32),
        in_specs=[SMEM, VMEM, VMEM],
        out_specs=VMEM,
        compiler_params=params(8),
        name="plan",
    )(place, pairs, owners)


def padded(planes):
    return (len(planes) * PLANE + 127) // 128 * 128


def screen_kernel(place, own_ref, other_ref, *outs):
    z = place[0]
    rows = 16
    lane = lax.broadcasted_iota(jnp.int32, (rows, 128), 1)

    def plane_of(ref, row, delta, offset):
        plane = lax.rem(z + delta, 8)
        odd = lax.rem(plane, 2)
        column = pl.multiple_of(plane * PLANE - odd * 64, 128)
        window = ref[row, pl.ds(column, 384)]
        turned = pltpu.roll(window, 64 if offset else 320, 1)
        return jnp.where((odd == 1) if offset else (odd == 0), window, turned)

    for source, ref in enumerate((own_ref, other_ref)):

        def body(step, carry, source=source, ref=ref):
            part = step // 10
            row = pl.ds(pl.multiple_of(step * rows, rows), rows)
            target = pl.multiple_of(part * PLANE + source * (PLANE // 2) + (step - part * 10) * rows, rows)
            for group, planes in enumerate((NEAR, MIDDLE, FAR)):
                for at in range(0, len(planes), 2):
                    a = plane_of(ref, row, planes[at], False)
                    if at + 1 < len(planes):
                        b = plane_of(ref, row, planes[at + 1], True)
                        middle = jnp.where(lane < 64, a[:, 256:], b[:, :128])
                        whole = jnp.concatenate([a[:, :256], middle, b[:, 128:]], axis=1)
                    else:
                        whole = jnp.concatenate([a[:, :256], jnp.where(lane < 64, a[:, 256:], 0.0)], axis=1)
                    top, rest = split(whole)
                    columns = slice(at * PLANE, at * PLANE + whole.shape[1])
                    outs[2 * group][pl.ds(target, rows), columns] = top
                    outs[2 * group + 1][pl.ds(target, rows), columns] = rest
            return carry

        lax.fori_loop(0, 20, body, 0)


def screen_call(place, own, other):
    shapes = [
        jax.ShapeDtypeStruct((2 * own.shape[0], padded(planes)), jnp.bfloat16)
        for planes in (NEAR, MIDDLE, FAR)
        for _ in range(2)
    ]
    return pl.pallas_call(
        screen_kernel,
        out_shape=shapes,
        in_specs=[SMEM, VMEM, VMEM],
        out_specs=[VMEM] * 6,
        compiler_params=params(20),
        name="screen",
    )(place, own, other)


def left_kernel(place, *refs):
    pieces, (high_ref, low_ref, work) = refs[:8], refs[8:]
    x = place[1]
    span = pieces[0].shape[0] // 2
    for core in range(2):
        for shift in range(4):
            shard = lax.rem(x - shift + 4, 4)
            for part in range(2):
                row = pl.multiple_of(part * 8 * span + core * 4 * span + shard * span, 8)
                work[pl.ds(row, span), :] = pieces[core * 4 + shift][part * span : (part + 1) * span, :]
    for block in range(work.shape[1] // 128):
        turned = work[:, block * 128 : (block + 1) * 128].T
        top, rest = split(turned)
        high_ref[block * 128 : (block + 1) * 128, :] = top
        low_ref[block * 128 : (block + 1) * 128, :] = rest


def left_call(place, pieces):
    depth, width = pieces[0].shape
    shape = jax.ShapeDtypeStruct((width, 8 * depth), jnp.bfloat16)
    return pl.pallas_call(
        left_kernel,
        out_shape=(shape, shape),
        in_specs=[SMEM] + [VMEM] * 8,
        out_specs=(VMEM, VMEM),
        scratch_shapes=[pltpu.VMEM((8 * depth, width), jnp.float32)],
        compiler_params=params(20),
        name="left",
    )(place, *pieces)


def load_right(place, units, planes, high, low):
    y = place[2]
    for delta, plane, part, ref, start in units:
        row = pl.multiple_of(plane * PLANE + lax.rem(y + delta, 4) * SPAN, 16)
        top, rest = split(ref[start : start + SPAN, :])
        high[pl.ds(row, SPAN), part * HALF : (part + 1) * HALF] = top
        low[pl.ds(row, SPAN), part * HALF : (part + 1) * HALF] = rest
    used = planes * PLANE
    if used < high.shape[0]:
        for ref in (high, low):
            ref[used:, :] = jnp.zeros((ref.shape[0] - used, ref.shape[1]), ref.dtype)


def near_units(first, first_down, first_up, second, second_down, second_up, two_down, two_up):
    units = []
    for base, planes, skip, own, below, above in (
        (0, 3, 0, first, first_down, first_up),
        (3, 2, 3, second, second_down, second_up),
    ):
        for unit in range(2 * planes):
            half, at = (two_down, unit + skip) if unit < planes else (two_up, unit - planes + skip)
            for delta, ref, index in ((0, own, unit), (3, below, unit), (1, above, unit), (2, half, at)):
                units.append((delta, base + unit // 2, unit % 2, ref, index * SPAN))
    return units


def middle_units(below, above, z_below, z_above, y_below, y_above):
    units = []
    for part in range(2):
        for plane, own, sides, across in ((0, below, z_below, y_below), (1, above, z_above, y_above)):
            for delta, ref, block in ((0, own, 0), (3, sides, 0), (1, sides, 1), (2, across, 0)):
                units.append((delta, plane, part, ref, (2 * block + part) * SPAN))
    return units


def far_units(z_below, z_above, below, above, across_low, across_high):
    units = []
    for part, own, across in ((0, z_below, across_low), (1, z_above, across_high)):
        for delta, ref, start in ((0, own, 4), (3, below, part), (1, above, part), (2, across, 0)):
            units.append((delta, 0, part, ref, start * SPAN))
    return units


def group_kernel(units, planes, place, *refs):
    count = len(refs) - 5 - (units is middle_units)
    rights, (high_ref, low_ref), rest = refs[:count], refs[count : count + 2], refs[count + 2 :]
    out_ref, rh, rl = rest[-3:]
    load_right(place, units(*rights), planes, rh, rl)
    value = dot3(high_ref[...], low_ref[...], rh[...], rl[...])
    out_ref[...] = value if len(rest) == 3 else value + rest[0][...]


def group_call(units, planes, place, rights, screens, total):
    rows, width = screens[0].shape
    return pl.pallas_call(
        functools.partial(group_kernel, units, planes),
        out_shape=jax.ShapeDtypeStruct((rows, 2 * HALF), jnp.float32),
        in_specs=[SMEM] + [VMEM] * (len(rights) + 2 + len(total)),
        out_specs=VMEM,
        scratch_shapes=[pltpu.VMEM((width, 2 * HALF), jnp.bfloat16)] * 2,
        compiler_params=params(32),
        name="group",
    )(place, *rights, *screens, *total)


def pair_kernel(place, table, *refs):
    rights, (high_ref, low_ref, sum_ref, left_high, left_low, give_ref, kern, rh, rl) = refs[:6], refs[6:]
    load_right(place, far_units(*rights), len(FAR), rh, rl)
    product = sum_ref[...] + dot3(high_ref[...], low_ref[...], rh[...], rl[...])
    mid = product.shape[0] // 2
    real = product[:mid, :HALF] - product[mid:, HALF:]
    imag = product[mid:, :HALF] + product[:mid, HALF:]
    applied = NG ** (-0.5) * jnp.concatenate(
        [jnp.concatenate([real, imag], axis=0), jnp.concatenate([imag, -real], axis=0)], axis=1
    )
    kern[...] = dot3(left_high[...], left_low[...], *split(applied))

    extract(place, table, 1 - place[3], kern, give_ref)


def extract(place, table, half, kern, out_ref):
    at = lambda x: lax.rem(x + 4 - place[1], 4)
    lane = lax.broadcasted_iota(jnp.int32, (8, 128), 1) // BLK
    upper = lax.broadcasted_iota(jnp.int32, (8, 128), 0) < 4

    def groups(pair, carry):
        for g in (pair * 2, pair * 2 + 1):
            tiles = [[jnp.zeros((8, 128), jnp.float32) for _ in range(2)] for _ in range(2)]
            for u in range(8):
                slot = g * 8 + u
                row = pl.multiple_of(table[4 * half, slot], BLK)
                column = pl.multiple_of(table[4 * half + 1, slot], 128)
                shift = table[4 * half + 2, slot]
                target = table[4 * half + 3, slot]
                for part in range(2):
                    for side in range(2):
                        tile = kern[pl.ds(row + side * 8, 8), pl.ds(column + part * HALF, 128)]
                        tile = pltpu.roll(tile, shift, 1)
                        tiles[part][side] = jnp.where(lane == target, tile, tiles[part][side])
            lanes = pl.ds(pl.multiple_of(g * 128, 128), 128)
            for side in range(2):
                real, imag = tiles[0][side], tiles[1][side]
                out_ref[at(2 * side), :, lanes] = jnp.where(upper, real, pltpu.roll(imag, 4, 0))
                out_ref[at(2 * side + 1), :, lanes] = jnp.where(upper, pltpu.roll(real, 4, 0), imag)
        return carry

    out_ref[...] = jnp.zeros_like(out_ref)
    lax.fori_loop(0, (table[11, half] + 1) // 2, groups, 0)


def pair_call(place, table, rights, screens, total, left_high, left_low):
    rows = left_high.shape[0]
    return pl.pallas_call(
        pair_kernel,
        out_shape=(
            jax.ShapeDtypeStruct((4, 8, ROOM * BLK), jnp.float32),
            jax.ShapeDtypeStruct((rows, 2 * HALF), jnp.float32),
        ),
        in_specs=[SMEM, SMEM] + [VMEM] * (len(rights) + 5),
        out_specs=(VMEM, VMEM),
        scratch_shapes=[pltpu.VMEM((screens[0].shape[1], 2 * HALF), jnp.bfloat16)] * 2,
        compiler_params=params(24),
        name="pair",
    )(place, table, *rights, *screens, total, left_high, left_low)


def extract_kernel(place, table, kern, out_ref):
    extract(place, table, place[3], kern, out_ref)


def extract_call(place, table, kern):
    return pl.pallas_call(
        extract_kernel,
        out_shape=jax.ShapeDtypeStruct((4, 8, ROOM * BLK), jnp.float32),
        in_specs=[SMEM, SMEM, VMEM],
        out_specs=VMEM,
        compiler_params=params(8),
        name="extract",
    )(place, table, kern)


def add_kernel(one_ref, two_ref, *outs):
    for at, out_ref in enumerate(outs):
        out_ref[...] = one_ref[at] + two_ref[at]


def add_call(one, two):
    return pl.pallas_call(
        add_kernel,
        out_shape=[jax.ShapeDtypeStruct(one.shape[1:], one.dtype)] * one.shape[0],
        in_specs=[VMEM, VMEM],
        out_specs=[VMEM] * one.shape[0],
        compiler_params=params(8),
        name="add",
    )(one, two)


def owner_kernel(place, table, one_ref, two_ref, three_ref, four_ref, out_ref, work):
    total = (one_ref[...] + two_ref[...]) + (three_ref[...] + four_ref[...])
    width = total.shape[1]
    work[:, :width] = total
    work[:, width:] = jnp.zeros((8, work.shape[1] - width), jnp.float32)
    for chip in range(out_ref.shape[0]):
        start = table[8, chip * 2 + place[3]]
        column = pl.multiple_of(start // 8 * 128, 128)
        shift = lax.rem(384 - lax.rem(start, 8) * BLK, 384)
        out_ref[chip] = pltpu.roll(work[:, pl.ds(column, 384)], shift, 1)[:, :256]


def owner_call(place, table, parts):
    return pl.pallas_call(
        owner_kernel,
        out_shape=jax.ShapeDtypeStruct((32, 8, 256), jnp.float32),
        in_specs=[SMEM, SMEM] + [VMEM] * 4,
        out_specs=VMEM,
        scratch_shapes=[pltpu.VMEM((8, parts[0].shape[1] + 384), jnp.float32)],
        compiler_params=params(8),
        name="owner",
    )(place, table, *parts)


def last_kernel(place, table, parts_ref, out_ref):
    total = parts_ref[0]
    for chip in range(1, parts_ref.shape[0]):
        total = total + parts_ref[chip]
    held = table[9, (place[0] * 4 + place[2]) * 2 + place[3]]
    for slot in range(CAP):
        tile = total[:, slot // 8 * 128 : slot // 8 * 128 + 128]
        tile = pltpu.roll(tile, (128 - slot % 8 * BLK) % 128, 1)
        out_ref[slot] = jnp.where(slot < held, tile[:, :BLK], 0.0)


def last_call(place, table, parts):
    return pl.pallas_call(
        last_kernel,
        out_shape=jax.ShapeDtypeStruct((CAP, 8, BLK), jnp.float32),
        in_specs=[SMEM, SMEM, VMEM],
        out_specs=VMEM,
        compiler_params=params(8),
        name="last",
    )(place, table, parts)


def pack_kernel(place, own_ref, other_ref, out_ref, work):
    core = place[3]
    width = own_ref.shape[2]
    for block in range(width // 128):
        lanes = pl.ds(block * 128, 128)
        rows = []
        for part in range(2):
            own, other = own_ref[part, :, lanes], other_ref[part, :, lanes]
            rows += [jnp.where(core == 0, own, other), jnp.where(core == 0, other, own)]
        rows = jnp.concatenate(rows + rows, axis=0)
        work[block * 128 : (block + 1) * 128, :] = rows.T
    half = lax.broadcasted_iota(jnp.int32, (8, 128), 1) < 64
    for chip in range(32):
        at = pl.multiple_of(chip * 80 + core * 40, 8)
        tiles = [work[pl.ds(at + 8 * t, 8), :] for t in range(5)]
        out_ref[chip * 20 : chip * 20 + 8, :] = jnp.where(half, tiles[0], tiles[1])
        out_ref[chip * 20 + 8 : chip * 20 + 16, :] = jnp.where(half, tiles[2], tiles[3])
        last = jnp.where(half, tiles[4], pltpu.roll(tiles[4], 4, 0))
        out_ref[chip * 20 + 16 : chip * 20 + 20, :] = last[:4]


def pack_call(place, own, other):
    width = own.shape[2]
    return pl.pallas_call(
        pack_kernel,
        out_shape=jax.ShapeDtypeStruct((32 * 20, 128), jnp.float32),
        in_specs=[SMEM, VMEM, VMEM],
        out_specs=VMEM,
        scratch_shapes=[pltpu.VMEM((width, 128), jnp.float32)],
        name="pack",
    )(place, own, other)


def unpack_kernel(place, table, in_ref, columns_ref, keep_ref, give_ref):
    core = place[3]
    quarter = lax.broadcasted_iota(jnp.int32, (8, 128), 1) // 32
    upper = lax.broadcasted_iota(jnp.int32, (8, 128), 0) < 4
    for group in range(8):
        tiles = [[None] * 5 for _ in range(2)]
        for u in range(4):
            at = (group * 4 + u) * 20
            one, two = in_ref[at : at + 8, :], in_ref[at + 8 : at + 16, :]
            end = in_ref[at + 12 : at + 20, :]
            end = jnp.where(upper, pltpu.roll(end, 4, 0), pltpu.roll(end, 64, 1))
            for t, (source, first) in enumerate(((one, 0), (one, 64), (two, 0), (two, 64), (end, 0))):
                for part in range(2):
                    by = (u * 32 - first - part * 32) % 128
                    turned = pltpu.roll(source, by, 1) if by else source
                    old = tiles[part][t]
                    tiles[part][t] = turned if old is None else jnp.where(quarter == u, turned, old)
        for part in range(2):
            for t in range(5):
                row = part * 40 + t * 8
                columns_ref[row : row + 8, group * 128 : (group + 1) * 128] = tiles[part][t]
    select(table, 1 - core, columns_ref, give_ref)
    select(table, core, columns_ref, keep_ref)


def select(table, which, columns_ref, out_ref):
    eighth = lax.broadcasted_iota(jnp.int32, (80, 128), 1) // BLK
    for group in range(2):
        slab = None
        for u in range(8):
            block = table[10, which * (USED // 2) + group * 8 + u]
            column = pl.multiple_of(block // 8 * 128, 128)
            by = lax.rem(u * BLK + 128 - lax.rem(block, 8) * BLK, 128)
            turned = pltpu.roll(columns_ref[:, pl.ds(column, 128)], by, 1)
            slab = turned if slab is None else jnp.where(eighth == u, turned, slab)
        out_ref[:, group * 128 : (group + 1) * 128] = slab


def unpack_call(place, table, pieces):
    return pl.pallas_call(
        unpack_kernel,
        out_shape=(
            jax.ShapeDtypeStruct((80, 1024), jnp.float32),
            jax.ShapeDtypeStruct((80, HALF), jnp.float32),
            jax.ShapeDtypeStruct((80, HALF), jnp.float32),
        ),
        in_specs=[SMEM, SMEM, VMEM],
        out_specs=(VMEM, VMEM, VMEM),
        compiler_params=params(8),
        name="unpack",
    )(place, table, pieces)


def shard_kernel(place, keep_ref, take_ref, out_ref):
    core = place[3]
    for part in range(2):
        out_ref[pl.ds(pl.multiple_of(part * 80 + core * 40, 8), 40), :] = keep_ref[part * 40 : part * 40 + 40, :]
        out_ref[pl.ds(pl.multiple_of(part * 80 + 40 - core * 40, 8), 40), :] = take_ref[part * 40 : part * 40 + 40, :]


def shard_call(place, keep, take):
    return pl.pallas_call(
        shard_kernel,
        out_shape=jax.ShapeDtypeStruct((160, HALF), jnp.float32),
        in_specs=[SMEM, VMEM, VMEM],
        out_specs=VMEM,
        compiler_params=params(8),
        name="shard",
    )(place, keep, take)


def after(array, *others):
    return lax.optimization_barrier((array, *others))[0]


def shards(densities, screened, pairs, owners):
    span = screened.shape[2]
    place = jnp.stack([lax.axis_index(axis) for axis in ("z", "x", "y", "core")]).astype(jnp.int32)
    shift = lambda array, axis, by: lax.ppermute(array, axis, ring(lax.axis_size(axis), by))
    swap = lambda array: lax.ppermute(array, "core", SWAP)
    join = lambda *arrays: jnp.concatenate(arrays, axis=0)
    hold = lax.optimization_barrier

    pieces = pack_call(place, densities, swap(densities))
    table = plan_call(place, after(pairs, pieces), owners.reshape(1, -1))
    mine = lax.all_to_all(pieces.reshape(32, 1, -1), ("z", "y"), 0, 0, tiled=True).reshape(pieces.shape)

    screen = screened.reshape(2 * 4 * span, -1)
    mine, other = hold((mine, swap(after(screen, pieces))))

    columns, keep, give = unpack_call(place, table, mine)
    shard = shard_call(place, keep, swap(give))

    block = 2 * SPAN
    below2, above2 = shift(shard, "z", 2), shift(shard, "z", -2)
    below, above, columns = hold((shift(shard, "z", 1), shift(shard, "z", -1), columns))
    first = join(shard, below, above)
    first_down, first_up = shift(first, "y", 1), shift(first, "y", -1)
    around = [columns, shift(columns, "x", 1), None, None]
    below2, above2, first, columns = hold((below2, above2, first, columns))
    second = join(below2, above2)
    second_down, second_up = shift(second, "y", 1), shift(second, "y", -1)
    around[3] = shift(columns, "x", 3)
    screens = screen_call(place, after(screen, second), other)
    first_down, first_up, around[1], below2, above2, *screens = hold(
        (first_down, first_up, around[1], below2, above2, *screens)
    )
    below3, above3 = shift(below2, "z", 1), shift(above2, "z", -1)
    below3, above3, second_down, second_up, around[3] = hold((below3, above3, second_down, second_up, around[3]))

    z_below = shift(join(second_down[:block], second_up[:block], below3[:SPAN]), "z", 1)
    z_above = shift(join(second_down[block:], second_up[block:], above3[SPAN:]), "z", -1)
    two_down = shift(join(first_down[: 3 * SPAN], second_down[:block]), "y", 1)
    two_up = shift(join(first_up[3 * SPAN :], second_up[block:]), "y", -1)
    around[2] = shift(after(columns, below3), "x", 2)
    swapped = [swap(around[0]), swap(around[1]), None, swap(around[3])]
    two_down, two_up, z_below, z_above, around[2], swapped[0], swapped[1], swapped[3] = hold(
        (two_down, two_up, z_below, z_above, around[2], swapped[0], swapped[1], swapped[3])
    )

    y_below, y_above = shift(z_below[:block], "y", 1), shift(z_above[block : 2 * block], "y", -1)
    far_below, far_above = shift(z_below[:block], "z", 1), shift(z_above[block : 2 * block], "z", -1)
    rights = (first, first_down, first_up, second, second_down, second_up, two_down, two_up)
    total = group_call(near_units, len(NEAR), place, rights, screens[:2], ())
    swapped[2] = swap(around[2])
    y_below, y_above, far_below, far_above, total, swapped[2] = hold(
        (y_below, y_above, far_below, far_above, total, swapped[2])
    )

    across_low, across_high = shift(far_below[:SPAN], "y", 1), shift(far_above[SPAN:], "y", -1)
    rights = (below3, above3, z_below, z_above, y_below, y_above)
    total = group_call(middle_units, len(MIDDLE), place, rights, screens[2:4], (total,))
    left_high, left_low = left_call(place, around + swapped)
    across_low, across_high, total, left_high, left_low = hold((across_low, across_high, total, left_high, left_low))
    rights = (z_below, z_above, far_below, far_above, across_low, across_high)
    give, kern = pair_call(place, table, rights, screens[4:], total, left_high, left_low)

    parts = add_call(extract_call(place, table, kern), swap(give))
    parts = [parts[0]] + [shift(parts[by], "x", by) for by in (1, 2, 3)]
    parts = owner_call(place, table, parts)
    parts = lax.all_to_all(parts, ("z", "y"), 0, 0, tiled=True)
    return last_call(place, table, parts).reshape(1, CAP, 2, 4, BLK)


def solution(mesh):
    fine = Mesh(mesh.devices.reshape(8, 4, 2, 4), ("z", "y", "core", "x"))
    in_specs = (P(None, BAND, "x"), P(None, None, BAND, "x"), P(), P())
    out_specs = P(BAND, None, None, "x", None)
    return jax.shard_map(shards, mesh=fine, in_specs=in_specs, out_specs=out_specs, check_vma=False)
```

```python
import functools

import jax
import jax.numpy as jnp
from jax import lax
from jax.experimental import pallas as pl
from jax.experimental.pallas import tpu as pltpu
from jax.sharding import Mesh
from jax.sharding import PartitionSpec as P

NG = 10240
CAP = 12
BLK = 16
USED = 32
HALF = USED // 2 * BLK
BAND = ("z", "y", "core")
SWAP = ((0, 1), (1, 0))
SMEM = pl.BlockSpec(memory_space=pltpu.SMEM)
VMEM = pl.BlockSpec(memory_space=pltpu.VMEM)
SPAN = 80
PLANE = 320
NEAR = (0, 7, 1, 6, 2)
MIDDLE = (5, 3)
FAR = (4,)
ROOM = 224


def ring(n, shift):
    return [(i, (i + shift) % n) for i in range(n)]


def params(mib):
    return pltpu.CompilerParams(vmem_limit_bytes=mib * 1024 * 1024)


def split(x):
    high = x.astype(jnp.bfloat16)
    return high, (x - high.astype(jnp.float32)).astype(jnp.bfloat16)


def dot(former, latter):
    return jnp.dot(former, latter, preferred_element_type=jnp.float32)


def dot3(high, low, former, latter):
    return dot(high, former) + dot(high, latter) + dot(low, former)


def plan_kernel(place, pairs_ref, owners_ref, out_ref):
    size = 256
    down = lax.broadcasted_iota(jnp.int32, (size, size), 0)
    across = lax.broadcasted_iota(jnp.int32, (size, size), 1)
    one = lambda condition: jnp.where(condition, 1.0, 0.0)
    to_row = lambda column: jnp.sum(jnp.where(down == across, column, 0.0), axis=0, keepdims=True)
    to_column = lambda row: jnp.sum(jnp.where(down == across, row, 0.0), axis=1, keepdims=True)
    rows, columns = down.astype(jnp.float32), across.astype(jnp.float32)
    left, right = pairs_ref[:, 0:1].astype(jnp.float32), pairs_ref[:, 1:2].astype(jnp.float32)
    owner_row = owners_ref[...].astype(jnp.float32)
    owner = to_column(owner_row)

    used = jnp.max(one(right == columns), axis=0, keepdims=True)
    used_column = to_column(used)
    rank = jnp.sum(jnp.where(columns < rows, used, 0.0), axis=1, keepdims=True)
    used_list = jnp.sum(jnp.where((rank == columns) & (used_column > 0), rows, 0.0), axis=0, keepdims=True)
    right_rank = jnp.sum(jnp.where(columns < right, used, 0.0), axis=1, keepdims=True)

    parity = lambda value: value - 2.0 * jnp.floor(value * 0.5)
    count = jnp.sum(one(owner == columns), axis=0, keepdims=True)
    same = parity(rows) == parity(columns)
    offset = jnp.sum(jnp.where((rows < columns) & same, to_column(count), 0.0), axis=0, keepdims=True)
    ahead = (owner_row < owner) | ((owner_row == owner) & (across < down))
    ahead = ahead & (parity(owner_row) == parity(owner))
    position = jnp.sum(one(ahead), axis=1, keepdims=True)

    core = place[3].astype(jnp.float32)
    local = right_rank - core * (USED // 2)
    here = (local >= 0) & (local < USED // 2)
    local = jnp.where(here, local, 0.0)
    lane = lax.broadcasted_iota(jnp.int32, (1, size), 1)
    groups = jnp.zeros((1, size), jnp.float32)
    for half in range(2):
        hit = (position == columns) & (parity(owner) == half)
        pick = lambda column: jnp.sum(jnp.where(hit, column, 0.0), axis=0, keepdims=True).astype(jnp.int32)
        at = pick(local)
        out_ref[4 * half : 4 * half + 1, :] = pick(left) * BLK
        out_ref[4 * half + 1 : 4 * half + 2, :] = at // 8 * 128
        out_ref[4 * half + 2 : 4 * half + 3, :] = (lane + 8 - at % 8) % 8 * BLK
        out_ref[4 * half + 3 : 4 * half + 4, :] = jnp.where(pick(one(here)) > 0, lane % 8, -1)
        total = jnp.sum(one(parity(owner_row) == half))
        groups = jnp.where(lane == half, jnp.floor((total + 7.0) / 8.0), groups)
    for at, row in enumerate((offset, count, used_list, groups)):
        out_ref[8 + at : 9 + at, :] = row.astype(jnp.int32)


def plan_call(place, pairs, owners):
    return pl.pallas_call(
        plan_kernel,
        out_shape=jax.ShapeDtypeStruct((16, pairs.shape[0]), jnp.int32),
        in_specs=[SMEM, VMEM, VMEM],
        out_specs=VMEM,
        compiler_params=params(8),
        name="plan",
    )(place, pairs, owners)


def padded(planes):
    return (len(planes) * PLANE + 127) // 128 * 128


def screen_kernel(place, own_ref, other_ref, *outs):
    z = place[0]
    rows = 16
    lane = lax.broadcasted_iota(jnp.int32, (rows, 128), 1)

    def plane_of(ref, row, delta, offset):
        plane = lax.rem(z + delta, 8)
        odd = lax.rem(plane, 2)
        column = pl.multiple_of(plane * PLANE - odd * 64, 128)
        window = ref[row, pl.ds(column, 384)]
        turned = pltpu.roll(window, 64 if offset else 320, 1)
        return jnp.where((odd == 1) if offset else (odd == 0), window, turned)

    for source, ref in enumerate((own_ref, other_ref)):

        def body(step, carry, source=source, ref=ref):
            part = step // 10
            row = pl.ds(pl.multiple_of(step * rows, rows), rows)
            target = pl.multiple_of(part * PLANE + source * (PLANE // 2) + (step - part * 10) * rows, rows)
            for group, planes in enumerate((NEAR, MIDDLE, FAR)):
                for at in range(0, len(planes), 2):
                    a = plane_of(ref, row, planes[at], False)
                    if at + 1 < len(planes):
                        b = plane_of(ref, row, planes[at + 1], True)
                        middle = jnp.where(lane < 64, a[:, 256:], b[:, :128])
                        whole = jnp.concatenate([a[:, :256], middle, b[:, 128:]], axis=1)
                    else:
                        whole = jnp.concatenate([a[:, :256], jnp.where(lane < 64, a[:, 256:], 0.0)], axis=1)
                    top, rest = split(whole)
                    columns = slice(at * PLANE, at * PLANE + whole.shape[1])
                    outs[2 * group][pl.ds(target, rows), columns] = top
                    outs[2 * group + 1][pl.ds(target, rows), columns] = rest
            return carry

        lax.fori_loop(0, 20, body, 0)


def screen_call(place, own, other):
    shapes = [
        jax.ShapeDtypeStruct((2 * own.shape[0], padded(planes)), jnp.bfloat16)
        for planes in (NEAR, MIDDLE, FAR)
        for _ in range(2)
    ]
    return pl.pallas_call(
        screen_kernel,
        out_shape=shapes,
        in_specs=[SMEM, VMEM, VMEM],
        out_specs=[VMEM] * 6,
        compiler_params=params(20),
        name="screen",
    )(place, own, other)


def left_kernel(place, *refs):
    pieces, (high_ref, low_ref, work) = refs[:8], refs[8:]
    x = place[1]
    span = pieces[0].shape[0] // 2
    for core in range(2):
        for shift in range(4):
            shard = lax.rem(x - shift + 4, 4)
            for part in range(2):
                row = pl.multiple_of(part * 8 * span + core * 4 * span + shard * span, 8)
                work[pl.ds(row, span), :] = pieces[core * 4 + shift][part * span : (part + 1) * span, :]

    def body(block, carry):
        at = pl.ds(pl.multiple_of(block * 128, 128), 128)
        high_ref[at, :], low_ref[at, :] = split(work[:, at].T)
        return carry

    lax.fori_loop(0, work.shape[1] // 128, body, 0)


def left_call(place, pieces):
    depth, width = pieces[0].shape
    shape = jax.ShapeDtypeStruct((width, 8 * depth), jnp.bfloat16)
    return pl.pallas_call(
        left_kernel,
        out_shape=(shape, shape),
        in_specs=[SMEM] + [VMEM] * 8,
        out_specs=(VMEM, VMEM),
        scratch_shapes=[pltpu.VMEM((8 * depth, width), jnp.float32)],
        compiler_params=params(20),
        name="left",
    )(place, *pieces)


def load_right(place, runs, planes, high, low):
    y = place[2]
    for delta, ref, start, first, count in runs:
        spread = lax.rem(y + delta, 4) * SPAN

        def body(step, carry, ref=ref, start=start, first=first, spread=spread):
            unit = first + step
            row = pl.ds(pl.multiple_of(unit // 2 * PLANE + spread, 16), SPAN)
            column = pl.ds(pl.multiple_of(lax.rem(unit, 2) * HALF, HALF), HALF)
            top, rest = split(ref[pl.ds(pl.multiple_of(start + step * SPAN, 8), SPAN), :])
            high[row, column] = top
            low[row, column] = rest
            return carry

        lax.fori_loop(0, count, body, 0)
    used = planes * PLANE
    if used < high.shape[0]:
        for ref in (high, low):
            ref[used:, :] = jnp.zeros((ref.shape[0] - used, ref.shape[1]), ref.dtype)


def near_runs(first, first_down, first_up, second, second_down, second_up, two_down, two_up):
    skip = 3 * SPAN
    return (
        ((0, first, 0, 0, 6), (3, first_down, 0, 0, 6), (1, first_up, 0, 0, 6))
        + ((0, second, 0, 6, 4), (3, second_down, 0, 6, 4), (1, second_up, 0, 6, 4))
        + ((2, two_down, 0, 0, 3), (2, two_up, 0, 3, 3), (2, two_down, skip, 6, 2), (2, two_up, skip, 8, 2))
    )


def middle_runs(z_below, z_above, y_below, y_above):
    runs = ()
    for first, sides, across in ((0, z_below, y_below), (2, z_above, y_above)):
        runs += ((3, sides, 0, first, 2), (1, sides, 2 * SPAN, first, 2), (0, sides, 4 * SPAN, first, 2))
        runs += ((2, across, 0, first, 2),)
    return runs


def far_runs(below, above, across_low, across_high):
    return (
        ((3, below, 0, 0, 2), (1, above, 0, 0, 2), (0, below, 2 * SPAN, 0, 1), (0, above, 2 * SPAN, 1, 1))
        + ((2, across_low, 0, 0, 1), (2, across_high, 0, 1, 1))
    )


def group_kernel(runs, planes, place, *refs):
    count = len(refs) - 5 - (runs is middle_runs)
    rights, (high_ref, low_ref), rest = refs[:count], refs[count : count + 2], refs[count + 2 :]
    out_ref, rh, rl = rest[-3:]
    load_right(place, runs(*rights), planes, rh, rl)
    value = dot3(high_ref[...], low_ref[...], rh[...], rl[...])
    out_ref[...] = value if len(rest) == 3 else value + rest[0][...]


def group_call(runs, planes, place, rights, screens, total):
    rows, width = screens[0].shape
    return pl.pallas_call(
        functools.partial(group_kernel, runs, planes),
        out_shape=jax.ShapeDtypeStruct((rows, 2 * HALF), jnp.float32),
        in_specs=[SMEM] + [VMEM] * (len(rights) + 2 + len(total)),
        out_specs=VMEM,
        scratch_shapes=[pltpu.VMEM((width, 2 * HALF), jnp.bfloat16)] * 2,
        compiler_params=params(32),
        name="group",
    )(place, *rights, *screens, *total)


def pair_kernel(place, table, *refs):
    rights, (high_ref, low_ref, sum_ref, left_high, left_low, give_ref, kern, rh, rl) = refs[:4], refs[4:]
    load_right(place, far_runs(*rights), len(FAR), rh, rl)
    product = sum_ref[...] + dot3(high_ref[...], low_ref[...], rh[...], rl[...])
    mid = product.shape[0] // 2
    real = product[:mid, :HALF] - product[mid:, HALF:]
    imag = product[mid:, :HALF] + product[:mid, HALF:]
    applied = NG ** (-0.5) * jnp.concatenate(
        [jnp.concatenate([real, imag], axis=0), jnp.concatenate([imag, -real], axis=0)], axis=1
    )
    kern[...] = dot3(left_high[...], left_low[...], *split(applied))

    extract(place, table, 1 - place[3], kern, give_ref)


def extract(place, table, half, kern, out_ref):
    at = lambda x: lax.rem(x + 4 - place[1], 4)
    lane = lax.broadcasted_iota(jnp.int32, (8, 128), 1) // BLK
    upper = lax.broadcasted_iota(jnp.int32, (8, 128), 0) < 4

    def groups(pair, carry):
        for g in (pair * 2, pair * 2 + 1):
            tiles = [[jnp.zeros((8, 128), jnp.float32) for _ in range(2)] for _ in range(2)]
            for u in range(8):
                slot = g * 8 + u
                row = pl.multiple_of(table[4 * half, slot], BLK)
                column = pl.multiple_of(table[4 * half + 1, slot], 128)
                shift = table[4 * half + 2, slot]
                target = table[4 * half + 3, slot]
                for part in range(2):
                    for side in range(2):
                        tile = kern[pl.ds(row + side * 8, 8), pl.ds(column + part * HALF, 128)]
                        tile = pltpu.roll(tile, shift, 1)
                        tiles[part][side] = jnp.where(lane == target, tile, tiles[part][side])
            lanes = pl.ds(pl.multiple_of(g * 128, 128), 128)
            for side in range(2):
                real, imag = tiles[0][side], tiles[1][side]
                out_ref[at(2 * side), :, lanes] = jnp.where(upper, real, pltpu.roll(imag, 4, 0))
                out_ref[at(2 * side + 1), :, lanes] = jnp.where(upper, pltpu.roll(real, 4, 0), imag)
        return carry

    out_ref[...] = jnp.zeros_like(out_ref)
    lax.fori_loop(0, (table[11, half] + 1) // 2, groups, 0)


def pair_call(place, table, rights, screens, total, left_high, left_low):
    rows = left_high.shape[0]
    return pl.pallas_call(
        pair_kernel,
        out_shape=(
            jax.ShapeDtypeStruct((4, 8, ROOM * BLK), jnp.float32),
            jax.ShapeDtypeStruct((rows, 2 * HALF), jnp.float32),
        ),
        in_specs=[SMEM, SMEM] + [VMEM] * (len(rights) + 5),
        out_specs=(VMEM, VMEM),
        scratch_shapes=[pltpu.VMEM((screens[0].shape[1], 2 * HALF), jnp.bfloat16)] * 2,
        compiler_params=params(24),
        name="pair",
    )(place, table, *rights, *screens, total, left_high, left_low)


def extract_kernel(place, table, kern, out_ref):
    extract(place, table, place[3], kern, out_ref)


def extract_call(place, table, kern):
    return pl.pallas_call(
        extract_kernel,
        out_shape=jax.ShapeDtypeStruct((4, 8, ROOM * BLK), jnp.float32),
        in_specs=[SMEM, SMEM, VMEM],
        out_specs=VMEM,
        compiler_params=params(8),
        name="extract",
    )(place, table, kern)


def add_kernel(one_ref, two_ref, *outs):
    for at, out_ref in enumerate(outs):
        out_ref[...] = one_ref[at] + two_ref[at]


def add_call(one, two):
    return pl.pallas_call(
        add_kernel,
        out_shape=[jax.ShapeDtypeStruct(one.shape[1:], one.dtype)] * one.shape[0],
        in_specs=[VMEM, VMEM],
        out_specs=[VMEM] * one.shape[0],
        compiler_params=params(8),
        name="add",
    )(one, two)


def owner_kernel(place, table, one_ref, two_ref, three_ref, four_ref, out_ref, work):
    total = (one_ref[...] + two_ref[...]) + (three_ref[...] + four_ref[...])
    width = total.shape[1]
    work[:, :width] = total
    work[:, width:] = jnp.zeros((8, work.shape[1] - width), jnp.float32)
    for chip in range(out_ref.shape[0]):
        start = table[8, chip * 2 + place[3]]
        column = pl.multiple_of(start // 8 * 128, 128)
        shift = lax.rem(384 - lax.rem(start, 8) * BLK, 384)
        out_ref[chip] = pltpu.roll(work[:, pl.ds(column, 384)], shift, 1)[:, :256]


def owner_call(place, table, parts):
    return pl.pallas_call(
        owner_kernel,
        out_shape=jax.ShapeDtypeStruct((32, 8, 256), jnp.float32),
        in_specs=[SMEM, SMEM] + [VMEM] * 4,
        out_specs=VMEM,
        scratch_shapes=[pltpu.VMEM((8, parts[0].shape[1] + 384), jnp.float32)],
        compiler_params=params(8),
        name="owner",
    )(place, table, *parts)


def last_kernel(place, table, parts_ref, out_ref):
    total = parts_ref[0]
    for chip in range(1, parts_ref.shape[0]):
        total = total + parts_ref[chip]
    held = table[9, (place[0] * 4 + place[2]) * 2 + place[3]]
    for slot in range(CAP):
        tile = total[:, slot // 8 * 128 : slot // 8 * 128 + 128]
        tile = pltpu.roll(tile, (128 - slot % 8 * BLK) % 128, 1)
        out_ref[slot] = jnp.where(slot < held, tile[:, :BLK], 0.0)


def last_call(place, table, parts):
    return pl.pallas_call(
        last_kernel,
        out_shape=jax.ShapeDtypeStruct((CAP, 8, BLK), jnp.float32),
        in_specs=[SMEM, SMEM, VMEM],
        out_specs=VMEM,
        compiler_params=params(8),
        name="last",
    )(place, table, parts)


def pack_kernel(place, own_ref, other_ref, out_ref, work):
    core = place[3]
    width = own_ref.shape[2]
    for block in range(width // 128):
        lanes = pl.ds(block * 128, 128)
        rows = []
        for part in range(2):
            own, other = own_ref[part, :, lanes], other_ref[part, :, lanes]
            rows += [jnp.where(core == 0, own, other), jnp.where(core == 0, other, own)]
        rows = jnp.concatenate(rows + rows, axis=0)
        work[block * 128 : (block + 1) * 128, :] = rows.T
    half = lax.broadcasted_iota(jnp.int32, (8, 128), 1) < 64
    for chip in range(32):
        at = pl.multiple_of(chip * 80 + core * 40, 8)
        tiles = [work[pl.ds(at + 8 * t, 8), :] for t in range(5)]
        out_ref[chip * 20 : chip * 20 + 8, :] = jnp.where(half, tiles[0], tiles[1])
        out_ref[chip * 20 + 8 : chip * 20 + 16, :] = jnp.where(half, tiles[2], tiles[3])
        last = jnp.where(half, tiles[4], pltpu.roll(tiles[4], 4, 0))
        out_ref[chip * 20 + 16 : chip * 20 + 20, :] = last[:4]


def pack_call(place, own, other):
    width = own.shape[2]
    return pl.pallas_call(
        pack_kernel,
        out_shape=jax.ShapeDtypeStruct((32 * 20, 128), jnp.float32),
        in_specs=[SMEM, VMEM, VMEM],
        out_specs=VMEM,
        scratch_shapes=[pltpu.VMEM((width, 128), jnp.float32)],
        name="pack",
    )(place, own, other)


def unpack_kernel(place, table, in_ref, columns_ref, keep_ref, give_ref):
    core = place[3]
    quarter = lax.broadcasted_iota(jnp.int32, (8, 128), 1) // 32
    upper = lax.broadcasted_iota(jnp.int32, (8, 128), 0) < 4
    for group in range(8):
        tiles = [[None] * 5 for _ in range(2)]
        for u in range(4):
            at = (group * 4 + u) * 20
            one, two = in_ref[at : at + 8, :], in_ref[at + 8 : at + 16, :]
            end = in_ref[at + 12 : at + 20, :]
            end = jnp.where(upper, pltpu.roll(end, 4, 0), pltpu.roll(end, 64, 1))
            for t, (source, first) in enumerate(((one, 0), (one, 64), (two, 0), (two, 64), (end, 0))):
                for part in range(2):
                    by = (u * 32 - first - part * 32) % 128
                    turned = pltpu.roll(source, by, 1) if by else source
                    old = tiles[part][t]
                    tiles[part][t] = turned if old is None else jnp.where(quarter == u, turned, old)
        for part in range(2):
            for t in range(5):
                row = part * 40 + t * 8
                columns_ref[row : row + 8, group * 128 : (group + 1) * 128] = tiles[part][t]
    select(table, 1 - core, columns_ref, give_ref)
    select(table, core, columns_ref, keep_ref)


def select(table, which, columns_ref, out_ref):
    eighth = lax.broadcasted_iota(jnp.int32, (80, 128), 1) // BLK
    for group in range(2):
        slab = None
        for u in range(8):
            block = table[10, which * (USED // 2) + group * 8 + u]
            column = pl.multiple_of(block // 8 * 128, 128)
            by = lax.rem(u * BLK + 128 - lax.rem(block, 8) * BLK, 128)
            turned = pltpu.roll(columns_ref[:, pl.ds(column, 128)], by, 1)
            slab = turned if slab is None else jnp.where(eighth == u, turned, slab)
        out_ref[:, group * 128 : (group + 1) * 128] = slab


def unpack_call(place, table, pieces):
    return pl.pallas_call(
        unpack_kernel,
        out_shape=(
            jax.ShapeDtypeStruct((80, 1024), jnp.float32),
            jax.ShapeDtypeStruct((80, HALF), jnp.float32),
            jax.ShapeDtypeStruct((80, HALF), jnp.float32),
        ),
        in_specs=[SMEM, SMEM, VMEM],
        out_specs=(VMEM, VMEM, VMEM),
        compiler_params=params(8),
        name="unpack",
    )(place, table, pieces)


def shard_kernel(place, keep_ref, take_ref, out_ref):
    core = place[3]
    for part in range(2):
        out_ref[pl.ds(pl.multiple_of(part * 80 + core * 40, 8), 40), :] = keep_ref[part * 40 : part * 40 + 40, :]
        out_ref[pl.ds(pl.multiple_of(part * 80 + 40 - core * 40, 8), 40), :] = take_ref[part * 40 : part * 40 + 40, :]


def shard_call(place, keep, take):
    return pl.pallas_call(
        shard_kernel,
        out_shape=jax.ShapeDtypeStruct((160, HALF), jnp.float32),
        in_specs=[SMEM, VMEM, VMEM],
        out_specs=VMEM,
        compiler_params=params(8),
        name="shard",
    )(place, keep, take)


def after(array, *others):
    return lax.optimization_barrier((array, *others))[0]


def shards(densities, screened, pairs, owners):
    span = screened.shape[2]
    place = jnp.stack([lax.axis_index(axis) for axis in ("z", "x", "y", "core")]).astype(jnp.int32)
    shift = lambda array, axis, by: lax.ppermute(array, axis, ring(lax.axis_size(axis), by))
    swap = lambda array: lax.ppermute(array, "core", SWAP)
    join = lambda *arrays: jnp.concatenate(arrays, axis=0)
    hold = lax.optimization_barrier

    pieces = pack_call(place, densities, swap(densities))
    table = plan_call(place, after(pairs, pieces), owners.reshape(1, -1))
    mine = lax.all_to_all(pieces.reshape(32, 1, -1), ("z", "y"), 0, 0, tiled=True).reshape(pieces.shape)

    screen = screened.reshape(2 * 4 * span, -1)
    mine, other = hold((mine, swap(after(screen, pieces))))

    columns, keep, give = unpack_call(place, table, mine)
    shard = shard_call(place, keep, swap(give))

    block = 2 * SPAN
    below2, above2 = shift(shard, "z", 2), shift(shard, "z", -2)
    below, above, columns = hold((shift(shard, "z", 1), shift(shard, "z", -1), columns))
    first = join(shard, below, above)
    first_down, first_up = shift(first, "y", 1), shift(first, "y", -1)
    around = [columns, shift(columns, "x", 1), None, None]
    below2, above2, first, columns = hold((below2, above2, first, columns))
    second = join(below2, above2)
    second_down, second_up = shift(second, "y", 1), shift(second, "y", -1)
    around[3] = shift(columns, "x", 3)
    screens = screen_call(place, after(screen, second), other)
    first_down, first_up, around[1], below2, above2, *screens = hold(
        (first_down, first_up, around[1], below2, above2, *screens)
    )
    around[2] = shift(after(columns, first_down), "x", 2)
    swapped = [swap(columns), swap(around[1]), None, None]
    second_down, second_up, first_down, swapped[0], swapped[1] = hold(
        (second_down, second_up, first_down, swapped[0], swapped[1])
    )

    z_below = shift(join(second_down[:block], second_up[:block], second[:block]), "z", 1)
    z_above = shift(join(second_down[block:], second_up[block:], second[block:]), "z", -1)
    two_down = shift(join(first_down[: 3 * SPAN], second_down[:block]), "y", 1)
    two_up = shift(join(first_up[3 * SPAN :], second_up[block:]), "y", -1)
    swapped[3] = swap(around[3])
    two_down, two_up, z_below, z_above, around[2], swapped[3] = hold(
        (two_down, two_up, z_below, z_above, around[2], swapped[3])
    )

    y_below, y_above = shift(z_below[:block], "y", 1), shift(z_above[block : 2 * block], "y", -1)
    far_below = shift(join(z_below[:block], z_below[2 * block : 2 * block + SPAN]), "z", 1)
    far_above = shift(join(z_above[block : 2 * block], z_above[2 * block + SPAN :]), "z", -1)
    rights = (first, first_down, first_up, second, second_down, second_up, two_down, two_up)
    total = group_call(near_runs, len(NEAR), place, rights, screens[:2], ())
    swapped[2] = swap(around[2])
    y_below, y_above, far_below, far_above, total, swapped[2] = hold(
        (y_below, y_above, far_below, far_above, total, swapped[2])
    )

    across_low, across_high = shift(far_below[:SPAN], "y", 1), shift(far_above[SPAN : 2 * SPAN], "y", -1)
    rights = (z_below, z_above, y_below, y_above)
    total = group_call(middle_runs, len(MIDDLE), place, rights, screens[2:4], (total,))
    left_high, left_low = left_call(place, around + swapped)
    across_low, across_high, total, left_high, left_low = hold((across_low, across_high, total, left_high, left_low))
    rights = (far_below, far_above, across_low, across_high)
    give, kern = pair_call(place, table, rights, screens[4:], total, left_high, left_low)

    parts = add_call(extract_call(place, table, kern), swap(give))
    parts = [parts[0]] + [shift(parts[by], "x", by) for by in (1, 2, 3)]
    parts = owner_call(place, table, parts)
    parts = lax.all_to_all(parts, ("z", "y"), 0, 0, tiled=True)
    return last_call(place, table, parts).reshape(1, CAP, 2, 4, BLK)


def solution(mesh):
    fine = Mesh(mesh.devices.reshape(8, 4, 2, 4), ("z", "y", "core", "x"))
    in_specs = (P(None, BAND, "x"), P(None, None, BAND, "x"), P(), P())
    out_specs = P(BAND, None, None, "x", None)
    return jax.shard_map(shards, mesh=fine, in_specs=in_specs, out_specs=out_specs, check_vma=False)
```

```python
import functools

import jax
import jax.numpy as jnp
from jax import lax
from jax.experimental import pallas as pl
from jax.experimental.pallas import tpu as pltpu
from jax.sharding import Mesh
from jax.sharding import PartitionSpec as P

NG = 10240
CAP = 12
BLK = 16
USED = 32
HALF = USED // 2 * BLK
BAND = ("z", "y", "core")
SWAP = ((0, 1), (1, 0))
SMEM = pl.BlockSpec(memory_space=pltpu.SMEM)
VMEM = pl.BlockSpec(memory_space=pltpu.VMEM)
SPAN = 80
PLANE = 320
NEAR = (0, 7, 1, 6, 2)
MIDDLE = (5, 3)
FAR = (4,)
ROOM = 224


def ring(n, shift):
    return [(i, (i + shift) % n) for i in range(n)]


def params(mib):
    return pltpu.CompilerParams(vmem_limit_bytes=mib * 1024 * 1024)


def split(x):
    high = x.astype(jnp.bfloat16)
    return high, (x - high.astype(jnp.float32)).astype(jnp.bfloat16)


def dot(former, latter):
    return jnp.dot(former, latter, preferred_element_type=jnp.float32)


def dot3(high, low, former, latter):
    return dot(high, former) + dot(high, latter) + dot(low, former)


def plan_kernel(place, pairs_ref, owners_ref, out_ref):
    size = 256
    down = lax.broadcasted_iota(jnp.int32, (size, size), 0)
    across = lax.broadcasted_iota(jnp.int32, (size, size), 1)
    one = lambda condition: jnp.where(condition, 1.0, 0.0)
    to_row = lambda column: jnp.sum(jnp.where(down == across, column, 0.0), axis=0, keepdims=True)
    to_column = lambda row: jnp.sum(jnp.where(down == across, row, 0.0), axis=1, keepdims=True)
    rows, columns = down.astype(jnp.float32), across.astype(jnp.float32)
    left, right = pairs_ref[:, 0:1].astype(jnp.float32), pairs_ref[:, 1:2].astype(jnp.float32)
    owner_row = owners_ref[...].astype(jnp.float32)
    owner = to_column(owner_row)

    used = jnp.max(one(right == columns), axis=0, keepdims=True)
    used_column = to_column(used)
    rank = jnp.sum(jnp.where(columns < rows, used, 0.0), axis=1, keepdims=True)
    used_list = jnp.sum(jnp.where((rank == columns) & (used_column > 0), rows, 0.0), axis=0, keepdims=True)
    right_rank = jnp.sum(jnp.where(columns < right, used, 0.0), axis=1, keepdims=True)

    parity = lambda value: value - 2.0 * jnp.floor(value * 0.5)
    count = jnp.sum(one(owner == columns), axis=0, keepdims=True)
    same = parity(rows) == parity(columns)
    offset = jnp.sum(jnp.where((rows < columns) & same, to_column(count), 0.0), axis=0, keepdims=True)
    ahead = (owner_row < owner) | ((owner_row == owner) & (across < down))
    ahead = ahead & (parity(owner_row) == parity(owner))
    position = jnp.sum(one(ahead), axis=1, keepdims=True)

    core = place[3].astype(jnp.float32)
    local = right_rank - core * (USED // 2)
    here = (local >= 0) & (local < USED // 2)
    local = jnp.where(here, local, 0.0)
    lane = lax.broadcasted_iota(jnp.int32, (1, size), 1)
    groups = jnp.zeros((1, size), jnp.float32)
    for half in range(2):
        hit = (position == columns) & (parity(owner) == half)
        pick = lambda column: jnp.sum(jnp.where(hit, column, 0.0), axis=0, keepdims=True).astype(jnp.int32)
        at = pick(local)
        out_ref[4 * half : 4 * half + 1, :] = pick(left) * BLK
        out_ref[4 * half + 1 : 4 * half + 2, :] = at // 8 * 128
        out_ref[4 * half + 2 : 4 * half + 3, :] = (lane + 8 - at % 8) % 8 * BLK
        out_ref[4 * half + 3 : 4 * half + 4, :] = jnp.where(pick(one(here)) > 0, lane % 8, -1)
        total = jnp.sum(one(parity(owner_row) == half))
        groups = jnp.where(lane == half, jnp.floor((total + 7.0) / 8.0), groups)
    for at, row in enumerate((offset, count, used_list, groups)):
        out_ref[8 + at : 9 + at, :] = row.astype(jnp.int32)


def plan_call(place, pairs, owners):
    return pl.pallas_call(
        plan_kernel,
        out_shape=jax.ShapeDtypeStruct((16, pairs.shape[0]), jnp.int32),
        in_specs=[SMEM, VMEM, VMEM],
        out_specs=VMEM,
        compiler_params=params(8),
        name="plan",
    )(place, pairs, owners)


def padded(planes):
    return (len(planes) * PLANE + 127) // 128 * 128


def screen_kernel(place, own_ref, other_ref, *outs):
    z = place[0]
    rows = 16
    lane = lax.broadcasted_iota(jnp.int32, (rows, 128), 1)

    def plane_of(ref, row, delta, offset):
        plane = lax.rem(z + delta, 8)
        odd = lax.rem(plane, 2)
        column = pl.multiple_of(plane * PLANE - odd * 64, 128)
        window = ref[row, pl.ds(column, 384)]
        turned = pltpu.roll(window, 64 if offset else 320, 1)
        return jnp.where((odd == 1) if offset else (odd == 0), window, turned)

    for source, ref in enumerate((own_ref, other_ref)):

        def body(step, carry, source=source, ref=ref):
            part = step // 10
            row = pl.ds(pl.multiple_of(step * rows, rows), rows)
            target = pl.multiple_of(part * PLANE + source * (PLANE // 2) + (step - part * 10) * rows, rows)
            for group, planes in enumerate((NEAR, MIDDLE, FAR)):
                for at in range(0, len(planes), 2):
                    a = plane_of(ref, row, planes[at], False)
                    if at + 1 < len(planes):
                        b = plane_of(ref, row, planes[at + 1], True)
                        middle = jnp.where(lane < 64, a[:, 256:], b[:, :128])
                        whole = jnp.concatenate([a[:, :256], middle, b[:, 128:]], axis=1)
                    else:
                        whole = jnp.concatenate([a[:, :256], jnp.where(lane < 64, a[:, 256:], 0.0)], axis=1)
                    top, rest = split(whole)
                    columns = slice(at * PLANE, at * PLANE + whole.shape[1])
                    outs[2 * group][pl.ds(target, rows), columns] = top
                    outs[2 * group + 1][pl.ds(target, rows), columns] = rest
            return carry

        lax.fori_loop(0, 20, body, 0)


def screen_call(place, own, other):
    shapes = [
        jax.ShapeDtypeStruct((2 * own.shape[0], padded(planes)), jnp.bfloat16)
        for planes in (NEAR, MIDDLE, FAR)
        for _ in range(2)
    ]
    return pl.pallas_call(
        screen_kernel,
        out_shape=shapes,
        in_specs=[SMEM, VMEM, VMEM],
        out_specs=[VMEM] * 6,
        compiler_params=params(20),
        name="screen",
    )(place, own, other)


def left_kernel(place, *refs):
    pieces, (high_ref, low_ref, work) = refs[:8], refs[8:]
    x = place[1]
    span = pieces[0].shape[0] // 2
    for core in range(2):
        for shift in range(4):
            shard = lax.rem(x - shift + 4, 4)
            for part in range(2):
                row = pl.multiple_of(part * 8 * span + core * 4 * span + shard * span, 8)
                work[pl.ds(row, span), :] = pieces[core * 4 + shift][part * span : (part + 1) * span, :]

    def body(block, carry):
        at = pl.ds(pl.multiple_of(block * 128, 128), 128)
        high_ref[at, :], low_ref[at, :] = split(work[:, at].T)
        return carry

    lax.fori_loop(0, work.shape[1] // 128, body, 0)


def left_call(place, pieces):
    depth, width = pieces[0].shape
    shape = jax.ShapeDtypeStruct((width, 8 * depth), jnp.bfloat16)
    return pl.pallas_call(
        left_kernel,
        out_shape=(shape, shape),
        in_specs=[SMEM] + [VMEM] * 8,
        out_specs=(VMEM, VMEM),
        scratch_shapes=[pltpu.VMEM((8 * depth, width), jnp.float32)],
        compiler_params=params(20),
        name="left",
    )(place, *pieces)


def load_right(place, runs, planes, high, low):
    y = place[2]
    for delta, ref, start, first, count in runs:
        spread = lax.rem(y + delta, 4) * SPAN

        def body(step, carry, ref=ref, start=start, first=first, spread=spread):
            unit = first + step
            row = pl.ds(pl.multiple_of(unit // 2 * PLANE + spread, 16), SPAN)
            column = pl.ds(pl.multiple_of(lax.rem(unit, 2) * HALF, HALF), HALF)
            top, rest = split(ref[pl.ds(pl.multiple_of(start + step * SPAN, 8), SPAN), :])
            high[row, column] = top
            low[row, column] = rest
            return carry

        lax.fori_loop(0, count, body, 0)
    used = planes * PLANE
    if used < high.shape[0]:
        for ref in (high, low):
            ref[used:, :] = jnp.zeros((ref.shape[0] - used, ref.shape[1]), ref.dtype)


def near_runs(first, first_down, first_up, second, second_down, second_up, two_down, two_up):
    skip = 3 * SPAN
    return (
        ((0, first, 0, 0, 6), (3, first_down, 0, 0, 6), (1, first_up, 0, 0, 6))
        + ((0, second, 0, 6, 4), (3, second_down, 0, 6, 4), (1, second_up, 0, 6, 4))
        + ((2, two_down, 0, 0, 3), (2, two_up, 0, 3, 3), (2, two_down, skip, 6, 2), (2, two_up, skip, 8, 2))
    )


def middle_runs(z_below, z_above, y_below, y_above):
    runs = ()
    for first, sides, across in ((0, z_below, y_below), (2, z_above, y_above)):
        runs += ((3, sides, 0, first, 2), (1, sides, 2 * SPAN, first, 2), (0, sides, 4 * SPAN, first, 2))
        runs += ((2, across, 0, first, 2),)
    return runs


def far_runs(below, above, across_low, across_high):
    return (
        ((3, below, 0, 0, 2), (1, above, 0, 0, 2), (0, below, 2 * SPAN, 0, 1), (0, above, 2 * SPAN, 1, 1))
        + ((2, across_low, 0, 0, 1), (2, across_high, 0, 1, 1))
    )


def group_kernel(runs, planes, place, *refs):
    count = len(refs) - 5 - (runs is middle_runs)
    rights, (high_ref, low_ref), rest = refs[:count], refs[count : count + 2], refs[count + 2 :]
    out_ref, rh, rl = rest[-3:]
    load_right(place, runs(*rights), planes, rh, rl)
    value = dot3(high_ref[...], low_ref[...], rh[...], rl[...])
    out_ref[...] = value if len(rest) == 3 else value + rest[0][...]


def group_call(runs, planes, place, rights, screens, total):
    rows, width = screens[0].shape
    return pl.pallas_call(
        functools.partial(group_kernel, runs, planes),
        out_shape=jax.ShapeDtypeStruct((rows, 2 * HALF), jnp.float32),
        in_specs=[SMEM] + [VMEM] * (len(rights) + 2 + len(total)),
        out_specs=VMEM,
        scratch_shapes=[pltpu.VMEM((width, 2 * HALF), jnp.bfloat16)] * 2,
        compiler_params=params(32),
        name="group",
    )(place, *rights, *screens, *total)


def pair_kernel(place, table, *refs):
    rights, (high_ref, low_ref, sum_ref, left_high, left_low, give_ref, kern, rh, rl) = refs[:4], refs[4:]
    load_right(place, far_runs(*rights), len(FAR), rh, rl)
    product = sum_ref[...] + dot3(high_ref[...], low_ref[...], rh[...], rl[...])
    mid = product.shape[0] // 2
    real = product[:mid, :HALF] - product[mid:, HALF:]
    imag = product[mid:, :HALF] + product[:mid, HALF:]
    applied = NG ** (-0.5) * jnp.concatenate(
        [jnp.concatenate([real, imag], axis=0), jnp.concatenate([imag, -real], axis=0)], axis=1
    )
    kern[...] = dot3(left_high[...], left_low[...], *split(applied))

    extract(place, table, 1 - place[3], kern, give_ref)


def extract(place, table, half, kern, out_ref):
    at = lambda x: lax.rem(x + 4 - place[1], 4)
    lane = lax.broadcasted_iota(jnp.int32, (8, 128), 1) // BLK
    upper = lax.broadcasted_iota(jnp.int32, (8, 128), 0) < 4

    def groups(pair, carry):
        for g in (pair * 2, pair * 2 + 1):
            tiles = [[jnp.zeros((8, 128), jnp.float32) for _ in range(2)] for _ in range(2)]
            for u in range(8):
                slot = g * 8 + u
                row = pl.multiple_of(table[4 * half, slot], BLK)
                column = pl.multiple_of(table[4 * half + 1, slot], 128)
                shift = table[4 * half + 2, slot]
                target = table[4 * half + 3, slot]
                for part in range(2):
                    for side in range(2):
                        tile = kern[pl.ds(row + side * 8, 8), pl.ds(column + part * HALF, 128)]
                        tile = pltpu.roll(tile, shift, 1)
                        tiles[part][side] = jnp.where(lane == target, tile, tiles[part][side])
            lanes = pl.ds(pl.multiple_of(g * 128, 128), 128)
            for side in range(2):
                real, imag = tiles[0][side], tiles[1][side]
                out_ref[at(2 * side), :, lanes] = jnp.where(upper, real, pltpu.roll(imag, 4, 0))
                out_ref[at(2 * side + 1), :, lanes] = jnp.where(upper, pltpu.roll(real, 4, 0), imag)
        return carry

    out_ref[...] = jnp.zeros_like(out_ref)
    lax.fori_loop(0, (table[11, half] + 1) // 2, groups, 0)


def pair_call(place, table, rights, screens, total, left_high, left_low):
    rows = left_high.shape[0]
    return pl.pallas_call(
        pair_kernel,
        out_shape=(
            jax.ShapeDtypeStruct((4, 8, ROOM * BLK), jnp.float32),
            jax.ShapeDtypeStruct((rows, 2 * HALF), jnp.float32),
        ),
        in_specs=[SMEM, SMEM] + [VMEM] * (len(rights) + 5),
        out_specs=(VMEM, VMEM),
        scratch_shapes=[pltpu.VMEM((screens[0].shape[1], 2 * HALF), jnp.bfloat16)] * 2,
        compiler_params=params(24),
        name="pair",
    )(place, table, *rights, *screens, total, left_high, left_low)


def extract_kernel(place, table, kern, out_ref):
    extract(place, table, place[3], kern, out_ref)


def extract_call(place, table, kern):
    return pl.pallas_call(
        extract_kernel,
        out_shape=jax.ShapeDtypeStruct((4, 8, ROOM * BLK), jnp.float32),
        in_specs=[SMEM, SMEM, VMEM],
        out_specs=VMEM,
        compiler_params=params(8),
        name="extract",
    )(place, table, kern)


def add_kernel(one_ref, two_ref, *outs):
    for at, out_ref in enumerate(outs):
        out_ref[...] = one_ref[at] + two_ref[at]


def add_call(one, two):
    return pl.pallas_call(
        add_kernel,
        out_shape=[jax.ShapeDtypeStruct(one.shape[1:], one.dtype)] * one.shape[0],
        in_specs=[VMEM, VMEM],
        out_specs=[VMEM] * one.shape[0],
        compiler_params=params(8),
        name="add",
    )(one, two)


def owner_kernel(place, table, one_ref, two_ref, three_ref, four_ref, out_ref, work):
    total = (one_ref[...] + two_ref[...]) + (three_ref[...] + four_ref[...])
    width = total.shape[1]
    work[:, :width] = total
    work[:, width:] = jnp.zeros((8, work.shape[1] - width), jnp.float32)
    for chip in range(out_ref.shape[0]):
        start = table[8, chip * 2 + place[3]]
        column = pl.multiple_of(start // 8 * 128, 128)
        shift = lax.rem(384 - lax.rem(start, 8) * BLK, 384)
        out_ref[chip] = pltpu.roll(work[:, pl.ds(column, 384)], shift, 1)[:, :256]


def owner_call(place, table, parts):
    return pl.pallas_call(
        owner_kernel,
        out_shape=jax.ShapeDtypeStruct((32, 8, 256), jnp.float32),
        in_specs=[SMEM, SMEM] + [VMEM] * 4,
        out_specs=VMEM,
        scratch_shapes=[pltpu.VMEM((8, parts[0].shape[1] + 384), jnp.float32)],
        compiler_params=params(8),
        name="owner",
    )(place, table, *parts)


def last_kernel(place, table, parts_ref, out_ref):
    total = parts_ref[0]
    for chip in range(1, parts_ref.shape[0]):
        total = total + parts_ref[chip]
    held = table[9, (place[0] * 4 + place[2]) * 2 + place[3]]
    for slot in range(CAP):
        tile = total[:, slot // 8 * 128 : slot // 8 * 128 + 128]
        tile = pltpu.roll(tile, (128 - slot % 8 * BLK) % 128, 1)
        out_ref[slot] = jnp.where(slot < held, tile[:, :BLK], 0.0)


def last_call(place, table, parts):
    return pl.pallas_call(
        last_kernel,
        out_shape=jax.ShapeDtypeStruct((CAP, 8, BLK), jnp.float32),
        in_specs=[SMEM, SMEM, VMEM],
        out_specs=VMEM,
        compiler_params=params(8),
        name="last",
    )(place, table, parts)


def pack_kernel(place, own_ref, other_ref, out_ref, work):
    core = place[3]
    width = own_ref.shape[2]
    for block in range(width // 128):
        lanes = pl.ds(block * 128, 128)
        rows = []
        for part in range(2):
            own, other = own_ref[part, :, lanes], other_ref[part, :, lanes]
            rows += [jnp.where(core == 0, own, other), jnp.where(core == 0, other, own)]
        rows = jnp.concatenate(rows + rows, axis=0)
        work[block * 128 : (block + 1) * 128, :] = rows.T
    half = lax.broadcasted_iota(jnp.int32, (8, 128), 1) < 64
    for chip in range(32):
        at = pl.multiple_of(chip * 80 + core * 40, 8)
        tiles = [work[pl.ds(at + 8 * t, 8), :] for t in range(5)]
        out_ref[chip * 20 : chip * 20 + 8, :] = jnp.where(half, tiles[0], tiles[1])
        out_ref[chip * 20 + 8 : chip * 20 + 16, :] = jnp.where(half, tiles[2], tiles[3])
        last = jnp.where(half, tiles[4], pltpu.roll(tiles[4], 4, 0))
        out_ref[chip * 20 + 16 : chip * 20 + 20, :] = last[:4]


def pack_call(place, own, other):
    width = own.shape[2]
    return pl.pallas_call(
        pack_kernel,
        out_shape=jax.ShapeDtypeStruct((32 * 20, 128), jnp.float32),
        in_specs=[SMEM, VMEM, VMEM],
        out_specs=VMEM,
        scratch_shapes=[pltpu.VMEM((width, 128), jnp.float32)],
        name="pack",
    )(place, own, other)


def unpack_kernel(place, table, in_ref, columns_ref, keep_ref, give_ref):
    core = place[3]
    quarter = lax.broadcasted_iota(jnp.int32, (8, 128), 1) // 32
    upper = lax.broadcasted_iota(jnp.int32, (8, 128), 0) < 4
    for group in range(8):
        tiles = [[None] * 5 for _ in range(2)]
        for u in range(4):
            at = (group * 4 + u) * 20
            one, two = in_ref[at : at + 8, :], in_ref[at + 8 : at + 16, :]
            end = in_ref[at + 12 : at + 20, :]
            end = jnp.where(upper, pltpu.roll(end, 4, 0), pltpu.roll(end, 64, 1))
            for t, (source, first) in enumerate(((one, 0), (one, 64), (two, 0), (two, 64), (end, 0))):
                for part in range(2):
                    by = (u * 32 - first - part * 32) % 128
                    turned = pltpu.roll(source, by, 1) if by else source
                    old = tiles[part][t]
                    tiles[part][t] = turned if old is None else jnp.where(quarter == u, turned, old)
        for part in range(2):
            for t in range(5):
                row = part * 40 + t * 8
                columns_ref[row : row + 8, group * 128 : (group + 1) * 128] = tiles[part][t]
    select(table, 1 - core, columns_ref, give_ref)
    select(table, core, columns_ref, keep_ref)


def select(table, which, columns_ref, out_ref):
    eighth = lax.broadcasted_iota(jnp.int32, (80, 128), 1) // BLK
    for group in range(2):
        slab = None
        for u in range(8):
            block = table[10, which * (USED // 2) + group * 8 + u]
            column = pl.multiple_of(block // 8 * 128, 128)
            by = lax.rem(u * BLK + 128 - lax.rem(block, 8) * BLK, 128)
            turned = pltpu.roll(columns_ref[:, pl.ds(column, 128)], by, 1)
            slab = turned if slab is None else jnp.where(eighth == u, turned, slab)
        out_ref[:, group * 128 : (group + 1) * 128] = slab


def unpack_call(place, table, pieces):
    return pl.pallas_call(
        unpack_kernel,
        out_shape=(
            jax.ShapeDtypeStruct((80, 1024), jnp.float32),
            jax.ShapeDtypeStruct((80, HALF), jnp.float32),
            jax.ShapeDtypeStruct((80, HALF), jnp.float32),
        ),
        in_specs=[SMEM, SMEM, VMEM],
        out_specs=(VMEM, VMEM, VMEM),
        compiler_params=params(8),
        name="unpack",
    )(place, table, pieces)


def shard_kernel(place, keep_ref, take_ref, out_ref):
    core = place[3]
    for part in range(2):
        out_ref[pl.ds(pl.multiple_of(part * 80 + core * 40, 8), 40), :] = keep_ref[part * 40 : part * 40 + 40, :]
        out_ref[pl.ds(pl.multiple_of(part * 80 + 40 - core * 40, 8), 40), :] = take_ref[part * 40 : part * 40 + 40, :]


def shard_call(place, keep, take):
    return pl.pallas_call(
        shard_kernel,
        out_shape=jax.ShapeDtypeStruct((160, HALF), jnp.float32),
        in_specs=[SMEM, VMEM, VMEM],
        out_specs=VMEM,
        compiler_params=params(8),
        name="shard",
    )(place, keep, take)


def after(array, *others):
    return lax.optimization_barrier((array, *others))[0]


def shards(densities, screened, pairs, owners):
    span = screened.shape[2]
    place = jnp.stack([lax.axis_index(axis) for axis in ("z", "x", "y", "core")]).astype(jnp.int32)
    shift = lambda array, axis, by: lax.ppermute(array, axis, ring(lax.axis_size(axis), by))
    swap = lambda array: lax.ppermute(array, "core", SWAP)
    join = lambda *arrays: jnp.concatenate(arrays, axis=0)
    hold = lax.optimization_barrier

    pieces = pack_call(place, densities, swap(densities))
    table = plan_call(place, after(pairs, pieces), owners.reshape(1, -1))
    mine = lax.all_to_all(pieces.reshape(32, 1, -1), ("z", "y"), 0, 0, tiled=True).reshape(pieces.shape)

    screen = screened.reshape(2 * 4 * span, -1)
    mine, other = hold((mine, swap(after(screen, pieces))))

    columns, keep, give = unpack_call(place, table, mine)
    shard = shard_call(place, keep, swap(give))

    block = 2 * SPAN
    columns, shard = hold((columns, shard))
    below2, above2 = shift(shard, "z", 2), shift(shard, "z", -2)
    below, above = hold((shift(shard, "z", 1), shift(shard, "z", -1)))
    first = join(shard, below, above)
    first_down, first_up = shift(first, "y", 1), shift(first, "y", -1)
    around = [columns, shift(columns, "x", 1)]
    below2, above2, first, columns, around[1] = hold((below2, above2, first, columns, around[1]))
    second = join(below2, above2)
    second_down, second_up = shift(second, "y", 1), shift(second, "y", -1)
    around += [shift(columns, "x", 2), shift(columns, "x", 3)]
    screens = screen_call(place, after(screen, second), other)
    first_down, first_up, *screens = hold((first_down, first_up, *screens))
    swapped = [swap(columns)]
    second_down, second_up, first_down, *rest = hold((second_down, second_up, first_down, *around[2:], *swapped))
    around[2:], swapped = rest[:2], rest[2:]

    z_below = shift(join(second_down[:block], second_up[:block], second[:block]), "z", 1)
    z_above = shift(join(second_down[block:], second_up[block:], second[block:]), "z", -1)
    two_down = shift(join(first_down[: 3 * SPAN], second_down[:block]), "y", 1)
    two_up = shift(join(first_up[3 * SPAN :], second_up[block:]), "y", -1)
    swapped += [swap(around[1]), swap(around[2])]
    two_down, two_up, z_below, z_above, *swapped = hold((two_down, two_up, z_below, z_above, *swapped))

    y_below, y_above = shift(z_below[:block], "y", 1), shift(z_above[block : 2 * block], "y", -1)
    far_below = shift(join(z_below[:block], z_below[2 * block : 2 * block + SPAN]), "z", 1)
    far_above = shift(join(z_above[block : 2 * block], z_above[2 * block + SPAN :]), "z", -1)
    rights = (first, first_down, first_up, second, second_down, second_up, two_down, two_up)
    total = group_call(near_runs, len(NEAR), place, rights, screens[:2], ())
    swapped.append(swap(around[3]))
    y_below, y_above, far_below, far_above, total, swapped[3] = hold(
        (y_below, y_above, far_below, far_above, total, swapped[3])
    )

    across_low, across_high = shift(far_below[:SPAN], "y", 1), shift(far_above[SPAN : 2 * SPAN], "y", -1)
    rights = (z_below, z_above, y_below, y_above)
    total = group_call(middle_runs, len(MIDDLE), place, rights, screens[2:4], (total,))
    left_high, left_low = left_call(place, around + swapped)
    across_low, across_high, total, left_high, left_low = hold((across_low, across_high, total, left_high, left_low))
    rights = (far_below, far_above, across_low, across_high)
    give, kern = pair_call(place, table, rights, screens[4:], total, left_high, left_low)

    parts = add_call(extract_call(place, table, kern), swap(give))
    parts = [parts[0]] + [shift(parts[by], "x", by) for by in (1, 2, 3)]
    parts = owner_call(place, table, parts)
    parts = lax.all_to_all(parts, ("z", "y"), 0, 0, tiled=True)
    return last_call(place, table, parts).reshape(1, CAP, 2, 4, BLK)


def solution(mesh):
    fine = Mesh(mesh.devices.reshape(8, 4, 2, 4), ("z", "y", "core", "x"))
    in_specs = (P(None, BAND, "x"), P(None, None, BAND, "x"), P(), P())
    out_specs = P(BAND, None, None, "x", None)
    return jax.shard_map(shards, mesh=fine, in_specs=in_specs, out_specs=out_specs, check_vma=False)
```

```python
import functools

import jax
import jax.numpy as jnp
from jax import lax
from jax.experimental import pallas as pl
from jax.experimental.pallas import tpu as pltpu
from jax.sharding import Mesh
from jax.sharding import PartitionSpec as P

NG = 10240
CAP = 12
BLK = 16
USED = 32
HALF = USED // 2 * BLK
BAND = ("z", "y", "core")
SWAP = ((0, 1), (1, 0))
SMEM = pl.BlockSpec(memory_space=pltpu.SMEM)
VMEM = pl.BlockSpec(memory_space=pltpu.VMEM)
SPAN = 80
PLANE = 320
NEAR = (0, 7, 1, 6, 2)
MIDDLE = (5, 3)
FAR = (4,)
ROOM = 224


def ring(n, shift):
    return [(i, (i + shift) % n) for i in range(n)]


def params(mib):
    return pltpu.CompilerParams(vmem_limit_bytes=mib * 1024 * 1024)


def split(x):
    high = x.astype(jnp.bfloat16)
    return high, (x - high.astype(jnp.float32)).astype(jnp.bfloat16)


def dot(former, latter):
    return jnp.dot(former, latter, preferred_element_type=jnp.float32)


def dot3(high, low, former, latter):
    return dot(high, former) + dot(high, latter) + dot(low, former)


def plan_kernel(place, pairs_ref, owners_ref, out_ref):
    size = 256
    down = lax.broadcasted_iota(jnp.int32, (size, size), 0)
    across = lax.broadcasted_iota(jnp.int32, (size, size), 1)
    one = lambda condition: jnp.where(condition, 1.0, 0.0)
    to_row = lambda column: jnp.sum(jnp.where(down == across, column, 0.0), axis=0, keepdims=True)
    to_column = lambda row: jnp.sum(jnp.where(down == across, row, 0.0), axis=1, keepdims=True)
    rows, columns = down.astype(jnp.float32), across.astype(jnp.float32)
    left, right = pairs_ref[:, 0:1].astype(jnp.float32), pairs_ref[:, 1:2].astype(jnp.float32)
    owner_row = owners_ref[...].astype(jnp.float32)
    owner = to_column(owner_row)

    used = jnp.max(one(right == columns), axis=0, keepdims=True)
    used_column = to_column(used)
    rank = jnp.sum(jnp.where(columns < rows, used, 0.0), axis=1, keepdims=True)
    used_list = jnp.sum(jnp.where((rank == columns) & (used_column > 0), rows, 0.0), axis=0, keepdims=True)
    right_rank = jnp.sum(jnp.where(columns < right, used, 0.0), axis=1, keepdims=True)

    parity = lambda value: value - 2.0 * jnp.floor(value * 0.5)
    count = jnp.sum(one(owner == columns), axis=0, keepdims=True)
    same = parity(rows) == parity(columns)
    offset = jnp.sum(jnp.where((rows < columns) & same, to_column(count), 0.0), axis=0, keepdims=True)
    ahead = (owner_row < owner) | ((owner_row == owner) & (across < down))
    ahead = ahead & (parity(owner_row) == parity(owner))
    position = jnp.sum(one(ahead), axis=1, keepdims=True)

    core = place[3].astype(jnp.float32)
    local = right_rank - core * (USED // 2)
    here = (local >= 0) & (local < USED // 2)
    local = jnp.where(here, local, 0.0)
    lane = lax.broadcasted_iota(jnp.int32, (1, size), 1)
    groups = jnp.zeros((1, size), jnp.float32)
    for half in range(2):
        hit = (position == columns) & (parity(owner) == half)
        pick = lambda column: jnp.sum(jnp.where(hit, column, 0.0), axis=0, keepdims=True).astype(jnp.int32)
        at = pick(local)
        out_ref[4 * half : 4 * half + 1, :] = pick(left) * BLK
        out_ref[4 * half + 1 : 4 * half + 2, :] = at // 8 * 128
        out_ref[4 * half + 2 : 4 * half + 3, :] = (lane + 8 - at % 8) % 8 * BLK
        out_ref[4 * half + 3 : 4 * half + 4, :] = jnp.where(pick(one(here)) > 0, lane % 8, -1)
        total = jnp.sum(one(parity(owner_row) == half))
        groups = jnp.where(lane == half, jnp.floor((total + 7.0) / 8.0), groups)
    for at, row in enumerate((offset, count, used_list, groups)):
        out_ref[8 + at : 9 + at, :] = row.astype(jnp.int32)


def plan_call(place, pairs, owners):
    return pl.pallas_call(
        plan_kernel,
        out_shape=jax.ShapeDtypeStruct((16, pairs.shape[0]), jnp.int32),
        in_specs=[SMEM, VMEM, VMEM],
        out_specs=VMEM,
        compiler_params=params(8),
        name="plan",
    )(place, pairs, owners)


def padded(planes):
    return (len(planes) * PLANE + 127) // 128 * 128


def screen_kernel(place, own_ref, other_ref, *outs):
    z = place[0]
    rows = 16
    lane = lax.broadcasted_iota(jnp.int32, (rows, 128), 1)

    def plane_of(ref, row, delta, offset):
        plane = lax.rem(z + delta, 8)
        odd = lax.rem(plane, 2)
        column = pl.multiple_of(plane * PLANE - odd * 64, 128)
        window = ref[row, pl.ds(column, 384)]
        turned = pltpu.roll(window, 64 if offset else 320, 1)
        return jnp.where((odd == 1) if offset else (odd == 0), window, turned)

    for source, ref in enumerate((own_ref, other_ref)):

        def body(step, carry, source=source, ref=ref):
            part = step // 10
            row = pl.ds(pl.multiple_of(step * rows, rows), rows)
            target = pl.multiple_of(part * PLANE + source * (PLANE // 2) + (step - part * 10) * rows, rows)
            for group, planes in enumerate((NEAR, MIDDLE, FAR)):
                for at in range(0, len(planes), 2):
                    a = plane_of(ref, row, planes[at], False)
                    if at + 1 < len(planes):
                        b = plane_of(ref, row, planes[at + 1], True)
                        middle = jnp.where(lane < 64, a[:, 256:], b[:, :128])
                        whole = jnp.concatenate([a[:, :256], middle, b[:, 128:]], axis=1)
                    else:
                        whole = jnp.concatenate([a[:, :256], jnp.where(lane < 64, a[:, 256:], 0.0)], axis=1)
                    top, rest = split(whole)
                    columns = slice(at * PLANE, at * PLANE + whole.shape[1])
                    outs[2 * group][pl.ds(target, rows), columns] = top
                    outs[2 * group + 1][pl.ds(target, rows), columns] = rest
            return carry

        lax.fori_loop(0, 20, body, 0)


def screen_call(place, own, other):
    shapes = [
        jax.ShapeDtypeStruct((2 * own.shape[0], padded(planes)), jnp.bfloat16)
        for planes in (NEAR, MIDDLE, FAR)
        for _ in range(2)
    ]
    return pl.pallas_call(
        screen_kernel,
        out_shape=shapes,
        in_specs=[SMEM, VMEM, VMEM],
        out_specs=[VMEM] * 6,
        compiler_params=params(20),
        name="screen",
    )(place, own, other)


def left_kernel(place, *refs):
    pieces, (high_ref, low_ref, work) = refs[:8], refs[8:]
    x = place[1]
    span = pieces[0].shape[0] // 2
    for core in range(2):
        for shift in range(4):
            shard = lax.rem(x - shift + 4, 4)
            for part in range(2):
                row = pl.multiple_of(part * 8 * span + core * 4 * span + shard * span, 8)
                work[pl.ds(row, span), :] = pieces[core * 4 + shift][part * span : (part + 1) * span, :]

    def body(block, carry):
        at = pl.ds(pl.multiple_of(block * 128, 128), 128)
        high_ref[at, :], low_ref[at, :] = split(work[:, at].T)
        return carry

    lax.fori_loop(0, work.shape[1] // 128, body, 0)


def left_call(place, pieces):
    depth, width = pieces[0].shape
    shape = jax.ShapeDtypeStruct((width, 8 * depth), jnp.bfloat16)
    return pl.pallas_call(
        left_kernel,
        out_shape=(shape, shape),
        in_specs=[SMEM] + [VMEM] * 8,
        out_specs=(VMEM, VMEM),
        scratch_shapes=[pltpu.VMEM((8 * depth, width), jnp.float32)],
        compiler_params=params(20),
        name="left",
    )(place, *pieces)


def load_right(place, runs, planes, high, low):
    y = place[2]
    for delta, ref, start, first, count in runs:
        spread = lax.rem(y + delta, 4) * SPAN

        def body(step, carry, ref=ref, start=start, first=first, spread=spread):
            unit = first + step
            row = pl.ds(pl.multiple_of(unit // 2 * PLANE + spread, 16), SPAN)
            column = pl.ds(pl.multiple_of(lax.rem(unit, 2) * HALF, HALF), HALF)
            top, rest = split(ref[pl.ds(pl.multiple_of(start + step * SPAN, 8), SPAN), :])
            high[row, column] = top
            low[row, column] = rest
            return carry

        lax.fori_loop(0, count, body, 0)
    used = planes * PLANE
    if used < high.shape[0]:
        for ref in (high, low):
            ref[used:, :] = jnp.zeros((ref.shape[0] - used, ref.shape[1]), ref.dtype)


def near_runs(first, first_down, first_up, second, second_down, second_up, two_down, two_up):
    skip = 3 * SPAN
    return (
        ((0, first, 0, 0, 6), (3, first_down, 0, 0, 6), (1, first_up, 0, 0, 6))
        + ((0, second, 0, 6, 4), (3, second_down, 0, 6, 4), (1, second_up, 0, 6, 4))
        + ((2, two_down, 0, 0, 3), (2, two_up, 0, 3, 3), (2, two_down, skip, 6, 2), (2, two_up, skip, 8, 2))
    )


def middle_runs(below, above, z_below, z_above, y_below, y_above):
    runs = ()
    for first, own, sides, across in ((0, below, z_below, y_below), (2, above, z_above, y_above)):
        runs += ((0, own, 0, first, 2), (3, sides, 0, first, 2), (1, sides, 2 * SPAN, first, 2))
        runs += ((2, across, 0, first, 2),)
    return runs


def far_runs(z_below, z_above, below, above, across_low, across_high):
    return (
        ((0, z_below, 4 * SPAN, 0, 1), (0, z_above, 4 * SPAN, 1, 1), (3, below, 0, 0, 2), (1, above, 0, 0, 2))
        + ((2, across_low, 0, 0, 1), (2, across_high, 0, 1, 1))
    )


def group_kernel(runs, planes, place, *refs):
    count = len(refs) - 5 - (runs is middle_runs)
    rights, (high_ref, low_ref), rest = refs[:count], refs[count : count + 2], refs[count + 2 :]
    out_ref, rh, rl = rest[-3:]
    load_right(place, runs(*rights), planes, rh, rl)
    value = dot3(high_ref[...], low_ref[...], rh[...], rl[...])
    out_ref[...] = value if len(rest) == 3 else value + rest[0][...]


def group_call(runs, planes, place, rights, screens, total):
    rows, width = screens[0].shape
    return pl.pallas_call(
        functools.partial(group_kernel, runs, planes),
        out_shape=jax.ShapeDtypeStruct((rows, 2 * HALF), jnp.float32),
        in_specs=[SMEM] + [VMEM] * (len(rights) + 2 + len(total)),
        out_specs=VMEM,
        scratch_shapes=[pltpu.VMEM((width, 2 * HALF), jnp.bfloat16)] * 2,
        compiler_params=params(32),
        name="group",
    )(place, *rights, *screens, *total)


def pair_kernel(place, table, *refs):
    rights, (high_ref, low_ref, sum_ref, left_high, left_low, give_ref, kern, rh, rl) = refs[:6], refs[6:]
    load_right(place, far_runs(*rights), len(FAR), rh, rl)
    product = sum_ref[...] + dot3(high_ref[...], low_ref[...], rh[...], rl[...])
    mid = product.shape[0] // 2
    real = product[:mid, :HALF] - product[mid:, HALF:]
    imag = product[mid:, :HALF] + product[:mid, HALF:]
    applied = NG ** (-0.5) * jnp.concatenate(
        [jnp.concatenate([real, imag], axis=0), jnp.concatenate([imag, -real], axis=0)], axis=1
    )
    kern[...] = dot3(left_high[...], left_low[...], *split(applied))

    extract(place, table, 1 - place[3], kern, give_ref)


def extract(place, table, half, kern, out_ref):
    at = lambda x: lax.rem(x + 4 - place[1], 4)
    lane = lax.broadcasted_iota(jnp.int32, (8, 128), 1) // BLK
    upper = lax.broadcasted_iota(jnp.int32, (8, 128), 0) < 4

    def groups(pair, carry):
        for g in (pair * 2, pair * 2 + 1):
            tiles = [[jnp.zeros((8, 128), jnp.float32) for _ in range(2)] for _ in range(2)]
            for u in range(8):
                slot = g * 8 + u
                row = pl.multiple_of(table[4 * half, slot], BLK)
                column = pl.multiple_of(table[4 * half + 1, slot], 128)
                shift = table[4 * half + 2, slot]
                target = table[4 * half + 3, slot]
                for part in range(2):
                    for side in range(2):
                        tile = kern[pl.ds(row + side * 8, 8), pl.ds(column + part * HALF, 128)]
                        tile = pltpu.roll(tile, shift, 1)
                        tiles[part][side] = jnp.where(lane == target, tile, tiles[part][side])
            lanes = pl.ds(pl.multiple_of(g * 128, 128), 128)
            for side in range(2):
                real, imag = tiles[0][side], tiles[1][side]
                out_ref[at(2 * side), :, lanes] = jnp.where(upper, real, pltpu.roll(imag, 4, 0))
                out_ref[at(2 * side + 1), :, lanes] = jnp.where(upper, pltpu.roll(real, 4, 0), imag)
        return carry

    out_ref[...] = jnp.zeros_like(out_ref)
    lax.fori_loop(0, (table[11, half] + 1) // 2, groups, 0)


def pair_call(place, table, rights, screens, total, left_high, left_low):
    rows = left_high.shape[0]
    return pl.pallas_call(
        pair_kernel,
        out_shape=(
            jax.ShapeDtypeStruct((4, 8, ROOM * BLK), jnp.float32),
            jax.ShapeDtypeStruct((rows, 2 * HALF), jnp.float32),
        ),
        in_specs=[SMEM, SMEM] + [VMEM] * (len(rights) + 5),
        out_specs=(VMEM, VMEM),
        scratch_shapes=[pltpu.VMEM((screens[0].shape[1], 2 * HALF), jnp.bfloat16)] * 2,
        compiler_params=params(24),
        name="pair",
    )(place, table, *rights, *screens, total, left_high, left_low)


def extract_kernel(place, table, kern, out_ref):
    extract(place, table, place[3], kern, out_ref)


def extract_call(place, table, kern):
    return pl.pallas_call(
        extract_kernel,
        out_shape=jax.ShapeDtypeStruct((4, 8, ROOM * BLK), jnp.float32),
        in_specs=[SMEM, SMEM, VMEM],
        out_specs=VMEM,
        compiler_params=params(8),
        name="extract",
    )(place, table, kern)


def add_kernel(one_ref, two_ref, *outs):
    for at, out_ref in enumerate(outs):
        out_ref[...] = one_ref[at] + two_ref[at]


def add_call(one, two):
    return pl.pallas_call(
        add_kernel,
        out_shape=[jax.ShapeDtypeStruct(one.shape[1:], one.dtype)] * one.shape[0],
        in_specs=[VMEM, VMEM],
        out_specs=[VMEM] * one.shape[0],
        compiler_params=params(8),
        name="add",
    )(one, two)


def owner_kernel(place, table, one_ref, two_ref, three_ref, four_ref, out_ref, work):
    total = (one_ref[...] + two_ref[...]) + (three_ref[...] + four_ref[...])
    width = total.shape[1]
    work[:, :width] = total
    work[:, width:] = jnp.zeros((8, work.shape[1] - width), jnp.float32)
    for chip in range(out_ref.shape[0]):
        start = table[8, chip * 2 + place[3]]
        column = pl.multiple_of(start // 8 * 128, 128)
        shift = lax.rem(384 - lax.rem(start, 8) * BLK, 384)
        out_ref[chip] = pltpu.roll(work[:, pl.ds(column, 384)], shift, 1)[:, :256]


def owner_call(place, table, parts):
    return pl.pallas_call(
        owner_kernel,
        out_shape=jax.ShapeDtypeStruct((32, 8, 256), jnp.float32),
        in_specs=[SMEM, SMEM] + [VMEM] * 4,
        out_specs=VMEM,
        scratch_shapes=[pltpu.VMEM((8, parts[0].shape[1] + 384), jnp.float32)],
        compiler_params=params(8),
        name="owner",
    )(place, table, *parts)


def last_kernel(place, table, parts_ref, out_ref):
    total = parts_ref[0]
    for chip in range(1, parts_ref.shape[0]):
        total = total + parts_ref[chip]
    held = table[9, (place[0] * 4 + place[2]) * 2 + place[3]]
    for slot in range(CAP):
        tile = total[:, slot // 8 * 128 : slot // 8 * 128 + 128]
        tile = pltpu.roll(tile, (128 - slot % 8 * BLK) % 128, 1)
        out_ref[slot] = jnp.where(slot < held, tile[:, :BLK], 0.0)


def last_call(place, table, parts):
    return pl.pallas_call(
        last_kernel,
        out_shape=jax.ShapeDtypeStruct((CAP, 8, BLK), jnp.float32),
        in_specs=[SMEM, SMEM, VMEM],
        out_specs=VMEM,
        compiler_params=params(8),
        name="last",
    )(place, table, parts)


def pack_kernel(place, own_ref, other_ref, out_ref, work):
    core = place[3]
    width = own_ref.shape[2]
    for block in range(width // 128):
        lanes = pl.ds(block * 128, 128)
        rows = []
        for part in range(2):
            own, other = own_ref[part, :, lanes], other_ref[part, :, lanes]
            rows += [jnp.where(core == 0, own, other), jnp.where(core == 0, other, own)]
        rows = jnp.concatenate(rows + rows, axis=0)
        work[block * 128 : (block + 1) * 128, :] = rows.T
    half = lax.broadcasted_iota(jnp.int32, (8, 128), 1) < 64
    for chip in range(32):
        at = pl.multiple_of(chip * 80 + core * 40, 8)
        tiles = [work[pl.ds(at + 8 * t, 8), :] for t in range(5)]
        out_ref[chip * 20 : chip * 20 + 8, :] = jnp.where(half, tiles[0], tiles[1])
        out_ref[chip * 20 + 8 : chip * 20 + 16, :] = jnp.where(half, tiles[2], tiles[3])
        last = jnp.where(half, tiles[4], pltpu.roll(tiles[4], 4, 0))
        out_ref[chip * 20 + 16 : chip * 20 + 20, :] = last[:4]


def pack_call(place, own, other):
    width = own.shape[2]
    return pl.pallas_call(
        pack_kernel,
        out_shape=jax.ShapeDtypeStruct((32 * 20, 128), jnp.float32),
        in_specs=[SMEM, VMEM, VMEM],
        out_specs=VMEM,
        scratch_shapes=[pltpu.VMEM((width, 128), jnp.float32)],
        name="pack",
    )(place, own, other)


def unpack_kernel(place, table, in_ref, columns_ref, keep_ref, give_ref):
    core = place[3]
    quarter = lax.broadcasted_iota(jnp.int32, (8, 128), 1) // 32
    upper = lax.broadcasted_iota(jnp.int32, (8, 128), 0) < 4
    for group in range(8):
        tiles = [[None] * 5 for _ in range(2)]
        for u in range(4):
            at = (group * 4 + u) * 20
            one, two = in_ref[at : at + 8, :], in_ref[at + 8 : at + 16, :]
            end = in_ref[at + 12 : at + 20, :]
            end = jnp.where(upper, pltpu.roll(end, 4, 0), pltpu.roll(end, 64, 1))
            for t, (source, first) in enumerate(((one, 0), (one, 64), (two, 0), (two, 64), (end, 0))):
                for part in range(2):
                    by = (u * 32 - first - part * 32) % 128
                    turned = pltpu.roll(source, by, 1) if by else source
                    old = tiles[part][t]
                    tiles[part][t] = turned if old is None else jnp.where(quarter == u, turned, old)
        for part in range(2):
            for t in range(5):
                row = part * 40 + t * 8
                columns_ref[row : row + 8, group * 128 : (group + 1) * 128] = tiles[part][t]
    select(table, 1 - core, columns_ref, give_ref)
    select(table, core, columns_ref, keep_ref)


def select(table, which, columns_ref, out_ref):
    eighth = lax.broadcasted_iota(jnp.int32, (80, 128), 1) // BLK
    for group in range(2):
        slab = None
        for u in range(8):
            block = table[10, which * (USED // 2) + group * 8 + u]
            column = pl.multiple_of(block // 8 * 128, 128)
            by = lax.rem(u * BLK + 128 - lax.rem(block, 8) * BLK, 128)
            turned = pltpu.roll(columns_ref[:, pl.ds(column, 128)], by, 1)
            slab = turned if slab is None else jnp.where(eighth == u, turned, slab)
        out_ref[:, group * 128 : (group + 1) * 128] = slab


def unpack_call(place, table, pieces):
    return pl.pallas_call(
        unpack_kernel,
        out_shape=(
            jax.ShapeDtypeStruct((80, 1024), jnp.float32),
            jax.ShapeDtypeStruct((80, HALF), jnp.float32),
            jax.ShapeDtypeStruct((80, HALF), jnp.float32),
        ),
        in_specs=[SMEM, SMEM, VMEM],
        out_specs=(VMEM, VMEM, VMEM),
        compiler_params=params(8),
        name="unpack",
    )(place, table, pieces)


def shard_kernel(place, keep_ref, take_ref, out_ref):
    core = place[3]
    for part in range(2):
        out_ref[pl.ds(pl.multiple_of(part * 80 + core * 40, 8), 40), :] = keep_ref[part * 40 : part * 40 + 40, :]
        out_ref[pl.ds(pl.multiple_of(part * 80 + 40 - core * 40, 8), 40), :] = take_ref[part * 40 : part * 40 + 40, :]


def shard_call(place, keep, take):
    return pl.pallas_call(
        shard_kernel,
        out_shape=jax.ShapeDtypeStruct((160, HALF), jnp.float32),
        in_specs=[SMEM, VMEM, VMEM],
        out_specs=VMEM,
        compiler_params=params(8),
        name="shard",
    )(place, keep, take)


def after(array, *others):
    return lax.optimization_barrier((array, *others))[0]


def shards(densities, screened, pairs, owners):
    span = screened.shape[2]
    place = jnp.stack([lax.axis_index(axis) for axis in ("z", "x", "y", "core")]).astype(jnp.int32)
    shift = lambda array, axis, by: lax.ppermute(array, axis, ring(lax.axis_size(axis), by))
    swap = lambda array: lax.ppermute(array, "core", SWAP)
    join = lambda *arrays: jnp.concatenate(arrays, axis=0)
    hold = lax.optimization_barrier

    pieces = pack_call(place, densities, swap(densities))
    table = plan_call(place, after(pairs, pieces), owners.reshape(1, -1))
    mine = lax.all_to_all(pieces.reshape(32, 1, -1), ("z", "y"), 0, 0, tiled=True).reshape(pieces.shape)

    screen = screened.reshape(2 * 4 * span, -1)
    mine, other = hold((mine, swap(after(screen, pieces))))

    columns, keep, give = unpack_call(place, table, mine)
    shard = shard_call(place, keep, swap(give))

    block = 2 * SPAN
    below2, above2 = shift(shard, "z", 2), shift(shard, "z", -2)
    below, above, columns = hold((shift(shard, "z", 1), shift(shard, "z", -1), columns))
    first = join(shard, below, above)
    first_down, first_up = shift(first, "y", 1), shift(first, "y", -1)
    around = [columns, shift(columns, "x", 1), None, None]
    below2, above2, first, columns = hold((below2, above2, first, columns))
    second = join(below2, above2)
    second_down, second_up = shift(second, "y", 1), shift(second, "y", -1)
    around[3] = shift(columns, "x", 3)
    screens = screen_call(place, after(screen, second), other)
    first_down, first_up, around[1], below2, above2, *screens = hold(
        (first_down, first_up, around[1], below2, above2, *screens)
    )
    below3, above3 = shift(below2, "z", 1), shift(above2, "z", -1)
    below3, above3, second_down, second_up, around[3] = hold((below3, above3, second_down, second_up, around[3]))

    z_below = shift(join(second_down[:block], second_up[:block], below3[:SPAN]), "z", 1)
    z_above = shift(join(second_down[block:], second_up[block:], above3[SPAN:]), "z", -1)
    two_down = shift(join(first_down[: 3 * SPAN], second_down[:block]), "y", 1)
    two_up = shift(join(first_up[3 * SPAN :], second_up[block:]), "y", -1)
    around[2] = shift(after(columns, below3), "x", 2)
    swapped = [swap(around[0]), swap(around[1]), None, swap(around[3])]
    two_down, two_up, z_below, z_above, around[2], swapped[0], swapped[1], swapped[3] = hold(
        (two_down, two_up, z_below, z_above, around[2], swapped[0], swapped[1], swapped[3])
    )

    y_below, y_above = shift(z_below[:block], "y", 1), shift(z_above[block : 2 * block], "y", -1)
    far_below, far_above = shift(z_below[:block], "z", 1), shift(z_above[block : 2 * block], "z", -1)
    rights = (first, first_down, first_up, second, second_down, second_up, two_down, two_up)
    total = group_call(near_runs, len(NEAR), place, rights, screens[:2], ())
    swapped[2] = swap(around[2])
    y_below, y_above, far_below, far_above, total, swapped[2] = hold(
        (y_below, y_above, far_below, far_above, total, swapped[2])
    )

    across_low, across_high = shift(far_below[:SPAN], "y", 1), shift(far_above[SPAN:], "y", -1)
    rights = (below3, above3, z_below, z_above, y_below, y_above)
    total = group_call(middle_runs, len(MIDDLE), place, rights, screens[2:4], (total,))
    left_high, left_low = left_call(place, around + swapped)
    across_low, across_high, total, left_high, left_low = hold((across_low, across_high, total, left_high, left_low))
    rights = (z_below, z_above, far_below, far_above, across_low, across_high)
    give, kern = pair_call(place, table, rights, screens[4:], total, left_high, left_low)

    parts = add_call(extract_call(place, table, kern), swap(give))
    parts = [parts[0]] + [shift(parts[by], "x", by) for by in (1, 2, 3)]
    parts = owner_call(place, table, parts)
    parts = lax.all_to_all(parts, ("z", "y"), 0, 0, tiled=True)
    return last_call(place, table, parts).reshape(1, CAP, 2, 4, BLK)


def solution(mesh):
    fine = Mesh(mesh.devices.reshape(8, 4, 2, 4), ("z", "y", "core", "x"))
    in_specs = (P(None, BAND, "x"), P(None, None, BAND, "x"), P(), P())
    out_specs = P(BAND, None, None, "x", None)
    return jax.shard_map(shards, mesh=fine, in_specs=in_specs, out_specs=out_specs, check_vma=False)
```

```python
import functools

import jax
import jax.numpy as jnp
from jax import lax
from jax.experimental import pallas as pl
from jax.experimental.pallas import tpu as pltpu
from jax.sharding import Mesh
from jax.sharding import PartitionSpec as P

NG = 10240
CAP = 12
BLK = 16
USED = 32
HALF = USED // 2 * BLK
BAND = ("z", "y", "core")
SWAP = ((0, 1), (1, 0))
SMEM = pl.BlockSpec(memory_space=pltpu.SMEM)
VMEM = pl.BlockSpec(memory_space=pltpu.VMEM)
SPAN = 80
PLANE = 320
NEAR = (0, 7, 1, 6, 2)
MIDDLE = (5, 3)
FAR = (4,)
ROOM = 224


def ring(n, shift):
    return [(i, (i + shift) % n) for i in range(n)]


def params(mib):
    return pltpu.CompilerParams(vmem_limit_bytes=mib * 1024 * 1024)


def split(x):
    high = x.astype(jnp.bfloat16)
    return high, (x - high.astype(jnp.float32)).astype(jnp.bfloat16)


def dot(former, latter):
    return jnp.dot(former, latter, preferred_element_type=jnp.float32)


def dot3(high, low, former, latter):
    return dot(high, former) + dot(high, latter) + dot(low, former)


def plan_kernel(place, pairs_ref, owners_ref, out_ref):
    size = 256
    down = lax.broadcasted_iota(jnp.int32, (size, size), 0)
    across = lax.broadcasted_iota(jnp.int32, (size, size), 1)
    one = lambda condition: jnp.where(condition, 1.0, 0.0)
    to_row = lambda column: jnp.sum(jnp.where(down == across, column, 0.0), axis=0, keepdims=True)
    to_column = lambda row: jnp.sum(jnp.where(down == across, row, 0.0), axis=1, keepdims=True)
    rows, columns = down.astype(jnp.float32), across.astype(jnp.float32)
    left, right = pairs_ref[:, 0:1].astype(jnp.float32), pairs_ref[:, 1:2].astype(jnp.float32)
    owner_row = owners_ref[...].astype(jnp.float32)
    owner = to_column(owner_row)

    used = jnp.max(one(right == columns), axis=0, keepdims=True)
    used_column = to_column(used)
    rank = jnp.sum(jnp.where(columns < rows, used, 0.0), axis=1, keepdims=True)
    used_list = jnp.sum(jnp.where((rank == columns) & (used_column > 0), rows, 0.0), axis=0, keepdims=True)
    right_rank = jnp.sum(jnp.where(columns < right, used, 0.0), axis=1, keepdims=True)

    parity = lambda value: value - 2.0 * jnp.floor(value * 0.5)
    count = jnp.sum(one(owner == columns), axis=0, keepdims=True)
    same = parity(rows) == parity(columns)
    offset = jnp.sum(jnp.where((rows < columns) & same, to_column(count), 0.0), axis=0, keepdims=True)
    ahead = (owner_row < owner) | ((owner_row == owner) & (across < down))
    ahead = ahead & (parity(owner_row) == parity(owner))
    position = jnp.sum(one(ahead), axis=1, keepdims=True)

    core = place[3].astype(jnp.float32)
    local = right_rank - core * (USED // 2)
    here = (local >= 0) & (local < USED // 2)
    local = jnp.where(here, local, 0.0)
    lane = lax.broadcasted_iota(jnp.int32, (1, size), 1)
    groups = jnp.zeros((1, size), jnp.float32)
    for half in range(2):
        hit = (position == columns) & (parity(owner) == half)
        pick = lambda column: jnp.sum(jnp.where(hit, column, 0.0), axis=0, keepdims=True).astype(jnp.int32)
        at = pick(local)
        out_ref[4 * half : 4 * half + 1, :] = pick(left) * BLK
        out_ref[4 * half + 1 : 4 * half + 2, :] = at // 8 * 128
        out_ref[4 * half + 2 : 4 * half + 3, :] = (lane + 8 - at % 8) % 8 * BLK
        out_ref[4 * half + 3 : 4 * half + 4, :] = jnp.where(pick(one(here)) > 0, lane % 8, -1)
        total = jnp.sum(one(parity(owner_row) == half))
        groups = jnp.where(lane == half, jnp.floor((total + 7.0) / 8.0), groups)
    for at, row in enumerate((offset, count, used_list, groups)):
        out_ref[8 + at : 9 + at, :] = row.astype(jnp.int32)


def plan_call(place, pairs, owners):
    return pl.pallas_call(
        plan_kernel,
        out_shape=jax.ShapeDtypeStruct((16, pairs.shape[0]), jnp.int32),
        in_specs=[SMEM, VMEM, VMEM],
        out_specs=VMEM,
        compiler_params=params(8),
        name="plan",
    )(place, pairs, owners)


def padded(planes):
    return (len(planes) * PLANE + 127) // 128 * 128


def screen_kernel(place, own_ref, other_ref, *outs):
    z = place[0]
    rows = 16
    lane = lax.broadcasted_iota(jnp.int32, (rows, 128), 1)

    def plane_of(ref, row, delta, offset):
        plane = lax.rem(z + delta, 8)
        odd = lax.rem(plane, 2)
        column = pl.multiple_of(plane * PLANE - odd * 64, 128)
        window = ref[row, pl.ds(column, 384)]
        turned = pltpu.roll(window, 64 if offset else 320, 1)
        return jnp.where((odd == 1) if offset else (odd == 0), window, turned)

    for source, ref in enumerate((own_ref, other_ref)):

        def body(step, carry, source=source, ref=ref):
            part = step // 10
            row = pl.ds(pl.multiple_of(step * rows, rows), rows)
            target = pl.multiple_of(part * PLANE + source * (PLANE // 2) + (step - part * 10) * rows, rows)
            for group, planes in enumerate((NEAR, MIDDLE, FAR)):
                for at in range(0, len(planes), 2):
                    a = plane_of(ref, row, planes[at], False)
                    if at + 1 < len(planes):
                        b = plane_of(ref, row, planes[at + 1], True)
                        middle = jnp.where(lane < 64, a[:, 256:], b[:, :128])
                        whole = jnp.concatenate([a[:, :256], middle, b[:, 128:]], axis=1)
                    else:
                        whole = jnp.concatenate([a[:, :256], jnp.where(lane < 64, a[:, 256:], 0.0)], axis=1)
                    top, rest = split(whole)
                    columns = slice(at * PLANE, at * PLANE + whole.shape[1])
                    outs[2 * group][pl.ds(target, rows), columns] = top
                    outs[2 * group + 1][pl.ds(target, rows), columns] = rest
            return carry

        lax.fori_loop(0, 20, body, 0)


def screen_call(place, own, other):
    shapes = [
        jax.ShapeDtypeStruct((2 * own.shape[0], padded(planes)), jnp.bfloat16)
        for planes in (NEAR, MIDDLE, FAR)
        for _ in range(2)
    ]
    return pl.pallas_call(
        screen_kernel,
        out_shape=shapes,
        in_specs=[SMEM, VMEM, VMEM],
        out_specs=[VMEM] * 6,
        compiler_params=params(20),
        name="screen",
    )(place, own, other)


def left_kernel(place, *refs):
    pieces, (high_ref, low_ref, work) = refs[:8], refs[8:]
    x = place[1]
    span = pieces[0].shape[0] // 2
    for core in range(2):
        for shift in range(4):
            shard = lax.rem(x - shift + 4, 4)
            for part in range(2):
                row = pl.multiple_of(part * 8 * span + core * 4 * span + shard * span, 8)
                work[pl.ds(row, span), :] = pieces[core * 4 + shift][part * span : (part + 1) * span, :]

    def body(block, carry):
        at = pl.ds(pl.multiple_of(block * 128, 128), 128)
        high_ref[at, :], low_ref[at, :] = split(work[:, at].T)
        return carry

    lax.fori_loop(0, work.shape[1] // 128, body, 0)


def left_call(place, pieces):
    depth, width = pieces[0].shape
    shape = jax.ShapeDtypeStruct((width, 8 * depth), jnp.bfloat16)
    return pl.pallas_call(
        left_kernel,
        out_shape=(shape, shape),
        in_specs=[SMEM] + [VMEM] * 8,
        out_specs=(VMEM, VMEM),
        scratch_shapes=[pltpu.VMEM((8 * depth, width), jnp.float32)],
        compiler_params=params(20),
        name="left",
    )(place, *pieces)


def load_right(place, runs, planes, high, low):
    y = place[2]
    for delta, ref, start, first, count in runs:
        spread = lax.rem(y + delta, 4) * SPAN

        def body(step, carry, ref=ref, start=start, first=first, spread=spread):
            unit = first + step
            row = pl.ds(pl.multiple_of(unit // 2 * PLANE + spread, 16), SPAN)
            column = pl.ds(pl.multiple_of(lax.rem(unit, 2) * HALF, HALF), HALF)
            top, rest = split(ref[pl.ds(pl.multiple_of(start + step * SPAN, 8), SPAN), :])
            high[row, column] = top
            low[row, column] = rest
            return carry

        lax.fori_loop(0, count, body, 0)
    used = planes * PLANE
    if used < high.shape[0]:
        for ref in (high, low):
            ref[used:, :] = jnp.zeros((ref.shape[0] - used, ref.shape[1]), ref.dtype)


def near_runs(first, first_down, first_up, second, second_down, second_up, two_down, two_up):
    skip = 3 * SPAN
    return (
        ((0, first, 0, 0, 6), (3, first_down, 0, 0, 6), (1, first_up, 0, 0, 6))
        + ((0, second, 0, 6, 4), (3, second_down, 0, 6, 4), (1, second_up, 0, 6, 4))
        + ((2, two_down, 0, 0, 3), (2, two_up, 0, 3, 3), (2, two_down, skip, 6, 2), (2, two_up, skip, 8, 2))
    )


def middle_runs(z_below, z_above, y_below, y_above):
    runs = ()
    for first, sides, across in ((0, z_below, y_below), (2, z_above, y_above)):
        runs += ((3, sides, 0, first, 2), (1, sides, 2 * SPAN, first, 2), (0, sides, 4 * SPAN, first, 2))
        runs += ((2, across, 0, first, 2),)
    return runs


def far_runs(below, above, across_low, across_high):
    return (
        ((3, below, 0, 0, 2), (1, above, 0, 0, 2), (0, below, 2 * SPAN, 0, 1), (0, above, 2 * SPAN, 1, 1))
        + ((2, across_low, 0, 0, 1), (2, across_high, 0, 1, 1))
    )


def group_kernel(runs, planes, place, *refs):
    count = len(refs) - 5 - (runs is middle_runs)
    rights, (high_ref, low_ref), rest = refs[:count], refs[count : count + 2], refs[count + 2 :]
    out_ref, rh, rl = rest[-3:]
    load_right(place, runs(*rights), planes, rh, rl)
    value = dot3(high_ref[...], low_ref[...], rh[...], rl[...])
    out_ref[...] = value if len(rest) == 3 else value + rest[0][...]


def group_call(runs, planes, place, rights, screens, total):
    rows, width = screens[0].shape
    return pl.pallas_call(
        functools.partial(group_kernel, runs, planes),
        out_shape=jax.ShapeDtypeStruct((rows, 2 * HALF), jnp.float32),
        in_specs=[SMEM] + [VMEM] * (len(rights) + 2 + len(total)),
        out_specs=VMEM,
        scratch_shapes=[pltpu.VMEM((width, 2 * HALF), jnp.bfloat16)] * 2,
        compiler_params=params(32),
        name="group",
    )(place, *rights, *screens, *total)


def pair_kernel(place, table, *refs):
    rights, (high_ref, low_ref, sum_ref, left_high, left_low, give_ref, kern, rh, rl) = refs[:4], refs[4:]
    load_right(place, far_runs(*rights), len(FAR), rh, rl)
    product = sum_ref[...] + dot3(high_ref[...], low_ref[...], rh[...], rl[...])
    mid = product.shape[0] // 2
    real = product[:mid, :HALF] - product[mid:, HALF:]
    imag = product[mid:, :HALF] + product[:mid, HALF:]
    applied = NG ** (-0.5) * jnp.concatenate(
        [jnp.concatenate([real, imag], axis=0), jnp.concatenate([imag, -real], axis=0)], axis=1
    )
    kern[...] = dot3(left_high[...], left_low[...], *split(applied))

    extract(place, table, 1 - place[3], kern, give_ref)


def extract(place, table, half, kern, out_ref):
    at = lambda x: lax.rem(x + 4 - place[1], 4)
    lane = lax.broadcasted_iota(jnp.int32, (8, 128), 1) // BLK
    upper = lax.broadcasted_iota(jnp.int32, (8, 128), 0) < 4

    def groups(pair, carry):
        for g in (pair * 2, pair * 2 + 1):
            tiles = [[jnp.zeros((8, 128), jnp.float32) for _ in range(2)] for _ in range(2)]
            for u in range(8):
                slot = g * 8 + u
                row = pl.multiple_of(table[4 * half, slot], BLK)
                column = pl.multiple_of(table[4 * half + 1, slot], 128)
                shift = table[4 * half + 2, slot]
                target = table[4 * half + 3, slot]
                for part in range(2):
                    for side in range(2):
                        tile = kern[pl.ds(row + side * 8, 8), pl.ds(column + part * HALF, 128)]
                        tile = pltpu.roll(tile, shift, 1)
                        tiles[part][side] = jnp.where(lane == target, tile, tiles[part][side])
            lanes = pl.ds(pl.multiple_of(g * 128, 128), 128)
            for side in range(2):
                real, imag = tiles[0][side], tiles[1][side]
                out_ref[at(2 * side), :, lanes] = jnp.where(upper, real, pltpu.roll(imag, 4, 0))
                out_ref[at(2 * side + 1), :, lanes] = jnp.where(upper, pltpu.roll(real, 4, 0), imag)
        return carry

    out_ref[...] = jnp.zeros_like(out_ref)
    lax.fori_loop(0, (table[11, half] + 1) // 2, groups, 0)


def pair_call(place, table, rights, screens, total, left_high, left_low):
    rows = left_high.shape[0]
    return pl.pallas_call(
        pair_kernel,
        out_shape=(
            jax.ShapeDtypeStruct((4, 8, ROOM * BLK), jnp.float32),
            jax.ShapeDtypeStruct((rows, 2 * HALF), jnp.float32),
        ),
        in_specs=[SMEM, SMEM] + [VMEM] * (len(rights) + 5),
        out_specs=(VMEM, VMEM),
        scratch_shapes=[pltpu.VMEM((screens[0].shape[1], 2 * HALF), jnp.bfloat16)] * 2,
        compiler_params=params(24),
        name="pair",
    )(place, table, *rights, *screens, total, left_high, left_low)


def extract_kernel(place, table, kern, out_ref):
    extract(place, table, place[3], kern, out_ref)


def extract_call(place, table, kern):
    return pl.pallas_call(
        extract_kernel,
        out_shape=jax.ShapeDtypeStruct((4, 8, ROOM * BLK), jnp.float32),
        in_specs=[SMEM, SMEM, VMEM],
        out_specs=VMEM,
        compiler_params=params(8),
        name="extract",
    )(place, table, kern)


def add_kernel(one_ref, two_ref, *outs):
    for at, out_ref in enumerate(outs):
        out_ref[...] = one_ref[at] + two_ref[at]


def add_call(one, two):
    return pl.pallas_call(
        add_kernel,
        out_shape=[jax.ShapeDtypeStruct(one.shape[1:], one.dtype)] * one.shape[0],
        in_specs=[VMEM, VMEM],
        out_specs=[VMEM] * one.shape[0],
        compiler_params=params(8),
        name="add",
    )(one, two)


def owner_kernel(place, table, one_ref, two_ref, three_ref, four_ref, out_ref, work):
    total = (one_ref[...] + two_ref[...]) + (three_ref[...] + four_ref[...])
    width = total.shape[1]
    work[:, :width] = total
    work[:, width:] = jnp.zeros((8, work.shape[1] - width), jnp.float32)
    for chip in range(out_ref.shape[0]):
        start = table[8, chip * 2 + place[3]]
        column = pl.multiple_of(start // 8 * 128, 128)
        shift = lax.rem(384 - lax.rem(start, 8) * BLK, 384)
        out_ref[chip] = pltpu.roll(work[:, pl.ds(column, 384)], shift, 1)[:, :256]


def owner_call(place, table, parts):
    return pl.pallas_call(
        owner_kernel,
        out_shape=jax.ShapeDtypeStruct((32, 8, 256), jnp.float32),
        in_specs=[SMEM, SMEM] + [VMEM] * 4,
        out_specs=VMEM,
        scratch_shapes=[pltpu.VMEM((8, parts[0].shape[1] + 384), jnp.float32)],
        compiler_params=params(8),
        name="owner",
    )(place, table, *parts)


def last_kernel(place, table, parts_ref, out_ref):
    total = parts_ref[0]
    for chip in range(1, parts_ref.shape[0]):
        total = total + parts_ref[chip]
    held = table[9, (place[0] * 4 + place[2]) * 2 + place[3]]
    for slot in range(CAP):
        tile = total[:, slot // 8 * 128 : slot // 8 * 128 + 128]
        tile = pltpu.roll(tile, (128 - slot % 8 * BLK) % 128, 1)
        out_ref[slot] = jnp.where(slot < held, tile[:, :BLK], 0.0)


def last_call(place, table, parts):
    return pl.pallas_call(
        last_kernel,
        out_shape=jax.ShapeDtypeStruct((CAP, 8, BLK), jnp.float32),
        in_specs=[SMEM, SMEM, VMEM],
        out_specs=VMEM,
        compiler_params=params(8),
        name="last",
    )(place, table, parts)


def pack_kernel(place, own_ref, other_ref, out_ref, work):
    core = place[3]
    width = own_ref.shape[2]
    for block in range(width // 128):
        lanes = pl.ds(block * 128, 128)
        rows = []
        for part in range(2):
            own, other = own_ref[part, :, lanes], other_ref[part, :, lanes]
            rows += [jnp.where(core == 0, own, other), jnp.where(core == 0, other, own)]
        rows = jnp.concatenate(rows + rows, axis=0)
        work[block * 128 : (block + 1) * 128, :] = rows.T
    half = lax.broadcasted_iota(jnp.int32, (8, 128), 1) < 64
    for chip in range(32):
        at = pl.multiple_of(chip * 80 + core * 40, 8)
        tiles = [work[pl.ds(at + 8 * t, 8), :] for t in range(5)]
        out_ref[chip * 20 : chip * 20 + 8, :] = jnp.where(half, tiles[0], tiles[1])
        out_ref[chip * 20 + 8 : chip * 20 + 16, :] = jnp.where(half, tiles[2], tiles[3])
        last = jnp.where(half, tiles[4], pltpu.roll(tiles[4], 4, 0))
        out_ref[chip * 20 + 16 : chip * 20 + 20, :] = last[:4]


def pack_call(place, own, other):
    width = own.shape[2]
    return pl.pallas_call(
        pack_kernel,
        out_shape=jax.ShapeDtypeStruct((32 * 20, 128), jnp.float32),
        in_specs=[SMEM, VMEM, VMEM],
        out_specs=VMEM,
        scratch_shapes=[pltpu.VMEM((width, 128), jnp.float32)],
        name="pack",
    )(place, own, other)


def unpack_kernel(place, table, in_ref, columns_ref, keep_ref, give_ref):
    core = place[3]
    quarter = lax.broadcasted_iota(jnp.int32, (8, 128), 1) // 32
    upper = lax.broadcasted_iota(jnp.int32, (8, 128), 0) < 4
    for group in range(8):
        tiles = [[None] * 5 for _ in range(2)]
        for u in range(4):
            at = (group * 4 + u) * 20
            one, two = in_ref[at : at + 8, :], in_ref[at + 8 : at + 16, :]
            end = in_ref[at + 12 : at + 20, :]
            end = jnp.where(upper, pltpu.roll(end, 4, 0), pltpu.roll(end, 64, 1))
            for t, (source, first) in enumerate(((one, 0), (one, 64), (two, 0), (two, 64), (end, 0))):
                for part in range(2):
                    by = (u * 32 - first - part * 32) % 128
                    turned = pltpu.roll(source, by, 1) if by else source
                    old = tiles[part][t]
                    tiles[part][t] = turned if old is None else jnp.where(quarter == u, turned, old)
        for part in range(2):
            for t in range(5):
                row = part * 40 + t * 8
                columns_ref[row : row + 8, group * 128 : (group + 1) * 128] = tiles[part][t]
    select(table, 1 - core, columns_ref, give_ref)
    select(table, core, columns_ref, keep_ref)


def select(table, which, columns_ref, out_ref):
    eighth = lax.broadcasted_iota(jnp.int32, (80, 128), 1) // BLK
    for group in range(2):
        slab = None
        for u in range(8):
            block = table[10, which * (USED // 2) + group * 8 + u]
            column = pl.multiple_of(block // 8 * 128, 128)
            by = lax.rem(u * BLK + 128 - lax.rem(block, 8) * BLK, 128)
            turned = pltpu.roll(columns_ref[:, pl.ds(column, 128)], by, 1)
            slab = turned if slab is None else jnp.where(eighth == u, turned, slab)
        out_ref[:, group * 128 : (group + 1) * 128] = slab


def unpack_call(place, table, pieces):
    return pl.pallas_call(
        unpack_kernel,
        out_shape=(
            jax.ShapeDtypeStruct((80, 1024), jnp.float32),
            jax.ShapeDtypeStruct((80, HALF), jnp.float32),
            jax.ShapeDtypeStruct((80, HALF), jnp.float32),
        ),
        in_specs=[SMEM, SMEM, VMEM],
        out_specs=(VMEM, VMEM, VMEM),
        compiler_params=params(8),
        name="unpack",
    )(place, table, pieces)


def shard_kernel(place, keep_ref, take_ref, out_ref):
    core = place[3]
    for part in range(2):
        out_ref[pl.ds(pl.multiple_of(part * 80 + core * 40, 8), 40), :] = keep_ref[part * 40 : part * 40 + 40, :]
        out_ref[pl.ds(pl.multiple_of(part * 80 + 40 - core * 40, 8), 40), :] = take_ref[part * 40 : part * 40 + 40, :]


def shard_call(place, keep, take):
    return pl.pallas_call(
        shard_kernel,
        out_shape=jax.ShapeDtypeStruct((160, HALF), jnp.float32),
        in_specs=[SMEM, VMEM, VMEM],
        out_specs=VMEM,
        compiler_params=params(8),
        name="shard",
    )(place, keep, take)


def after(array, *others):
    return lax.optimization_barrier((array, *others))[0]


def shards(densities, screened, pairs, owners):
    span = screened.shape[2]
    place = jnp.stack([lax.axis_index(axis) for axis in ("z", "x", "y", "core")]).astype(jnp.int32)
    shift = lambda array, axis, by: lax.ppermute(array, axis, ring(lax.axis_size(axis), by))
    swap = lambda array: lax.ppermute(array, "core", SWAP)
    join = lambda *arrays: jnp.concatenate(arrays, axis=0)
    hold = lax.optimization_barrier

    pieces = pack_call(place, densities, swap(densities))
    table = plan_call(place, after(pairs, pieces), owners.reshape(1, -1))
    mine = lax.all_to_all(pieces.reshape(32, 1, -1), ("z", "y"), 0, 0, tiled=True).reshape(pieces.shape)

    screen = screened.reshape(2 * 4 * span, -1)
    mine, other = hold((mine, swap(after(screen, pieces))))

    columns, keep, give = unpack_call(place, table, mine)
    shard = shard_call(place, keep, swap(give))

    block = 2 * SPAN
    below2, above2 = shift(shard, "z", 2), shift(shard, "z", -2)
    below, above, columns = hold((shift(shard, "z", 1), shift(shard, "z", -1), columns))
    first = join(shard, below, above)
    first_down, first_up = shift(first, "y", 1), shift(first, "y", -1)
    around = [columns, shift(columns, "x", 1), None, None]
    below2, above2, first, columns = hold((below2, above2, first, columns))
    second = join(below2, above2)
    second_down, second_up = shift(second, "y", 1), shift(second, "y", -1)
    around[3] = shift(columns, "x", 3)
    screens = screen_call(place, after(screen, second), other)
    first_down, first_up, around[1], below2, above2, *screens = hold(
        (first_down, first_up, around[1], below2, above2, *screens)
    )
    second_down, second_up, first_down, around[3] = hold((second_down, second_up, first_down, around[3]))

    z_below = shift(join(second_down[:block], second_up[:block], second[:block]), "z", 1)
    z_above = shift(join(second_down[block:], second_up[block:], second[block:]), "z", -1)
    two_down = shift(join(first_down[: 3 * SPAN], second_down[:block]), "y", 1)
    two_up = shift(join(first_up[3 * SPAN :], second_up[block:]), "y", -1)
    around[2] = shift(after(columns, second_down), "x", 2)
    swapped = [swap(columns), swap(around[1]), None, None]
    two_down, two_up, z_below, z_above, around[2], swapped[0], swapped[1] = hold(
        (two_down, two_up, z_below, z_above, around[2], swapped[0], swapped[1])
    )

    y_below, y_above = shift(z_below[:block], "y", 1), shift(z_above[block : 2 * block], "y", -1)
    far_below = shift(join(z_below[:block], z_below[2 * block : 2 * block + SPAN]), "z", 1)
    far_above = shift(join(z_above[block : 2 * block], z_above[2 * block + SPAN :]), "z", -1)
    rights = (first, first_down, first_up, second, second_down, second_up, two_down, two_up)
    total = group_call(near_runs, len(NEAR), place, rights, screens[:2], ())
    swapped[2:] = [swap(array) for array in around[2:]]
    y_below, y_above, far_below, far_above, total, *swapped[2:] = hold(
        (y_below, y_above, far_below, far_above, total, *swapped[2:])
    )

    across_low, across_high = shift(far_below[:SPAN], "y", 1), shift(far_above[SPAN : 2 * SPAN], "y", -1)
    rights = (z_below, z_above, y_below, y_above)
    total = group_call(middle_runs, len(MIDDLE), place, rights, screens[2:4], (total,))
    left_high, left_low = left_call(place, around + swapped)
    across_low, across_high, total, left_high, left_low = hold((across_low, across_high, total, left_high, left_low))
    rights = (far_below, far_above, across_low, across_high)
    give, kern = pair_call(place, table, rights, screens[4:], total, left_high, left_low)

    parts = add_call(extract_call(place, table, kern), swap(give))
    parts = [parts[0]] + [shift(parts[by], "x", by) for by in (1, 2, 3)]
    parts = owner_call(place, table, parts)
    parts = lax.all_to_all(parts, ("z", "y"), 0, 0, tiled=True)
    return last_call(place, table, parts).reshape(1, CAP, 2, 4, BLK)


def solution(mesh):
    fine = Mesh(mesh.devices.reshape(8, 4, 2, 4), ("z", "y", "core", "x"))
    in_specs = (P(None, BAND, "x"), P(None, None, BAND, "x"), P(), P())
    out_specs = P(BAND, None, None, "x", None)
    return jax.shard_map(shards, mesh=fine, in_specs=in_specs, out_specs=out_specs, check_vma=False)
```

```python
import functools

import jax
import jax.numpy as jnp
from jax import lax
from jax.experimental import pallas as pl
from jax.experimental.pallas import tpu as pltpu
from jax.sharding import Mesh
from jax.sharding import PartitionSpec as P

NG = 10240
CAP = 12
BLK = 16
USED = 32
HALF = USED // 2 * BLK
BAND = ("z", "y", "core")
SWAP = ((0, 1), (1, 0))
SMEM = pl.BlockSpec(memory_space=pltpu.SMEM)
VMEM = pl.BlockSpec(memory_space=pltpu.VMEM)
SPAN = 80
PLANE = 320
NEAR = (0, 7, 1, 6, 2)
MIDDLE = (5, 3)
FAR = (4,)
ROOM = 224


def ring(n, shift):
    return [(i, (i + shift) % n) for i in range(n)]


def params(mib):
    return pltpu.CompilerParams(vmem_limit_bytes=mib * 1024 * 1024)


def split(x):
    high = x.astype(jnp.bfloat16)
    return high, (x - high.astype(jnp.float32)).astype(jnp.bfloat16)


def dot(former, latter):
    return jnp.dot(former, latter, preferred_element_type=jnp.float32)


def dot3(high, low, former, latter):
    return dot(high, former) + dot(high, latter) + dot(low, former)


def plan_kernel(place, pairs_ref, owners_ref, out_ref):
    size = 256
    down = lax.broadcasted_iota(jnp.int32, (size, size), 0)
    across = lax.broadcasted_iota(jnp.int32, (size, size), 1)
    one = lambda condition: jnp.where(condition, 1.0, 0.0)
    to_row = lambda column: jnp.sum(jnp.where(down == across, column, 0.0), axis=0, keepdims=True)
    to_column = lambda row: jnp.sum(jnp.where(down == across, row, 0.0), axis=1, keepdims=True)
    rows, columns = down.astype(jnp.float32), across.astype(jnp.float32)
    left, right = pairs_ref[:, 0:1].astype(jnp.float32), pairs_ref[:, 1:2].astype(jnp.float32)
    owner_row = owners_ref[...].astype(jnp.float32)
    owner = to_column(owner_row)

    used = jnp.max(one(right == columns), axis=0, keepdims=True)
    used_column = to_column(used)
    rank = jnp.sum(jnp.where(columns < rows, used, 0.0), axis=1, keepdims=True)
    used_list = jnp.sum(jnp.where((rank == columns) & (used_column > 0), rows, 0.0), axis=0, keepdims=True)
    right_rank = jnp.sum(jnp.where(columns < right, used, 0.0), axis=1, keepdims=True)

    parity = lambda value: value - 2.0 * jnp.floor(value * 0.5)
    count = jnp.sum(one(owner == columns), axis=0, keepdims=True)
    same = parity(rows) == parity(columns)
    offset = jnp.sum(jnp.where((rows < columns) & same, to_column(count), 0.0), axis=0, keepdims=True)
    ahead = (owner_row < owner) | ((owner_row == owner) & (across < down))
    ahead = ahead & (parity(owner_row) == parity(owner))
    position = jnp.sum(one(ahead), axis=1, keepdims=True)

    core = place[3].astype(jnp.float32)
    local = right_rank - core * (USED // 2)
    here = (local >= 0) & (local < USED // 2)
    local = jnp.where(here, local, 0.0)
    lane = lax.broadcasted_iota(jnp.int32, (1, size), 1)
    groups = jnp.zeros((1, size), jnp.float32)
    for half in range(2):
        hit = (position == columns) & (parity(owner) == half)
        pick = lambda column: jnp.sum(jnp.where(hit, column, 0.0), axis=0, keepdims=True).astype(jnp.int32)
        at = pick(local)
        out_ref[4 * half : 4 * half + 1, :] = pick(left) * BLK
        out_ref[4 * half + 1 : 4 * half + 2, :] = at // 8 * 128
        out_ref[4 * half + 2 : 4 * half + 3, :] = (lane + 8 - at % 8) % 8 * BLK
        out_ref[4 * half + 3 : 4 * half + 4, :] = jnp.where(pick(one(here)) > 0, lane % 8, -1)
        total = jnp.sum(one(parity(owner_row) == half))
        groups = jnp.where(lane == half, jnp.floor((total + 7.0) / 8.0), groups)
    for at, row in enumerate((offset, count, used_list, groups)):
        out_ref[8 + at : 9 + at, :] = row.astype(jnp.int32)


def plan_call(place, pairs, owners):
    return pl.pallas_call(
        plan_kernel,
        out_shape=jax.ShapeDtypeStruct((16, pairs.shape[0]), jnp.int32),
        in_specs=[SMEM, VMEM, VMEM],
        out_specs=VMEM,
        compiler_params=params(8),
        name="plan",
    )(place, pairs, owners)


def padded(planes):
    return (len(planes) * PLANE + 127) // 128 * 128


def screen_kernel(place, own_ref, other_ref, *outs):
    z = place[0]
    rows = 16
    lane = lax.broadcasted_iota(jnp.int32, (rows, 128), 1)

    def plane_of(ref, row, delta, offset):
        plane = lax.rem(z + delta, 8)
        odd = lax.rem(plane, 2)
        column = pl.multiple_of(plane * PLANE - odd * 64, 128)
        window = ref[row, pl.ds(column, 384)]
        turned = pltpu.roll(window, 64 if offset else 320, 1)
        return jnp.where((odd == 1) if offset else (odd == 0), window, turned)

    for source, ref in enumerate((own_ref, other_ref)):

        def body(step, carry, source=source, ref=ref):
            part = step // 10
            row = pl.ds(pl.multiple_of(step * rows, rows), rows)
            target = pl.multiple_of(part * PLANE + source * (PLANE // 2) + (step - part * 10) * rows, rows)
            for group, planes in enumerate((NEAR, MIDDLE, FAR)):
                for at in range(0, len(planes), 2):
                    a = plane_of(ref, row, planes[at], False)
                    if at + 1 < len(planes):
                        b = plane_of(ref, row, planes[at + 1], True)
                        middle = jnp.where(lane < 64, a[:, 256:], b[:, :128])
                        whole = jnp.concatenate([a[:, :256], middle, b[:, 128:]], axis=1)
                    else:
                        whole = jnp.concatenate([a[:, :256], jnp.where(lane < 64, a[:, 256:], 0.0)], axis=1)
                    top, rest = split(whole)
                    columns = slice(at * PLANE, at * PLANE + whole.shape[1])
                    outs[2 * group][pl.ds(target, rows), columns] = top
                    outs[2 * group + 1][pl.ds(target, rows), columns] = rest
            return carry

        lax.fori_loop(0, 20, body, 0)


def screen_call(place, own, other):
    shapes = [
        jax.ShapeDtypeStruct((2 * own.shape[0], padded(planes)), jnp.bfloat16)
        for planes in (NEAR, MIDDLE, FAR)
        for _ in range(2)
    ]
    return pl.pallas_call(
        screen_kernel,
        out_shape=shapes,
        in_specs=[SMEM, VMEM, VMEM],
        out_specs=[VMEM] * 6,
        compiler_params=params(20),
        name="screen",
    )(place, own, other)


def left_kernel(place, *refs):
    pieces, (high_ref, low_ref, work) = refs[:8], refs[8:]
    x = place[1]
    span = pieces[0].shape[0] // 2
    for core in range(2):
        for shift in range(4):
            shard = lax.rem(x - shift + 4, 4)
            for part in range(2):
                row = pl.multiple_of(part * 8 * span + core * 4 * span + shard * span, 8)
                work[pl.ds(row, span), :] = pieces[core * 4 + shift][part * span : (part + 1) * span, :]

    def body(block, carry):
        at = pl.ds(pl.multiple_of(block * 128, 128), 128)
        high_ref[at, :], low_ref[at, :] = split(work[:, at].T)
        return carry

    lax.fori_loop(0, work.shape[1] // 128, body, 0)


def left_call(place, pieces):
    depth, width = pieces[0].shape
    shape = jax.ShapeDtypeStruct((width, 8 * depth), jnp.bfloat16)
    return pl.pallas_call(
        left_kernel,
        out_shape=(shape, shape),
        in_specs=[SMEM] + [VMEM] * 8,
        out_specs=(VMEM, VMEM),
        scratch_shapes=[pltpu.VMEM((8 * depth, width), jnp.float32)],
        compiler_params=params(20),
        name="left",
    )(place, *pieces)


def load_right(place, runs, planes, high, low):
    y = place[2]
    for delta, ref, start, first, count in runs:
        spread = lax.rem(y + delta, 4) * SPAN

        def body(step, carry, ref=ref, start=start, first=first, spread=spread):
            unit = first + step
            row = pl.ds(pl.multiple_of(unit // 2 * PLANE + spread, 16), SPAN)
            column = pl.ds(pl.multiple_of(lax.rem(unit, 2) * HALF, HALF), HALF)
            top, rest = split(ref[pl.ds(pl.multiple_of(start + step * SPAN, 8), SPAN), :])
            high[row, column] = top
            low[row, column] = rest
            return carry

        lax.fori_loop(0, count, body, 0)
    used = planes * PLANE
    if used < high.shape[0]:
        for ref in (high, low):
            ref[used:, :] = jnp.zeros((ref.shape[0] - used, ref.shape[1]), ref.dtype)


def near_runs(first, first_down, first_up, second, second_down, second_up, two_down, two_up):
    skip = 3 * SPAN
    return (
        ((0, first, 0, 0, 6), (3, first_down, 0, 0, 6), (1, first_up, 0, 0, 6))
        + ((0, second, 0, 6, 4), (3, second_down, 0, 6, 4), (1, second_up, 0, 6, 4))
        + ((2, two_down, 0, 0, 3), (2, two_up, 0, 3, 3), (2, two_down, skip, 6, 2), (2, two_up, skip, 8, 2))
    )


def middle_runs(z_below, z_above, y_below, y_above):
    runs = ()
    for first, sides, across in ((0, z_below, y_below), (2, z_above, y_above)):
        runs += ((3, sides, 0, first, 2), (1, sides, 2 * SPAN, first, 2), (0, sides, 4 * SPAN, first, 2))
        runs += ((2, across, 0, first, 2),)
    return runs


def far_runs(below, above, across_low, across_high):
    return (
        ((3, below, 0, 0, 2), (1, above, 0, 0, 2), (0, below, 2 * SPAN, 0, 1), (0, above, 2 * SPAN, 1, 1))
        + ((2, across_low, 0, 0, 1), (2, across_high, 0, 1, 1))
    )


def group_kernel(runs, planes, place, *refs):
    count = len(refs) - 5 - (runs is middle_runs)
    rights, (high_ref, low_ref), rest = refs[:count], refs[count : count + 2], refs[count + 2 :]
    out_ref, rh, rl = rest[-3:]
    load_right(place, runs(*rights), planes, rh, rl)
    value = dot3(high_ref[...], low_ref[...], rh[...], rl[...])
    out_ref[...] = value if len(rest) == 3 else value + rest[0][...]


def group_call(runs, planes, place, rights, screens, total):
    rows, width = screens[0].shape
    return pl.pallas_call(
        functools.partial(group_kernel, runs, planes),
        out_shape=jax.ShapeDtypeStruct((rows, 2 * HALF), jnp.float32),
        in_specs=[SMEM] + [VMEM] * (len(rights) + 2 + len(total)),
        out_specs=VMEM,
        scratch_shapes=[pltpu.VMEM((width, 2 * HALF), jnp.bfloat16)] * 2,
        compiler_params=params(32),
        name="group",
    )(place, *rights, *screens, *total)


def pair_kernel(place, table, *refs):
    rights, (high_ref, low_ref, sum_ref, left_high, left_low, give_ref, kern, rh, rl) = refs[:4], refs[4:]
    load_right(place, far_runs(*rights), len(FAR), rh, rl)
    product = sum_ref[...] + dot3(high_ref[...], low_ref[...], rh[...], rl[...])
    mid = product.shape[0] // 2
    real = product[:mid, :HALF] - product[mid:, HALF:]
    imag = product[mid:, :HALF] + product[:mid, HALF:]
    applied = NG ** (-0.5) * jnp.concatenate(
        [jnp.concatenate([real, imag], axis=0), jnp.concatenate([imag, -real], axis=0)], axis=1
    )
    kern[...] = dot3(left_high[...], left_low[...], *split(applied))

    extract(place, table, 1 - place[3], kern, give_ref)


def extract(place, table, half, kern, out_ref):
    at = lambda x: lax.rem(x + 4 - place[1], 4)
    lane = lax.broadcasted_iota(jnp.int32, (8, 128), 1) // BLK
    upper = lax.broadcasted_iota(jnp.int32, (8, 128), 0) < 4

    def groups(pair, carry):
        for g in (pair * 2, pair * 2 + 1):
            tiles = [[jnp.zeros((8, 128), jnp.float32) for _ in range(2)] for _ in range(2)]
            for u in range(8):
                slot = g * 8 + u
                row = pl.multiple_of(table[4 * half, slot], BLK)
                column = pl.multiple_of(table[4 * half + 1, slot], 128)
                shift = table[4 * half + 2, slot]
                target = table[4 * half + 3, slot]
                for part in range(2):
                    for side in range(2):
                        tile = kern[pl.ds(row + side * 8, 8), pl.ds(column + part * HALF, 128)]
                        tile = pltpu.roll(tile, shift, 1)
                        tiles[part][side] = jnp.where(lane == target, tile, tiles[part][side])
            lanes = pl.ds(pl.multiple_of(g * 128, 128), 128)
            for side in range(2):
                real, imag = tiles[0][side], tiles[1][side]
                out_ref[at(2 * side), :, lanes] = jnp.where(upper, real, pltpu.roll(imag, 4, 0))
                out_ref[at(2 * side + 1), :, lanes] = jnp.where(upper, pltpu.roll(real, 4, 0), imag)
        return carry

    out_ref[...] = jnp.zeros_like(out_ref)
    lax.fori_loop(0, (table[11, half] + 1) // 2, groups, 0)


def pair_call(place, table, rights, screens, total, left_high, left_low):
    rows = left_high.shape[0]
    return pl.pallas_call(
        pair_kernel,
        out_shape=(
            jax.ShapeDtypeStruct((4, 8, ROOM * BLK), jnp.float32),
            jax.ShapeDtypeStruct((rows, 2 * HALF), jnp.float32),
        ),
        in_specs=[SMEM, SMEM] + [VMEM] * (len(rights) + 5),
        out_specs=(VMEM, VMEM),
        scratch_shapes=[pltpu.VMEM((screens[0].shape[1], 2 * HALF), jnp.bfloat16)] * 2,
        compiler_params=params(24),
        name="pair",
    )(place, table, *rights, *screens, total, left_high, left_low)


def extract_kernel(place, table, kern, out_ref):
    extract(place, table, place[3], kern, out_ref)


def extract_call(place, table, kern):
    return pl.pallas_call(
        extract_kernel,
        out_shape=jax.ShapeDtypeStruct((4, 8, ROOM * BLK), jnp.float32),
        in_specs=[SMEM, SMEM, VMEM],
        out_specs=VMEM,
        compiler_params=params(8),
        name="extract",
    )(place, table, kern)


def add_kernel(one_ref, two_ref, *outs):
    for at, out_ref in enumerate(outs):
        out_ref[...] = one_ref[at] + two_ref[at]


def add_call(one, two):
    return pl.pallas_call(
        add_kernel,
        out_shape=[jax.ShapeDtypeStruct(one.shape[1:], one.dtype)] * one.shape[0],
        in_specs=[VMEM, VMEM],
        out_specs=[VMEM] * one.shape[0],
        compiler_params=params(8),
        name="add",
    )(one, two)


def owner_kernel(place, table, one_ref, two_ref, three_ref, four_ref, out_ref, work):
    total = (one_ref[...] + two_ref[...]) + (three_ref[...] + four_ref[...])
    width = total.shape[1]
    work[:, :width] = total
    work[:, width:] = jnp.zeros((8, work.shape[1] - width), jnp.float32)
    for chip in range(out_ref.shape[0]):
        start = table[8, chip * 2 + place[3]]
        column = pl.multiple_of(start // 8 * 128, 128)
        shift = lax.rem(384 - lax.rem(start, 8) * BLK, 384)
        out_ref[chip] = pltpu.roll(work[:, pl.ds(column, 384)], shift, 1)[:, :256]


def owner_call(place, table, parts):
    return pl.pallas_call(
        owner_kernel,
        out_shape=jax.ShapeDtypeStruct((32, 8, 256), jnp.float32),
        in_specs=[SMEM, SMEM] + [VMEM] * 4,
        out_specs=VMEM,
        scratch_shapes=[pltpu.VMEM((8, parts[0].shape[1] + 384), jnp.float32)],
        compiler_params=params(8),
        name="owner",
    )(place, table, *parts)


def last_kernel(place, table, parts_ref, out_ref):
    total = parts_ref[0]
    for chip in range(1, parts_ref.shape[0]):
        total = total + parts_ref[chip]
    held = table[9, (place[0] * 4 + place[2]) * 2 + place[3]]
    for slot in range(CAP):
        tile = total[:, slot // 8 * 128 : slot // 8 * 128 + 128]
        tile = pltpu.roll(tile, (128 - slot % 8 * BLK) % 128, 1)
        out_ref[slot] = jnp.where(slot < held, tile[:, :BLK], 0.0)


def last_call(place, table, parts):
    return pl.pallas_call(
        last_kernel,
        out_shape=jax.ShapeDtypeStruct((CAP, 8, BLK), jnp.float32),
        in_specs=[SMEM, SMEM, VMEM],
        out_specs=VMEM,
        compiler_params=params(8),
        name="last",
    )(place, table, parts)


def pack_kernel(place, own_ref, other_ref, out_ref, work):
    core = place[3]
    width = own_ref.shape[2]
    for block in range(width // 128):
        lanes = pl.ds(block * 128, 128)
        rows = []
        for part in range(2):
            own, other = own_ref[part, :, lanes], other_ref[part, :, lanes]
            rows += [jnp.where(core == 0, own, other), jnp.where(core == 0, other, own)]
        rows = jnp.concatenate(rows + rows, axis=0)
        work[block * 128 : (block + 1) * 128, :] = rows.T
    half = lax.broadcasted_iota(jnp.int32, (8, 128), 1) < 64
    for chip in range(32):
        at = pl.multiple_of(chip * 80 + core * 40, 8)
        tiles = [work[pl.ds(at + 8 * t, 8), :] for t in range(5)]
        out_ref[chip * 20 : chip * 20 + 8, :] = jnp.where(half, tiles[0], tiles[1])
        out_ref[chip * 20 + 8 : chip * 20 + 16, :] = jnp.where(half, tiles[2], tiles[3])
        last = jnp.where(half, tiles[4], pltpu.roll(tiles[4], 4, 0))
        out_ref[chip * 20 + 16 : chip * 20 + 20, :] = last[:4]


def pack_call(place, own, other):
    width = own.shape[2]
    return pl.pallas_call(
        pack_kernel,
        out_shape=jax.ShapeDtypeStruct((32 * 20, 128), jnp.float32),
        in_specs=[SMEM, VMEM, VMEM],
        out_specs=VMEM,
        scratch_shapes=[pltpu.VMEM((width, 128), jnp.float32)],
        name="pack",
    )(place, own, other)


def unpack_kernel(place, table, in_ref, columns_ref, keep_ref, give_ref):
    core = place[3]
    quarter = lax.broadcasted_iota(jnp.int32, (8, 128), 1) // 32
    upper = lax.broadcasted_iota(jnp.int32, (8, 128), 0) < 4
    for group in range(8):
        tiles = [[None] * 5 for _ in range(2)]
        for u in range(4):
            at = (group * 4 + u) * 20
            one, two = in_ref[at : at + 8, :], in_ref[at + 8 : at + 16, :]
            end = in_ref[at + 12 : at + 20, :]
            end = jnp.where(upper, pltpu.roll(end, 4, 0), pltpu.roll(end, 64, 1))
            for t, (source, first) in enumerate(((one, 0), (one, 64), (two, 0), (two, 64), (end, 0))):
                for part in range(2):
                    by = (u * 32 - first - part * 32) % 128
                    turned = pltpu.roll(source, by, 1) if by else source
                    old = tiles[part][t]
                    tiles[part][t] = turned if old is None else jnp.where(quarter == u, turned, old)
        for part in range(2):
            for t in range(5):
                row = part * 40 + t * 8
                columns_ref[row : row + 8, group * 128 : (group + 1) * 128] = tiles[part][t]
    select(table, 1 - core, columns_ref, give_ref)
    select(table, core, columns_ref, keep_ref)


def select(table, which, columns_ref, out_ref):
    eighth = lax.broadcasted_iota(jnp.int32, (80, 128), 1) // BLK
    for group in range(2):
        slab = None
        for u in range(8):
            block = table[10, which * (USED // 2) + group * 8 + u]
            column = pl.multiple_of(block // 8 * 128, 128)
            by = lax.rem(u * BLK + 128 - lax.rem(block, 8) * BLK, 128)
            turned = pltpu.roll(columns_ref[:, pl.ds(column, 128)], by, 1)
            slab = turned if slab is None else jnp.where(eighth == u, turned, slab)
        out_ref[:, group * 128 : (group + 1) * 128] = slab


def unpack_call(place, table, pieces):
    return pl.pallas_call(
        unpack_kernel,
        out_shape=(
            jax.ShapeDtypeStruct((80, 1024), jnp.float32),
            jax.ShapeDtypeStruct((80, HALF), jnp.float32),
            jax.ShapeDtypeStruct((80, HALF), jnp.float32),
        ),
        in_specs=[SMEM, SMEM, VMEM],
        out_specs=(VMEM, VMEM, VMEM),
        compiler_params=params(8),
        name="unpack",
    )(place, table, pieces)


def shard_kernel(place, keep_ref, take_ref, out_ref):
    core = place[3]
    for part in range(2):
        out_ref[pl.ds(pl.multiple_of(part * 80 + core * 40, 8), 40), :] = keep_ref[part * 40 : part * 40 + 40, :]
        out_ref[pl.ds(pl.multiple_of(part * 80 + 40 - core * 40, 8), 40), :] = take_ref[part * 40 : part * 40 + 40, :]


def shard_call(place, keep, take):
    return pl.pallas_call(
        shard_kernel,
        out_shape=jax.ShapeDtypeStruct((160, HALF), jnp.float32),
        in_specs=[SMEM, VMEM, VMEM],
        out_specs=VMEM,
        compiler_params=params(8),
        name="shard",
    )(place, keep, take)


def after(array, *others):
    return lax.optimization_barrier((array, *others))[0]


def shards(densities, screened, pairs, owners):
    span = screened.shape[2]
    place = jnp.stack([lax.axis_index(axis) for axis in ("z", "x", "y", "core")]).astype(jnp.int32)
    shift = lambda array, axis, by: lax.ppermute(array, axis, ring(lax.axis_size(axis), by))
    swap = lambda array: lax.ppermute(array, "core", SWAP)
    join = lambda *arrays: jnp.concatenate(arrays, axis=0)
    hold = lax.optimization_barrier

    pieces = pack_call(place, densities, swap(densities))
    table = plan_call(place, after(pairs, pieces), owners.reshape(1, -1))
    mine = lax.all_to_all(pieces.reshape(32, 1, -1), ("z", "y"), 0, 0, tiled=True).reshape(pieces.shape)

    screen = screened.reshape(2 * 4 * span, -1)
    mine, other = hold((mine, swap(after(screen, pieces))))

    columns, keep, give = unpack_call(place, table, mine)
    shard = shard_call(place, keep, swap(give))

    block = 2 * SPAN
    below2, above2 = shift(shard, "z", 2), shift(shard, "z", -2)
    below, above, columns = hold((shift(shard, "z", 1), shift(shard, "z", -1), columns))
    first = join(shard, below, above)
    first_down, first_up = shift(first, "y", 1), shift(first, "y", -1)
    around = [columns, shift(columns, "x", 1), None, None]
    below2, above2, first, columns = hold((below2, above2, first, columns))
    second = join(below2, above2)
    second_down, second_up = shift(second, "y", 1), shift(second, "y", -1)
    around[3] = shift(columns, "x", 3)
    screens = screen_call(place, after(screen, second), other)
    first_down, first_up, around[1], below2, above2, *screens = hold(
        (first_down, first_up, around[1], below2, above2, *screens)
    )
    around[2] = shift(after(columns, first_down), "x", 2)
    second_down, second_up, first_down, around[3] = hold((second_down, second_up, first_down, around[3]))

    z_below = shift(join(second_down[:block], second_up[:block], second[:block]), "z", 1)
    z_above = shift(join(second_down[block:], second_up[block:], second[block:]), "z", -1)
    two_down = shift(join(first_down[: 3 * SPAN], second_down[:block]), "y", 1)
    two_up = shift(join(first_up[3 * SPAN :], second_up[block:]), "y", -1)
    swapped = [swap(columns), swap(around[1]), None, None]
    two_down, two_up, z_below, z_above, around[2], swapped[0], swapped[1] = hold(
        (two_down, two_up, z_below, z_above, around[2], swapped[0], swapped[1])
    )

    y_below, y_above = shift(z_below[:block], "y", 1), shift(z_above[block : 2 * block], "y", -1)
    far_below = shift(join(z_below[:block], z_below[2 * block : 2 * block + SPAN]), "z", 1)
    far_above = shift(join(z_above[block : 2 * block], z_above[2 * block + SPAN :]), "z", -1)
    rights = (first, first_down, first_up, second, second_down, second_up, two_down, two_up)
    total = group_call(near_runs, len(NEAR), place, rights, screens[:2], ())
    swapped[2:] = [swap(array) for array in around[2:]]
    y_below, y_above, far_below, far_above, total, *swapped[2:] = hold(
        (y_below, y_above, far_below, far_above, total, *swapped[2:])
    )

    across_low, across_high = shift(far_below[:SPAN], "y", 1), shift(far_above[SPAN : 2 * SPAN], "y", -1)
    rights = (z_below, z_above, y_below, y_above)
    total = group_call(middle_runs, len(MIDDLE), place, rights, screens[2:4], (total,))
    left_high, left_low = left_call(place, around + swapped)
    across_low, across_high, total, left_high, left_low = hold((across_low, across_high, total, left_high, left_low))
    rights = (far_below, far_above, across_low, across_high)
    give, kern = pair_call(place, table, rights, screens[4:], total, left_high, left_low)

    parts = add_call(extract_call(place, table, kern), swap(give))
    parts = [parts[0]] + [shift(parts[by], "x", by) for by in (1, 2, 3)]
    parts = owner_call(place, table, parts)
    parts = lax.all_to_all(parts, ("z", "y"), 0, 0, tiled=True)
    return last_call(place, table, parts).reshape(1, CAP, 2, 4, BLK)


def solution(mesh):
    fine = Mesh(mesh.devices.reshape(8, 4, 2, 4), ("z", "y", "core", "x"))
    in_specs = (P(None, BAND, "x"), P(None, None, BAND, "x"), P(), P())
    out_specs = P(BAND, None, None, "x", None)
    return jax.shard_map(shards, mesh=fine, in_specs=in_specs, out_specs=out_specs, check_vma=False)
```

```python
import functools

import jax
import jax.numpy as jnp
from jax import lax
from jax.experimental import pallas as pl
from jax.experimental.pallas import tpu as pltpu
from jax.sharding import Mesh
from jax.sharding import PartitionSpec as P

NG = 10240
CAP = 12
BLK = 16
USED = 32
HALF = USED // 2 * BLK
BAND = ("z", "y", "core")
SWAP = ((0, 1), (1, 0))
SMEM = pl.BlockSpec(memory_space=pltpu.SMEM)
VMEM = pl.BlockSpec(memory_space=pltpu.VMEM)
SPAN = 80
PLANE = 320
NEAR = (0, 7, 1, 6, 2)
MIDDLE = (5, 3)
FAR = (4,)
ROOM = 224


def ring(n, shift):
    return [(i, (i + shift) % n) for i in range(n)]


def params(mib):
    return pltpu.CompilerParams(vmem_limit_bytes=mib * 1024 * 1024)


def split(x):
    high = x.astype(jnp.bfloat16)
    return high, (x - high.astype(jnp.float32)).astype(jnp.bfloat16)


def dot(former, latter):
    return jnp.dot(former, latter, preferred_element_type=jnp.float32)


def dot3(high, low, former, latter):
    return dot(high, former) + dot(high, latter) + dot(low, former)


def plan_kernel(place, pairs_ref, owners_ref, out_ref):
    size = 256
    down = lax.broadcasted_iota(jnp.int32, (size, size), 0)
    across = lax.broadcasted_iota(jnp.int32, (size, size), 1)
    one = lambda condition: jnp.where(condition, 1.0, 0.0)
    to_row = lambda column: jnp.sum(jnp.where(down == across, column, 0.0), axis=0, keepdims=True)
    to_column = lambda row: jnp.sum(jnp.where(down == across, row, 0.0), axis=1, keepdims=True)
    rows, columns = down.astype(jnp.float32), across.astype(jnp.float32)
    left, right = pairs_ref[:, 0:1].astype(jnp.float32), pairs_ref[:, 1:2].astype(jnp.float32)
    owner_row = owners_ref[...].astype(jnp.float32)
    owner = to_column(owner_row)

    used = jnp.max(one(right == columns), axis=0, keepdims=True)
    used_column = to_column(used)
    rank = jnp.sum(jnp.where(columns < rows, used, 0.0), axis=1, keepdims=True)
    used_list = jnp.sum(jnp.where((rank == columns) & (used_column > 0), rows, 0.0), axis=0, keepdims=True)
    right_rank = jnp.sum(jnp.where(columns < right, used, 0.0), axis=1, keepdims=True)

    parity = lambda value: value - 2.0 * jnp.floor(value * 0.5)
    count = jnp.sum(one(owner == columns), axis=0, keepdims=True)
    same = parity(rows) == parity(columns)
    offset = jnp.sum(jnp.where((rows < columns) & same, to_column(count), 0.0), axis=0, keepdims=True)
    ahead = (owner_row < owner) | ((owner_row == owner) & (across < down))
    ahead = ahead & (parity(owner_row) == parity(owner))
    position = jnp.sum(one(ahead), axis=1, keepdims=True)

    core = place[3].astype(jnp.float32)
    local = right_rank - core * (USED // 2)
    here = (local >= 0) & (local < USED // 2)
    local = jnp.where(here, local, 0.0)
    lane = lax.broadcasted_iota(jnp.int32, (1, size), 1)
    groups = jnp.zeros((1, size), jnp.float32)
    for half in range(2):
        hit = (position == columns) & (parity(owner) == half)
        pick = lambda column: jnp.sum(jnp.where(hit, column, 0.0), axis=0, keepdims=True).astype(jnp.int32)
        at = pick(local)
        out_ref[4 * half : 4 * half + 1, :] = pick(left) * BLK
        out_ref[4 * half + 1 : 4 * half + 2, :] = at // 8 * 128
        out_ref[4 * half + 2 : 4 * half + 3, :] = (lane + 8 - at % 8) % 8 * BLK
        out_ref[4 * half + 3 : 4 * half + 4, :] = jnp.where(pick(one(here)) > 0, lane % 8, -1)
        total = jnp.sum(one(parity(owner_row) == half))
        groups = jnp.where(lane == half, jnp.floor((total + 7.0) / 8.0), groups)
    for at, row in enumerate((offset, count, used_list, groups)):
        out_ref[8 + at : 9 + at, :] = row.astype(jnp.int32)


def plan_call(place, pairs, owners):
    return pl.pallas_call(
        plan_kernel,
        out_shape=jax.ShapeDtypeStruct((16, pairs.shape[0]), jnp.int32),
        in_specs=[SMEM, VMEM, VMEM],
        out_specs=VMEM,
        compiler_params=params(8),
        name="plan",
    )(place, pairs, owners)


def padded(planes):
    return (len(planes) * PLANE + 127) // 128 * 128


def screen_kernel(place, own_ref, other_ref, *outs):
    z = place[0]
    rows = 16
    lane = lax.broadcasted_iota(jnp.int32, (rows, 128), 1)

    def plane_of(ref, row, delta, offset):
        plane = lax.rem(z + delta, 8)
        odd = lax.rem(plane, 2)
        column = pl.multiple_of(plane * PLANE - odd * 64, 128)
        window = ref[row, pl.ds(column, 384)]
        turned = pltpu.roll(window, 64 if offset else 320, 1)
        return jnp.where((odd == 1) if offset else (odd == 0), window, turned)

    for source, ref in enumerate((own_ref, other_ref)):

        def body(step, carry, source=source, ref=ref):
            part = step // 10
            row = pl.ds(pl.multiple_of(step * rows, rows), rows)
            target = pl.multiple_of(part * PLANE + source * (PLANE // 2) + (step - part * 10) * rows, rows)
            for group, planes in enumerate((NEAR, MIDDLE, FAR)):
                for at in range(0, len(planes), 2):
                    a = plane_of(ref, row, planes[at], False)
                    if at + 1 < len(planes):
                        b = plane_of(ref, row, planes[at + 1], True)
                        middle = jnp.where(lane < 64, a[:, 256:], b[:, :128])
                        whole = jnp.concatenate([a[:, :256], middle, b[:, 128:]], axis=1)
                    else:
                        whole = jnp.concatenate([a[:, :256], jnp.where(lane < 64, a[:, 256:], 0.0)], axis=1)
                    top, rest = split(whole)
                    columns = slice(at * PLANE, at * PLANE + whole.shape[1])
                    outs[2 * group][pl.ds(target, rows), columns] = top
                    outs[2 * group + 1][pl.ds(target, rows), columns] = rest
            return carry

        lax.fori_loop(0, 20, body, 0)


def screen_call(place, own, other):
    shapes = [
        jax.ShapeDtypeStruct((2 * own.shape[0], padded(planes)), jnp.bfloat16)
        for planes in (NEAR, MIDDLE, FAR)
        for _ in range(2)
    ]
    return pl.pallas_call(
        screen_kernel,
        out_shape=shapes,
        in_specs=[SMEM, VMEM, VMEM],
        out_specs=[VMEM] * 6,
        compiler_params=params(20),
        name="screen",
    )(place, own, other)


def left_kernel(place, *refs):
    pieces, (high_ref, low_ref, work) = refs[:8], refs[8:]
    x = place[1]
    span = pieces[0].shape[0] // 2
    for core in range(2):
        for shift in range(4):
            shard = lax.rem(x - shift + 4, 4)
            for part in range(2):
                row = pl.multiple_of(part * 8 * span + core * 4 * span + shard * span, 8)
                work[pl.ds(row, span), :] = pieces[core * 4 + shift][part * span : (part + 1) * span, :]

    def body(block, carry):
        at = pl.ds(pl.multiple_of(block * 128, 128), 128)
        high_ref[at, :], low_ref[at, :] = split(work[:, at].T)
        return carry

    lax.fori_loop(0, work.shape[1] // 128, body, 0)


def left_call(place, pieces):
    depth, width = pieces[0].shape
    shape = jax.ShapeDtypeStruct((width, 8 * depth), jnp.bfloat16)
    return pl.pallas_call(
        left_kernel,
        out_shape=(shape, shape),
        in_specs=[SMEM] + [VMEM] * 8,
        out_specs=(VMEM, VMEM),
        scratch_shapes=[pltpu.VMEM((8 * depth, width), jnp.float32)],
        compiler_params=params(20),
        name="left",
    )(place, *pieces)


def load_right(place, runs, planes, high, low):
    y = place[2]
    for delta, ref, start, first, count in runs:
        spread = lax.rem(y + delta, 4) * SPAN

        def body(step, carry, ref=ref, start=start, first=first, spread=spread):
            unit = first + step
            row = pl.ds(pl.multiple_of(unit // 2 * PLANE + spread, 16), SPAN)
            column = pl.ds(pl.multiple_of(lax.rem(unit, 2) * HALF, HALF), HALF)
            top, rest = split(ref[pl.ds(pl.multiple_of(start + step * SPAN, 8), SPAN), :])
            high[row, column] = top
            low[row, column] = rest
            return carry

        lax.fori_loop(0, count, body, 0)
    used = planes * PLANE
    if used < high.shape[0]:
        for ref in (high, low):
            ref[used:, :] = jnp.zeros((ref.shape[0] - used, ref.shape[1]), ref.dtype)


def near_runs(first, first_down, first_up, second, second_down, second_up, two_down, two_up):
    skip = 3 * SPAN
    return (
        ((0, first, 0, 0, 6), (3, first_down, 0, 0, 6), (1, first_up, 0, 0, 6))
        + ((0, second, 0, 6, 4), (3, second_down, 0, 6, 4), (1, second_up, 0, 6, 4))
        + ((2, two_down, 0, 0, 3), (2, two_up, 0, 3, 3), (2, two_down, skip, 6, 2), (2, two_up, skip, 8, 2))
    )


def middle_runs(z_below, z_above, y_below, y_above):
    runs = ()
    for first, sides, across in ((0, z_below, y_below), (2, z_above, y_above)):
        runs += ((3, sides, 0, first, 2), (1, sides, 2 * SPAN, first, 2), (0, sides, 4 * SPAN, first, 2))
        runs += ((2, across, 0, first, 2),)
    return runs


def far_runs(below, above, across_low, across_high):
    return (
        ((3, below, 0, 0, 2), (1, above, 0, 0, 2), (0, below, 2 * SPAN, 0, 1), (0, above, 2 * SPAN, 1, 1))
        + ((2, across_low, 0, 0, 1), (2, across_high, 0, 1, 1))
    )


def group_kernel(runs, planes, place, *refs):
    count = len(refs) - 5 - (runs is middle_runs)
    rights, (high_ref, low_ref), rest = refs[:count], refs[count : count + 2], refs[count + 2 :]
    out_ref, rh, rl = rest[-3:]
    load_right(place, runs(*rights), planes, rh, rl)
    value = dot3(high_ref[...], low_ref[...], rh[...], rl[...])
    out_ref[...] = value if len(rest) == 3 else value + rest[0][...]


def group_call(runs, planes, place, rights, screens, total):
    rows, width = screens[0].shape
    return pl.pallas_call(
        functools.partial(group_kernel, runs, planes),
        out_shape=jax.ShapeDtypeStruct((rows, 2 * HALF), jnp.float32),
        in_specs=[SMEM] + [VMEM] * (len(rights) + 2 + len(total)),
        out_specs=VMEM,
        scratch_shapes=[pltpu.VMEM((width, 2 * HALF), jnp.bfloat16)] * 2,
        compiler_params=params(32),
        name="group",
    )(place, *rights, *screens, *total)


def pair_kernel(place, table, *refs):
    rights, (high_ref, low_ref, sum_ref, left_high, left_low, give_ref, kern, rh, rl) = refs[:4], refs[4:]
    load_right(place, far_runs(*rights), len(FAR), rh, rl)
    product = sum_ref[...] + dot3(high_ref[...], low_ref[...], rh[...], rl[...])
    mid = product.shape[0] // 2
    real = product[:mid, :HALF] - product[mid:, HALF:]
    imag = product[mid:, :HALF] + product[:mid, HALF:]
    applied = NG ** (-0.5) * jnp.concatenate(
        [jnp.concatenate([real, imag], axis=0), jnp.concatenate([imag, -real], axis=0)], axis=1
    )
    kern[...] = dot3(left_high[...], left_low[...], *split(applied))

    extract(place, table, 1 - place[3], kern, give_ref)


def extract(place, table, half, kern, out_ref):
    at = lambda x: lax.rem(x + 4 - place[1], 4)
    lane = lax.broadcasted_iota(jnp.int32, (BLK, 128), 1) // BLK
    upper = lax.broadcasted_iota(jnp.int32, (8, 128), 0) < 4

    def groups(pair, carry):
        for g in (pair * 2, pair * 2 + 1):
            slabs = [None, None]
            for u in range(8):
                slot = g * 8 + u
                row = pl.ds(pl.multiple_of(table[4 * half, slot], BLK), BLK)
                column = pl.multiple_of(table[4 * half + 1, slot], 128)
                shift = table[4 * half + 2, slot]
                target = lane == table[4 * half + 3, slot]
                for part in range(2):
                    slab = pltpu.roll(kern[row, pl.ds(column + part * HALF, 128)], shift, 1)
                    slabs[part] = jnp.where(target, slab, 0.0 if u == 0 else slabs[part])
            lanes = pl.ds(pl.multiple_of(g * 128, 128), 128)
            for side in range(2):
                real, imag = (slab[side * 8 : side * 8 + 8] for slab in slabs)
                out_ref[at(2 * side), :, lanes] = jnp.where(upper, real, pltpu.roll(imag, 4, 0))
                out_ref[at(2 * side + 1), :, lanes] = jnp.where(upper, pltpu.roll(real, 4, 0), imag)
        return carry

    out_ref[...] = jnp.zeros_like(out_ref)
    lax.fori_loop(0, (table[11, half] + 1) // 2, groups, 0)


def pair_call(place, table, rights, screens, total, left_high, left_low):
    rows = left_high.shape[0]
    return pl.pallas_call(
        pair_kernel,
        out_shape=(
            jax.ShapeDtypeStruct((4, 8, ROOM * BLK), jnp.float32),
            jax.ShapeDtypeStruct((rows, 2 * HALF), jnp.float32),
        ),
        in_specs=[SMEM, SMEM] + [VMEM] * (len(rights) + 5),
        out_specs=(VMEM, VMEM),
        scratch_shapes=[pltpu.VMEM((screens[0].shape[1], 2 * HALF), jnp.bfloat16)] * 2,
        compiler_params=params(24),
        name="pair",
    )(place, table, *rights, *screens, total, left_high, left_low)


def extract_kernel(place, table, kern, out_ref):
    extract(place, table, place[3], kern, out_ref)


def extract_call(place, table, kern):
    return pl.pallas_call(
        extract_kernel,
        out_shape=jax.ShapeDtypeStruct((4, 8, ROOM * BLK), jnp.float32),
        in_specs=[SMEM, SMEM, VMEM],
        out_specs=VMEM,
        compiler_params=params(8),
        name="extract",
    )(place, table, kern)


def add_kernel(one_ref, two_ref, *outs):
    for at, out_ref in enumerate(outs):
        out_ref[...] = one_ref[at] + two_ref[at]


def add_call(one, two):
    return pl.pallas_call(
        add_kernel,
        out_shape=[jax.ShapeDtypeStruct(one.shape[1:], one.dtype)] * one.shape[0],
        in_specs=[VMEM, VMEM],
        out_specs=[VMEM] * one.shape[0],
        compiler_params=params(8),
        name="add",
    )(one, two)


def owner_kernel(place, table, one_ref, two_ref, three_ref, four_ref, out_ref, work):
    total = (one_ref[...] + two_ref[...]) + (three_ref[...] + four_ref[...])
    width = total.shape[1]
    work[:, :width] = total
    work[:, width:] = jnp.zeros((8, work.shape[1] - width), jnp.float32)
    for chip in range(out_ref.shape[0]):
        start = table[8, chip * 2 + place[3]]
        column = pl.multiple_of(start // 8 * 128, 128)
        shift = lax.rem(384 - lax.rem(start, 8) * BLK, 384)
        out_ref[chip] = pltpu.roll(work[:, pl.ds(column, 384)], shift, 1)[:, :256]


def owner_call(place, table, parts):
    return pl.pallas_call(
        owner_kernel,
        out_shape=jax.ShapeDtypeStruct((32, 8, 256), jnp.float32),
        in_specs=[SMEM, SMEM] + [VMEM] * 4,
        out_specs=VMEM,
        scratch_shapes=[pltpu.VMEM((8, parts[0].shape[1] + 384), jnp.float32)],
        compiler_params=params(8),
        name="owner",
    )(place, table, *parts)


def last_kernel(place, table, parts_ref, out_ref):
    total = parts_ref[0]
    for chip in range(1, parts_ref.shape[0]):
        total = total + parts_ref[chip]
    held = table[9, (place[0] * 4 + place[2]) * 2 + place[3]]
    for slot in range(CAP):
        tile = total[:, slot // 8 * 128 : slot // 8 * 128 + 128]
        tile = pltpu.roll(tile, (128 - slot % 8 * BLK) % 128, 1)
        out_ref[slot] = jnp.where(slot < held, tile[:, :BLK], 0.0)


def last_call(place, table, parts):
    return pl.pallas_call(
        last_kernel,
        out_shape=jax.ShapeDtypeStruct((CAP, 8, BLK), jnp.float32),
        in_specs=[SMEM, SMEM, VMEM],
        out_specs=VMEM,
        compiler_params=params(8),
        name="last",
    )(place, table, parts)


def pack_kernel(place, own_ref, other_ref, out_ref, work):
    core = place[3]
    width = own_ref.shape[2]
    for block in range(width // 128):
        lanes = pl.ds(block * 128, 128)
        rows = []
        for part in range(2):
            own, other = own_ref[part, :, lanes], other_ref[part, :, lanes]
            rows += [jnp.where(core == 0, own, other), jnp.where(core == 0, other, own)]
        rows = jnp.concatenate(rows + rows, axis=0)
        work[block * 128 : (block + 1) * 128, :] = rows.T
    half = lax.broadcasted_iota(jnp.int32, (8, 128), 1) < 64
    for chip in range(32):
        at = pl.multiple_of(chip * 80 + core * 40, 8)
        tiles = [work[pl.ds(at + 8 * t, 8), :] for t in range(5)]
        out_ref[chip * 20 : chip * 20 + 8, :] = jnp.where(half, tiles[0], tiles[1])
        out_ref[chip * 20 + 8 : chip * 20 + 16, :] = jnp.where(half, tiles[2], tiles[3])
        last = jnp.where(half, tiles[4], pltpu.roll(tiles[4], 4, 0))
        out_ref[chip * 20 + 16 : chip * 20 + 20, :] = last[:4]


def pack_call(place, own, other):
    width = own.shape[2]
    return pl.pallas_call(
        pack_kernel,
        out_shape=jax.ShapeDtypeStruct((32 * 20, 128), jnp.float32),
        in_specs=[SMEM, VMEM, VMEM],
        out_specs=VMEM,
        scratch_shapes=[pltpu.VMEM((width, 128), jnp.float32)],
        name="pack",
    )(place, own, other)


def unpack_kernel(place, table, in_ref, columns_ref, keep_ref, give_ref):
    core = place[3]
    quarter = lax.broadcasted_iota(jnp.int32, (8, 128), 1) // 32
    upper = lax.broadcasted_iota(jnp.int32, (8, 128), 0) < 4
    for group in range(8):
        tiles = [[None] * 5 for _ in range(2)]
        for u in range(4):
            at = (group * 4 + u) * 20
            one, two = in_ref[at : at + 8, :], in_ref[at + 8 : at + 16, :]
            end = in_ref[at + 12 : at + 20, :]
            end = jnp.where(upper, pltpu.roll(end, 4, 0), pltpu.roll(end, 64, 1))
            for t, (source, first) in enumerate(((one, 0), (one, 64), (two, 0), (two, 64), (end, 0))):
                for part in range(2):
                    by = (u * 32 - first - part * 32) % 128
                    turned = pltpu.roll(source, by, 1) if by else source
                    old = tiles[part][t]
                    tiles[part][t] = turned if old is None else jnp.where(quarter == u, turned, old)
        for part in range(2):
            for t in range(5):
                row = part * 40 + t * 8
                columns_ref[row : row + 8, group * 128 : (group + 1) * 128] = tiles[part][t]
    select(table, 1 - core, columns_ref, give_ref)
    select(table, core, columns_ref, keep_ref)


def select(table, which, columns_ref, out_ref):
    eighth = lax.broadcasted_iota(jnp.int32, (80, 128), 1) // BLK
    for group in range(2):
        slab = None
        for u in range(8):
            block = table[10, which * (USED // 2) + group * 8 + u]
            column = pl.multiple_of(block // 8 * 128, 128)
            by = lax.rem(u * BLK + 128 - lax.rem(block, 8) * BLK, 128)
            turned = pltpu.roll(columns_ref[:, pl.ds(column, 128)], by, 1)
            slab = turned if slab is None else jnp.where(eighth == u, turned, slab)
        out_ref[:, group * 128 : (group + 1) * 128] = slab


def unpack_call(place, table, pieces):
    return pl.pallas_call(
        unpack_kernel,
        out_shape=(
            jax.ShapeDtypeStruct((80, 1024), jnp.float32),
            jax.ShapeDtypeStruct((80, HALF), jnp.float32),
            jax.ShapeDtypeStruct((80, HALF), jnp.float32),
        ),
        in_specs=[SMEM, SMEM, VMEM],
        out_specs=(VMEM, VMEM, VMEM),
        compiler_params=params(8),
        name="unpack",
    )(place, table, pieces)


def shard_kernel(place, keep_ref, take_ref, out_ref):
    core = place[3]
    for part in range(2):
        out_ref[pl.ds(pl.multiple_of(part * 80 + core * 40, 8), 40), :] = keep_ref[part * 40 : part * 40 + 40, :]
        out_ref[pl.ds(pl.multiple_of(part * 80 + 40 - core * 40, 8), 40), :] = take_ref[part * 40 : part * 40 + 40, :]


def shard_call(place, keep, take):
    return pl.pallas_call(
        shard_kernel,
        out_shape=jax.ShapeDtypeStruct((160, HALF), jnp.float32),
        in_specs=[SMEM, VMEM, VMEM],
        out_specs=VMEM,
        compiler_params=params(8),
        name="shard",
    )(place, keep, take)


def after(array, *others):
    return lax.optimization_barrier((array, *others))[0]


def shards(densities, screened, pairs, owners):
    span = screened.shape[2]
    place = jnp.stack([lax.axis_index(axis) for axis in ("z", "x", "y", "core")]).astype(jnp.int32)
    shift = lambda array, axis, by: lax.ppermute(array, axis, ring(lax.axis_size(axis), by))
    swap = lambda array: lax.ppermute(array, "core", SWAP)
    join = lambda *arrays: jnp.concatenate(arrays, axis=0)
    hold = lax.optimization_barrier

    pieces = pack_call(place, densities, swap(densities))
    table = plan_call(place, after(pairs, pieces), owners.reshape(1, -1))
    mine = lax.all_to_all(pieces.reshape(32, 1, -1), ("z", "y"), 0, 0, tiled=True).reshape(pieces.shape)

    screen = screened.reshape(2 * 4 * span, -1)
    mine, other = hold((mine, swap(after(screen, pieces))))

    columns, keep, give = unpack_call(place, table, mine)
    shard = shard_call(place, keep, swap(give))

    block = 2 * SPAN
    below2, above2 = shift(shard, "z", 2), shift(shard, "z", -2)
    below, above, columns = hold((shift(shard, "z", 1), shift(shard, "z", -1), columns))
    first = join(shard, below, above)
    first_down, first_up = shift(first, "y", 1), shift(first, "y", -1)
    around = [columns, shift(columns, "x", 1), None, None]
    below2, above2, first, columns = hold((below2, above2, first, columns))
    second = join(below2, above2)
    second_down, second_up = shift(second, "y", 1), shift(second, "y", -1)
    around[3] = shift(columns, "x", 3)
    screens = screen_call(place, after(screen, second), other)
    first_down, first_up, around[1], below2, above2, *screens = hold(
        (first_down, first_up, around[1], below2, above2, *screens)
    )
    second_down, second_up, first_down, around[3] = hold((second_down, second_up, first_down, around[3]))

    z_below = shift(join(second_down[:block], second_up[:block], second[:block]), "z", 1)
    z_above = shift(join(second_down[block:], second_up[block:], second[block:]), "z", -1)
    two_down = shift(join(first_down[: 3 * SPAN], second_down[:block]), "y", 1)
    two_up = shift(join(first_up[3 * SPAN :], second_up[block:]), "y", -1)
    around[2] = shift(after(columns, second_down), "x", 2)
    swapped = [swap(columns), swap(around[1]), None, None]
    two_down, two_up, z_below, z_above, around[2], swapped[0], swapped[1] = hold(
        (two_down, two_up, z_below, z_above, around[2], swapped[0], swapped[1])
    )

    y_below, y_above = shift(z_below[:block], "y", 1), shift(z_above[block : 2 * block], "y", -1)
    far_below = shift(join(z_below[:block], z_below[2 * block : 2 * block + SPAN]), "z", 1)
    far_above = shift(join(z_above[block : 2 * block], z_above[2 * block + SPAN :]), "z", -1)
    rights = (first, first_down, first_up, second, second_down, second_up, two_down, two_up)
    total = group_call(near_runs, len(NEAR), place, rights, screens[:2], ())
    swapped[2:] = [swap(array) for array in around[2:]]
    left_high, left_low = left_call(place, around + swapped)
    y_below, y_above, far_below, far_above, total, left_high, left_low = hold(
        (y_below, y_above, far_below, far_above, total, left_high, left_low)
    )

    across_low, across_high = shift(far_below[:SPAN], "y", 1), shift(far_above[SPAN : 2 * SPAN], "y", -1)
    rights = (z_below, z_above, y_below, y_above)
    total = group_call(middle_runs, len(MIDDLE), place, rights, screens[2:4], (total,))
    across_low, across_high, total = hold((across_low, across_high, total))
    rights = (far_below, far_above, across_low, across_high)
    give, kern = pair_call(place, table, rights, screens[4:], total, left_high, left_low)

    parts = add_call(extract_call(place, table, kern), swap(give))
    parts = [parts[0]] + [shift(parts[by], "x", by) for by in (1, 2, 3)]
    parts = owner_call(place, table, parts)
    parts = lax.all_to_all(parts, ("z", "y"), 0, 0, tiled=True)
    return last_call(place, table, parts).reshape(1, CAP, 2, 4, BLK)


def solution(mesh):
    fine = Mesh(mesh.devices.reshape(8, 4, 2, 4), ("z", "y", "core", "x"))
    in_specs = (P(None, BAND, "x"), P(None, None, BAND, "x"), P(), P())
    out_specs = P(BAND, None, None, "x", None)
    return jax.shard_map(shards, mesh=fine, in_specs=in_specs, out_specs=out_specs, check_vma=False)
```

```python
import functools

import jax
import jax.numpy as jnp
from jax import lax
from jax.experimental import pallas as pl
from jax.experimental.pallas import tpu as pltpu
from jax.sharding import Mesh
from jax.sharding import PartitionSpec as P

NG = 10240
CAP = 12
BLK = 16
USED = 32
HALF = USED // 2 * BLK
BAND = ("z", "y", "core")
SWAP = ((0, 1), (1, 0))
SMEM = pl.BlockSpec(memory_space=pltpu.SMEM)
VMEM = pl.BlockSpec(memory_space=pltpu.VMEM)
SPAN = 80
PLANE = 320
NEAR = (0, 7, 1, 6, 2)
MIDDLE = (5, 3)
FAR = (4,)
ROOM = 224


def ring(n, shift):
    return [(i, (i + shift) % n) for i in range(n)]


def params(mib):
    return pltpu.CompilerParams(vmem_limit_bytes=mib * 1024 * 1024)


def split(x):
    high = x.astype(jnp.bfloat16)
    return high, (x - high.astype(jnp.float32)).astype(jnp.bfloat16)


def dot(former, latter):
    return jnp.dot(former, latter, preferred_element_type=jnp.float32)


def dot3(high, low, former, latter):
    return dot(high, former) + dot(high, latter) + dot(low, former)


def plan_kernel(place, pairs_ref, owners_ref, out_ref):
    size = 256
    down = lax.broadcasted_iota(jnp.int32, (size, size), 0)
    across = lax.broadcasted_iota(jnp.int32, (size, size), 1)
    one = lambda condition: jnp.where(condition, 1.0, 0.0)
    to_row = lambda column: jnp.sum(jnp.where(down == across, column, 0.0), axis=0, keepdims=True)
    to_column = lambda row: jnp.sum(jnp.where(down == across, row, 0.0), axis=1, keepdims=True)
    rows, columns = down.astype(jnp.float32), across.astype(jnp.float32)
    left, right = pairs_ref[:, 0:1].astype(jnp.float32), pairs_ref[:, 1:2].astype(jnp.float32)
    owner_row = owners_ref[...].astype(jnp.float32)
    owner = to_column(owner_row)

    used = jnp.max(one(right == columns), axis=0, keepdims=True)
    used_column = to_column(used)
    rank = jnp.sum(jnp.where(columns < rows, used, 0.0), axis=1, keepdims=True)
    used_list = jnp.sum(jnp.where((rank == columns) & (used_column > 0), rows, 0.0), axis=0, keepdims=True)
    right_rank = jnp.sum(jnp.where(columns < right, used, 0.0), axis=1, keepdims=True)

    parity = lambda value: value - 2.0 * jnp.floor(value * 0.5)
    count = jnp.sum(one(owner == columns), axis=0, keepdims=True)
    same = parity(rows) == parity(columns)
    offset = jnp.sum(jnp.where((rows < columns) & same, to_column(count), 0.0), axis=0, keepdims=True)
    ahead = (owner_row < owner) | ((owner_row == owner) & (across < down))
    ahead = ahead & (parity(owner_row) == parity(owner))
    position = jnp.sum(one(ahead), axis=1, keepdims=True)

    core = place[3].astype(jnp.float32)
    local = right_rank - core * (USED // 2)
    here = (local >= 0) & (local < USED // 2)
    local = jnp.where(here, local, 0.0)
    lane = lax.broadcasted_iota(jnp.int32, (1, size), 1)
    groups = jnp.zeros((1, size), jnp.float32)
    for half in range(2):
        hit = (position == columns) & (parity(owner) == half)
        pick = lambda column: jnp.sum(jnp.where(hit, column, 0.0), axis=0, keepdims=True).astype(jnp.int32)
        at = pick(local)
        out_ref[4 * half : 4 * half + 1, :] = pick(left) * BLK
        out_ref[4 * half + 1 : 4 * half + 2, :] = at // 8 * 128
        out_ref[4 * half + 2 : 4 * half + 3, :] = (lane + 8 - at % 8) % 8 * BLK
        out_ref[4 * half + 3 : 4 * half + 4, :] = jnp.where(pick(one(here)) > 0, lane % 8, -1)
        total = jnp.sum(one(parity(owner_row) == half))
        groups = jnp.where(lane == half, jnp.floor((total + 7.0) / 8.0), groups)
    for at, row in enumerate((offset, count, used_list, groups)):
        out_ref[8 + at : 9 + at, :] = row.astype(jnp.int32)


def plan_call(place, pairs, owners):
    return pl.pallas_call(
        plan_kernel,
        out_shape=jax.ShapeDtypeStruct((16, pairs.shape[0]), jnp.int32),
        in_specs=[SMEM, VMEM, VMEM],
        out_specs=VMEM,
        compiler_params=params(8),
        name="plan",
    )(place, pairs, owners)


def padded(planes):
    return (len(planes) * PLANE + 127) // 128 * 128


def screen_kernel(place, own_ref, other_ref, *outs):
    z = place[0]
    rows = 16
    lane = lax.broadcasted_iota(jnp.int32, (rows, 128), 1)

    def plane_of(ref, row, delta, offset):
        plane = lax.rem(z + delta, 8)
        odd = lax.rem(plane, 2)
        column = pl.multiple_of(plane * PLANE - odd * 64, 128)
        window = ref[row, pl.ds(column, 384)]
        turned = pltpu.roll(window, 64 if offset else 320, 1)
        return jnp.where((odd == 1) if offset else (odd == 0), window, turned)

    for source, ref in enumerate((own_ref, other_ref)):

        def body(step, carry, source=source, ref=ref):
            part = step // 10
            row = pl.ds(pl.multiple_of(step * rows, rows), rows)
            target = pl.multiple_of(part * PLANE + source * (PLANE // 2) + (step - part * 10) * rows, rows)
            for group, planes in enumerate((NEAR, MIDDLE, FAR)):
                for at in range(0, len(planes), 2):
                    a = plane_of(ref, row, planes[at], False)
                    if at + 1 < len(planes):
                        b = plane_of(ref, row, planes[at + 1], True)
                        middle = jnp.where(lane < 64, a[:, 256:], b[:, :128])
                        whole = jnp.concatenate([a[:, :256], middle, b[:, 128:]], axis=1)
                    else:
                        whole = jnp.concatenate([a[:, :256], jnp.where(lane < 64, a[:, 256:], 0.0)], axis=1)
                    top, rest = split(whole)
                    columns = slice(at * PLANE, at * PLANE + whole.shape[1])
                    outs[2 * group][pl.ds(target, rows), columns] = top
                    outs[2 * group + 1][pl.ds(target, rows), columns] = rest
            return carry

        lax.fori_loop(0, 20, body, 0)


def screen_call(place, own, other):
    shapes = [
        jax.ShapeDtypeStruct((2 * own.shape[0], padded(planes)), jnp.bfloat16)
        for planes in (NEAR, MIDDLE, FAR)
        for _ in range(2)
    ]
    return pl.pallas_call(
        screen_kernel,
        out_shape=shapes,
        in_specs=[SMEM, VMEM, VMEM],
        out_specs=[VMEM] * 6,
        compiler_params=params(20),
        name="screen",
    )(place, own, other)


def left_kernel(place, *refs):
    pieces, (high_ref, low_ref, work) = refs[:8], refs[8:]
    x = place[1]
    span = pieces[0].shape[0] // 2
    for core in range(2):
        for shift in range(4):
            shard = lax.rem(x - shift + 4, 4)
            for part in range(2):
                row = pl.multiple_of(part * 8 * span + core * 4 * span + shard * span, 8)
                work[pl.ds(row, span), :] = pieces[core * 4 + shift][part * span : (part + 1) * span, :]

    def body(block, carry):
        at = pl.ds(pl.multiple_of(block * 128, 128), 128)
        high_ref[at, :], low_ref[at, :] = split(work[:, at].T)
        return carry

    lax.fori_loop(0, work.shape[1] // 128, body, 0)


def left_call(place, pieces):
    depth, width = pieces[0].shape
    shape = jax.ShapeDtypeStruct((width, 8 * depth), jnp.bfloat16)
    return pl.pallas_call(
        left_kernel,
        out_shape=(shape, shape),
        in_specs=[SMEM] + [VMEM] * 8,
        out_specs=(VMEM, VMEM),
        scratch_shapes=[pltpu.VMEM((8 * depth, width), jnp.float32)],
        compiler_params=params(20),
        name="left",
    )(place, *pieces)


def load_right(place, runs, planes, high, low):
    y = place[2]
    for delta, ref, start, first, count in runs:
        spread = lax.rem(y + delta, 4) * SPAN

        def body(step, carry, ref=ref, start=start, first=first, spread=spread):
            unit = first + step
            row = pl.ds(pl.multiple_of(unit // 2 * PLANE + spread, 16), SPAN)
            column = pl.ds(pl.multiple_of(lax.rem(unit, 2) * HALF, HALF), HALF)
            top, rest = split(ref[pl.ds(pl.multiple_of(start + step * SPAN, 8), SPAN), :])
            high[row, column] = top
            low[row, column] = rest
            return carry

        lax.fori_loop(0, count, body, 0)
    used = planes * PLANE
    if used < high.shape[0]:
        for ref in (high, low):
            ref[used:, :] = jnp.zeros((ref.shape[0] - used, ref.shape[1]), ref.dtype)


def near_runs(first, first_down, first_up, second, second_down, second_up, two_down, two_up):
    skip = 3 * SPAN
    return (
        ((0, first, 0, 0, 6), (3, first_down, 0, 0, 6), (1, first_up, 0, 0, 6))
        + ((0, second, 0, 6, 4), (3, second_down, 0, 6, 4), (1, second_up, 0, 6, 4))
        + ((2, two_down, 0, 0, 3), (2, two_up, 0, 3, 3), (2, two_down, skip, 6, 2), (2, two_up, skip, 8, 2))
    )


def middle_runs(z_below, z_above, y_below, y_above):
    runs = ()
    for first, sides, across in ((0, z_below, y_below), (2, z_above, y_above)):
        runs += ((3, sides, 0, first, 2), (1, sides, 2 * SPAN, first, 2), (0, sides, 4 * SPAN, first, 2))
        runs += ((2, across, 0, first, 2),)
    return runs


def far_runs(below, above, across_low, across_high):
    return (
        ((3, below, 0, 0, 2), (1, above, 0, 0, 2), (0, below, 2 * SPAN, 0, 1), (0, above, 2 * SPAN, 1, 1))
        + ((2, across_low, 0, 0, 1), (2, across_high, 0, 1, 1))
    )


def group_kernel(runs, planes, place, *refs):
    count = len(refs) - 5 - (runs is middle_runs)
    rights, (high_ref, low_ref), rest = refs[:count], refs[count : count + 2], refs[count + 2 :]
    out_ref, rh, rl = rest[-3:]
    load_right(place, runs(*rights), planes, rh, rl)
    value = dot3(high_ref[...], low_ref[...], rh[...], rl[...])
    out_ref[...] = value if len(rest) == 3 else value + rest[0][...]


def group_call(runs, planes, place, rights, screens, total):
    rows, width = screens[0].shape
    return pl.pallas_call(
        functools.partial(group_kernel, runs, planes),
        out_shape=jax.ShapeDtypeStruct((rows, 2 * HALF), jnp.float32),
        in_specs=[SMEM] + [VMEM] * (len(rights) + 2 + len(total)),
        out_specs=VMEM,
        scratch_shapes=[pltpu.VMEM((width, 2 * HALF), jnp.bfloat16)] * 2,
        compiler_params=params(32),
        name="group",
    )(place, *rights, *screens, *total)


def pair_kernel(place, table, *refs):
    rights, (high_ref, low_ref, sum_ref, left_high, left_low, give_ref, kern, rh, rl) = refs[:4], refs[4:]
    load_right(place, far_runs(*rights), len(FAR), rh, rl)
    product = sum_ref[...] + dot3(high_ref[...], low_ref[...], rh[...], rl[...])
    mid = product.shape[0] // 2
    real = product[:mid, :HALF] - product[mid:, HALF:]
    imag = product[mid:, :HALF] + product[:mid, HALF:]
    applied = NG ** (-0.5) * jnp.concatenate(
        [jnp.concatenate([real, imag], axis=0), jnp.concatenate([imag, -real], axis=0)], axis=1
    )
    kern[...] = dot3(left_high[...], left_low[...], *split(applied))

    extract(place, table, 1 - place[3], kern, give_ref)


def extract(place, table, half, kern, out_ref):
    at = lambda x: lax.rem(x + 4 - place[1], 4)
    lane = lax.broadcasted_iota(jnp.int32, (BLK, 128), 1) // BLK
    upper = lax.broadcasted_iota(jnp.int32, (8, 128), 0) < 4

    def groups(pair, carry):
        for g in (pair * 2, pair * 2 + 1):
            slabs = [None, None]
            for u in range(8):
                slot = g * 8 + u
                row = pl.ds(pl.multiple_of(table[4 * half, slot], BLK), BLK)
                column = pl.multiple_of(table[4 * half + 1, slot], 128)
                shift = table[4 * half + 2, slot]
                target = lane == table[4 * half + 3, slot]
                for part in range(2):
                    slab = pltpu.roll(kern[row, pl.ds(column + part * HALF, 128)], shift, 1)
                    slabs[part] = jnp.where(target, slab, 0.0 if u == 0 else slabs[part])
            lanes = pl.ds(pl.multiple_of(g * 128, 128), 128)
            for side in range(2):
                real, imag = (slab[side * 8 : side * 8 + 8] for slab in slabs)
                out_ref[at(2 * side), :, lanes] = jnp.where(upper, real, pltpu.roll(imag, 4, 0))
                out_ref[at(2 * side + 1), :, lanes] = jnp.where(upper, pltpu.roll(real, 4, 0), imag)
        return carry

    out_ref[...] = jnp.zeros_like(out_ref)
    lax.fori_loop(0, (table[11, half] + 1) // 2, groups, 0)


def pair_call(place, table, rights, screens, total, left_high, left_low):
    rows = left_high.shape[0]
    return pl.pallas_call(
        pair_kernel,
        out_shape=(
            jax.ShapeDtypeStruct((4, 8, ROOM * BLK), jnp.float32),
            jax.ShapeDtypeStruct((rows, 2 * HALF), jnp.float32),
        ),
        in_specs=[SMEM, SMEM] + [VMEM] * (len(rights) + 5),
        out_specs=(VMEM, VMEM),
        scratch_shapes=[pltpu.VMEM((screens[0].shape[1], 2 * HALF), jnp.bfloat16)] * 2,
        compiler_params=params(24),
        name="pair",
    )(place, table, *rights, *screens, total, left_high, left_low)


def extract_kernel(place, table, kern, out_ref):
    extract(place, table, place[3], kern, out_ref)


def extract_call(place, table, kern):
    return pl.pallas_call(
        extract_kernel,
        out_shape=jax.ShapeDtypeStruct((4, 8, ROOM * BLK), jnp.float32),
        in_specs=[SMEM, SMEM, VMEM],
        out_specs=VMEM,
        compiler_params=params(8),
        name="extract",
    )(place, table, kern)


def add_kernel(one_ref, two_ref, *outs):
    for at, out_ref in enumerate(outs):
        out_ref[...] = one_ref[at] + two_ref[at]


def add_call(one, two):
    return pl.pallas_call(
        add_kernel,
        out_shape=[jax.ShapeDtypeStruct(one.shape[1:], one.dtype)] * one.shape[0],
        in_specs=[VMEM, VMEM],
        out_specs=[VMEM] * one.shape[0],
        compiler_params=params(8),
        name="add",
    )(one, two)


def owner_kernel(place, table, one_ref, two_ref, three_ref, four_ref, out_ref, work):
    total = (one_ref[...] + two_ref[...]) + (three_ref[...] + four_ref[...])
    width = total.shape[1]
    work[:, :width] = total
    work[:, width:] = jnp.zeros((8, work.shape[1] - width), jnp.float32)
    for chip in range(out_ref.shape[0]):
        start = table[8, chip * 2 + place[3]]
        column = pl.multiple_of(start // 8 * 128, 128)
        shift = lax.rem(384 - lax.rem(start, 8) * BLK, 384)
        out_ref[chip] = pltpu.roll(work[:, pl.ds(column, 384)], shift, 1)[:, :256]


def owner_call(place, table, parts):
    return pl.pallas_call(
        owner_kernel,
        out_shape=jax.ShapeDtypeStruct((32, 8, 256), jnp.float32),
        in_specs=[SMEM, SMEM] + [VMEM] * 4,
        out_specs=VMEM,
        scratch_shapes=[pltpu.VMEM((8, parts[0].shape[1] + 384), jnp.float32)],
        compiler_params=params(8),
        name="owner",
    )(place, table, *parts)


def last_kernel(place, table, parts_ref, out_ref):
    total = parts_ref[0]
    for chip in range(1, parts_ref.shape[0]):
        total = total + parts_ref[chip]
    held = table[9, (place[0] * 4 + place[2]) * 2 + place[3]]
    for slot in range(CAP):
        tile = total[:, slot // 8 * 128 : slot // 8 * 128 + 128]
        tile = pltpu.roll(tile, (128 - slot % 8 * BLK) % 128, 1)
        out_ref[slot] = jnp.where(slot < held, tile[:, :BLK], 0.0)


def last_call(place, table, parts):
    return pl.pallas_call(
        last_kernel,
        out_shape=jax.ShapeDtypeStruct((CAP, 8, BLK), jnp.float32),
        in_specs=[SMEM, SMEM, VMEM],
        out_specs=VMEM,
        compiler_params=params(8),
        name="last",
    )(place, table, parts)


def pack_kernel(place, own_ref, other_ref, out_ref, work):
    core = place[3]
    width = own_ref.shape[2]
    for block in range(width // 128):
        lanes = pl.ds(block * 128, 128)
        rows = []
        for part in range(2):
            own, other = own_ref[part, :, lanes], other_ref[part, :, lanes]
            rows += [jnp.where(core == 0, own, other), jnp.where(core == 0, other, own)]
        rows = jnp.concatenate(rows + rows, axis=0)
        work[block * 128 : (block + 1) * 128, :] = rows.T
    half = lax.broadcasted_iota(jnp.int32, (8, 128), 1) < 64
    for chip in range(32):
        at = pl.multiple_of(chip * 80 + core * 40, 8)
        tiles = [work[pl.ds(at + 8 * t, 8), :] for t in range(5)]
        out_ref[chip * 20 : chip * 20 + 8, :] = jnp.where(half, tiles[0], tiles[1])
        out_ref[chip * 20 + 8 : chip * 20 + 16, :] = jnp.where(half, tiles[2], tiles[3])
        last = jnp.where(half, tiles[4], pltpu.roll(tiles[4], 4, 0))
        out_ref[chip * 20 + 16 : chip * 20 + 20, :] = last[:4]


def pack_call(place, own, other):
    width = own.shape[2]
    return pl.pallas_call(
        pack_kernel,
        out_shape=jax.ShapeDtypeStruct((32 * 20, 128), jnp.float32),
        in_specs=[SMEM, VMEM, VMEM],
        out_specs=VMEM,
        scratch_shapes=[pltpu.VMEM((width, 128), jnp.float32)],
        name="pack",
    )(place, own, other)


def unpack_kernel(place, table, in_ref, columns_ref, keep_ref, give_ref):
    core = place[3]
    quarter = lax.broadcasted_iota(jnp.int32, (8, 128), 1) // 32
    upper = lax.broadcasted_iota(jnp.int32, (8, 128), 0) < 4
    for group in range(8):
        tiles = [[None] * 5 for _ in range(2)]
        for u in range(4):
            at = (group * 4 + u) * 20
            one, two = in_ref[at : at + 8, :], in_ref[at + 8 : at + 16, :]
            end = in_ref[at + 12 : at + 20, :]
            end = jnp.where(upper, pltpu.roll(end, 4, 0), pltpu.roll(end, 64, 1))
            for t, (source, first) in enumerate(((one, 0), (one, 64), (two, 0), (two, 64), (end, 0))):
                for part in range(2):
                    by = (u * 32 - first - part * 32) % 128
                    turned = pltpu.roll(source, by, 1) if by else source
                    old = tiles[part][t]
                    tiles[part][t] = turned if old is None else jnp.where(quarter == u, turned, old)
        for part in range(2):
            for t in range(5):
                row = part * 40 + t * 8
                columns_ref[row : row + 8, group * 128 : (group + 1) * 128] = tiles[part][t]
    select(table, 1 - core, columns_ref, give_ref)
    select(table, core, columns_ref, keep_ref)


def select(table, which, columns_ref, out_ref):
    eighth = lax.broadcasted_iota(jnp.int32, (80, 128), 1) // BLK
    for group in range(2):
        slab = None
        for u in range(8):
            block = table[10, which * (USED // 2) + group * 8 + u]
            column = pl.multiple_of(block // 8 * 128, 128)
            by = lax.rem(u * BLK + 128 - lax.rem(block, 8) * BLK, 128)
            turned = pltpu.roll(columns_ref[:, pl.ds(column, 128)], by, 1)
            slab = turned if slab is None else jnp.where(eighth == u, turned, slab)
        out_ref[:, group * 128 : (group + 1) * 128] = slab


def unpack_call(place, table, pieces):
    return pl.pallas_call(
        unpack_kernel,
        out_shape=(
            jax.ShapeDtypeStruct((80, 1024), jnp.float32),
            jax.ShapeDtypeStruct((80, HALF), jnp.float32),
            jax.ShapeDtypeStruct((80, HALF), jnp.float32),
        ),
        in_specs=[SMEM, SMEM, VMEM],
        out_specs=(VMEM, VMEM, VMEM),
        compiler_params=params(8),
        name="unpack",
    )(place, table, pieces)


def shard_kernel(place, keep_ref, take_ref, out_ref):
    core = place[3]
    for part in range(2):
        out_ref[pl.ds(pl.multiple_of(part * 80 + core * 40, 8), 40), :] = keep_ref[part * 40 : part * 40 + 40, :]
        out_ref[pl.ds(pl.multiple_of(part * 80 + 40 - core * 40, 8), 40), :] = take_ref[part * 40 : part * 40 + 40, :]


def shard_call(place, keep, take):
    return pl.pallas_call(
        shard_kernel,
        out_shape=jax.ShapeDtypeStruct((160, HALF), jnp.float32),
        in_specs=[SMEM, VMEM, VMEM],
        out_specs=VMEM,
        compiler_params=params(8),
        name="shard",
    )(place, keep, take)


def after(array, *others):
    return lax.optimization_barrier((array, *others))[0]


def shards(densities, screened, pairs, owners):
    span = screened.shape[2]
    place = jnp.stack([lax.axis_index(axis) for axis in ("z", "x", "y", "core")]).astype(jnp.int32)
    shift = lambda array, axis, by: lax.ppermute(array, axis, ring(lax.axis_size(axis), by))
    swap = lambda array: lax.ppermute(array, "core", SWAP)
    join = lambda *arrays: jnp.concatenate(arrays, axis=0)
    hold = lax.optimization_barrier

    pieces = pack_call(place, densities, swap(densities))
    table = plan_call(place, after(pairs, pieces), owners.reshape(1, -1))
    mine = lax.all_to_all(pieces.reshape(32, 1, -1), ("z", "y"), 0, 0, tiled=True).reshape(pieces.shape)

    screen = screened.reshape(2 * 4 * span, -1)
    mine, other = hold((mine, swap(after(screen, pieces))))

    columns, keep, give = unpack_call(place, table, mine)
    shard = shard_call(place, keep, swap(give))

    block = 2 * SPAN
    below2, above2 = shift(shard, "z", 2), shift(shard, "z", -2)
    below, above, columns = hold((shift(shard, "z", 1), shift(shard, "z", -1), columns))
    first = join(shard, below, above)
    first_down, first_up = shift(first, "y", 1), shift(first, "y", -1)
    around = [columns, shift(columns, "x", 1), None, None]
    below2, above2, first, columns = hold((below2, above2, first, columns))
    second = join(below2, above2)
    second_down, second_up = shift(second, "y", 1), shift(second, "y", -1)
    around[3] = shift(columns, "x", 3)
    screens = screen_call(place, after(screen, second), other)
    first_down, first_up, around[1], below2, above2, *screens = hold(
        (first_down, first_up, around[1], below2, above2, *screens)
    )
    second_down, second_up, first_down, around[3] = hold((second_down, second_up, first_down, around[3]))

    z_below = shift(join(second_down[:block], second_up[:block], second[:block]), "z", 1)
    z_above = shift(join(second_down[block:], second_up[block:], second[block:]), "z", -1)
    two_down = shift(join(first_down[: 3 * SPAN], second_down[:block]), "y", 1)
    two_up = shift(join(first_up[3 * SPAN :], second_up[block:]), "y", -1)
    around[2] = shift(after(columns, second_down), "x", 2)
    swapped = [swap(columns), swap(around[1]), None, None]
    two_down, two_up, z_below, z_above, around[2], swapped[0], swapped[1] = hold(
        (two_down, two_up, z_below, z_above, around[2], swapped[0], swapped[1])
    )

    y_below, y_above = shift(z_below[:block], "y", 1), shift(z_above[block : 2 * block], "y", -1)
    far_below = shift(join(z_below[:block], z_below[2 * block : 2 * block + SPAN]), "z", 1)
    far_above = shift(join(z_above[block : 2 * block], z_above[2 * block + SPAN :]), "z", -1)
    rights = (first, first_down, first_up, second, second_down, second_up, two_down, two_up)
    total = group_call(near_runs, len(NEAR), place, rights, screens[:2], ())
    swapped[2:] = [swap(array) for array in around[2:]]
    y_below, y_above, far_below, far_above, total, *swapped[2:] = hold(
        (y_below, y_above, far_below, far_above, total, *swapped[2:])
    )

    across_low, across_high = shift(far_below[:SPAN], "y", 1), shift(far_above[SPAN : 2 * SPAN], "y", -1)
    rights = (z_below, z_above, y_below, y_above)
    total = group_call(middle_runs, len(MIDDLE), place, rights, screens[2:4], (total,))
    left_high, left_low = left_call(place, around + swapped)
    across_low, across_high, total, left_high, left_low = hold((across_low, across_high, total, left_high, left_low))
    rights = (far_below, far_above, across_low, across_high)
    give, kern = pair_call(place, table, rights, screens[4:], total, left_high, left_low)

    parts = add_call(extract_call(place, table, kern), swap(give))
    parts = [parts[0]] + [shift(parts[by], "x", by) for by in (1, 2, 3)]
    parts = owner_call(place, table, parts)
    parts = lax.all_to_all(parts, ("z", "y"), 0, 0, tiled=True)
    return last_call(place, table, parts).reshape(1, CAP, 2, 4, BLK)


def solution(mesh):
    fine = Mesh(mesh.devices.reshape(8, 4, 2, 4), ("z", "y", "core", "x"))
    in_specs = (P(None, BAND, "x"), P(None, None, BAND, "x"), P(), P())
    out_specs = P(BAND, None, None, "x", None)
    return jax.shard_map(shards, mesh=fine, in_specs=in_specs, out_specs=out_specs, check_vma=False)
```

```python
import functools

import jax
import jax.numpy as jnp
from jax import lax
from jax.experimental import pallas as pl
from jax.experimental.pallas import tpu as pltpu
from jax.sharding import Mesh
from jax.sharding import PartitionSpec as P

NG = 10240
CAP = 12
BLK = 16
USED = 32
HALF = USED // 2 * BLK
BAND = ("z", "y", "core")
SWAP = ((0, 1), (1, 0))
SMEM = pl.BlockSpec(memory_space=pltpu.SMEM)
VMEM = pl.BlockSpec(memory_space=pltpu.VMEM)
SPAN = 80
PLANE = 320
NEAR = (0, 7, 1, 6, 2)
MIDDLE = (5, 3)
FAR = (4,)
ROOM = 224


def ring(n, shift):
    return [(i, (i + shift) % n) for i in range(n)]


def params(mib):
    return pltpu.CompilerParams(vmem_limit_bytes=mib * 1024 * 1024)


def split(x):
    high = x.astype(jnp.bfloat16)
    return high, (x - high.astype(jnp.float32)).astype(jnp.bfloat16)


def dot(former, latter):
    return jnp.dot(former, latter, preferred_element_type=jnp.float32)


def dot3(high, low, former, latter):
    return dot(high, former) + dot(high, latter) + dot(low, former)


def plan_kernel(place, pairs_ref, owners_ref, out_ref):
    size = 256
    down = lax.broadcasted_iota(jnp.int32, (size, size), 0)
    across = lax.broadcasted_iota(jnp.int32, (size, size), 1)
    one = lambda condition: jnp.where(condition, 1.0, 0.0)
    to_row = lambda column: jnp.sum(jnp.where(down == across, column, 0.0), axis=0, keepdims=True)
    to_column = lambda row: jnp.sum(jnp.where(down == across, row, 0.0), axis=1, keepdims=True)
    rows, columns = down.astype(jnp.float32), across.astype(jnp.float32)
    left, right = pairs_ref[:, 0:1].astype(jnp.float32), pairs_ref[:, 1:2].astype(jnp.float32)
    owner_row = owners_ref[...].astype(jnp.float32)
    owner = to_column(owner_row)

    used = jnp.max(one(right == columns), axis=0, keepdims=True)
    used_column = to_column(used)
    rank = jnp.sum(jnp.where(columns < rows, used, 0.0), axis=1, keepdims=True)
    used_list = jnp.sum(jnp.where((rank == columns) & (used_column > 0), rows, 0.0), axis=0, keepdims=True)
    right_rank = jnp.sum(jnp.where(columns < right, used, 0.0), axis=1, keepdims=True)

    parity = lambda value: value - 2.0 * jnp.floor(value * 0.5)
    count = jnp.sum(one(owner == columns), axis=0, keepdims=True)
    same = parity(rows) == parity(columns)
    offset = jnp.sum(jnp.where((rows < columns) & same, to_column(count), 0.0), axis=0, keepdims=True)
    ahead = (owner_row < owner) | ((owner_row == owner) & (across < down))
    ahead = ahead & (parity(owner_row) == parity(owner))
    position = jnp.sum(one(ahead), axis=1, keepdims=True)

    core = place[3].astype(jnp.float32)
    local = right_rank - core * (USED // 2)
    here = (local >= 0) & (local < USED // 2)
    local = jnp.where(here, local, 0.0)
    lane = lax.broadcasted_iota(jnp.int32, (1, size), 1)
    groups = jnp.zeros((1, size), jnp.float32)
    for half in range(2):
        hit = (position == columns) & (parity(owner) == half)
        pick = lambda column: jnp.sum(jnp.where(hit, column, 0.0), axis=0, keepdims=True).astype(jnp.int32)
        at = pick(local)
        out_ref[4 * half : 4 * half + 1, :] = pick(left) * BLK
        out_ref[4 * half + 1 : 4 * half + 2, :] = at // 8 * 128
        out_ref[4 * half + 2 : 4 * half + 3, :] = (lane + 8 - at % 8) % 8 * BLK
        out_ref[4 * half + 3 : 4 * half + 4, :] = jnp.where(pick(one(here)) > 0, lane % 8, -1)
        total = jnp.sum(one(parity(owner_row) == half))
        groups = jnp.where(lane == half, jnp.floor((total + 7.0) / 8.0), groups)
    for at, row in enumerate((offset, count, used_list, groups)):
        out_ref[8 + at : 9 + at, :] = row.astype(jnp.int32)


def plan_call(place, pairs, owners):
    return pl.pallas_call(
        plan_kernel,
        out_shape=jax.ShapeDtypeStruct((16, pairs.shape[0]), jnp.int32),
        in_specs=[SMEM, VMEM, VMEM],
        out_specs=VMEM,
        compiler_params=params(8),
        name="plan",
    )(place, pairs, owners)


def padded(planes):
    return (len(planes) * PLANE + 127) // 128 * 128


def screen_kernel(place, own_ref, other_ref, *outs):
    z = place[0]
    rows = 16
    lane = lax.broadcasted_iota(jnp.int32, (rows, 128), 1)

    def plane_of(ref, row, delta, offset):
        plane = lax.rem(z + delta, 8)
        odd = lax.rem(plane, 2)
        column = pl.multiple_of(plane * PLANE - odd * 64, 128)
        window = ref[row, pl.ds(column, 384)]
        turned = pltpu.roll(window, 64 if offset else 320, 1)
        return jnp.where((odd == 1) if offset else (odd == 0), window, turned)

    for source, ref in enumerate((own_ref, other_ref)):

        def body(step, carry, source=source, ref=ref):
            part = step // 10
            row = pl.ds(pl.multiple_of(step * rows, rows), rows)
            target = pl.multiple_of(part * PLANE + source * (PLANE // 2) + (step - part * 10) * rows, rows)
            for group, planes in enumerate((NEAR, MIDDLE, FAR)):
                for at in range(0, len(planes), 2):
                    a = plane_of(ref, row, planes[at], False)
                    if at + 1 < len(planes):
                        b = plane_of(ref, row, planes[at + 1], True)
                        middle = jnp.where(lane < 64, a[:, 256:], b[:, :128])
                        whole = jnp.concatenate([a[:, :256], middle, b[:, 128:]], axis=1)
                    else:
                        whole = jnp.concatenate([a[:, :256], jnp.where(lane < 64, a[:, 256:], 0.0)], axis=1)
                    top, rest = split(whole)
                    columns = slice(at * PLANE, at * PLANE + whole.shape[1])
                    outs[2 * group][pl.ds(target, rows), columns] = top
                    outs[2 * group + 1][pl.ds(target, rows), columns] = rest
            return carry

        lax.fori_loop(0, 20, body, 0)


def screen_call(place, own, other):
    shapes = [
        jax.ShapeDtypeStruct((2 * own.shape[0], padded(planes)), jnp.bfloat16)
        for planes in (NEAR, MIDDLE, FAR)
        for _ in range(2)
    ]
    return pl.pallas_call(
        screen_kernel,
        out_shape=shapes,
        in_specs=[SMEM, VMEM, VMEM],
        out_specs=[VMEM] * 6,
        compiler_params=params(20),
        name="screen",
    )(place, own, other)


def left_kernel(place, *refs):
    pieces, (high_ref, low_ref, work) = refs[:8], refs[8:]
    x = place[1]
    span = pieces[0].shape[0] // 2
    for core in range(2):
        for shift in range(4):
            shard = lax.rem(x - shift + 4, 4)
            for part in range(2):
                row = pl.multiple_of(part * 8 * span + core * 4 * span + shard * span, 8)
                work[pl.ds(row, span), :] = pieces[core * 4 + shift][part * span : (part + 1) * span, :]

    def body(block, carry):
        at = pl.ds(pl.multiple_of(block * 128, 128), 128)
        high_ref[at, :], low_ref[at, :] = split(work[:, at].T)
        return carry

    lax.fori_loop(0, work.shape[1] // 128, body, 0)


def left_call(place, pieces):
    depth, width = pieces[0].shape
    shape = jax.ShapeDtypeStruct((width, 8 * depth), jnp.bfloat16)
    return pl.pallas_call(
        left_kernel,
        out_shape=(shape, shape),
        in_specs=[SMEM] + [VMEM] * 8,
        out_specs=(VMEM, VMEM),
        scratch_shapes=[pltpu.VMEM((8 * depth, width), jnp.float32)],
        compiler_params=params(20),
        name="left",
    )(place, *pieces)


def load_right(place, runs, planes, high, low):
    y = place[2]
    for delta, ref, start, first, count in runs:
        spread = lax.rem(y + delta, 4) * SPAN

        def body(step, carry, ref=ref, start=start, first=first, spread=spread):
            unit = first + step
            row = pl.ds(pl.multiple_of(unit // 2 * PLANE + spread, 16), SPAN)
            column = pl.ds(pl.multiple_of(lax.rem(unit, 2) * HALF, HALF), HALF)
            top, rest = split(ref[pl.ds(pl.multiple_of(start + step * SPAN, 8), SPAN), :])
            high[row, column] = top
            low[row, column] = rest
            return carry

        lax.fori_loop(0, count, body, 0)
    used = planes * PLANE
    if used < high.shape[0]:
        for ref in (high, low):
            ref[used:, :] = jnp.zeros((ref.shape[0] - used, ref.shape[1]), ref.dtype)


def near_runs(first, first_down, first_up, second, second_down, second_up, two_down, two_up):
    skip = 3 * SPAN
    return (
        ((0, first, 0, 0, 6), (3, first_down, 0, 0, 6), (1, first_up, 0, 0, 6))
        + ((0, second, 0, 6, 4), (3, second_down, 0, 6, 4), (1, second_up, 0, 6, 4))
        + ((2, two_down, 0, 0, 3), (2, two_up, 0, 3, 3), (2, two_down, skip, 6, 2), (2, two_up, skip, 8, 2))
    )


def middle_runs(z_below, z_above, y_below, y_above):
    runs = ()
    for first, sides, across in ((0, z_below, y_below), (2, z_above, y_above)):
        runs += ((3, sides, 0, first, 2), (1, sides, 2 * SPAN, first, 2), (0, sides, 4 * SPAN, first, 2))
        runs += ((2, across, 0, first, 2),)
    return runs


def far_runs(below, above, across_low, across_high):
    return (
        ((3, below, 0, 0, 2), (1, above, 0, 0, 2), (0, below, 2 * SPAN, 0, 1), (0, above, 2 * SPAN, 1, 1))
        + ((2, across_low, 0, 0, 1), (2, across_high, 0, 1, 1))
    )


def group_kernel(runs, planes, place, *refs):
    count = len(refs) - 5 - (runs is middle_runs)
    rights, (high_ref, low_ref), rest = refs[:count], refs[count : count + 2], refs[count + 2 :]
    out_ref, rh, rl = rest[-3:]
    load_right(place, runs(*rights), planes, rh, rl)
    value = dot3(high_ref[...], low_ref[...], rh[...], rl[...])
    out_ref[...] = value if len(rest) == 3 else value + rest[0][...]


def group_call(runs, planes, place, rights, screens, total):
    rows, width = screens[0].shape
    return pl.pallas_call(
        functools.partial(group_kernel, runs, planes),
        out_shape=jax.ShapeDtypeStruct((rows, 2 * HALF), jnp.float32),
        in_specs=[SMEM] + [VMEM] * (len(rights) + 2 + len(total)),
        out_specs=VMEM,
        scratch_shapes=[pltpu.VMEM((width, 2 * HALF), jnp.bfloat16)] * 2,
        compiler_params=params(32),
        name="group",
    )(place, *rights, *screens, *total)


def pair_kernel(place, table, *refs):
    rights, (high_ref, low_ref, sum_ref, left_high, left_low, give_ref, kern, rh, rl) = refs[:4], refs[4:]
    load_right(place, far_runs(*rights), len(FAR), rh, rl)
    product = sum_ref[...] + dot3(high_ref[...], low_ref[...], rh[...], rl[...])
    mid = product.shape[0] // 2
    real = product[:mid, :HALF] - product[mid:, HALF:]
    imag = product[mid:, :HALF] + product[:mid, HALF:]
    applied = NG ** (-0.5) * jnp.concatenate(
        [jnp.concatenate([real, imag], axis=0), jnp.concatenate([imag, -real], axis=0)], axis=1
    )
    kern[...] = dot3(left_high[...], left_low[...], *split(applied))

    extract(place, table, 1 - place[3], kern, give_ref)


def extract(place, table, half, kern, out_ref):
    at = lambda x: lax.rem(x + 4 - place[1], 4)
    lane = lax.broadcasted_iota(jnp.int32, (BLK, 128), 1) // BLK
    upper = lax.broadcasted_iota(jnp.int32, (8, 128), 0) < 4

    def groups(pair, carry):
        for g in (pair * 2, pair * 2 + 1):
            slabs = [None, None]
            for u in range(8):
                slot = g * 8 + u
                row = pl.ds(pl.multiple_of(table[4 * half, slot], BLK), BLK)
                column = pl.multiple_of(table[4 * half + 1, slot], 128)
                shift = table[4 * half + 2, slot]
                target = lane == table[4 * half + 3, slot]
                for part in range(2):
                    slab = pltpu.roll(kern[row, pl.ds(column + part * HALF, 128)], shift, 1)
                    slabs[part] = jnp.where(target, slab, 0.0 if u == 0 else slabs[part])
            lanes = pl.ds(pl.multiple_of(g * 128, 128), 128)
            for side in range(2):
                real, imag = (slab[side * 8 : side * 8 + 8] for slab in slabs)
                out_ref[at(2 * side), :, lanes] = jnp.where(upper, real, pltpu.roll(imag, 4, 0))
                out_ref[at(2 * side + 1), :, lanes] = jnp.where(upper, pltpu.roll(real, 4, 0), imag)
        return carry

    out_ref[...] = jnp.zeros_like(out_ref)
    lax.fori_loop(0, (table[11, half] + 1) // 2, groups, 0)


def pair_call(place, table, rights, screens, total, left_high, left_low):
    rows = left_high.shape[0]
    return pl.pallas_call(
        pair_kernel,
        out_shape=(
            jax.ShapeDtypeStruct((4, 8, ROOM * BLK), jnp.float32),
            jax.ShapeDtypeStruct((rows, 2 * HALF), jnp.float32),
        ),
        in_specs=[SMEM, SMEM] + [VMEM] * (len(rights) + 5),
        out_specs=(VMEM, VMEM),
        scratch_shapes=[pltpu.VMEM((screens[0].shape[1], 2 * HALF), jnp.bfloat16)] * 2,
        compiler_params=params(24),
        name="pair",
    )(place, table, *rights, *screens, total, left_high, left_low)


def extract_kernel(place, table, kern, out_ref):
    extract(place, table, place[3], kern, out_ref)


def extract_call(place, table, kern):
    return pl.pallas_call(
        extract_kernel,
        out_shape=jax.ShapeDtypeStruct((4, 8, ROOM * BLK), jnp.float32),
        in_specs=[SMEM, SMEM, VMEM],
        out_specs=VMEM,
        compiler_params=params(8),
        name="extract",
    )(place, table, kern)


def add_kernel(one_ref, two_ref, *outs):
    for at, out_ref in enumerate(outs):
        out_ref[...] = one_ref[at] + two_ref[at]


def add_call(one, two):
    return pl.pallas_call(
        add_kernel,
        out_shape=[jax.ShapeDtypeStruct(one.shape[1:], one.dtype)] * one.shape[0],
        in_specs=[VMEM, VMEM],
        out_specs=[VMEM] * one.shape[0],
        compiler_params=params(8),
        name="add",
    )(one, two)


def owner_kernel(place, table, one_ref, two_ref, three_ref, four_ref, out_ref, work):
    total = (one_ref[...] + two_ref[...]) + (three_ref[...] + four_ref[...])
    width = total.shape[1]
    work[:, :width] = total
    work[:, width:] = jnp.zeros((8, work.shape[1] - width), jnp.float32)
    for chip in range(out_ref.shape[0]):
        start = table[8, chip * 2 + place[3]]
        column = pl.multiple_of(start // 8 * 128, 128)
        shift = lax.rem(384 - lax.rem(start, 8) * BLK, 384)
        out_ref[chip] = pltpu.roll(work[:, pl.ds(column, 384)], shift, 1)[:, :256]


def owner_call(place, table, parts):
    return pl.pallas_call(
        owner_kernel,
        out_shape=jax.ShapeDtypeStruct((32, 8, 256), jnp.float32),
        in_specs=[SMEM, SMEM] + [VMEM] * 4,
        out_specs=VMEM,
        scratch_shapes=[pltpu.VMEM((8, parts[0].shape[1] + 384), jnp.float32)],
        compiler_params=params(8),
        name="owner",
    )(place, table, *parts)


def last_kernel(place, table, parts_ref, out_ref):
    total = parts_ref[0]
    for chip in range(1, parts_ref.shape[0]):
        total = total + parts_ref[chip]
    held = table[9, (place[0] * 4 + place[2]) * 2 + place[3]]
    for slot in range(CAP):
        tile = total[:, slot // 8 * 128 : slot // 8 * 128 + 128]
        tile = pltpu.roll(tile, (128 - slot % 8 * BLK) % 128, 1)
        out_ref[slot] = jnp.where(slot < held, tile[:, :BLK], 0.0)


def last_call(place, table, parts):
    return pl.pallas_call(
        last_kernel,
        out_shape=jax.ShapeDtypeStruct((CAP, 8, BLK), jnp.float32),
        in_specs=[SMEM, SMEM, VMEM],
        out_specs=VMEM,
        compiler_params=params(8),
        name="last",
    )(place, table, parts)


def pack_kernel(place, own_ref, other_ref, out_ref, work):
    core = place[3]
    width = own_ref.shape[2]
    for block in range(width // 128):
        lanes = pl.ds(block * 128, 128)
        rows = []
        for part in range(2):
            own, other = own_ref[part, :, lanes], other_ref[part, :, lanes]
            rows += [jnp.where(core == 0, own, other), jnp.where(core == 0, other, own)]
        rows = jnp.concatenate(rows + rows, axis=0)
        work[block * 128 : (block + 1) * 128, :] = rows.T
    half = lax.broadcasted_iota(jnp.int32, (8, 128), 1) < 64
    for chip in range(32):
        at = pl.multiple_of(chip * 80 + core * 40, 8)
        tiles = [work[pl.ds(at + 8 * t, 8), :] for t in range(5)]
        out_ref[chip * 20 : chip * 20 + 8, :] = jnp.where(half, tiles[0], tiles[1])
        out_ref[chip * 20 + 8 : chip * 20 + 16, :] = jnp.where(half, tiles[2], tiles[3])
        last = jnp.where(half, tiles[4], pltpu.roll(tiles[4], 4, 0))
        out_ref[chip * 20 + 16 : chip * 20 + 20, :] = last[:4]


def pack_call(place, own, other):
    width = own.shape[2]
    return pl.pallas_call(
        pack_kernel,
        out_shape=jax.ShapeDtypeStruct((32 * 20, 128), jnp.float32),
        in_specs=[SMEM, VMEM, VMEM],
        out_specs=VMEM,
        scratch_shapes=[pltpu.VMEM((width, 128), jnp.float32)],
        name="pack",
    )(place, own, other)


def unpack_kernel(place, table, in_ref, columns_ref, keep_ref, give_ref):
    core = place[3]
    quarter = lax.broadcasted_iota(jnp.int32, (8, 128), 1) // 32
    upper = lax.broadcasted_iota(jnp.int32, (8, 128), 0) < 4
    for group in range(8):
        tiles = [[None] * 5 for _ in range(2)]
        for u in range(4):
            at = (group * 4 + u) * 20
            one, two = in_ref[at : at + 8, :], in_ref[at + 8 : at + 16, :]
            end = in_ref[at + 12 : at + 20, :]
            end = jnp.where(upper, pltpu.roll(end, 4, 0), pltpu.roll(end, 64, 1))
            for t, (source, first) in enumerate(((one, 0), (one, 64), (two, 0), (two, 64), (end, 0))):
                for part in range(2):
                    by = (u * 32 - first - part * 32) % 128
                    turned = pltpu.roll(source, by, 1) if by else source
                    old = tiles[part][t]
                    tiles[part][t] = turned if old is None else jnp.where(quarter == u, turned, old)
        for part in range(2):
            for t in range(5):
                row = part * 40 + t * 8
                columns_ref[row : row + 8, group * 128 : (group + 1) * 128] = tiles[part][t]
    select(table, 1 - core, columns_ref, give_ref)
    select(table, core, columns_ref, keep_ref)


def select(table, which, columns_ref, out_ref):
    eighth = lax.broadcasted_iota(jnp.int32, (80, 128), 1) // BLK
    for group in range(2):
        slab = None
        for u in range(8):
            block = table[10, which * (USED // 2) + group * 8 + u]
            column = pl.multiple_of(block // 8 * 128, 128)
            by = lax.rem(u * BLK + 128 - lax.rem(block, 8) * BLK, 128)
            turned = pltpu.roll(columns_ref[:, pl.ds(column, 128)], by, 1)
            slab = turned if slab is None else jnp.where(eighth == u, turned, slab)
        out_ref[:, group * 128 : (group + 1) * 128] = slab


def unpack_call(place, table, pieces):
    return pl.pallas_call(
        unpack_kernel,
        out_shape=(
            jax.ShapeDtypeStruct((80, 1024), jnp.float32),
            jax.ShapeDtypeStruct((80, HALF), jnp.float32),
            jax.ShapeDtypeStruct((80, HALF), jnp.float32),
        ),
        in_specs=[SMEM, SMEM, VMEM],
        out_specs=(VMEM, VMEM, VMEM),
        compiler_params=params(8),
        name="unpack",
    )(place, table, pieces)


def shard_kernel(place, keep_ref, take_ref, out_ref):
    core = place[3]
    for part in range(2):
        out_ref[pl.ds(pl.multiple_of(part * 80 + core * 40, 8), 40), :] = keep_ref[part * 40 : part * 40 + 40, :]
        out_ref[pl.ds(pl.multiple_of(part * 80 + 40 - core * 40, 8), 40), :] = take_ref[part * 40 : part * 40 + 40, :]


def shard_call(place, keep, take):
    return pl.pallas_call(
        shard_kernel,
        out_shape=jax.ShapeDtypeStruct((160, HALF), jnp.float32),
        in_specs=[SMEM, VMEM, VMEM],
        out_specs=VMEM,
        compiler_params=params(8),
        name="shard",
    )(place, keep, take)


def after(array, *others):
    return lax.optimization_barrier((array, *others))[0]


def shards(densities, screened, pairs, owners):
    span = screened.shape[2]
    place = jnp.stack([lax.axis_index(axis) for axis in ("z", "x", "y", "core")]).astype(jnp.int32)
    shift = lambda array, axis, by: lax.ppermute(array, axis, ring(lax.axis_size(axis), by))
    swap = lambda array: lax.ppermute(array, "core", SWAP)
    join = lambda *arrays: jnp.concatenate(arrays, axis=0)
    hold = lax.optimization_barrier

    pieces = pack_call(place, densities, swap(densities))
    table = plan_call(place, after(pairs, pieces), owners.reshape(1, -1))
    mine = lax.all_to_all(pieces.reshape(32, 1, -1), ("z", "y"), 0, 0, tiled=True).reshape(pieces.shape)

    screen = screened.reshape(2 * 4 * span, -1)
    mine, other = hold((mine, swap(after(screen, pieces))))

    columns, keep, give = unpack_call(place, table, mine)
    shard = shard_call(place, keep, swap(give))

    block = 2 * SPAN
    below2, above2 = shift(shard, "z", 2), shift(shard, "z", -2)
    below, above, columns = hold((shift(shard, "z", 1), shift(shard, "z", -1), columns))
    first = join(shard, below, above)
    first_down, first_up = shift(first, "y", 1), shift(first, "y", -1)
    below2, above2, first, columns = hold((below2, above2, first, columns))
    around = [columns, shift(columns, "x", 1), None, None]
    second = join(below2, above2)
    second_down, second_up = shift(second, "y", 1), shift(second, "y", -1)
    screens = screen_call(place, after(screen, second), other)
    first_down, first_up, around[1], below2, above2, *screens = hold(
        (first_down, first_up, around[1], below2, above2, *screens)
    )
    around[2:] = [shift(after(columns, first_down), "x", by) for by in (2, 3)]
    second_down, second_up, first_down = hold((second_down, second_up, first_down))

    z_below = shift(join(second_down[:block], second_up[:block], second[:block]), "z", 1)
    z_above = shift(join(second_down[block:], second_up[block:], second[block:]), "z", -1)
    two_down = shift(join(first_down[: 3 * SPAN], second_down[:block]), "y", 1)
    two_up = shift(join(first_up[3 * SPAN :], second_up[block:]), "y", -1)
    swapped = [swap(columns), swap(around[1]), None, None]
    two_down, two_up, z_below, z_above, *around[2:] = hold((two_down, two_up, z_below, z_above, *around[2:]))

    y_below, y_above = shift(z_below[:block], "y", 1), shift(z_above[block : 2 * block], "y", -1)
    far_below = shift(join(z_below[:block], z_below[2 * block : 2 * block + SPAN]), "z", 1)
    far_above = shift(join(z_above[block : 2 * block], z_above[2 * block + SPAN :]), "z", -1)
    rights = (first, first_down, first_up, second, second_down, second_up, two_down, two_up)
    total = group_call(near_runs, len(NEAR), place, rights, screens[:2], ())
    swapped[2:] = [swap(array) for array in around[2:]]
    y_below, y_above, far_below, far_above, total, *swapped = hold(
        (y_below, y_above, far_below, far_above, total, *swapped)
    )

    across_low, across_high = shift(far_below[:SPAN], "y", 1), shift(far_above[SPAN : 2 * SPAN], "y", -1)
    rights = (z_below, z_above, y_below, y_above)
    total = group_call(middle_runs, len(MIDDLE), place, rights, screens[2:4], (total,))
    left_high, left_low = left_call(place, around + swapped)
    across_low, across_high, total, left_high, left_low = hold((across_low, across_high, total, left_high, left_low))
    rights = (far_below, far_above, across_low, across_high)
    give, kern = pair_call(place, table, rights, screens[4:], total, left_high, left_low)

    parts = add_call(extract_call(place, table, kern), swap(give))
    parts = [parts[0]] + [shift(parts[by], "x", by) for by in (1, 2, 3)]
    parts = owner_call(place, table, parts)
    parts = lax.all_to_all(parts, ("z", "y"), 0, 0, tiled=True)
    return last_call(place, table, parts).reshape(1, CAP, 2, 4, BLK)


def solution(mesh):
    fine = Mesh(mesh.devices.reshape(8, 4, 2, 4), ("z", "y", "core", "x"))
    in_specs = (P(None, BAND, "x"), P(None, None, BAND, "x"), P(), P())
    out_specs = P(BAND, None, None, "x", None)
    return jax.shard_map(shards, mesh=fine, in_specs=in_specs, out_specs=out_specs, check_vma=False)
```

```python
import functools

import jax
import jax.numpy as jnp
from jax import lax
from jax.experimental import pallas as pl
from jax.experimental.pallas import tpu as pltpu
from jax.sharding import Mesh
from jax.sharding import PartitionSpec as P

NG = 10240
CAP = 12
BLK = 16
USED = 32
HALF = USED // 2 * BLK
BAND = ("z", "y", "core")
SWAP = ((0, 1), (1, 0))
SMEM = pl.BlockSpec(memory_space=pltpu.SMEM)
VMEM = pl.BlockSpec(memory_space=pltpu.VMEM)
SPAN = 80
PLANE = 320
NEAR = (0, 7, 1, 6, 2)
MIDDLE = (5, 3)
FAR = (4,)
ROOM = 224


def ring(n, shift):
    return [(i, (i + shift) % n) for i in range(n)]


def params(mib):
    return pltpu.CompilerParams(vmem_limit_bytes=mib * 1024 * 1024)


def split(x):
    high = x.astype(jnp.bfloat16)
    return high, (x - high.astype(jnp.float32)).astype(jnp.bfloat16)


def dot(former, latter):
    return jnp.dot(former, latter, preferred_element_type=jnp.float32)


def dot3(high, low, former, latter):
    return dot(high, former) + dot(high, latter) + dot(low, former)


def plan_kernel(place, pairs_ref, owners_ref, out_ref):
    size = 256
    down = lax.broadcasted_iota(jnp.int32, (size, size), 0)
    across = lax.broadcasted_iota(jnp.int32, (size, size), 1)
    one = lambda condition: jnp.where(condition, 1.0, 0.0)
    to_row = lambda column: jnp.sum(jnp.where(down == across, column, 0.0), axis=0, keepdims=True)
    to_column = lambda row: jnp.sum(jnp.where(down == across, row, 0.0), axis=1, keepdims=True)
    rows, columns = down.astype(jnp.float32), across.astype(jnp.float32)
    left, right = pairs_ref[:, 0:1].astype(jnp.float32), pairs_ref[:, 1:2].astype(jnp.float32)
    owner_row = owners_ref[...].astype(jnp.float32)
    owner = to_column(owner_row)

    used = jnp.max(one(right == columns), axis=0, keepdims=True)
    used_column = to_column(used)
    rank = jnp.sum(jnp.where(columns < rows, used, 0.0), axis=1, keepdims=True)
    used_list = jnp.sum(jnp.where((rank == columns) & (used_column > 0), rows, 0.0), axis=0, keepdims=True)
    right_rank = jnp.sum(jnp.where(columns < right, used, 0.0), axis=1, keepdims=True)

    parity = lambda value: value - 2.0 * jnp.floor(value * 0.5)
    count = jnp.sum(one(owner == columns), axis=0, keepdims=True)
    same = parity(rows) == parity(columns)
    offset = jnp.sum(jnp.where((rows < columns) & same, to_column(count), 0.0), axis=0, keepdims=True)
    ahead = (owner_row < owner) | ((owner_row == owner) & (across < down))
    ahead = ahead & (parity(owner_row) == parity(owner))
    position = jnp.sum(one(ahead), axis=1, keepdims=True)

    core = place[3].astype(jnp.float32)
    local = right_rank - core * (USED // 2)
    here = (local >= 0) & (local < USED // 2)
    local = jnp.where(here, local, 0.0)
    lane = lax.broadcasted_iota(jnp.int32, (1, size), 1)
    groups = jnp.zeros((1, size), jnp.float32)
    for half in range(2):
        hit = (position == columns) & (parity(owner) == half)
        pick = lambda column: jnp.sum(jnp.where(hit, column, 0.0), axis=0, keepdims=True).astype(jnp.int32)
        at = pick(local)
        out_ref[4 * half : 4 * half + 1, :] = pick(left) * BLK
        out_ref[4 * half + 1 : 4 * half + 2, :] = at // 8 * 128
        out_ref[4 * half + 2 : 4 * half + 3, :] = (lane + 8 - at % 8) % 8 * BLK
        out_ref[4 * half + 3 : 4 * half + 4, :] = jnp.where(pick(one(here)) > 0, lane % 8, -1)
        total = jnp.sum(one(parity(owner_row) == half))
        groups = jnp.where(lane == half, jnp.floor((total + 7.0) / 8.0), groups)
    for at, row in enumerate((offset, count, used_list, groups)):
        out_ref[8 + at : 9 + at, :] = row.astype(jnp.int32)


def plan_call(place, pairs, owners):
    return pl.pallas_call(
        plan_kernel,
        out_shape=jax.ShapeDtypeStruct((16, pairs.shape[0]), jnp.int32),
        in_specs=[SMEM, VMEM, VMEM],
        out_specs=VMEM,
        compiler_params=params(8),
        name="plan",
    )(place, pairs, owners)


def padded(planes):
    return (len(planes) * PLANE + 127) // 128 * 128


def screen_kernel(place, own_ref, other_ref, *outs):
    z = place[0]
    rows = 16
    lane = lax.broadcasted_iota(jnp.int32, (rows, 128), 1)

    def plane_of(ref, row, delta, offset):
        plane = lax.rem(z + delta, 8)
        odd = lax.rem(plane, 2)
        column = pl.multiple_of(plane * PLANE - odd * 64, 128)
        window = ref[row, pl.ds(column, 384)]
        turned = pltpu.roll(window, 64 if offset else 320, 1)
        return jnp.where((odd == 1) if offset else (odd == 0), window, turned)

    for source, ref in enumerate((own_ref, other_ref)):

        def body(step, carry, source=source, ref=ref):
            part = step // 10
            row = pl.ds(pl.multiple_of(step * rows, rows), rows)
            target = pl.multiple_of(part * PLANE + source * (PLANE // 2) + (step - part * 10) * rows, rows)
            for group, planes in enumerate((NEAR, MIDDLE, FAR)):
                for at in range(0, len(planes), 2):
                    a = plane_of(ref, row, planes[at], False)
                    if at + 1 < len(planes):
                        b = plane_of(ref, row, planes[at + 1], True)
                        middle = jnp.where(lane < 64, a[:, 256:], b[:, :128])
                        whole = jnp.concatenate([a[:, :256], middle, b[:, 128:]], axis=1)
                    else:
                        whole = jnp.concatenate([a[:, :256], jnp.where(lane < 64, a[:, 256:], 0.0)], axis=1)
                    top, rest = split(whole)
                    columns = slice(at * PLANE, at * PLANE + whole.shape[1])
                    outs[2 * group][pl.ds(target, rows), columns] = top
                    outs[2 * group + 1][pl.ds(target, rows), columns] = rest
            return carry

        lax.fori_loop(0, 20, body, 0)


def screen_call(place, own, other):
    shapes = [
        jax.ShapeDtypeStruct((2 * own.shape[0], padded(planes)), jnp.bfloat16)
        for planes in (NEAR, MIDDLE, FAR)
        for _ in range(2)
    ]
    return pl.pallas_call(
        screen_kernel,
        out_shape=shapes,
        in_specs=[SMEM, VMEM, VMEM],
        out_specs=[VMEM] * 6,
        compiler_params=params(20),
        name="screen",
    )(place, own, other)


def left_kernel(place, *refs):
    pieces, (high_ref, low_ref, work) = refs[:8], refs[8:]
    x = place[1]
    span = pieces[0].shape[0] // 2
    for core in range(2):
        for shift in range(4):
            shard = lax.rem(x - shift + 4, 4)
            for part in range(2):
                row = pl.multiple_of(part * 8 * span + core * 4 * span + shard * span, 8)
                work[pl.ds(row, span), :] = pieces[core * 4 + shift][part * span : (part + 1) * span, :]

    def body(block, carry):
        at = pl.ds(pl.multiple_of(block * 128, 128), 128)
        high_ref[at, :], low_ref[at, :] = split(work[:, at].T)
        return carry

    lax.fori_loop(0, work.shape[1] // 128, body, 0)


def left_call(place, pieces):
    depth, width = pieces[0].shape
    shape = jax.ShapeDtypeStruct((width, 8 * depth), jnp.bfloat16)
    return pl.pallas_call(
        left_kernel,
        out_shape=(shape, shape),
        in_specs=[SMEM] + [VMEM] * 8,
        out_specs=(VMEM, VMEM),
        scratch_shapes=[pltpu.VMEM((8 * depth, width), jnp.float32)],
        compiler_params=params(20),
        name="left",
    )(place, *pieces)


def load_right(place, runs, planes, high, low):
    y = place[2]
    for delta, ref, start, first, count in runs:
        spread = lax.rem(y + delta, 4) * SPAN

        def body(step, carry, ref=ref, start=start, first=first, spread=spread):
            unit = first + step
            row = pl.ds(pl.multiple_of(unit // 2 * PLANE + spread, 16), SPAN)
            column = pl.ds(pl.multiple_of(lax.rem(unit, 2) * HALF, HALF), HALF)
            top, rest = split(ref[pl.ds(pl.multiple_of(start + step * SPAN, 8), SPAN), :])
            high[row, column] = top
            low[row, column] = rest
            return carry

        lax.fori_loop(0, count, body, 0)
    used = planes * PLANE
    if used < high.shape[0]:
        for ref in (high, low):
            ref[used:, :] = jnp.zeros((ref.shape[0] - used, ref.shape[1]), ref.dtype)


def near_runs(first, first_down, first_up, second, second_down, second_up, two_down, two_up):
    skip = 3 * SPAN
    return (
        ((0, first, 0, 0, 6), (3, first_down, 0, 0, 6), (1, first_up, 0, 0, 6))
        + ((0, second, 0, 6, 4), (3, second_down, 0, 6, 4), (1, second_up, 0, 6, 4))
        + ((2, two_down, 0, 0, 3), (2, two_up, 0, 3, 3), (2, two_down, skip, 6, 2), (2, two_up, skip, 8, 2))
    )


def middle_runs(z_below, z_above, y_below, y_above):
    runs = ()
    for first, sides, across in ((0, z_below, y_below), (2, z_above, y_above)):
        runs += ((3, sides, 0, first, 2), (1, sides, 2 * SPAN, first, 2), (0, sides, 4 * SPAN, first, 2))
        runs += ((2, across, 0, first, 2),)
    return runs


def far_runs(below, above, across_low, across_high):
    return (
        ((3, below, 0, 0, 2), (1, above, 0, 0, 2), (0, below, 2 * SPAN, 0, 1), (0, above, 2 * SPAN, 1, 1))
        + ((2, across_low, 0, 0, 1), (2, across_high, 0, 1, 1))
    )


def group_kernel(runs, planes, place, *refs):
    count = len(refs) - 5 - (runs is middle_runs)
    rights, (high_ref, low_ref), rest = refs[:count], refs[count : count + 2], refs[count + 2 :]
    out_ref, rh, rl = rest[-3:]
    load_right(place, runs(*rights), planes, rh, rl)
    value = dot3(high_ref[...], low_ref[...], rh[...], rl[...])
    out_ref[...] = value if len(rest) == 3 else value + rest[0][...]


def group_call(runs, planes, place, rights, screens, total):
    rows, width = screens[0].shape
    return pl.pallas_call(
        functools.partial(group_kernel, runs, planes),
        out_shape=jax.ShapeDtypeStruct((rows, 2 * HALF), jnp.float32),
        in_specs=[SMEM] + [VMEM] * (len(rights) + 2 + len(total)),
        out_specs=VMEM,
        scratch_shapes=[pltpu.VMEM((width, 2 * HALF), jnp.bfloat16)] * 2,
        compiler_params=params(32),
        name="group",
    )(place, *rights, *screens, *total)


def pair_kernel(place, table, *refs):
    rights, (high_ref, low_ref, sum_ref, left_high, left_low, give_ref, kern, rh, rl) = refs[:4], refs[4:]
    load_right(place, far_runs(*rights), len(FAR), rh, rl)
    product = sum_ref[...] + dot3(high_ref[...], low_ref[...], rh[...], rl[...])
    mid = product.shape[0] // 2
    real = product[:mid, :HALF] - product[mid:, HALF:]
    imag = product[mid:, :HALF] + product[:mid, HALF:]
    applied = NG ** (-0.5) * jnp.concatenate(
        [jnp.concatenate([real, imag], axis=0), jnp.concatenate([imag, -real], axis=0)], axis=1
    )
    kern[...] = dot3(left_high[...], left_low[...], *split(applied))

    extract(place, table, 1 - place[3], kern, give_ref)


def extract(place, table, half, kern, out_ref):
    at = lambda x: lax.rem(x + 4 - place[1], 4)
    lane = lax.broadcasted_iota(jnp.int32, (BLK, 128), 1) // BLK
    upper = lax.broadcasted_iota(jnp.int32, (8, 128), 0) < 4

    def groups(pair, carry):
        for g in (pair * 2, pair * 2 + 1):
            slabs = [None, None]
            for u in range(8):
                slot = g * 8 + u
                row = pl.ds(pl.multiple_of(table[4 * half, slot], BLK), BLK)
                column = pl.multiple_of(table[4 * half + 1, slot], 128)
                shift = table[4 * half + 2, slot]
                target = lane == table[4 * half + 3, slot]
                for part in range(2):
                    slab = pltpu.roll(kern[row, pl.ds(column + part * HALF, 128)], shift, 1)
                    slabs[part] = jnp.where(target, slab, 0.0 if u == 0 else slabs[part])
            lanes = pl.ds(pl.multiple_of(g * 128, 128), 128)
            for side in range(2):
                real, imag = (slab[side * 8 : side * 8 + 8] for slab in slabs)
                out_ref[at(2 * side), :, lanes] = jnp.where(upper, real, pltpu.roll(imag, 4, 0))
                out_ref[at(2 * side + 1), :, lanes] = jnp.where(upper, pltpu.roll(real, 4, 0), imag)
        return carry

    out_ref[...] = jnp.zeros_like(out_ref)
    lax.fori_loop(0, (table[11, half] + 1) // 2, groups, 0)


def pair_call(place, table, rights, screens, total, left_high, left_low):
    rows = left_high.shape[0]
    return pl.pallas_call(
        pair_kernel,
        out_shape=(
            jax.ShapeDtypeStruct((4, 8, ROOM * BLK), jnp.float32),
            jax.ShapeDtypeStruct((rows, 2 * HALF), jnp.float32),
        ),
        in_specs=[SMEM, SMEM] + [VMEM] * (len(rights) + 5),
        out_specs=(VMEM, VMEM),
        scratch_shapes=[pltpu.VMEM((screens[0].shape[1], 2 * HALF), jnp.bfloat16)] * 2,
        compiler_params=params(24),
        name="pair",
    )(place, table, *rights, *screens, total, left_high, left_low)


def extract_kernel(place, table, kern, out_ref):
    extract(place, table, place[3], kern, out_ref)


def extract_call(place, table, kern):
    return pl.pallas_call(
        extract_kernel,
        out_shape=jax.ShapeDtypeStruct((4, 8, ROOM * BLK), jnp.float32),
        in_specs=[SMEM, SMEM, VMEM],
        out_specs=VMEM,
        compiler_params=params(8),
        name="extract",
    )(place, table, kern)


def add_kernel(one_ref, two_ref, *outs):
    for at, out_ref in enumerate(outs):
        out_ref[...] = one_ref[at] + two_ref[at]


def add_call(one, two):
    return pl.pallas_call(
        add_kernel,
        out_shape=[jax.ShapeDtypeStruct(one.shape[1:], one.dtype)] * one.shape[0],
        in_specs=[VMEM, VMEM],
        out_specs=[VMEM] * one.shape[0],
        compiler_params=params(8),
        name="add",
    )(one, two)


def owner_kernel(place, table, one_ref, two_ref, three_ref, four_ref, out_ref, work):
    total = (one_ref[...] + two_ref[...]) + (three_ref[...] + four_ref[...])
    width = total.shape[1]
    work[:, :width] = total
    work[:, width:] = jnp.zeros((8, work.shape[1] - width), jnp.float32)
    for chip in range(out_ref.shape[0]):
        start = table[8, chip * 2 + place[3]]
        column = pl.multiple_of(start // 8 * 128, 128)
        shift = lax.rem(384 - lax.rem(start, 8) * BLK, 384)
        out_ref[chip] = pltpu.roll(work[:, pl.ds(column, 384)], shift, 1)[:, :256]


def owner_call(place, table, parts):
    return pl.pallas_call(
        owner_kernel,
        out_shape=jax.ShapeDtypeStruct((32, 8, 256), jnp.float32),
        in_specs=[SMEM, SMEM] + [VMEM] * 4,
        out_specs=VMEM,
        scratch_shapes=[pltpu.VMEM((8, parts[0].shape[1] + 384), jnp.float32)],
        compiler_params=params(8),
        name="owner",
    )(place, table, *parts)


def last_kernel(place, table, parts_ref, out_ref):
    total = parts_ref[0]
    for chip in range(1, parts_ref.shape[0]):
        total = total + parts_ref[chip]
    held = table[9, (place[0] * 4 + place[2]) * 2 + place[3]]
    for slot in range(CAP):
        tile = total[:, slot // 8 * 128 : slot // 8 * 128 + 128]
        tile = pltpu.roll(tile, (128 - slot % 8 * BLK) % 128, 1)
        out_ref[slot] = jnp.where(slot < held, tile[:, :BLK], 0.0)


def last_call(place, table, parts):
    return pl.pallas_call(
        last_kernel,
        out_shape=jax.ShapeDtypeStruct((CAP, 8, BLK), jnp.float32),
        in_specs=[SMEM, SMEM, VMEM],
        out_specs=VMEM,
        compiler_params=params(8),
        name="last",
    )(place, table, parts)


def pack_kernel(place, own_ref, other_ref, out_ref, work):
    core = place[3]
    width = own_ref.shape[2]
    for block in range(width // 128):
        lanes = pl.ds(block * 128, 128)
        rows = []
        for part in range(2):
            own, other = own_ref[part, :, lanes], other_ref[part, :, lanes]
            rows += [jnp.where(core == 0, own, other), jnp.where(core == 0, other, own)]
        rows = jnp.concatenate(rows + rows, axis=0)
        work[block * 128 : (block + 1) * 128, :] = rows.T
    half = lax.broadcasted_iota(jnp.int32, (8, 128), 1) < 64
    for chip in range(32):
        at = pl.multiple_of(chip * 80 + core * 40, 8)
        tiles = [work[pl.ds(at + 8 * t, 8), :] for t in range(5)]
        out_ref[chip * 20 : chip * 20 + 8, :] = jnp.where(half, tiles[0], tiles[1])
        out_ref[chip * 20 + 8 : chip * 20 + 16, :] = jnp.where(half, tiles[2], tiles[3])
        last = jnp.where(half, tiles[4], pltpu.roll(tiles[4], 4, 0))
        out_ref[chip * 20 + 16 : chip * 20 + 20, :] = last[:4]


def pack_call(place, own, other):
    width = own.shape[2]
    return pl.pallas_call(
        pack_kernel,
        out_shape=jax.ShapeDtypeStruct((32 * 20, 128), jnp.float32),
        in_specs=[SMEM, VMEM, VMEM],
        out_specs=VMEM,
        scratch_shapes=[pltpu.VMEM((width, 128), jnp.float32)],
        name="pack",
    )(place, own, other)


def unpack_kernel(place, table, in_ref, columns_ref, keep_ref, give_ref):
    core = place[3]
    quarter = lax.broadcasted_iota(jnp.int32, (8, 128), 1) // 32
    upper = lax.broadcasted_iota(jnp.int32, (8, 128), 0) < 4
    for group in range(8):
        tiles = [[None] * 5 for _ in range(2)]
        for u in range(4):
            at = (group * 4 + u) * 20
            one, two = in_ref[at : at + 8, :], in_ref[at + 8 : at + 16, :]
            end = in_ref[at + 12 : at + 20, :]
            end = jnp.where(upper, pltpu.roll(end, 4, 0), pltpu.roll(end, 64, 1))
            for t, (source, first) in enumerate(((one, 0), (one, 64), (two, 0), (two, 64), (end, 0))):
                for part in range(2):
                    by = (u * 32 - first - part * 32) % 128
                    turned = pltpu.roll(source, by, 1) if by else source
                    old = tiles[part][t]
                    tiles[part][t] = turned if old is None else jnp.where(quarter == u, turned, old)
        for part in range(2):
            for t in range(5):
                row = part * 40 + t * 8
                columns_ref[row : row + 8, group * 128 : (group + 1) * 128] = tiles[part][t]
    select(table, 1 - core, columns_ref, give_ref)
    select(table, core, columns_ref, keep_ref)


def select(table, which, columns_ref, out_ref):
    eighth = lax.broadcasted_iota(jnp.int32, (80, 128), 1) // BLK
    for group in range(2):
        slab = None
        for u in range(8):
            block = table[10, which * (USED // 2) + group * 8 + u]
            column = pl.multiple_of(block // 8 * 128, 128)
            by = lax.rem(u * BLK + 128 - lax.rem(block, 8) * BLK, 128)
            turned = pltpu.roll(columns_ref[:, pl.ds(column, 128)], by, 1)
            slab = turned if slab is None else jnp.where(eighth == u, turned, slab)
        out_ref[:, group * 128 : (group + 1) * 128] = slab


def unpack_call(place, table, pieces):
    return pl.pallas_call(
        unpack_kernel,
        out_shape=(
            jax.ShapeDtypeStruct((80, 1024), jnp.float32),
            jax.ShapeDtypeStruct((80, HALF), jnp.float32),
            jax.ShapeDtypeStruct((80, HALF), jnp.float32),
        ),
        in_specs=[SMEM, SMEM, VMEM],
        out_specs=(VMEM, VMEM, VMEM),
        compiler_params=params(8),
        name="unpack",
    )(place, table, pieces)


def shard_kernel(place, keep_ref, take_ref, out_ref):
    core = place[3]
    for part in range(2):
        out_ref[pl.ds(pl.multiple_of(part * 80 + core * 40, 8), 40), :] = keep_ref[part * 40 : part * 40 + 40, :]
        out_ref[pl.ds(pl.multiple_of(part * 80 + 40 - core * 40, 8), 40), :] = take_ref[part * 40 : part * 40 + 40, :]


def shard_call(place, keep, take):
    return pl.pallas_call(
        shard_kernel,
        out_shape=jax.ShapeDtypeStruct((160, HALF), jnp.float32),
        in_specs=[SMEM, VMEM, VMEM],
        out_specs=VMEM,
        compiler_params=params(8),
        name="shard",
    )(place, keep, take)


def after(array, *others):
    return lax.optimization_barrier((array, *others))[0]


def shards(densities, screened, pairs, owners):
    span = screened.shape[2]
    place = jnp.stack([lax.axis_index(axis) for axis in ("z", "x", "y", "core")]).astype(jnp.int32)
    shift = lambda array, axis, by: lax.ppermute(array, axis, ring(lax.axis_size(axis), by))
    swap = lambda array: lax.ppermute(array, "core", SWAP)
    join = lambda *arrays: jnp.concatenate(arrays, axis=0)
    hold = lax.optimization_barrier

    pieces = pack_call(place, densities, swap(densities))
    table = plan_call(place, after(pairs, pieces), owners.reshape(1, -1))
    mine = lax.all_to_all(pieces.reshape(32, 1, -1), ("z", "y"), 0, 0, tiled=True).reshape(pieces.shape)

    screen = screened.reshape(2 * 4 * span, -1)
    mine, other = hold((mine, swap(after(screen, pieces))))

    columns, keep, give = unpack_call(place, table, mine)
    shard = shard_call(place, keep, swap(give))

    block = 2 * SPAN
    below2, above2 = shift(shard, "z", 2), shift(shard, "z", -2)
    below, above, columns = hold((shift(shard, "z", 1), shift(shard, "z", -1), columns))
    first = join(shard, below, above)
    first_down, first_up = shift(first, "y", 1), shift(first, "y", -1)
    around = [columns, shift(columns, "x", 1), None, None]
    below2, above2, first, columns = hold((below2, above2, first, columns))
    second = join(below2, above2)
    second_down, second_up = shift(second, "y", 1), shift(second, "y", -1)
    around[3] = shift(columns, "x", 3)
    screens = screen_call(place, after(screen, second), other)
    first_down, first_up, around[1], below2, above2, *screens = hold(
        (first_down, first_up, around[1], below2, above2, *screens)
    )
    around[2] = shift(after(columns, first_down), "x", 2)
    second_down, second_up, first_down, around[3] = hold((second_down, second_up, first_down, around[3]))

    z_below = shift(join(second_down[:block], second_up[:block], second[:block]), "z", 1)
    z_above = shift(join(second_down[block:], second_up[block:], second[block:]), "z", -1)
    two_down = shift(join(first_down[: 3 * SPAN], second_down[:block]), "y", 1)
    two_up = shift(join(first_up[3 * SPAN :], second_up[block:]), "y", -1)
    swapped = [swap(columns), swap(around[1]), None, None]
    two_down, two_up, z_below, z_above, around[2], swapped[0], swapped[1] = hold(
        (two_down, two_up, z_below, z_above, around[2], swapped[0], swapped[1])
    )

    y_below, y_above = shift(z_below[:block], "y", 1), shift(z_above[block : 2 * block], "y", -1)
    far_below = shift(join(z_below[:block], z_below[2 * block : 2 * block + SPAN]), "z", 1)
    far_above = shift(join(z_above[block : 2 * block], z_above[2 * block + SPAN :]), "z", -1)
    rights = (first, first_down, first_up, second, second_down, second_up, two_down, two_up)
    total = group_call(near_runs, len(NEAR), place, rights, screens[:2], ())
    swapped[2:] = [swap(array) for array in around[2:]]
    y_below, y_above, far_below, far_above, total, *swapped[2:] = hold(
        (y_below, y_above, far_below, far_above, total, *swapped[2:])
    )

    across_low, across_high = shift(far_below[:SPAN], "y", 1), shift(far_above[SPAN : 2 * SPAN], "y", -1)
    rights = (z_below, z_above, y_below, y_above)
    total = group_call(middle_runs, len(MIDDLE), place, rights, screens[2:4], (total,))
    left_high, left_low = left_call(place, around + swapped)
    across_low, across_high, total, left_high, left_low = hold((across_low, across_high, total, left_high, left_low))
    rights = (far_below, far_above, across_low, across_high)
    give, kern = pair_call(place, table, rights, screens[4:], total, left_high, left_low)

    parts = add_call(extract_call(place, table, kern), swap(give))
    parts = [parts[0]] + [shift(parts[by], "x", by) for by in (1, 2, 3)]
    parts = owner_call(place, table, parts)
    parts = lax.all_to_all(parts, ("z", "y"), 0, 0, tiled=True)
    return last_call(place, table, parts).reshape(1, CAP, 2, 4, BLK)


def solution(mesh):
    fine = Mesh(mesh.devices.reshape(8, 4, 2, 4), ("z", "y", "core", "x"))
    in_specs = (P(None, BAND, "x"), P(None, None, BAND, "x"), P(), P())
    out_specs = P(BAND, None, None, "x", None)
    return jax.shard_map(shards, mesh=fine, in_specs=in_specs, out_specs=out_specs, check_vma=False)
```
